32 devices in a mesh: dp: 16 (over z, x, core), head: 2 (over y).
Axes of the slice: x: 2, y: 2, z: 4, core: 2. Of those that a mesh axis runs over, the one named last changes fastest.
Arguments:
- tokens: bfloat16 [32, 392, 768], P('dp', 'head'), may hold values from -6 to 6
- ln1_gain: float32 [768], replicated, may hold values from 0.5 to 1.5
- ln1_bias: float32 [768], replicated, may hold values from -1.75 to 1.75
- w_qkv: bfloat16 [768, 3, 768], P(None, None, 'head'), may hold values from -0.21875 to 0.21875
- pool_q: float32 [27, 96], replicated, may hold values from -1.25 to 1.25
- pool_k: float32 [27, 96], replicated, may hold values from -1.25 to 1.25
- pool_v: float32 [27, 96], replicated, may hold values from -1.25 to 1.25
- squeeze_k: float32 [27, 96], replicated, may hold values from -1.25 to 1.25
- squeeze_v: float32 [27, 96], replicated, may hold values from -1.25 to 1.25
- rel_t: float32 [15, 96], replicated, may hold values from -0.375 to 0.375
- rel_h: float32 [13, 96], replicated, may hold values from -0.375 to 0.375
- rel_w: float32 [13, 96], replicated, may hold values from -0.375 to 0.375
- w_proj: bfloat16 [768, 768], P('head'), may hold values from -0.21875 to 0.21875
- proj_bias: float32 [768], replicated, may hold values from -1.75 to 1.75
- ln2_gain: float32 [768], replicated, may hold values from 0.5 to 1.5
- ln2_bias: float32 [768], replicated, may hold values from -1.75 to 1.75
- w_fc1: bfloat16 [768, 3072], P(None, 'head'), may hold values from -0.21875 to 0.21875
- fc1_bias: float32 [3072], P('head'), may hold values from -1.75 to 1.75
- w_fc2: bfloat16 [3072, 768], P('head'), may hold values from -0.109375 to 0.109375
- fc2_bias: float32 [768], replicated, may hold values from -1.75 to 1.75
- memory_valid: int32 [32, 2], P('dp'), may hold values from 0 to 1, as said below
- cotangent: bfloat16 [32, 392, 768], P('dp', 'head'), may hold values from -6 to 6
Outputs:
- output: bfloat16 [32, 392, 768], P('dp', 'head')
- grad_tokens: float32 [32, 392, 768], P('dp', 'head')
- grad_ln1_gain: float32 [768], replicated
- grad_ln1_bias: float32 [768], replicated
- grad_w_qkv: float32 [768, 3, 768], P(None, None, 'head')
- grad_pool_q: float32 [27, 96], replicated
- grad_pool_k: float32 [27, 96], replicated
- grad_pool_v: float32 [27, 96], replicated
- grad_squeeze_k: float32 [27, 96], replicated
- grad_squeeze_v: float32 [27, 96], replicated
- grad_rel_t: float32 [15, 96], replicated
- grad_rel_h: float32 [13, 96], replicated
- grad_rel_w: float32 [13, 96], replicated
- grad_w_proj: float32 [768, 768], P('head')
- grad_proj_bias: float32 [768], replicated
- grad_ln2_gain: float32 [768], replicated
- grad_ln2_bias: float32 [768], replicated
- grad_w_fc1: float32 [768, 3072], P(None, 'head')
- grad_fc1_bias: float32 [3072], P('head')
- grad_w_fc2: float32 [3072, 768], P('head')
- grad_fc2_bias: float32 [768], replicated
The draws below stay inside these ranges and needn't reach their ends.
Inputs may be any that keep to these rules, and one draw needn't show every extreme that they name: Videos are runs of 1 to 12 consecutive clips starting at clip 0; memory_valid[c, s] is 1 exactly when clip c - 1 - s exists and belongs to the same video as clip c.
All inputs are finite; a program needn't handle non-finite values.
Results may differ from the reference program's by a relative error of at most 0.012.
The reference program's roundings to bfloat16 on the way count: a program that leaves them out, or rounds other values in their place, can miss the bound.
Values may be sent and summed in bfloat16 or wider, within the bound.
A program may use at most 320 MiB of HBM per device.

```python
import jax
import jax.numpy as jnp
from jax import lax

HEAD_DIM = 96
HEADS = 8
D = 768
MLP = 3072
T_LEN = 8
HGT = 7
WID = 7
L = 392
M = 196
CLIP_DEV = 2
CLIPS = 32


def draw_memory_valid(key, part):
    lengths = jax.random.randint(key, (CLIPS,), 1, 13)
    bounds = jnp.cumsum(lengths)
    clip_at = jnp.arange(CLIPS, dtype=jnp.int32)
    starts = jnp.max(jnp.where(bounds[None, :] <= clip_at[:, None], bounds[None, :], 0), axis=1)
    slots = jnp.arange(2, dtype=jnp.int32)
    return (clip_at[:, None] - 1 - slots[None, :] >= starts[:, None]).astype(jnp.int32)


def steps_of(key, shape, split, least, top_value):
    level = 1.0
    for dim, shards_of in split:
        heights = jax.random.uniform(jax.random.fold_in(jax.random.fold_in(key, 6), dim), (shards_of,), jnp.float32, least / len(split), top_value / len(split))
        level = level * jnp.repeat(jnp.exp(heights), shape[dim] // shards_of).reshape((-1,) + (1,) * (len(shape) - 1 - dim))
    return level


def scatter_about(own_key, dims, deviation, bound, split=(), held_as=jnp.bfloat16):
    factor_of = steps_of(own_key, dims, split, -0.22, 0.18) if split else 1.0
    drawn = jax.random.normal(own_key, dims, jnp.float32) * deviation * factor_of
    return jnp.minimum(jnp.maximum(drawn, -bound), bound).astype(held_as)


def setup_inputs(seed: int = 0) -> dict:
    keys = jax.random.split(jax.random.key(seed), 23)
    tokens = scatter_about(keys[0], (CLIPS, L, D), 1.0, 6.0, ((0, 16), (1, 2)))
    ln1_gain = jnp.clip(1.0 + 0.1 * jax.random.normal(keys[1], (D,), jnp.float32), 0.5, 1.5)
    ln1_bias = scatter_about(keys[2], (D,), 0.3, 1.75, (), jnp.float32)
    w_qkv = scatter_about(keys[3], (D, 3, D), D ** -0.5, 0.21875, ((2, 2),))
    pool_q = scatter_about(keys[4], (27, HEAD_DIM), 27 ** -0.5, 1.25, (), jnp.float32)
    pool_k = scatter_about(keys[5], (27, HEAD_DIM), 27 ** -0.5, 1.25, (), jnp.float32)
    pool_v = scatter_about(keys[6], (27, HEAD_DIM), 27 ** -0.5, 1.25, (), jnp.float32)
    squeeze_k = scatter_about(keys[7], (27, HEAD_DIM), 27 ** -0.5, 1.25, (), jnp.float32)
    squeeze_v = scatter_about(keys[8], (27, HEAD_DIM), 27 ** -0.5, 1.25, (), jnp.float32)
    rel_t = scatter_about(keys[9], (2 * T_LEN - 1, HEAD_DIM), 0.06, 0.375, (), jnp.float32)
    rel_h = scatter_about(keys[10], (2 * HGT - 1, HEAD_DIM), 0.06, 0.375, (), jnp.float32)
    rel_w = scatter_about(keys[11], (2 * WID - 1, HEAD_DIM), 0.06, 0.375, (), jnp.float32)
    w_proj = scatter_about(keys[12], (D, D), D ** -0.5, 0.21875, ((0, 2),))
    proj_bias = scatter_about(keys[13], (D,), 0.3, 1.75, (), jnp.float32)
    ln2_gain = jnp.clip(1.0 + 0.1 * jax.random.normal(keys[14], (D,), jnp.float32), 0.5, 1.5)
    ln2_bias = scatter_about(keys[15], (D,), 0.3, 1.75, (), jnp.float32)
    w_fc1 = scatter_about(keys[16], (D, MLP), D ** -0.5, 0.21875, ((1, 2),))
    fc1_bias = scatter_about(keys[17], (MLP,), 0.3, 1.75, ((0, 2),), jnp.float32)
    w_fc2 = scatter_about(keys[18], (MLP, D), MLP ** -0.5, 0.109375, ((0, 2),))
    fc2_bias = scatter_about(keys[19], (D,), 0.3, 1.75, (), jnp.float32)
    memory_valid = draw_memory_valid(jax.random.fold_in(keys[22], 71), 0)
    cotangent = scatter_about(keys[21], (CLIPS, L, D), 1.0, 6.0, ((0, 16), (1, 2)))
    return dict(tokens=tokens, ln1_gain=ln1_gain, ln1_bias=ln1_bias, w_qkv=w_qkv, pool_q=pool_q, pool_k=pool_k, pool_v=pool_v, squeeze_k=squeeze_k, squeeze_v=squeeze_v, rel_t=rel_t, rel_h=rel_h, rel_w=rel_w, w_proj=w_proj, proj_bias=proj_bias, ln2_gain=ln2_gain, ln2_bias=ln2_bias, w_fc1=w_fc1, fc1_bias=fc1_bias, w_fc2=w_fc2, fc2_bias=fc2_bias, memory_valid=memory_valid, cotangent=cotangent)


EPSILON = 1e-06
HIGHEST = lax.Precision.HIGHEST

@jax.custom_vjp
def low(v):
    return lax.optimization_barrier(v.astype(jnp.bfloat16)).astype(jnp.float32)

@jax.custom_vjp
def low_back(v):
    return v

def low_keep(v):
    return (low(v), None)

def low_pass(kept, grad):
    return (grad,)

def back_keep(v):
    return (v, None)

def back_low(kept, grad):
    return (low(grad),)
low.defvjp(low_keep, low_pass)
low_back.defvjp(back_keep, back_low)

def layer_norm(values, scaling, offset):
    average = lax.optimization_barrier(jnp.mean(values, axis=-1, keepdims=True))
    centred = values - average
    variance = lax.optimization_barrier(jnp.mean(centred * centred, axis=-1, keepdims=True))
    return centred * lax.rsqrt(variance + EPSILON) * scaling + offset

def depthwise(volume, kernel, stride):
    channels = volume.shape[-1]
    tiled = jnp.tile(kernel, (1, channels // kernel.shape[-1]))
    padded = jnp.pad(volume, ((0, 0), (1, 1), (1, 1), (1, 1), (0, 0)))
    time_count = volume.shape[1]
    row_count = volume.shape[2]
    column_count = volume.shape[3]
    time_out = (time_count - 1) // stride + 1
    summed = jnp.zeros((volume.shape[0], time_out, row_count, column_count, channels), jnp.float32)
    for depth_tap in range(3):
        for row_tap in range(3):
            for column_tap in range(3):
                window = padded[:, depth_tap:depth_tap + stride * (time_out - 1) + 1:stride, row_tap:row_tap + row_count, column_tap:column_tap + column_count, :]
                summed = summed + window * tiled[depth_tap * 9 + row_tap * 3 + column_tap]
    return summed

def offsets(length):
    places = jnp.arange(length, dtype=jnp.int32)
    distance = places[:, None] - places[None, :] + length - 1
    entries = jnp.arange(2 * length - 1, dtype=jnp.int32)
    return (distance[:, :, None] == entries[None, None, :]).astype(jnp.float32)

def relative_bias(queries, rel_t, rel_h, rel_w):
    clip_count = queries.shape[0]
    head_count = queries.shape[2]
    gridded = queries.reshape(clip_count, T_LEN, HGT, WID, head_count, HEAD_DIM)
    along_t = jnp.einsum('athwnd,jd->athwnj', gridded, rel_t, precision=HIGHEST)
    along_t = jnp.einsum('athwnj,tsj->anthws', along_t, offsets(T_LEN), precision=HIGHEST)
    along_h = jnp.einsum('athwnd,jd->athwnj', gridded, rel_h, precision=HIGHEST)
    along_h = jnp.einsum('athwnj,hsj->anthws', along_h, offsets(HGT), precision=HIGHEST)
    along_w = jnp.einsum('athwnd,jd->athwnj', gridded, rel_w, precision=HIGHEST)
    along_w = jnp.einsum('athwnj,wsj->anthws', along_w, offsets(WID), precision=HIGHEST)
    summed = along_t[..., :, None, None] + along_h[..., None, :, None] + along_w[..., None, None, :]
    return summed.reshape(clip_count, head_count, L, L)

def attend(queries, own_keys, own_values, memory_keys, memory_values, key_valid, rel_t, rel_h, rel_w):
    clip_count = queries.shape[0]
    heads_q = queries.reshape(clip_count, L, HEADS, HEAD_DIM)
    all_keys = jnp.concatenate([own_keys, memory_keys], axis=1).reshape(clip_count, L + 2 * M, HEADS, HEAD_DIM)
    all_values = jnp.concatenate([own_values, memory_values], axis=1).reshape(clip_count, L + 2 * M, HEADS, HEAD_DIM)
    scores = jnp.einsum('alnd,amnd->anlm', heads_q, all_keys, precision=HIGHEST) * HEAD_DIM ** (-0.5)
    position_bias = relative_bias(heads_q, rel_t, rel_h, rel_w)
    padding = jnp.zeros((clip_count, HEADS, L, 2 * M), jnp.float32)
    scores = scores + jnp.concatenate([position_bias, padding], axis=-1)
    scores = jnp.where(key_valid[:, None, None, :], scores, -1e+30)
    scores = low_back(scores)
    weights = low(jax.nn.softmax(scores, axis=-1))
    attended = jnp.einsum('anlm,amnd->alnd', weights, all_values, precision=HIGHEST) + heads_q
    return attended.reshape(clip_count, L, D)

def reference(tokens, ln1_gain, ln1_bias, w_qkv, pool_q, pool_k, pool_v, squeeze_k, squeeze_v, rel_t, rel_h, rel_w, w_proj, proj_bias, ln2_gain, ln2_bias, w_fc1, fc1_bias, w_fc2, fc2_bias, memory_valid, cotangent):
    own_valid = jnp.ones((CLIPS, L), dtype=bool)
    slot_valid = jnp.repeat(memory_valid > 0, M, axis=1)
    key_valid = jnp.concatenate([own_valid, slot_valid], axis=1)
    pooling = jax.checkpoint(depthwise, static_argnums=(2,))

    def regroup(array):
        return array.reshape((CLIPS // CLIP_DEV, CLIP_DEV) + array.shape[1:])

    def forward(inputs, ln1_gain, ln1_bias, w_qkv, pool_q, pool_k, pool_v, squeeze_k, squeeze_v, rel_t, rel_h, rel_w, w_proj, proj_bias, ln2_gain, ln2_bias, w_fc1, fc1_bias, w_fc2, fc2_bias):
        normed = low(layer_norm(inputs, ln1_gain, ln1_bias))
        qkv_out = jnp.einsum('ald,dke->kale', normed, w_qkv, precision=HIGHEST)
        grid_shape = (CLIPS, T_LEN, HGT, WID, D)
        queries = pooling(low_back(qkv_out[0]).reshape(grid_shape), pool_q, 1)
        key_field = pooling(low_back(qkv_out[1]).reshape(grid_shape), pool_k, 1)
        value_field = pooling(low_back(qkv_out[2]).reshape(grid_shape), pool_v, 1)
        memory_k = low(pooling(key_field, squeeze_k, 2)).reshape(CLIPS, M, D)
        memory_v = low(pooling(value_field, squeeze_v, 2)).reshape(CLIPS, M, D)
        queries = low(queries).reshape(CLIPS, L, D)
        key_field = low(key_field).reshape(CLIPS, L, D)
        value_field = low(value_field).reshape(CLIPS, L, D)
        padding = jnp.zeros((2, M, D), jnp.float32)
        extended_k = jnp.concatenate([padding, memory_k], axis=0)
        extended_v = jnp.concatenate([padding, memory_v], axis=0)
        slots_k = jnp.concatenate([extended_k[1:-1], extended_k[:-2]], axis=1)
        slots_v = jnp.concatenate([extended_v[1:-1], extended_v[:-2]], axis=1)

        def group_step(pieces):
            x_group, q_group, k_group, v_group, mk_group, mv_group, mask_group = pieces
            attended = attend(q_group, k_group, v_group, mk_group, mv_group, mask_group, rel_t, rel_h, rel_w)
            branch = low(low_back(attended))
            middle = x_group + low_back(jnp.einsum('ale,ef->alf', branch, w_proj, precision=HIGHEST)) + proj_bias
            second = low(layer_norm(middle, ln2_gain, ln2_bias))
            hidden = low_back(jnp.einsum('ald,df->alf', second, w_fc1, precision=HIGHEST)) + fc1_bias
            active = low(jax.nn.gelu(hidden, approximate=True))
            return middle + low_back(jnp.einsum('alf,fd->ald', active, w_fc2, precision=HIGHEST)) + fc2_bias
        stacked = lax.map(jax.checkpoint(group_step), (regroup(inputs), regroup(queries), regroup(key_field), regroup(value_field), regroup(slots_k), regroup(slots_v), regroup(key_valid)))
        return stacked.reshape(CLIPS, L, D)
    floats = (tokens.astype(jnp.float32), ln1_gain.astype(jnp.float32), ln1_bias.astype(jnp.float32), w_qkv.astype(jnp.float32), pool_q.astype(jnp.float32), pool_k.astype(jnp.float32), pool_v.astype(jnp.float32), squeeze_k.astype(jnp.float32), squeeze_v.astype(jnp.float32), rel_t.astype(jnp.float32), rel_h.astype(jnp.float32), rel_w.astype(jnp.float32), w_proj.astype(jnp.float32), proj_bias.astype(jnp.float32), ln2_gain.astype(jnp.float32), ln2_bias.astype(jnp.float32), w_fc1.astype(jnp.float32), fc1_bias.astype(jnp.float32), w_fc2.astype(jnp.float32), fc2_bias.astype(jnp.float32))
    outputs, pullback = jax.vjp(forward, *floats)
    gradients = pullback(cotangent.astype(jnp.float32))
    return (outputs.astype(jnp.bfloat16), gradients[0], gradients[1], gradients[2], gradients[3], gradients[4], gradients[5], gradients[6], gradients[7], gradients[8], gradients[9], gradients[10], gradients[11], gradients[12], gradients[13], gradients[14], gradients[15], gradients[16], gradients[17], gradients[18], gradients[19])
```

```python
from functools import partial

import jax
import jax.numpy as jnp
import numpy as np
from jax import lax
from jax.experimental import pallas as pl
from jax.experimental.pallas import tpu as pltpu
from jax.sharding import PartitionSpec as P

HEAD_DIM = 96
T_LEN = 8
HGT = 7
WID = 7
PADW = 8
L = 392
ROWS = T_LEN * HGT * PADW
TM = 4
MROWS = TM * HGT * PADW
KEYS = ROWS + 2 * MROWS
LH = 4
LW = LH * HEAD_DIM
WIN = 256
BLOCK = 128
NBLOCK = KEYS // BLOCK

EPSILON = 1e-06
HIGHEST = lax.Precision.HIGHEST
SCALE = HEAD_DIM ** (-0.5)
LOG2E = 1.4426950408889634
F32 = jnp.float32
BF16 = jnp.bfloat16
VMEM_LIMIT = 56 * 1024 * 1024

NB = T_LEN + HGT + WID
NREL = 2 * T_LEN - 1 + 2 * HGT - 1 + 2 * WID - 1
NPAIR = T_LEN * T_LEN + HGT * HGT + WID * WID


def params(**extra):
    return pltpu.CompilerParams(vmem_limit_bytes=VMEM_LIMIT, **extra)


def window_of(head):
    return 0 if head < 2 else BLOCK


def slot_of(head):
    return 192 if head < 2 else 0


def position_constants():
    t, h, w = np.meshgrid(np.arange(T_LEN), np.arange(HGT), np.arange(PADW), indexing="ij")
    t, h, w = t.ravel(), h.ravel(), w.ravel()
    valid = w < WID
    own = np.zeros((256, ROWS), np.float32)
    pick = np.zeros((256, NREL), np.float32)
    fold = np.zeros((256, 32), np.float32)
    ekey = np.zeros((32, KEYS), np.float32)
    row = 0
    base_entry = 0
    base_bias = 0
    for places, length in ((t, T_LEN), (h, HGT), (w, WID)):
        for a in range(length):
            for b in range(length):
                own[row] = (places == a) & valid
                pick[row, base_entry + a - b + length - 1] = 1
                fold[row, base_bias + b] = 1
                row += 1
        for b in range(length):
            ekey[base_bias + b, :ROWS] = (places == b) & valid
        base_entry += 2 * length - 1
        base_bias += length
    return own, pick, fold, ekey, valid


OWN_T, PICK, FOLD, EKEY, ROW_VALID = position_constants()


def fold_constants():
    out = np.zeros((2, 2, 256, WIN), np.float32)
    for variant, slot in enumerate((192, 0)):
        out[variant, 0, :, slot : slot + 32] = FOLD
        out[variant, 1, :, slot + 32 : slot + 64] = FOLD
    return out


def one_lane():
    out = np.zeros((2, 8, WIN), np.float32)
    for variant, slot in enumerate((192, 0)):
        out[variant, :, slot + NB] = 1
    return out


def head_lanes():
    out = np.zeros((LH, ROWS, WIN), np.float32)
    for head in range(LH):
        first = head * HEAD_DIM - window_of(head)
        out[head, :, first : first + HEAD_DIM] = 1
    return out


def key_constants(memory_valid):
    clip_count = memory_valid.shape[0]
    base = np.zeros((2, KEYS, WIN), np.float32)
    lane = np.zeros((2, 1, WIN), np.float32)
    for variant, slot in enumerate((192, 0)):
        base[variant, :, slot : slot + 32] = EKEY.T
        base[variant, :, slot + 32 : slot + 64] = EKEY.T
        lane[variant, :, slot + NB] = 1
    pads = np.concatenate([ROW_VALID, ROW_VALID[:MROWS], ROW_VALID[:MROWS]])
    use = jnp.concatenate(
        [jnp.ones((clip_count, ROWS), bool), jnp.repeat(memory_valid > 0, MROWS, axis=1)], axis=1
    )
    drop = jnp.where(use & jnp.asarray(pads)[None], 0.0, -1e30).astype(F32)
    return (jnp.asarray(base)[None] + drop[:, None, :, None] * jnp.asarray(lane)[None]).astype(BF16)


def nt(a, b):
    return lax.dot_general(a, b, (((1,), (1,)), ((), ())), preferred_element_type=F32)


def nn(a, b):
    return jnp.dot(a, b, preferred_element_type=F32)


def keep_rows(block):
    place = lax.broadcasted_iota(jnp.int32, block.shape, block.ndim - 2)
    return jnp.where(place < WID, block, 0.0)


def spread(dst, first, value):
    n, _, _, c = value.shape
    flat = value.reshape(n * HGT, PADW, c)
    dst[0, pl.ds(first, n), 1 : HGT + 1] = pltpu.roll(flat, 1, axis=1).reshape(n, HGT, PADW, c)
    dst[1, pl.ds(first, n), 1 : HGT + 1] = value
    dst[2, pl.ds(first, n), 1 : HGT + 1] = pltpu.roll(flat, PADW - 1, axis=1).reshape(n, HGT, PADW, c)


def pool_forward(squeeze, *refs):
    if squeeze:
        a_ref, w_ref, k_ref, s_ref, x0_ref, xp_ref, xf_ref, m_ref, xs, ys = refs
    else:
        a_ref, w_ref, k_ref, x0_ref, xp_ref, xs = refs

    @pl.when((pl.program_id(0) == 0) & (pl.program_id(1) == 0))
    def _():
        xs[...] = jnp.zeros_like(xs)
        if squeeze:
            ys[...] = jnp.zeros_like(ys)

    x = nn(a_ref[0], w_ref[0])
    x0_ref[0, 0] = x
    spread(xs, 1, x.reshape(T_LEN, HGT, PADW, LW))
    for tile in range(LW // 128):
        lanes = slice(tile * 128, tile * 128 + 128)

        def step(pair, _):
            acc = [jnp.zeros((HGT, PADW, 128), F32) for _ in range(2)]
            for a in range(3):
                for c in range(3):
                    for d in range(2):
                        block = xs[c, 2 * pair + d + a, :, :, lanes]
                        for b in range(3):
                            acc[d] = acc[d] + k_ref[0, a * 9 + b * 3 + c, :, lanes][None] * block[b : b + HGT]
            both = keep_rows(jnp.stack(acc))
            rows = pl.ds(pl.multiple_of(pair * 112, 112), 112)
            flat = both.reshape(112, 128)
            xp_ref[0, 0, rows, lanes] = flat.astype(BF16)
            if squeeze:
                xf_ref[0, 0, rows, lanes] = flat
                both = both.reshape(2 * HGT, PADW, 128)
                for c, shift in ((0, 1), (1, 0), (2, PADW - 1)):
                    moved = pltpu.roll(both, shift, axis=1) if shift else both
                    ys[c, pl.ds(2 * pair + 1, 2), 1 : HGT + 1, :, lanes] = moved.reshape(2, HGT, PADW, 128)
            return 0

        lax.fori_loop(0, T_LEN // 2, step, 0)
        if squeeze:

            def squeeze_step(pair, _):
                acc = [jnp.zeros((HGT, PADW, 128), F32) for _ in range(2)]
                for a in range(3):
                    for c in range(3):
                        for d in range(2):
                            block = ys[c, 4 * pair + 2 * d + a, :, :, lanes]
                            for b in range(3):
                                acc[d] = acc[d] + s_ref[0, a * 9 + b * 3 + c, :, lanes][None] * block[b : b + HGT]
                rows = pl.ds(pl.multiple_of(pair * 112, 112), 112)
                m_ref[0, 0, rows, lanes] = keep_rows(jnp.stack(acc)).reshape(112, 128).astype(BF16)
                return 0

            lax.fori_loop(0, TM // 2, squeeze_step, 0)


def call_pool_forward(rows, weights, kernels, squeezes=None):
    clips = rows.shape[0]
    count = weights.shape[0]
    squeeze = squeezes is not None
    tap = pl.BlockSpec((1, 27, 8, LW), lambda j, i: (j, 0, 0, 0))

    def out(n):
        return pl.BlockSpec((1, 1, n, LW), lambda j, i: (i, j, 0, 0))

    frame = pltpu.VMEM((3, T_LEN + 2, HGT + 2, PADW, LW), F32)
    shapes = [
        jax.ShapeDtypeStruct((clips, count, ROWS, LW), F32),
        jax.ShapeDtypeStruct((clips, count, ROWS, LW), BF16),
    ]
    specs = [out(ROWS), out(ROWS)]
    if squeeze:
        shapes += [
            jax.ShapeDtypeStruct((clips, count, ROWS, LW), F32),
            jax.ShapeDtypeStruct((clips, count, MROWS, LW), BF16),
        ]
        specs += [out(ROWS), out(MROWS)]
    return pl.pallas_call(
        partial(pool_forward, squeeze),
        grid=(count, clips),
        in_specs=[
            pl.BlockSpec((1, ROWS, rows.shape[2]), lambda j, i: (i, 0, 0)),
            pl.BlockSpec((1, weights.shape[1], LW), lambda j, i: (j, 0, 0)),
            tap,
        ]
        + ([tap] if squeeze else []),
        out_specs=specs,
        out_shape=shapes,
        scratch_shapes=[frame] * (2 if squeeze else 1),
        compiler_params=params(),
        cost_estimate=pl.CostEstimate(
            flops=60_000_000_000 * count // 10, bytes_accessed=4_000_000 * count, transcendentals=0
        ),
    )(rows, weights, kernels, *([squeezes] if squeeze else []))


def pool_backward(squeeze, *refs):
    if squeeze:
        u_ref, x0_ref, k_ref, m_ref, xf_ref, s_ref, dx_ref, dk_ref, ds_ref, us, ms = refs
    else:
        u_ref, x0_ref, k_ref, dx_ref, dk_ref, us = refs

    @pl.when((pl.program_id(0) == 0) & (pl.program_id(1) == 0))
    def _():
        us[...] = jnp.zeros_like(us)
        if squeeze:
            ms[...] = jnp.zeros_like(ms)

    @pl.when(pl.program_id(1) == 0)
    def _():
        dk_ref[...] = jnp.zeros_like(dk_ref)
        if squeeze:
            ds_ref[...] = jnp.zeros_like(ds_ref)

    if squeeze:
        spread(ms, 0, m_ref[0, 0].reshape(TM, HGT, PADW, LW))
    else:
        spread(us, 1, u_ref[0].reshape(T_LEN, HGT, PADW, LW))
    for tile in range(LW // 128):
        lanes = slice(tile * 128, tile * 128 + 128)
        if squeeze:

            def squeeze_step(pair, _):
                rows = pl.ds(pl.multiple_of(pair * 112, 112), 112)
                own = u_ref[0, rows, lanes].reshape(2, HGT, PADW, 128)
                fields = xf_ref[0, 0, rows, lanes].reshape(2, HGT, PADW, 128)
                acc = [own[0], own[1]]
                for a, d, frame in ((1, 0, 0), (0, 1, 1), (2, 1, 0)):
                    for c in range(3):
                        block = ms[2 - c, pair + frame, :, :, lanes]
                        for b in range(3):
                            at = block[2 - b : 2 - b + HGT]
                            number = a * 9 + b * 3 + c
                            acc[d] = acc[d] + s_ref[0, number, :, lanes][None] * at
                            ds_ref[0, number, :, lanes] += jnp.sum(fields[d] * at, axis=0)
                both = keep_rows(jnp.stack(acc)).reshape(2 * HGT, PADW, 128)
                for c, shift in ((0, 1), (1, 0), (2, PADW - 1)):
                    moved = pltpu.roll(both, shift, axis=1) if shift else both
                    us[c, pl.ds(2 * pair + 1, 2), 1 : HGT + 1, :, lanes] = moved.reshape(2, HGT, PADW, 128)
                return 0

            lax.fori_loop(0, TM, squeeze_step, 0)

        def step(pair, _):
            rows = pl.ds(pl.multiple_of(pair * 112, 112), 112)
            fields = x0_ref[0, 0, rows, lanes].reshape(2, HGT, PADW, 128)
            acc = [jnp.zeros((HGT, PADW, 128), F32) for _ in range(2)]
            for a in range(3):
                for c in range(3):
                    sums = [jnp.zeros((PADW, 128), F32) for _ in range(3)]
                    for d in range(2):
                        block = us[2 - c, 2 * pair + d + 2 - a, :, :, lanes]
                        for b in range(3):
                            at = block[2 - b : 2 - b + HGT]
                            acc[d] = acc[d] + k_ref[0, a * 9 + b * 3 + c, :, lanes][None] * at
                            sums[b] = sums[b] + jnp.sum(fields[d] * at, axis=0)
                    for b in range(3):
                        dk_ref[0, a * 9 + b * 3 + c, :, lanes] += sums[b]
            both = keep_rows(jnp.stack(acc))
            dx_ref[0, 0, rows, lanes] = both.reshape(112, 128).astype(BF16)
            return 0

        lax.fori_loop(0, T_LEN // 2, step, 0)


def call_pool_backward(upstream, fields, kernels, memory=None, pooled=None, squeezes=None):
    clips, count = fields.shape[:2]
    squeeze = memory is not None
    tap = pl.BlockSpec((1, 27, 8, LW), lambda j, i: (j, 0, 0, 0))

    def block(n):
        return pl.BlockSpec((1, 1, n, LW), lambda j, i: (i, j, 0, 0))

    grads = jax.ShapeDtypeStruct((count, 27, 8, LW), F32)
    frame = pltpu.VMEM((3, T_LEN + 2, HGT + 2, PADW, LW), F32)
    in_specs = [
        pl.BlockSpec((1, ROWS, LW), lambda j, i: (i, 0, j)),
        block(ROWS),
        tap,
    ]
    args = [upstream, fields, kernels]
    shapes = [jax.ShapeDtypeStruct((clips, count, ROWS, LW), BF16), grads]
    specs = [block(ROWS), tap]
    scratch = [frame]
    if squeeze:
        in_specs += [block(MROWS), block(ROWS), tap]
        args += [memory, pooled, squeezes]
        shapes.append(grads)
        specs.append(tap)
        scratch += [
            pltpu.VMEM((3, TM + 1, HGT + 2, PADW, LW), F32),
        ]
    return pl.pallas_call(
        partial(pool_backward, squeeze),
        grid=(count, clips),
        in_specs=in_specs,
        out_specs=specs,
        out_shape=shapes,
        scratch_shapes=scratch,
        compiler_params=params(),
        cost_estimate=pl.CostEstimate(
            flops=12_000_000_000 * count, bytes_accessed=6_000_000 * count, transcendentals=0
        ),
    )(*args)


def attention_forward(
    q_ref, kv_ref, m1_ref, m2_ref, ke_ref, tab_ref, fold_ref, one_ref, own_ref, lanes_ref,
    branch_ref, qa_ref, at_ref, lse_ref, keys, vt, scores, expo,
):
    keys[0:ROWS] = kv_ref[0, 0]
    keys[ROWS : ROWS + MROWS] = m1_ref[0, 0]
    keys[ROWS + MROWS :] = m2_ref[0, 0]
    vt[:, 0:ROWS] = kv_ref[0, 1].T
    memory = jnp.concatenate([m1_ref[0, 1], m2_ref[0, 1]], axis=0).T
    vt[:, ROWS:] = memory
    for head in range(LH):
        first = window_of(head)
        variant = head // 2
        win = slice(first, first + WIN)
        heads = lanes_ref[head]
        qm = q_ref[0, 0, :, win] * heads
        raw = nn(qm, tab_ref[head, 0]) + nn(qm, tab_ref[head, 1])
        raw = raw * own_ref[...]
        high = raw.astype(BF16)
        rest = (raw - high.astype(F32)).astype(BF16)
        placed = nn(high, fold_ref[variant, 0]) + nn(rest, fold_ref[variant, 1]) + one_ref[variant, 0:1]
        qa = qm + placed.astype(BF16)
        qa_ref[0, head] = qa

        def score(number, peak):
            rows = pl.ds(pl.multiple_of(number * BLOCK, BLOCK), BLOCK)
            ka = keys[rows, win] * heads[0:BLOCK] + ke_ref[0, variant, rows]
            s = nt(ka, qa)
            scores[rows] = s
            return jnp.maximum(peak, jnp.max(s, axis=0, keepdims=True))

        peak = lax.fori_loop(0, NBLOCK, score, jnp.full((1, ROWS), -3e38, F32))
        shift = peak * (SCALE * LOG2E)

        def soften(number, total):
            rows = pl.ds(pl.multiple_of(number * BLOCK, BLOCK), BLOCK)
            e = jnp.exp2(scores[rows] * (SCALE * LOG2E) - shift)
            expo[rows] = e.astype(BF16)
            return total + jnp.sum(e, axis=0, keepdims=True)

        total = lax.fori_loop(0, NBLOCK, soften, jnp.zeros((1, ROWS), F32))
        out = nn(vt[head * HEAD_DIM : (head + 1) * HEAD_DIM], expo[...]) * (1.0 / total)
        at_ref[0, head * HEAD_DIM : (head + 1) * HEAD_DIM] = out
        lse_ref[0, head : head + 1] = shift + jnp.log2(total)
    branch_ref[0] = (at_ref[0].T + q_ref[0, 0].astype(F32)).astype(BF16)


def whole(shape):
    return pl.BlockSpec(shape, lambda i: (0,) * len(shape))


def clip_block(*shape):
    return pl.BlockSpec((1,) + shape, lambda i: (i,) + (0,) * len(shape))


def call_attention_forward(q, kv, memory, keys_extra, tables, consts):
    clips = q.shape[0]
    return pl.pallas_call(
        attention_forward,
        grid=(clips,),
        in_specs=[
            clip_block(1, ROWS, LW),
            clip_block(2, ROWS, LW),
            pl.BlockSpec((1, 2, MROWS, LW), lambda i: (i + 1, 0, 0, 0)),
            pl.BlockSpec((1, 2, MROWS, LW), lambda i: (i, 0, 0, 0)),
            clip_block(2, KEYS, WIN),
            whole((LH, 2, WIN, 256)),
            whole((2, 2, 256, WIN)),
            whole((2, 8, WIN)),
            whole((ROWS, 256)),
            whole((LH, ROWS, WIN)),
        ],
        out_specs=[
            clip_block(ROWS, LW),
            clip_block(LH, ROWS, WIN),
            clip_block(LW, ROWS),
            clip_block(8, ROWS),
        ],
        out_shape=[
            jax.ShapeDtypeStruct((clips, ROWS, LW), BF16),
            jax.ShapeDtypeStruct((clips, LH, ROWS, WIN), BF16),
            jax.ShapeDtypeStruct((clips, LW, ROWS), F32),
            jax.ShapeDtypeStruct((clips, 8, ROWS), F32),
        ],
        scratch_shapes=[
            pltpu.VMEM((KEYS, LW), BF16),
            pltpu.VMEM((LW, KEYS), BF16),
            pltpu.VMEM((KEYS, ROWS), F32),
            pltpu.VMEM((KEYS, ROWS), BF16),
        ],
        compiler_params=params(),
        cost_estimate=pl.CostEstimate(
            flops=20_000_000_000, bytes_accessed=10_000_000, transcendentals=3_000_000
        ),
    )(q, kv, memory, memory, keys_extra, tables, consts["fold"], consts["one"], consts["own"], consts["lanes"])


def attention_backward(
    q_ref, kv_ref, m1_ref, m2_ref, ke_ref, qa_ref, dm_ref, at_ref, lse_ref, rt_ref, grow_ref, ownt_ref, ekey_ref,
    lanes_ref, dq_ref, dkv_ref, dr_ref, keys, values, kt, dmt, qms, dms, dqt,
):
    @pl.when(pl.program_id(0) == 0)
    def _():
        dr_ref[...] = jnp.zeros_like(dr_ref)

    keys[0:ROWS] = kv_ref[0, 0]
    keys[ROWS : ROWS + MROWS] = m1_ref[0, 0]
    keys[ROWS + MROWS :] = m2_ref[0, 0]
    values[0:ROWS] = kv_ref[0, 1]
    values[ROWS : ROWS + MROWS] = m1_ref[0, 1]
    values[ROWS + MROWS :] = m2_ref[0, 1]
    kt[0:LW] = keys[...].T
    kt[LW:] = ekey_ref[...]
    dmt[...] = dm_ref[0].astype(F32).T
    dqt[...] = jnp.zeros_like(dqt)
    deltas = []
    for head in range(LH):
        first = window_of(head)
        win = slice(first, first + WIN)
        span = slice(head * HEAD_DIM, (head + 1) * HEAD_DIM)
        qms[head] = q_ref[0, 0, :, win] * lanes_ref[head]
        dms[head] = dm_ref[0, :, win] * lanes_ref[head]
        deltas.append(jnp.sum(dmt[span] * at_ref[0, span], axis=0, keepdims=True))

    def step(number, _):
        rows = pl.ds(pl.multiple_of(number * BLOCK, BLOCK), BLOCK)
        dk_parts, dv_parts = [], []
        for head in range(LH):
            first = window_of(head)
            variant = head // 2
            win = slice(first, first + WIN)
            ka = keys[rows, win] * lanes_ref[head, 0:BLOCK] + ke_ref[0, variant, rows]
            s = nt(ka, qa_ref[0, head])
            p = jnp.exp2(s * (SCALE * LOG2E) - lse_ref[0, head : head + 1])
            dp = nt(values[rows, win], dms[head])
            ds = (p * (dp - deltas[head])).astype(BF16)
            dv_parts.append(nn(p.astype(BF16), dms[head]))
            dk_parts.append(nn(ds, qms[head]) * SCALE)
            kts = jnp.concatenate(
                [kt[head * HEAD_DIM : (head + 1) * HEAD_DIM, rows], kt[LW:, rows]], axis=0
            )
            dqt[head] += nn(kts, ds)
        for which, parts in ((0, dk_parts), (1, dv_parts)):
            full = jnp.concatenate(
                [
                    parts[0][:, 0:128] + parts[1][:, 0:128],
                    parts[1][:, 128:256] + parts[2][:, 0:128],
                    parts[2][:, 128:256] + parts[3][:, 128:256],
                ],
                axis=1,
            )
            both[which, rows] = full
        return 0

    both = dkv_ref.at[0]
    lax.fori_loop(0, NBLOCK, step, 0)
    for head in range(LH):
        first = window_of(head)
        span = slice(head * HEAD_DIM, (head + 1) * HEAD_DIM)
        total = dqt[head]
        grown = nn(grow_ref[...], total[HEAD_DIM:].astype(BF16)) * ownt_ref[...]
        grown = grown.astype(BF16)
        dmt[span] = dmt[span] + total[0:HEAD_DIM] * SCALE + nn(rt_ref[...], grown)
        dr_ref[:, first : first + WIN] += nn(grown, qms[head])
    dq_ref[0] = dmt[...].T


def call_attention_backward(q, kv, memory, keys_extra, qa, dmix, at, lse, rt, consts):
    clips = q.shape[0]
    return pl.pallas_call(
        attention_backward,
        grid=(clips,),
        in_specs=[
            clip_block(1, ROWS, LW),
            clip_block(2, ROWS, LW),
            pl.BlockSpec((1, 2, MROWS, LW), lambda i: (i + 1, 0, 0, 0)),
            pl.BlockSpec((1, 2, MROWS, LW), lambda i: (i, 0, 0, 0)),
            clip_block(2, KEYS, WIN),
            clip_block(LH, ROWS, WIN),
            clip_block(ROWS, LW),
            clip_block(LW, ROWS),
            clip_block(8, ROWS),
            whole((HEAD_DIM, 256)),
            whole((256, 32)),
            whole((256, ROWS)),
            whole((32, KEYS)),
            whole((LH, ROWS, WIN)),
        ],
        out_specs=[
            clip_block(ROWS, LW),
            clip_block(2, KEYS, LW),
            whole((256, LW)),
        ],
        out_shape=[
            jax.ShapeDtypeStruct((clips, ROWS, LW), F32),
            jax.ShapeDtypeStruct((clips, 2, KEYS, LW), F32),
            jax.ShapeDtypeStruct((256, LW), F32),
        ],
        scratch_shapes=[
            pltpu.VMEM((KEYS, LW), BF16),
            pltpu.VMEM((KEYS, LW), BF16),
            pltpu.VMEM((LW + 32, KEYS), BF16),
            pltpu.VMEM((LW, ROWS), F32),
            pltpu.VMEM((LH, ROWS, WIN), BF16),
            pltpu.VMEM((LH, ROWS, WIN), BF16),
            pltpu.VMEM((LH, HEAD_DIM + 32, ROWS), F32),
        ],
        compiler_params=params(),
        cost_estimate=pl.CostEstimate(
            flops=40_000_000_000, bytes_accessed=20_000_000, transcendentals=3_000_000
        ),
    )(
        q, kv, memory, memory, keys_extra, qa, dmix, at, lse, rt,
        consts["grow"], consts["ownt"], consts["ekey"], consts["lanes"],
    )


def from_behind(x, axis, by):
    count = lax.axis_size(axis)
    pairs = [(i, i + by) for i in range(count) if 0 <= i + by < count]
    return lax.ppermute(x, axis, pairs)


def layer_norm(values, scaling, offset):
    average = jnp.mean(values, axis=-1, keepdims=True)
    centred = values - average
    variance = jnp.mean(centred * centred, axis=-1, keepdims=True)
    return centred * lax.rsqrt(variance + EPSILON) * scaling + offset


def pad_rows(x):
    lead = x.shape[0]
    frames = x.shape[1] // (HGT * WID)
    grid = x.reshape(lead, frames, HGT, WID, x.shape[-1])
    grid = jnp.pad(grid, ((0, 0), (0, 0), (0, 0), (0, PADW - WID), (0, 0)))
    return grid.reshape(lead, frames * HGT * PADW, x.shape[-1])


def drop_rows(x):
    lead = x.shape[0]
    frames = x.shape[1] // (HGT * PADW)
    grid = x.reshape(lead, frames, HGT, PADW, x.shape[-1])[:, :, :, :WID]
    return grid.reshape(lead, frames * HGT * WID, x.shape[-1])


def swap(x):
    return lax.ppermute(x, "head", [(0, 1), (1, 0)])


def gather_rows(x):
    return lax.all_gather(x, "head", axis=1, tiled=True)


def scatter_sum(x):
    half = x.shape[1] // 2
    mine = lax.axis_index("head") * half
    theirs = half - mine
    sent = lax.dynamic_slice_in_dim(x, theirs, half, axis=1).astype(BF16)
    kept = lax.dynamic_slice_in_dim(x, mine, half, axis=1)
    return kept + swap(sent).astype(F32)


def taps(kernel):
    return jnp.broadcast_to(jnp.tile(kernel, (1, LH))[:, None, :], (27, 8, LW))


def on_device(
    tokens,
    ln1_gain,
    ln1_bias,
    w_qkv,
    pool_q,
    pool_k,
    pool_v,
    squeeze_k,
    squeeze_v,
    rel_t,
    rel_h,
    rel_w,
    w_proj,
    proj_bias,
    ln2_gain,
    ln2_bias,
    w_fc1,
    fc1_bias,
    w_fc2,
    fc2_bias,
    memory_valid,
    cotangent,
):
    clip_count = tokens.shape[0]
    consts = {
        "fold": jnp.asarray(fold_constants(), BF16),
        "one": jnp.asarray(one_lane(), F32),
        "own": jnp.asarray(OWN_T.T, F32),
        "ownt": jnp.asarray(OWN_T, F32),
        "lanes": jnp.asarray(head_lanes(), BF16),
        "grow": jnp.asarray(FOLD, BF16),
        "ekey": jnp.asarray(EKEY, BF16),
    }
    keys_extra = key_constants(memory_valid)
    rel_all = jnp.concatenate([rel_t, rel_h, rel_w], axis=0)
    pairs = jnp.dot(jnp.asarray(PICK), rel_all, precision=HIGHEST)
    pair_table = (pairs * HEAD_DIM**0.5).T
    table_high = pair_table.astype(BF16)
    table_rest = (pair_table - table_high.astype(F32)).astype(BF16)
    tables = jnp.stack(
        [
            jnp.stack(
                [
                    jnp.pad(
                        part,
                        (
                            (head * HEAD_DIM - window_of(head), WIN - HEAD_DIM - head * HEAD_DIM + window_of(head)),
                            (0, 0),
                        ),
                    )
                    for part in (table_high, table_rest)
                ]
            )
            for head in range(LH)
        ]
    )
    rel_rows = pairs.T.astype(BF16)
    tap_q, tap_kv = taps(pool_q)[None], jnp.stack([taps(pool_k), taps(pool_v)])
    tap_s = jnp.stack([taps(squeeze_k), taps(squeeze_v)])

    inputs = pad_rows(tokens).astype(F32)
    upstream_low = pad_rows(cotangent)
    real = (jnp.arange(inputs.shape[1]) % PADW < WID)[None, :, None]
    first_normed, first_pull = jax.vjp(layer_norm, inputs, ln1_gain, ln1_bias)
    first_rows = gather_rows(jnp.where(real, first_normed, 0.0).astype(BF16))
    w_heads = w_qkv.transpose(1, 0, 2)
    kv0, kv, kvf, mem = call_pool_forward(first_rows, w_heads[1:], tap_kv, tap_s)
    before = from_behind(mem[-2:], "dp", 1)
    q0, q = call_pool_forward(first_rows, w_heads[:1], tap_q)
    memory = jnp.concatenate([before, mem], axis=0)
    branch, qa, at, lse = call_attention_forward(q, kv, memory, keys_extra, tables, consts)
    partial_z = jnp.einsum("ale,ef->alf", branch, w_proj, preferred_element_type=F32)
    middle = inputs + scatter_sum(partial_z) + proj_bias
    second_normed, second_pull = jax.vjp(layer_norm, middle, ln2_gain, ln2_bias)
    second_rows = gather_rows(second_normed.astype(BF16))
    hidden = jnp.einsum("ald,df->alf", second_rows, w_fc1, preferred_element_type=F32) + fc1_bias
    active, gelu_pull = jax.vjp(partial(jax.nn.gelu, approximate=True), hidden)
    active_low = active.astype(BF16)
    partial_m = jnp.einsum("alf,fd->ald", active_low, w_fc2, preferred_element_type=F32)
    output = drop_rows((middle + scatter_sum(partial_m) + fc2_bias).astype(BF16))
    upstream = upstream_low.astype(F32)
    fc2_bias_grad = jnp.sum(upstream, axis=(0, 1))
    upstream_rows = gather_rows(upstream_low)
    w_fc2_grad = jnp.einsum("alf,ald->fd", active_low, upstream_rows, preferred_element_type=F32)
    (hidden_grad,) = gelu_pull(
        jnp.einsum("ald,fd->alf", upstream_rows, w_fc2, preferred_element_type=F32)
    )
    fc1_bias_grad = jnp.sum(hidden_grad, axis=(0, 1))
    hidden_low = hidden_grad.astype(BF16)
    w_fc1_grad = jnp.einsum("ald,alf->df", second_rows, hidden_low, preferred_element_type=F32)
    partial_second = jnp.einsum("alf,df->ald", hidden_low, w_fc1, preferred_element_type=F32)
    middle_part, ln2_gain_grad, ln2_bias_grad = second_pull(scatter_sum(partial_second))
    middle_grad = middle_part + upstream
    proj_bias_grad = jnp.sum(middle_grad, axis=(0, 1))
    middle_rows = gather_rows(middle_grad.astype(BF16))
    w_proj_grad = jnp.einsum("ale,alf->ef", branch, middle_rows, preferred_element_type=F32)
    dmix = jnp.einsum("alf,ef->ale", middle_rows, w_proj, preferred_element_type=F32).astype(BF16)

    w_fc2_grad, w_fc1_grad, w_proj_grad = lax.psum(
        (w_fc2_grad.astype(BF16), w_fc1_grad.astype(BF16), w_proj_grad.astype(BF16)), "dp"
    )
    dq, dkv, dr = call_attention_backward(
        q, kv, memory, keys_extra, qa, dmix, at, lse, rel_rows, consts
    )
    slots = dkv[:, :, ROWS:]
    near, far = slots[:, :, :MROWS], slots[:, :, MROWS:]
    zero = jnp.zeros((1,) + near.shape[1:], F32)
    spread_out = jnp.concatenate([zero, near, zero], axis=0) + jnp.concatenate([far, zero, zero], axis=0)
    later = from_behind(spread_out[:2].astype(BF16), "dp", -1).astype(F32)
    dq0, pool_q_grad = call_pool_backward(dq, q0, tap_q)
    leading = jnp.zeros((clip_count - 2,) + near.shape[1:], F32)
    dmem = spread_out[2:] + jnp.concatenate([leading, later], axis=0)
    own = dkv[:, :, :ROWS].transpose(0, 2, 1, 3).reshape(clip_count, ROWS, 2 * LW)
    dkv0, pool_kv_grad, squeeze_grad = call_pool_backward(own, kv0, tap_kv, dmem, kvf, tap_s)
    qkv_grad = jnp.concatenate([dq0, dkv0], axis=1)
    w_qkv_grad = jnp.einsum("ald,akle->dke", first_rows, qkv_grad, preferred_element_type=F32)
    w_qkv_grad = lax.psum(w_qkv_grad.astype(BF16), "dp")
    partial_first = jnp.einsum("akle,dke->ald", qkv_grad, w_qkv, preferred_element_type=F32)
    input_part, ln1_gain_grad, ln1_bias_grad = first_pull(scatter_sum(partial_first))
    input_grad = drop_rows(middle_grad + input_part)

    def tap_grad(g):
        return jnp.sum(jnp.sum(g, axis=1).reshape(27, LH, HEAD_DIM), axis=1)

    pair_grad = jnp.sum(dr.reshape(256, LH, HEAD_DIM), axis=1)
    rel_grad = jnp.dot(jnp.asarray(PICK.T), pair_grad, precision=HIGHEST)
    shared = lax.psum(
        (
            ln1_gain_grad,
            ln1_bias_grad,
            tap_grad(pool_q_grad[0]),
            tap_grad(pool_kv_grad[0]),
            tap_grad(pool_kv_grad[1]),
            tap_grad(squeeze_grad[0]),
            tap_grad(squeeze_grad[1]),
            rel_grad[: 2 * T_LEN - 1],
            rel_grad[2 * T_LEN - 1 : 2 * T_LEN + 2 * HGT - 2],
            rel_grad[2 * T_LEN + 2 * HGT - 2 :],
            proj_bias_grad,
            ln2_gain_grad,
            ln2_bias_grad,
            fc2_bias_grad,
        ),
        ("dp", "head"),
    )
    fc1_bias_grad = lax.psum(fc1_bias_grad, "dp")
    return (
        output,
        input_grad,
        shared[0],
        shared[1],
        w_qkv_grad.astype(F32),
        shared[2],
        shared[3],
        shared[4],
        shared[5],
        shared[6],
        shared[7],
        shared[8],
        shared[9],
        w_proj_grad.astype(F32),
        shared[10],
        shared[11],
        shared[12],
        w_fc1_grad.astype(F32),
        fc1_bias_grad,
        w_fc2_grad.astype(F32),
        shared[13],
    )


def solution(mesh):
    return jax.shard_map(
        on_device,
        mesh=mesh,
        in_specs=(
            P("dp", "head", None),
            P(),
            P(),
            P(None, None, "head"),
            P(),
            P(),
            P(),
            P(),
            P(),
            P(),
            P(),
            P(),
            P("head", None),
            P(),
            P(),
            P(),
            P(None, "head"),
            P("head"),
            P("head", None),
            P(),
            P("dp", None),
            P("dp", "head", None),
        ),
        out_specs=(
            P("dp", "head", None),
            P("dp", "head", None),
            P(),
            P(),
            P(None, None, "head"),
            P(),
            P(),
            P(),
            P(),
            P(),
            P(),
            P(),
            P(),
            P("head", None),
            P(),
            P(),
            P(),
            P(None, "head"),
            P("head"),
            P("head", None),
            P(),
        ),
        check_vma=False,
    )
```

```python
from functools import partial

import jax
import jax.numpy as jnp
import numpy as np
from jax import lax
from jax.experimental import pallas as pl
from jax.experimental.pallas import tpu as pltpu
from jax.sharding import PartitionSpec as P

HEAD_DIM = 96
T_LEN = 8
HGT = 7
WID = 7
PADW = 8
L = 392
ROWS = T_LEN * HGT * PADW
TM = 4
MROWS = TM * HGT * PADW
KEYS = ROWS + 2 * MROWS
LH = 4
LW = LH * HEAD_DIM
WIN = 256
BLOCK = 128
NBLOCK = KEYS // BLOCK

EPSILON = 1e-06
HIGHEST = lax.Precision.HIGHEST
SCALE = HEAD_DIM ** (-0.5)
LOG2E = 1.4426950408889634
F32 = jnp.float32
BF16 = jnp.bfloat16
VMEM_LIMIT = 56 * 1024 * 1024

NB = T_LEN + HGT + WID
NREL = 2 * T_LEN - 1 + 2 * HGT - 1 + 2 * WID - 1
NPAIR = T_LEN * T_LEN + HGT * HGT + WID * WID


def params(**extra):
    return pltpu.CompilerParams(vmem_limit_bytes=VMEM_LIMIT, **extra)


def window_of(head):
    return 0 if head < 2 else BLOCK


def slot_of(head):
    return 192 if head < 2 else 0


def position_constants():
    t, h, w = np.meshgrid(np.arange(T_LEN), np.arange(HGT), np.arange(PADW), indexing="ij")
    t, h, w = t.ravel(), h.ravel(), w.ravel()
    valid = w < WID
    own = np.zeros((256, ROWS), np.float32)
    pick = np.zeros((256, NREL), np.float32)
    fold = np.zeros((256, 32), np.float32)
    ekey = np.zeros((32, KEYS), np.float32)
    row = 0
    base_entry = 0
    base_bias = 0
    for places, length in ((t, T_LEN), (h, HGT), (w, WID)):
        for a in range(length):
            for b in range(length):
                own[row] = (places == a) & valid
                pick[row, base_entry + a - b + length - 1] = 1
                fold[row, base_bias + b] = 1
                row += 1
        for b in range(length):
            ekey[base_bias + b, :ROWS] = (places == b) & valid
        base_entry += 2 * length - 1
        base_bias += length
    return own, pick, fold, ekey, valid


OWN_T, PICK, FOLD, EKEY, ROW_VALID = position_constants()


def fold_constants():
    out = np.zeros((2, 2, 256, WIN), np.float32)
    for variant, slot in enumerate((192, 0)):
        out[variant, 0, :, slot : slot + 32] = FOLD
        out[variant, 1, :, slot + 32 : slot + 64] = FOLD
    return out


def one_lane():
    out = np.zeros((2, 8, WIN), np.float32)
    for variant, slot in enumerate((192, 0)):
        out[variant, :, slot + NB] = 1
    return out


def head_lanes():
    out = np.zeros((LH, ROWS, WIN), np.float32)
    for head in range(LH):
        first = head * HEAD_DIM - window_of(head)
        out[head, :, first : first + HEAD_DIM] = 1
    return out


def key_constants(memory_valid):
    clip_count = memory_valid.shape[0]
    base = np.zeros((2, KEYS, WIN), np.float32)
    lane = np.zeros((2, 1, WIN), np.float32)
    for variant, slot in enumerate((192, 0)):
        base[variant, :, slot : slot + 32] = EKEY.T
        base[variant, :, slot + 32 : slot + 64] = EKEY.T
        lane[variant, :, slot + NB] = 1
    pads = np.concatenate([ROW_VALID, ROW_VALID[:MROWS], ROW_VALID[:MROWS]])
    use = jnp.concatenate(
        [jnp.ones((clip_count, ROWS), bool), jnp.repeat(memory_valid > 0, MROWS, axis=1)], axis=1
    )
    drop = jnp.where(use & jnp.asarray(pads)[None], 0.0, -1e30).astype(F32)
    return (jnp.asarray(base)[None] + drop[:, None, :, None] * jnp.asarray(lane)[None]).astype(BF16)


def nt(a, b):
    return lax.dot_general(a, b, (((1,), (1,)), ((), ())), preferred_element_type=F32)


def nn(a, b):
    return jnp.dot(a, b, preferred_element_type=F32)


def keep_rows(block):
    place = lax.broadcasted_iota(jnp.int32, block.shape, block.ndim - 2)
    return jnp.where(place < WID, block, 0.0)


def spread(dst, first, value):
    n, _, _, c = value.shape
    flat = value.reshape(n * HGT, PADW, c)
    dst[0, pl.ds(first, n), 1 : HGT + 1] = pltpu.roll(flat, 1, axis=1).reshape(n, HGT, PADW, c)
    dst[1, pl.ds(first, n), 1 : HGT + 1] = value
    dst[2, pl.ds(first, n), 1 : HGT + 1] = pltpu.roll(flat, PADW - 1, axis=1).reshape(n, HGT, PADW, c)


def pool_forward(squeeze, *refs):
    if squeeze:
        a_ref, w_ref, k_ref, s_ref, x0_ref, xp_ref, xf_ref, m_ref, xs, ys = refs
    else:
        a_ref, w_ref, k_ref, x0_ref, xp_ref, xs = refs

    @pl.when((pl.program_id(0) == 0) & (pl.program_id(1) == 0))
    def _():
        xs[...] = jnp.zeros_like(xs)
        if squeeze:
            ys[...] = jnp.zeros_like(ys)

    x = nn(a_ref[0], w_ref[0])
    x0_ref[0, 0] = x
    spread(xs, 1, x.reshape(T_LEN, HGT, PADW, LW))
    for tile in range(LW // 128):
        lanes = slice(tile * 128, tile * 128 + 128)

        def step(pair, _):
            acc = [jnp.zeros((HGT, PADW, 128), F32) for _ in range(2)]
            for a in range(3):
                for c in range(3):
                    for d in range(2):
                        block = xs[c, 2 * pair + d + a, :, :, lanes]
                        for b in range(3):
                            acc[d] = acc[d] + k_ref[0, a * 9 + b * 3 + c, :, lanes][None] * block[b : b + HGT]
            both = keep_rows(jnp.stack(acc))
            rows = pl.ds(pl.multiple_of(pair * 112, 112), 112)
            flat = both.reshape(112, 128)
            xp_ref[0, 0, rows, lanes] = flat.astype(BF16)
            if squeeze:
                xf_ref[0, 0, rows, lanes] = flat
                both = both.reshape(2 * HGT, PADW, 128)
                for c, shift in ((0, 1), (1, 0), (2, PADW - 1)):
                    moved = pltpu.roll(both, shift, axis=1) if shift else both
                    ys[c, pl.ds(2 * pair + 1, 2), 1 : HGT + 1, :, lanes] = moved.reshape(2, HGT, PADW, 128)
            return 0

        lax.fori_loop(0, T_LEN // 2, step, 0)
        if squeeze:

            def squeeze_step(pair, _):
                acc = [jnp.zeros((HGT, PADW, 128), F32) for _ in range(2)]
                for a in range(3):
                    for c in range(3):
                        for d in range(2):
                            block = ys[c, 4 * pair + 2 * d + a, :, :, lanes]
                            for b in range(3):
                                acc[d] = acc[d] + s_ref[0, a * 9 + b * 3 + c, :, lanes][None] * block[b : b + HGT]
                rows = pl.ds(pl.multiple_of(pair * 112, 112), 112)
                m_ref[0, 0, rows, lanes] = keep_rows(jnp.stack(acc)).reshape(112, 128).astype(BF16)
                return 0

            lax.fori_loop(0, TM // 2, squeeze_step, 0)


def call_pool_forward(rows, weights, kernels, squeezes=None):
    clips = rows.shape[0]
    count = weights.shape[0]
    squeeze = squeezes is not None
    tap = pl.BlockSpec((1, 27, 8, LW), lambda j, i: (j, 0, 0, 0))

    def out(n):
        return pl.BlockSpec((1, 1, n, LW), lambda j, i: (i, j, 0, 0))

    frame = pltpu.VMEM((3, T_LEN + 2, HGT + 2, PADW, LW), F32)
    shapes = [
        jax.ShapeDtypeStruct((clips, count, ROWS, LW), F32),
        jax.ShapeDtypeStruct((clips, count, ROWS, LW), BF16),
    ]
    specs = [out(ROWS), out(ROWS)]
    if squeeze:
        shapes += [
            jax.ShapeDtypeStruct((clips, count, ROWS, LW), F32),
            jax.ShapeDtypeStruct((clips, count, MROWS, LW), BF16),
        ]
        specs += [out(ROWS), out(MROWS)]
    return pl.pallas_call(
        partial(pool_forward, squeeze),
        grid=(count, clips),
        in_specs=[
            pl.BlockSpec((1, ROWS, rows.shape[2]), lambda j, i: (i, 0, 0)),
            pl.BlockSpec((1, weights.shape[1], LW), lambda j, i: (j, 0, 0)),
            tap,
        ]
        + ([tap] if squeeze else []),
        out_specs=specs,
        out_shape=shapes,
        scratch_shapes=[frame] * (2 if squeeze else 1),
        compiler_params=params(),
        cost_estimate=pl.CostEstimate(
            flops=60_000_000_000 * count // 10, bytes_accessed=4_000_000 * count, transcendentals=0
        ),
    )(rows, weights, kernels, *([squeezes] if squeeze else []))


def pool_backward(squeeze, *refs):
    if squeeze:
        u_ref, x0_ref, k_ref, m_ref, xf_ref, s_ref, dx_ref, dk_ref, ds_ref, us, ms = refs
    else:
        u_ref, x0_ref, k_ref, dx_ref, dk_ref, us = refs

    @pl.when((pl.program_id(0) == 0) & (pl.program_id(1) == 0))
    def _():
        us[...] = jnp.zeros_like(us)
        if squeeze:
            ms[...] = jnp.zeros_like(ms)

    @pl.when(pl.program_id(1) == 0)
    def _():
        dk_ref[...] = jnp.zeros_like(dk_ref)
        if squeeze:
            ds_ref[...] = jnp.zeros_like(ds_ref)

    if squeeze:
        spread(ms, 0, m_ref[0, 0].reshape(TM, HGT, PADW, LW))
    else:
        spread(us, 1, u_ref[0].reshape(T_LEN, HGT, PADW, LW))
    for tile in range(LW // 128):
        lanes = slice(tile * 128, tile * 128 + 128)
        if squeeze:

            def squeeze_step(pair, _):
                rows = pl.ds(pl.multiple_of(pair * 112, 112), 112)
                own = u_ref[0, rows, lanes].reshape(2, HGT, PADW, 128)
                fields = xf_ref[0, 0, rows, lanes].reshape(2, HGT, PADW, 128)
                acc = [own[0], own[1]]
                for a, d, frame in ((1, 0, 0), (0, 1, 1), (2, 1, 0)):
                    for c in range(3):
                        block = ms[2 - c, pair + frame, :, :, lanes]
                        for b in range(3):
                            at = block[2 - b : 2 - b + HGT]
                            number = a * 9 + b * 3 + c
                            acc[d] = acc[d] + s_ref[0, number, :, lanes][None] * at
                            ds_ref[0, number, :, lanes] += jnp.sum(fields[d] * at, axis=0)
                both = keep_rows(jnp.stack(acc)).reshape(2 * HGT, PADW, 128)
                for c, shift in ((0, 1), (1, 0), (2, PADW - 1)):
                    moved = pltpu.roll(both, shift, axis=1) if shift else both
                    us[c, pl.ds(2 * pair + 1, 2), 1 : HGT + 1, :, lanes] = moved.reshape(2, HGT, PADW, 128)
                return 0

            lax.fori_loop(0, TM, squeeze_step, 0)

        def step(pair, _):
            rows = pl.ds(pl.multiple_of(pair * 112, 112), 112)
            fields = x0_ref[0, 0, rows, lanes].reshape(2, HGT, PADW, 128)
            acc = [jnp.zeros((HGT, PADW, 128), F32) for _ in range(2)]
            for a in range(3):
                for c in range(3):
                    sums = [jnp.zeros((PADW, 128), F32) for _ in range(3)]
                    for d in range(2):
                        block = us[2 - c, 2 * pair + d + 2 - a, :, :, lanes]
                        for b in range(3):
                            at = block[2 - b : 2 - b + HGT]
                            acc[d] = acc[d] + k_ref[0, a * 9 + b * 3 + c, :, lanes][None] * at
                            sums[b] = sums[b] + jnp.sum(fields[d] * at, axis=0)
                    for b in range(3):
                        dk_ref[0, a * 9 + b * 3 + c, :, lanes] += sums[b]
            both = keep_rows(jnp.stack(acc))
            dx_ref[0, 0, rows, lanes] = both.reshape(112, 128).astype(BF16)
            return 0

        lax.fori_loop(0, T_LEN // 2, step, 0)


def call_pool_backward(upstream, fields, kernels, memory=None, pooled=None, squeezes=None):
    clips, count = fields.shape[:2]
    squeeze = memory is not None
    tap = pl.BlockSpec((1, 27, 8, LW), lambda j, i: (j, 0, 0, 0))

    def block(n):
        return pl.BlockSpec((1, 1, n, LW), lambda j, i: (i, j, 0, 0))

    grads = jax.ShapeDtypeStruct((count, 27, 8, LW), F32)
    frame = pltpu.VMEM((3, T_LEN + 2, HGT + 2, PADW, LW), F32)
    in_specs = [
        pl.BlockSpec((1, ROWS, LW), lambda j, i: (i, 0, j)),
        block(ROWS),
        tap,
    ]
    args = [upstream, fields, kernels]
    shapes = [jax.ShapeDtypeStruct((count, clips, ROWS, LW), BF16), grads]
    specs = [pl.BlockSpec((1, 1, ROWS, LW), lambda j, i: (j, i, 0, 0)), tap]
    scratch = [frame]
    if squeeze:
        in_specs += [block(MROWS), block(ROWS), tap]
        args += [memory, pooled, squeezes]
        shapes.append(grads)
        specs.append(tap)
        scratch += [
            pltpu.VMEM((3, TM + 1, HGT + 2, PADW, LW), F32),
        ]
    return pl.pallas_call(
        partial(pool_backward, squeeze),
        grid=(count, clips),
        in_specs=in_specs,
        out_specs=specs,
        out_shape=shapes,
        scratch_shapes=scratch,
        compiler_params=params(),
        cost_estimate=pl.CostEstimate(
            flops=12_000_000_000 * count, bytes_accessed=6_000_000 * count, transcendentals=0
        ),
    )(*args)


def attention_forward(
    q_ref, kv_ref, m1_ref, m2_ref, ke_ref, tab_ref, fold_ref, one_ref, own_ref, lanes_ref,
    branch_ref, qa_ref, at_ref, lse_ref, keys, vt, scores, expo,
):
    keys[0:ROWS] = kv_ref[0, 0]
    keys[ROWS : ROWS + MROWS] = m1_ref[0, 0]
    keys[ROWS + MROWS :] = m2_ref[0, 0]
    vt[:, 0:ROWS] = kv_ref[0, 1].T
    memory = jnp.concatenate([m1_ref[0, 1], m2_ref[0, 1]], axis=0).T
    vt[:, ROWS:] = memory
    for head in range(LH):
        first = window_of(head)
        variant = head // 2
        win = slice(first, first + WIN)
        heads = lanes_ref[head]
        qm = q_ref[0, 0, :, win] * heads
        raw = nn(qm, tab_ref[head, 0]) + nn(qm, tab_ref[head, 1])
        raw = raw * own_ref[...]
        high = raw.astype(BF16)
        rest = (raw - high.astype(F32)).astype(BF16)
        placed = nn(high, fold_ref[variant, 0]) + nn(rest, fold_ref[variant, 1]) + one_ref[variant, 0:1]
        qa = qm + placed.astype(BF16)
        qa_ref[0, head] = qa

        def score(number, peak):
            rows = pl.ds(pl.multiple_of(number * BLOCK, BLOCK), BLOCK)
            ka = keys[rows, win] * heads[0:BLOCK] + ke_ref[0, variant, rows]
            s = nt(ka, qa)
            scores[rows] = s
            return jnp.maximum(peak, jnp.max(s, axis=0, keepdims=True))

        peak = lax.fori_loop(0, NBLOCK, score, jnp.full((1, ROWS), -3e38, F32))
        shift = peak * (SCALE * LOG2E)

        def soften(number, total):
            rows = pl.ds(pl.multiple_of(number * BLOCK, BLOCK), BLOCK)
            e = jnp.exp2(scores[rows] * (SCALE * LOG2E) - shift)
            expo[rows] = e.astype(BF16)
            return total + jnp.sum(e, axis=0, keepdims=True)

        total = lax.fori_loop(0, NBLOCK, soften, jnp.zeros((1, ROWS), F32))
        out = nn(vt[head * HEAD_DIM : (head + 1) * HEAD_DIM], expo[...]) * (1.0 / total)
        at_ref[0, head * HEAD_DIM : (head + 1) * HEAD_DIM] = out
        lse_ref[0, head : head + 1] = shift + jnp.log2(total)
    branch_ref[0] = (at_ref[0].T + q_ref[0, 0].astype(F32)).astype(BF16)


def whole(shape):
    return pl.BlockSpec(shape, lambda i: (0,) * len(shape))


def clip_block(*shape):
    return pl.BlockSpec((1,) + shape, lambda i: (i,) + (0,) * len(shape))


def call_attention_forward(q, kv, memory, keys_extra, tables, consts):
    clips = q.shape[0]
    return pl.pallas_call(
        attention_forward,
        grid=(clips,),
        in_specs=[
            clip_block(1, ROWS, LW),
            clip_block(2, ROWS, LW),
            pl.BlockSpec((1, 2, MROWS, LW), lambda i: (i + 1, 0, 0, 0)),
            pl.BlockSpec((1, 2, MROWS, LW), lambda i: (i, 0, 0, 0)),
            clip_block(2, KEYS, WIN),
            whole((LH, 2, WIN, 256)),
            whole((2, 2, 256, WIN)),
            whole((2, 8, WIN)),
            whole((ROWS, 256)),
            whole((LH, ROWS, WIN)),
        ],
        out_specs=[
            clip_block(ROWS, LW),
            clip_block(LH, ROWS, WIN),
            clip_block(LW, ROWS),
            clip_block(8, ROWS),
        ],
        out_shape=[
            jax.ShapeDtypeStruct((clips, ROWS, LW), BF16),
            jax.ShapeDtypeStruct((clips, LH, ROWS, WIN), BF16),
            jax.ShapeDtypeStruct((clips, LW, ROWS), F32),
            jax.ShapeDtypeStruct((clips, 8, ROWS), F32),
        ],
        scratch_shapes=[
            pltpu.VMEM((KEYS, LW), BF16),
            pltpu.VMEM((LW, KEYS), BF16),
            pltpu.VMEM((KEYS, ROWS), F32),
            pltpu.VMEM((KEYS, ROWS), BF16),
        ],
        compiler_params=params(),
        cost_estimate=pl.CostEstimate(
            flops=20_000_000_000, bytes_accessed=10_000_000, transcendentals=3_000_000
        ),
    )(q, kv, memory, memory, keys_extra, tables, consts["fold"], consts["one"], consts["own"], consts["lanes"])


def attention_backward(
    q_ref, kv_ref, m1_ref, m2_ref, ke_ref, qa_ref, dm_ref, at_ref, lse_ref, rt_ref, grow_ref, ownt_ref, ekey_ref,
    lanes_ref, dq_ref, dkv_ref, dr_ref, keys, values, kt, dmt, qms, dms, dqt,
):
    @pl.when(pl.program_id(0) == 0)
    def _():
        dr_ref[...] = jnp.zeros_like(dr_ref)

    keys[0:ROWS] = kv_ref[0, 0]
    keys[ROWS : ROWS + MROWS] = m1_ref[0, 0]
    keys[ROWS + MROWS :] = m2_ref[0, 0]
    values[0:ROWS] = kv_ref[0, 1]
    values[ROWS : ROWS + MROWS] = m1_ref[0, 1]
    values[ROWS + MROWS :] = m2_ref[0, 1]
    kt[0:LW] = keys[...].T
    kt[LW:] = ekey_ref[...]
    dmt[...] = dm_ref[0].astype(F32).T
    dqt[...] = jnp.zeros_like(dqt)
    deltas = []
    for head in range(LH):
        first = window_of(head)
        win = slice(first, first + WIN)
        span = slice(head * HEAD_DIM, (head + 1) * HEAD_DIM)
        qms[head] = q_ref[0, 0, :, win] * lanes_ref[head]
        dms[head] = dm_ref[0, :, win] * lanes_ref[head]
        deltas.append(jnp.sum(dmt[span] * at_ref[0, span], axis=0, keepdims=True))

    def step(number, _):
        rows = pl.ds(pl.multiple_of(number * BLOCK, BLOCK), BLOCK)
        dk_parts, dv_parts = [], []
        for head in range(LH):
            first = window_of(head)
            variant = head // 2
            win = slice(first, first + WIN)
            ka = keys[rows, win] * lanes_ref[head, 0:BLOCK] + ke_ref[0, variant, rows]
            s = nt(ka, qa_ref[0, head])
            p = jnp.exp2(s * (SCALE * LOG2E) - lse_ref[0, head : head + 1])
            dp = nt(values[rows, win], dms[head])
            ds = (p * (dp - deltas[head])).astype(BF16)
            dv_parts.append(nn(p.astype(BF16), dms[head]))
            dk_parts.append(nn(ds, qms[head]) * SCALE)
            kts = jnp.concatenate(
                [kt[head * HEAD_DIM : (head + 1) * HEAD_DIM, rows], kt[LW:, rows]], axis=0
            )
            dqt[head] += nn(kts, ds)
        for which, parts in ((0, dk_parts), (1, dv_parts)):
            full = jnp.concatenate(
                [
                    parts[0][:, 0:128] + parts[1][:, 0:128],
                    parts[1][:, 128:256] + parts[2][:, 0:128],
                    parts[2][:, 128:256] + parts[3][:, 128:256],
                ],
                axis=1,
            )
            both[which, rows] = full
        return 0

    both = dkv_ref.at[0]
    lax.fori_loop(0, NBLOCK, step, 0)
    for head in range(LH):
        first = window_of(head)
        span = slice(head * HEAD_DIM, (head + 1) * HEAD_DIM)
        total = dqt[head]
        grown = nn(grow_ref[...], total[HEAD_DIM:].astype(BF16)) * ownt_ref[...]
        grown = grown.astype(BF16)
        dmt[span] = dmt[span] + total[0:HEAD_DIM] * SCALE + nn(rt_ref[...], grown)
        dr_ref[:, first : first + WIN] += nn(grown, qms[head])
    dq_ref[0] = dmt[...].T


def call_attention_backward(q, kv, memory, keys_extra, qa, dmix, at, lse, rt, consts):
    clips = q.shape[0]
    return pl.pallas_call(
        attention_backward,
        grid=(clips,),
        in_specs=[
            clip_block(1, ROWS, LW),
            clip_block(2, ROWS, LW),
            pl.BlockSpec((1, 2, MROWS, LW), lambda i: (i + 1, 0, 0, 0)),
            pl.BlockSpec((1, 2, MROWS, LW), lambda i: (i, 0, 0, 0)),
            clip_block(2, KEYS, WIN),
            clip_block(LH, ROWS, WIN),
            clip_block(ROWS, LW),
            clip_block(LW, ROWS),
            clip_block(8, ROWS),
            whole((HEAD_DIM, 256)),
            whole((256, 32)),
            whole((256, ROWS)),
            whole((32, KEYS)),
            whole((LH, ROWS, WIN)),
        ],
        out_specs=[
            clip_block(ROWS, LW),
            clip_block(2, KEYS, LW),
            whole((256, LW)),
        ],
        out_shape=[
            jax.ShapeDtypeStruct((clips, ROWS, LW), F32),
            jax.ShapeDtypeStruct((clips, 2, KEYS, LW), F32),
            jax.ShapeDtypeStruct((256, LW), F32),
        ],
        scratch_shapes=[
            pltpu.VMEM((KEYS, LW), BF16),
            pltpu.VMEM((KEYS, LW), BF16),
            pltpu.VMEM((LW + 32, KEYS), BF16),
            pltpu.VMEM((LW, ROWS), F32),
            pltpu.VMEM((LH, ROWS, WIN), BF16),
            pltpu.VMEM((LH, ROWS, WIN), BF16),
            pltpu.VMEM((LH, HEAD_DIM + 32, ROWS), F32),
        ],
        compiler_params=params(),
        cost_estimate=pl.CostEstimate(
            flops=40_000_000_000, bytes_accessed=20_000_000, transcendentals=3_000_000
        ),
    )(
        q, kv, memory, memory, keys_extra, qa, dmix, at, lse, rt,
        consts["grow"], consts["ownt"], consts["ekey"], consts["lanes"],
    )


EARLY = 40
HEAD_EARLY = 32
LATE = 8


def tail_kernel(
    groups,
    rows_a, rows_x, branch, dq, dkv, w_ref, tokens, middle, gain, early,
    out, grad, early_out, late_out,
    acc, send_a, recv_a, send_b, recv_b, send_c, recv_c, result,
    send_y, recv_y, ebuf, e_y, e_core, e_x, e_z, lbuf, l_y, l_core, l_x, l_z,
    sems_send, sems_recv, small_send, small_recv,
):
    dp = lax.axis_index("dp")
    head = lax.axis_index("head")
    core = lax.rem(dp, 2)
    xbit = lax.rem(lax.div(dp, 2), 2)
    group = lax.div(dp, 4)
    to_core = (dp + 1 - 2 * core, head)
    to_x = (dp + 2 - 4 * xbit, head)
    to_y = (dp, 1 - head)
    peers = [
        (lax.rem(group + o, groups) * 4 + lax.rem(dp, 4), head) for o in range(1, groups)
    ]
    barrier = pltpu.get_barrier_semaphore()
    everyone = [to_core, to_x, to_y] + peers
    for peer in everyone:
        pl.semaphore_signal(barrier, inc=1, device_id=peer, device_id_type=pl.DeviceIdType.MESH)
    pl.semaphore_wait(barrier, len(everyone))

    total = out.shape[1]
    half, quarter, chunk = total // 2, total // 4, total // 4 // groups
    depth = rows_a.shape[1]

    def copy(src, dst, send, recv, peer):
        made = pltpu.make_async_remote_copy(
            src_ref=src, dst_ref=dst, send_sem=send, recv_sem=recv,
            device_id=peer, device_id_type=pl.DeviceIdType.MESH,
        )
        made.start()
        return made

    pieces = ((rows_x, branch), (rows_a, dq), (rows_a, dkv.at[0]), (rows_a, dkv.at[1]))

    def product(number, first):
        left, right = pieces[number]
        return lax.dot_general(
            left[:, pl.ds(pl.multiple_of(first, 128), half)], right[...], (((0,), (0,)), ((), ())),
            preferred_element_type=F32,
        )

    flights = {}

    def phase_a(number):
        send_a[number] = product(number, (1 - core) * half).astype(BF16)
        flights[number, "a"] = copy(
            send_a.at[number], recv_a.at[number], sems_send.at[number, 0], sems_recv.at[number, 0], to_core
        )
        acc[number] = product(number, core * half)

    def phase_b(number):
        flights[number, "a"].wait()
        theirs = pl.ds(pl.multiple_of((1 - xbit) * quarter, 16), quarter)
        send_b[number] = (acc[number, theirs] + recv_a[number, theirs].astype(F32)).astype(BF16)
        flights[number, "b"] = copy(
            send_b.at[number], recv_b.at[number], sems_send.at[number, 1], sems_recv.at[number, 1], to_x
        )

    def phase_c(number):
        mine = pl.ds(pl.multiple_of(xbit * quarter, 16), quarter)
        flights[number, "b"].wait()
        both = acc[number, mine] + recv_a[number, mine].astype(F32) + recv_b[number].astype(F32)
        acc[number, 0:quarter] = both
        send_c[number] = both.astype(BF16)
        for o in range(1, groups):
            rows = pl.ds(pl.multiple_of(lax.rem(group + o, groups) * chunk, 16), chunk)
            flights[number, "c", o] = copy(
                send_c.at[number, rows], recv_c.at[number, o - 1],
                sems_send.at[number, 1 + o], sems_recv.at[number, 1 + o], peers[o - 1],
            )

    def place(g):
        return core * half + xbit * quarter + g * chunk

    def phase_d(number):
        own = acc[number, pl.ds(pl.multiple_of(group * chunk, 16), chunk)]
        for o in range(1, groups):
            flights[number, "c", o].wait()
            own = own + recv_c[number, o - 1].astype(F32)
        rows = pl.ds(pl.multiple_of(place(group), 16), chunk)
        result[number, rows] = own.astype(BF16)
        for o in range(1, groups):
            flights[number, "d", o] = copy(
                result.at[number, rows], result.at[number, rows],
                sems_send.at[number, groups + o], sems_recv.at[number, groups + o], peers[o - 1],
            )

    def phase_e(number):
        for o in range(1, groups):
            flights[number, "d", o].wait()
        rows = pl.ds(pl.multiple_of(place(0), 16), quarter)
        flights[number, "e"] = copy(
            result.at[number, rows], result.at[number, rows],
            sems_send.at[number, 2 * groups], sems_recv.at[number, 2 * groups], to_x,
        )

    def phase_f(number):
        flights[number, "e"].wait()
        rows = pl.ds(pl.multiple_of(core * half, 16), half)
        flights[number, "f"] = copy(
            result.at[number, rows], result.at[number, rows],
            sems_send.at[number, 2 * groups + 1], sems_recv.at[number, 2 * groups + 1], to_core,
        )

    def phase_g(number):
        flights[number, "f"].wait()
        out[number] = result[number]

    def small(buffer, slots, rows_y, base):
        slot_y, slot_core, slot_x, slot_z = slots

        def one():
            flights[base, 0] = copy(
                buffer.at[0, 0:rows_y], slot_y, small_send.at[base], small_recv.at[base], to_y
            )

        def two():
            flights[base, 0].wait()
            buffer[1] = buffer[0]
            buffer[1, 0:rows_y] = buffer[0, 0:rows_y] + slot_y[...]
            flights[base, 1] = copy(
                buffer.at[1], slot_core, small_send.at[base + 1], small_recv.at[base + 1], to_core
            )

        def three():
            flights[base, 1].wait()
            buffer[2] = buffer[1] + slot_core[...]
            flights[base, 2] = copy(
                buffer.at[2], slot_x, small_send.at[base + 2], small_recv.at[base + 2], to_x
            )

        def four():
            flights[base, 2].wait()
            buffer[3] = buffer[2] + slot_x[...]
            for o in range(1, groups):
                flights[base, 2 + o] = copy(
                    buffer.at[3], slot_z.at[o - 1],
                    small_send.at[base + 2 + o], small_recv.at[base + 2 + o], peers[o - 1],
                )

        def five(target):
            added = buffer[3]
            for o in range(1, groups):
                flights[base, 2 + o].wait()
                added = added + slot_z[o - 1]
            target[...] = added

        return one, two, three, four, five

    local = tokens.shape[1]
    clips = tokens.shape[0]

    def input_gradient(clip, side):
        rows = pl.ds(pl.multiple_of(clip * 2 * local + side * local, 16), local)
        return nt(dq[rows], w_ref[0]) + nt(dkv[0, rows], w_ref[1]) + nt(dkv[1, rows], w_ref[2])

    ebuf[0] = early[...]
    e1, e2, e3, e4, e5 = small(ebuf, (e_y, e_core, e_x, e_z), HEAD_EARLY, 0)
    l1, l2, l3, l4, l5 = small(lbuf, (l_y, l_core, l_x, l_z), LATE, 2 + groups)
    e1()
    for clip in range(clips):
        send_y[clip] = input_gradient(clip, 1 - head).astype(BF16)
    across = copy(send_y, recv_y, small_send.at[4 + 2 * groups], small_recv.at[4 + 2 * groups], to_y)
    phase_a(0)
    e2()
    phase_a(1)
    phase_b(0)
    e3()
    phase_a(2)
    phase_b(1)
    phase_c(0)
    phase_a(3)
    phase_b(2)
    phase_c(1)
    phase_d(0)
    e4()
    mine = [input_gradient(clip, head) for clip in range(clips)]
    across.wait()
    bias_sum = jnp.zeros((8, gain.shape[1]), F32)
    gain_sum = jnp.zeros((8, gain.shape[1]), F32)
    for clip in range(clips):
        u = mine[clip] + recv_y[clip].astype(F32)
        v = tokens[clip]
        centred = v - jnp.mean(v, axis=-1, keepdims=True)
        scale = lax.rsqrt(jnp.mean(centred * centred, axis=-1, keepdims=True) + EPSILON)
        xhat = centred * scale
        w = u * gain[0:1]
        dv = scale * (
            w - jnp.mean(w, axis=-1, keepdims=True) - xhat * jnp.mean(w * xhat, axis=-1, keepdims=True)
        )
        grad[clip] = middle[clip] + dv
        gain_sum = gain_sum + jnp.sum((u * xhat).reshape(-1, 8, u.shape[1]), axis=0)
        bias_sum = bias_sum + jnp.sum(u.reshape(-1, 8, u.shape[1]), axis=0)
    lbuf[0, 0:1] = jnp.sum(gain_sum, axis=0, keepdims=True)
    lbuf[0, 1:2] = jnp.sum(bias_sum, axis=0, keepdims=True)
    lbuf[0, 2:8] = jnp.zeros((6, gain.shape[1]), F32)
    l1()
    phase_b(3)
    phase_c(2)
    phase_d(1)
    phase_e(0)
    l2()
    phase_c(3)
    phase_d(2)
    phase_e(1)
    phase_f(0)
    l3()
    phase_d(3)
    phase_e(2)
    phase_f(1)
    l4()
    phase_g(0)
    phase_e(3)
    phase_f(2)
    phase_g(1)
    e5(early_out)
    l5(late_out)
    phase_f(3)
    phase_g(2)
    phase_g(3)


def call_tail(rows_a, rows_x, branch, dq, dkv, weights, tokens, middle, gain, early):
    groups = lax.axis_size("dp") // 4
    width = tokens.shape[2]
    chunk = -(-width // (4 * groups) // 16) * 16
    total = chunk * 4 * groups
    clips, local = tokens.shape[:2]
    if total != width:
        extra = ((0, 0), (0, total - width))
        rows_a, rows_x = jnp.pad(rows_a, extra), jnp.pad(rows_x, extra)
    half, quarter = total // 2, total // 4
    vmem = pl.BlockSpec(memory_space=pltpu.VMEM)
    smalls = 5 + 2 * groups

    def slots(n):
        return [
            pltpu.VMEM((n, width), F32),
            pltpu.VMEM((n, width), F32),
            pltpu.VMEM((groups - 1, n, width), F32),
        ]

    return pl.pallas_call(
        partial(tail_kernel, groups),
        in_specs=[vmem] * 10,
        out_specs=[vmem] * 4,
        out_shape=[
            jax.ShapeDtypeStruct((4, total, LW), BF16),
            jax.ShapeDtypeStruct(tokens.shape, F32),
            jax.ShapeDtypeStruct((EARLY, width), F32),
            jax.ShapeDtypeStruct((LATE, width), F32),
        ],
        scratch_shapes=[
            pltpu.VMEM((4, half, LW), F32),
            pltpu.VMEM((4, half, LW), BF16),
            pltpu.VMEM((4, half, LW), BF16),
            pltpu.VMEM((4, quarter, LW), BF16),
            pltpu.VMEM((4, quarter, LW), BF16),
            pltpu.VMEM((4, quarter, LW), BF16),
            pltpu.VMEM((4, groups - 1, chunk, LW), BF16),
            pltpu.VMEM((4, total, LW), BF16),
            pltpu.VMEM((clips, local, width), BF16),
            pltpu.VMEM((clips, local, width), BF16),
            pltpu.VMEM((4, EARLY, width), F32),
            pltpu.VMEM((HEAD_EARLY, width), F32),
            *slots(EARLY),
            pltpu.VMEM((4, LATE, width), F32),
            pltpu.VMEM((LATE, width), F32),
            *slots(LATE),
            pltpu.SemaphoreType.DMA((4, 2 * groups + 2)),
            pltpu.SemaphoreType.DMA((4, 2 * groups + 2)),
            pltpu.SemaphoreType.DMA((smalls,)),
            pltpu.SemaphoreType.DMA((smalls,)),
        ],
        compiler_params=params(collective_id=0, has_side_effects=True),
        cost_estimate=pl.CostEstimate(
            flops=30_000_000_000, bytes_accessed=20_000_000, transcendentals=0
        ),
    )(rows_a, rows_x, branch, dq, dkv, weights, tokens, middle, gain, early)


def from_behind(x, axis, by):
    count = lax.axis_size(axis)
    pairs = [(i, i + by) for i in range(count) if 0 <= i + by < count]
    return lax.ppermute(x, axis, pairs)


def layer_norm(values, scaling, offset):
    average = jnp.mean(values, axis=-1, keepdims=True)
    centred = values - average
    variance = jnp.mean(centred * centred, axis=-1, keepdims=True)
    return centred * lax.rsqrt(variance + EPSILON) * scaling + offset


def pad_rows(x):
    lead = x.shape[0]
    frames = x.shape[1] // (HGT * WID)
    grid = x.reshape(lead, frames, HGT, WID, x.shape[-1])
    grid = jnp.pad(grid, ((0, 0), (0, 0), (0, 0), (0, PADW - WID), (0, 0)))
    return grid.reshape(lead, frames * HGT * PADW, x.shape[-1])


def drop_rows(x):
    lead = x.shape[0]
    frames = x.shape[1] // (HGT * PADW)
    grid = x.reshape(lead, frames, HGT, PADW, x.shape[-1])[:, :, :, :WID]
    return grid.reshape(lead, frames * HGT * WID, x.shape[-1])


def swap(x):
    return lax.ppermute(x, "head", [(0, 1), (1, 0)])


def gather_rows(x):
    half = x.shape[1]
    mine = lax.axis_index("head") * half
    both = jnp.concatenate([x, x], axis=1)
    return lax.dynamic_update_slice_in_dim(both, swap(x), half - mine, axis=1)


def scatter_sum(x):
    half = x.shape[1] // 2
    mine = lax.axis_index("head") * half
    theirs = half - mine
    sent = lax.dynamic_slice_in_dim(x, theirs, half, axis=1).astype(BF16)
    kept = lax.dynamic_slice_in_dim(x, mine, half, axis=1)
    return kept + swap(sent).astype(F32)


def taps(kernel):
    return jnp.broadcast_to(jnp.tile(kernel, (1, LH))[:, None, :], (27, 8, LW))


def on_device(
    tokens,
    ln1_gain,
    ln1_bias,
    w_qkv,
    pool_q,
    pool_k,
    pool_v,
    squeeze_k,
    squeeze_v,
    rel_t,
    rel_h,
    rel_w,
    w_proj,
    proj_bias,
    ln2_gain,
    ln2_bias,
    w_fc1,
    fc1_bias,
    w_fc2,
    fc2_bias,
    memory_valid,
    cotangent,
):
    clip_count = tokens.shape[0]
    consts = {
        "fold": jnp.asarray(fold_constants(), BF16),
        "one": jnp.asarray(one_lane(), F32),
        "own": jnp.asarray(OWN_T.T, F32),
        "ownt": jnp.asarray(OWN_T, F32),
        "lanes": jnp.asarray(head_lanes(), BF16),
        "grow": jnp.asarray(FOLD, BF16),
        "ekey": jnp.asarray(EKEY, BF16),
    }
    keys_extra = key_constants(memory_valid)
    rel_all = jnp.concatenate([rel_t, rel_h, rel_w], axis=0)
    pairs = jnp.dot(jnp.asarray(PICK), rel_all, precision=HIGHEST)
    pair_table = (pairs * HEAD_DIM**0.5).T
    table_high = pair_table.astype(BF16)
    table_rest = (pair_table - table_high.astype(F32)).astype(BF16)
    tables = jnp.stack(
        [
            jnp.stack(
                [
                    jnp.pad(
                        part,
                        (
                            (head * HEAD_DIM - window_of(head), WIN - HEAD_DIM - head * HEAD_DIM + window_of(head)),
                            (0, 0),
                        ),
                    )
                    for part in (table_high, table_rest)
                ]
            )
            for head in range(LH)
        ]
    )
    rel_rows = pairs.T.astype(BF16)
    tap_q, tap_kv = taps(pool_q)[None], jnp.stack([taps(pool_k), taps(pool_v)])
    tap_s = jnp.stack([taps(squeeze_k), taps(squeeze_v)])

    inputs = pad_rows(tokens).astype(F32)
    upstream_low = pad_rows(cotangent)
    real = (jnp.arange(inputs.shape[1]) % PADW < WID)[None, :, None]
    first_normed = layer_norm(inputs, ln1_gain, ln1_bias)
    first_rows = gather_rows(jnp.where(real, first_normed, 0.0).astype(BF16))
    w_heads = w_qkv.transpose(1, 0, 2)
    upstream_rows = gather_rows(lax.optimization_barrier((upstream_low, first_rows))[0])
    kv0, kv, kvf, mem = call_pool_forward(first_rows, w_heads[1:], tap_kv, tap_s)
    before = from_behind(mem[-2:], "dp", 1)
    q0, q = call_pool_forward(first_rows, w_heads[:1], tap_q)
    memory = jnp.concatenate([before, mem], axis=0)
    branch, qa, at, lse = call_attention_forward(q, kv, memory, keys_extra, tables, consts)
    partial_z = jnp.einsum("ale,ef->alf", branch, w_proj, preferred_element_type=F32)
    middle = inputs + scatter_sum(partial_z) + proj_bias
    second_normed, second_pull = jax.vjp(layer_norm, middle, ln2_gain, ln2_bias)
    second_rows = gather_rows(second_normed.astype(BF16))
    hidden = jnp.einsum("ald,df->alf", second_rows, w_fc1, preferred_element_type=F32) + fc1_bias
    active, gelu_pull = jax.vjp(partial(jax.nn.gelu, approximate=True), hidden)
    active_low = active.astype(BF16)
    partial_m = jnp.einsum("alf,fd->ald", active_low, w_fc2, preferred_element_type=F32)
    output = drop_rows((middle + scatter_sum(partial_m) + fc2_bias).astype(BF16))
    upstream = upstream_low.astype(F32)
    fc2_bias_grad = jnp.sum(upstream, axis=(0, 1))
    w_fc2_grad = jnp.einsum("alf,ald->fd", active_low, upstream_rows, preferred_element_type=F32)
    (hidden_grad,) = gelu_pull(
        jnp.einsum("ald,fd->alf", upstream_rows, w_fc2, preferred_element_type=F32)
    )
    fc1_bias_grad = jnp.sum(hidden_grad, axis=(0, 1))
    hidden_low = hidden_grad.astype(BF16)
    w_fc1_grad = jnp.einsum("ald,alf->df", second_rows, hidden_low, preferred_element_type=F32)
    partial_second = jnp.einsum("alf,df->ald", hidden_low, w_fc1, preferred_element_type=F32)
    middle_part, ln2_gain_grad, ln2_bias_grad = second_pull(scatter_sum(partial_second))
    middle_grad = middle_part + upstream
    proj_bias_grad = jnp.sum(middle_grad, axis=(0, 1))
    middle_rows = gather_rows(middle_grad.astype(BF16))
    dmix = jnp.einsum("alf,ef->ale", middle_rows, w_proj, preferred_element_type=F32).astype(BF16)

    w_fc2_grad, w_fc1_grad = lax.psum((w_fc2_grad.astype(BF16), w_fc1_grad.astype(BF16)), "dp")
    dq, dkv, dr = call_attention_backward(
        q, kv, memory, keys_extra, qa, dmix, at, lse, rel_rows, consts
    )
    slots = dkv[:, :, ROWS:]
    near, far = slots[:, :, :MROWS], slots[:, :, MROWS:]
    zero = jnp.zeros((1,) + near.shape[1:], F32)
    spread_out = jnp.concatenate([zero, near, zero], axis=0) + jnp.concatenate([far, zero, zero], axis=0)
    later = from_behind(spread_out[:2].astype(BF16), "dp", -1).astype(F32)
    dq0, pool_q_grad = call_pool_backward(dq, q0, tap_q)
    leading = jnp.zeros((clip_count - 2,) + near.shape[1:], F32)
    dmem = spread_out[2:] + jnp.concatenate([leading, later], axis=0)
    own = dkv[:, :, :ROWS].transpose(0, 2, 1, 3).reshape(clip_count, ROWS, 2 * LW)
    dkv0, pool_kv_grad, squeeze_grad = call_pool_backward(own, kv0, tap_kv, dmem, kvf, tap_s)
    def tap_grad(g):
        return jnp.sum(jnp.sum(g, axis=1).reshape(27, LH, HEAD_DIM), axis=1)

    pair_grad = jnp.sum(dr.reshape(256, LH, HEAD_DIM), axis=1)
    rel_grad = jnp.dot(jnp.asarray(PICK.T), pair_grad, precision=HIGHEST)
    parts = (
        tap_grad(pool_q_grad[0]),
        tap_grad(pool_kv_grad[0]),
        tap_grad(pool_kv_grad[1]),
        tap_grad(squeeze_grad[0]),
        tap_grad(squeeze_grad[1]),
        rel_grad,
        proj_bias_grad,
        ln2_gain_grad,
        ln2_bias_grad,
        fc2_bias_grad,
    )
    flat = jnp.concatenate([part.reshape(-1) for part in parts])
    width = tokens.shape[2]
    early = jnp.concatenate(
        [
            jnp.pad(flat, (0, HEAD_EARLY * width - flat.size)).reshape(HEAD_EARLY, width),
            jnp.pad(fc1_bias_grad, (0, (EARLY - HEAD_EARLY) * width - fc1_bias_grad.size)).reshape(-1, width),
        ]
    )
    tail, input_grad, early, late = call_tail(
        first_rows.reshape(-1, width),
        middle_rows.reshape(-1, width),
        branch.reshape(-1, LW),
        dq0.reshape(-1, LW),
        dkv0.reshape(2, -1, LW),
        w_heads,
        inputs,
        middle_grad,
        ln1_gain.reshape(1, -1),
        early,
    )
    input_grad = drop_rows(input_grad)
    flat = early[:HEAD_EARLY].reshape(-1)
    shared = [late[0], late[1]]
    for part in parts:
        shared.append(flat[: part.size].reshape(part.shape))
        flat = flat[part.size :]
    rel_grad = shared.pop(7)
    shared[7:7] = [
        rel_grad[: 2 * T_LEN - 1],
        rel_grad[2 * T_LEN - 1 : 2 * T_LEN + 2 * HGT - 2],
        rel_grad[2 * T_LEN + 2 * HGT - 2 :],
    ]
    fc1_bias_grad = early[HEAD_EARLY:].reshape(-1)[: fc1_bias_grad.size]
    tail = tail[:, :width].astype(F32)
    w_proj_grad = tail[0].T
    w_qkv_grad = tail[1:].transpose(1, 0, 2)
    return (
        output,
        input_grad,
        shared[0],
        shared[1],
        w_qkv_grad,
        shared[2],
        shared[3],
        shared[4],
        shared[5],
        shared[6],
        shared[7],
        shared[8],
        shared[9],
        w_proj_grad,
        shared[10],
        shared[11],
        shared[12],
        w_fc1_grad.astype(F32),
        fc1_bias_grad,
        w_fc2_grad.astype(F32),
        shared[13],
    )


def solution(mesh):
    return jax.shard_map(
        on_device,
        mesh=mesh,
        in_specs=(
            P("dp", "head", None),
            P(),
            P(),
            P(None, None, "head"),
            P(),
            P(),
            P(),
            P(),
            P(),
            P(),
            P(),
            P(),
            P("head", None),
            P(),
            P(),
            P(),
            P(None, "head"),
            P("head"),
            P("head", None),
            P(),
            P("dp", None),
            P("dp", "head", None),
        ),
        out_specs=(
            P("dp", "head", None),
            P("dp", "head", None),
            P(),
            P(),
            P(None, None, "head"),
            P(),
            P(),
            P(),
            P(),
            P(),
            P(),
            P(),
            P(),
            P("head", None),
            P(),
            P(),
            P(),
            P(None, "head"),
            P("head"),
            P("head", None),
            P(),
        ),
        check_vma=False,
    )
```

```python
from functools import partial

import jax
import jax.numpy as jnp
import numpy as np
from jax import lax
from jax.experimental import pallas as pl
from jax.experimental.pallas import tpu as pltpu
from jax.sharding import PartitionSpec as P

HEAD_DIM = 96
T_LEN = 8
HGT = 7
WID = 7
PADW = 8
L = 392
ROWS = T_LEN * HGT * PADW
TM = 4
MROWS = TM * HGT * PADW
KEYS = ROWS + 2 * MROWS
LH = 4
LW = LH * HEAD_DIM
WIN = 256
BLOCK = 128
NBLOCK = KEYS // BLOCK

EPSILON = 1e-06
HIGHEST = lax.Precision.HIGHEST
SCALE = HEAD_DIM ** (-0.5)
LOG2E = 1.4426950408889634
F32 = jnp.float32
BF16 = jnp.bfloat16
VMEM_LIMIT = 58 * 1024 * 1024

NB = T_LEN + HGT + WID
NREL = 2 * T_LEN - 1 + 2 * HGT - 1 + 2 * WID - 1
NPAIR = T_LEN * T_LEN + HGT * HGT + WID * WID


def params(**extra):
    return pltpu.CompilerParams(vmem_limit_bytes=VMEM_LIMIT, **extra)


def window_of(head):
    return 0 if head < 2 else BLOCK


def slot_of(head):
    return 192 if head < 2 else 0


def position_constants():
    t, h, w = np.meshgrid(np.arange(T_LEN), np.arange(HGT), np.arange(PADW), indexing="ij")
    t, h, w = t.ravel(), h.ravel(), w.ravel()
    valid = w < WID
    own = np.zeros((256, ROWS), np.float32)
    pick = np.zeros((256, NREL), np.float32)
    fold = np.zeros((256, 32), np.float32)
    ekey = np.zeros((32, KEYS), np.float32)
    row = 0
    base_entry = 0
    base_bias = 0
    for places, length in ((t, T_LEN), (h, HGT), (w, WID)):
        for a in range(length):
            for b in range(length):
                own[row] = (places == a) & valid
                pick[row, base_entry + a - b + length - 1] = 1
                fold[row, base_bias + b] = 1
                row += 1
        for b in range(length):
            ekey[base_bias + b, :ROWS] = (places == b) & valid
        base_entry += 2 * length - 1
        base_bias += length
    return own, pick, fold, ekey, valid


OWN_T, PICK, FOLD, EKEY, ROW_VALID = position_constants()


def fold_constants():
    out = np.zeros((2, 2, 256, WIN), np.float32)
    for variant, slot in enumerate((192, 0)):
        out[variant, 0, :, slot : slot + 32] = FOLD
        out[variant, 1, :, slot + 32 : slot + 64] = FOLD
    return out


def one_lane():
    out = np.zeros((2, 8, WIN), np.float32)
    for variant, slot in enumerate((192, 0)):
        out[variant, :, slot + NB] = 1
    return out


def head_lanes():
    out = np.zeros((LH, ROWS, WIN), np.float32)
    for head in range(LH):
        first = head * HEAD_DIM - window_of(head)
        out[head, :, first : first + HEAD_DIM] = 1
    return out


def key_constants(memory_valid):
    clip_count = memory_valid.shape[0]
    base = np.zeros((2, KEYS, WIN), np.float32)
    lane = np.zeros((2, 1, WIN), np.float32)
    for variant, slot in enumerate((192, 0)):
        base[variant, :, slot : slot + 32] = EKEY.T
        base[variant, :, slot + 32 : slot + 64] = EKEY.T
        lane[variant, :, slot + NB] = 1
    pads = np.concatenate([ROW_VALID, ROW_VALID[:MROWS], ROW_VALID[:MROWS]])
    use = jnp.concatenate(
        [jnp.ones((clip_count, ROWS), bool), jnp.repeat(memory_valid > 0, MROWS, axis=1)], axis=1
    )
    drop = jnp.where(use & jnp.asarray(pads)[None], 0.0, -1e30).astype(F32)
    return (jnp.asarray(base)[None] + drop[:, None, :, None] * jnp.asarray(lane)[None]).astype(BF16)


def nt(a, b):
    return lax.dot_general(a, b, (((1,), (1,)), ((), ())), preferred_element_type=F32)


def nn(a, b):
    return jnp.dot(a, b, preferred_element_type=F32)


def keep_rows(block):
    place = lax.broadcasted_iota(jnp.int32, block.shape, block.ndim - 2)
    return jnp.where(place < WID, block, 0.0)


def spread(dst, first, value):
    n, _, _, c = value.shape
    flat = value.reshape(n * HGT, PADW, c)
    dst[0, pl.ds(first, n), 1 : HGT + 1] = pltpu.roll(flat, 1, axis=1).reshape(n, HGT, PADW, c)
    dst[1, pl.ds(first, n), 1 : HGT + 1] = value
    dst[2, pl.ds(first, n), 1 : HGT + 1] = pltpu.roll(flat, PADW - 1, axis=1).reshape(n, HGT, PADW, c)


def pool_forward(squeeze, *refs):
    if squeeze:
        a_ref, w_ref, k_ref, s_ref, x0_ref, xp_ref, xf_ref, m_ref, xs, ys = refs
    else:
        a_ref, w_ref, k_ref, x0_ref, xp_ref, xs = refs

    @pl.when((pl.program_id(0) == 0) & (pl.program_id(1) == 0))
    def _():
        xs[...] = jnp.zeros_like(xs)
        if squeeze:
            ys[...] = jnp.zeros_like(ys)

    x = nn(a_ref[0], w_ref[0])
    x0_ref[0, 0] = x.astype(BF16)
    spread(xs, 1, x.reshape(T_LEN, HGT, PADW, LW))
    for tile in range(LW // 128):
        lanes = slice(tile * 128, tile * 128 + 128)

        def step(pair, _):
            acc = [jnp.zeros((HGT, PADW, 128), F32) for _ in range(2)]
            for a in range(3):
                for c in range(3):
                    for d in range(2):
                        block = xs[c, 2 * pair + d + a, :, :, lanes]
                        for b in range(3):
                            acc[d] = acc[d] + k_ref[0, a * 9 + b * 3 + c, :, lanes][None] * block[b : b + HGT]
            both = keep_rows(jnp.stack(acc))
            rows = pl.ds(pl.multiple_of(pair * 112, 112), 112)
            flat = both.reshape(112, 128)
            xp_ref[0, 0, rows, lanes] = flat.astype(BF16)
            if squeeze:
                xf_ref[0, 0, rows, lanes] = flat.astype(BF16)
                both = both.reshape(2 * HGT, PADW, 128)
                for c, shift in ((0, 1), (1, 0), (2, PADW - 1)):
                    moved = pltpu.roll(both, shift, axis=1) if shift else both
                    ys[c, pl.ds(2 * pair + 1, 2), 1 : HGT + 1, :, lanes] = moved.reshape(2, HGT, PADW, 128)
            return 0

        lax.fori_loop(0, T_LEN // 2, step, 0)
        if squeeze:

            def squeeze_step(pair, _):
                acc = [jnp.zeros((HGT, PADW, 128), F32) for _ in range(2)]
                for a in range(3):
                    for c in range(3):
                        for d in range(2):
                            block = ys[c, 4 * pair + 2 * d + a, :, :, lanes]
                            for b in range(3):
                                acc[d] = acc[d] + s_ref[0, a * 9 + b * 3 + c, :, lanes][None] * block[b : b + HGT]
                rows = pl.ds(pl.multiple_of(pair * 112, 112), 112)
                m_ref[0, 0, rows, lanes] = keep_rows(jnp.stack(acc)).reshape(112, 128).astype(BF16)
                return 0

            lax.fori_loop(0, TM // 2, squeeze_step, 0)


def call_pool_forward(rows, weights, kernels, squeezes=None):
    clips = rows.shape[0]
    count = weights.shape[0]
    squeeze = squeezes is not None
    tap = pl.BlockSpec((1, 27, 8, LW), lambda j, i: (j, 0, 0, 0))

    def out(n):
        return pl.BlockSpec((1, 1, n, LW), lambda j, i: (i, j, 0, 0))

    frame = pltpu.VMEM((3, T_LEN + 2, HGT + 2, PADW, LW), F32)
    shapes = [
        jax.ShapeDtypeStruct((clips, count, ROWS, LW), BF16),
        jax.ShapeDtypeStruct((clips, count, ROWS, LW), BF16),
    ]
    specs = [out(ROWS), out(ROWS)]
    if squeeze:
        shapes += [
            jax.ShapeDtypeStruct((clips, count, ROWS, LW), BF16),
            jax.ShapeDtypeStruct((clips, count, MROWS, LW), BF16),
        ]
        specs += [out(ROWS), out(MROWS)]
    return pl.pallas_call(
        partial(pool_forward, squeeze),
        grid=(count, clips),
        in_specs=[
            pl.BlockSpec((1, ROWS, rows.shape[2]), lambda j, i: (i, 0, 0)),
            pl.BlockSpec((1, weights.shape[1], LW), lambda j, i: (j, 0, 0)),
            tap,
        ]
        + ([tap] if squeeze else []),
        out_specs=specs,
        out_shape=shapes,
        scratch_shapes=[frame] * (2 if squeeze else 1),
        compiler_params=params(),
        cost_estimate=pl.CostEstimate(
            flops=60_000_000_000 * count // 10, bytes_accessed=4_000_000 * count, transcendentals=0
        ),
    )(rows, weights, kernels, *([squeezes] if squeeze else []))


def attention_forward(
    q_ref, kv_ref, m1_ref, m2_ref, ke_ref, tab_ref, fold_ref, one_ref, own_ref, lanes_ref,
    branch_ref, qa_ref, at_ref, lse_ref, keys, vt, scores, expo,
):
    keys[0:ROWS] = kv_ref[0, 0]
    keys[ROWS : ROWS + MROWS] = m1_ref[0, 0]
    keys[ROWS + MROWS :] = m2_ref[0, 0]
    vt[:, 0:ROWS] = kv_ref[0, 1].T
    memory = jnp.concatenate([m1_ref[0, 1], m2_ref[0, 1]], axis=0).T
    vt[:, ROWS:] = memory
    for head in range(LH):
        first = window_of(head)
        variant = head // 2
        win = slice(first, first + WIN)
        heads = lanes_ref[head]
        qm = q_ref[0, 0, :, win] * heads
        raw = nn(qm, tab_ref[head, 0]) + nn(qm, tab_ref[head, 1])
        raw = raw * own_ref[...]
        high = raw.astype(BF16)
        rest = (raw - high.astype(F32)).astype(BF16)
        placed = nn(high, fold_ref[variant, 0]) + nn(rest, fold_ref[variant, 1]) + one_ref[variant, 0:1]
        qa = qm + placed.astype(BF16)
        qa_ref[0, head] = qa

        def score(number, peak):
            rows = pl.ds(pl.multiple_of(number * BLOCK, BLOCK), BLOCK)
            ka = keys[rows, win] * heads[0:BLOCK] + ke_ref[0, variant, rows]
            s = nt(ka, qa)
            scores[rows] = s
            return jnp.maximum(peak, jnp.max(s, axis=0, keepdims=True))

        peak = lax.fori_loop(0, NBLOCK, score, jnp.full((1, ROWS), -3e38, F32))
        shift = peak * (SCALE * LOG2E)

        def soften(number, total):
            rows = pl.ds(pl.multiple_of(number * BLOCK, BLOCK), BLOCK)
            e = jnp.exp2(scores[rows] * (SCALE * LOG2E) - shift)
            expo[rows] = e.astype(BF16)
            return total + jnp.sum(e, axis=0, keepdims=True)

        total = lax.fori_loop(0, NBLOCK, soften, jnp.zeros((1, ROWS), F32))
        out = nn(vt[head * HEAD_DIM : (head + 1) * HEAD_DIM], expo[...]) * (1.0 / total)
        at_ref[0, head * HEAD_DIM : (head + 1) * HEAD_DIM] = out
        lse_ref[0, head : head + 1] = shift + jnp.log2(total)
    branch_ref[0] = (at_ref[0].T + q_ref[0, 0].astype(F32)).astype(BF16)


def whole(shape):
    return pl.BlockSpec(shape, lambda i: (0,) * len(shape))


def clip_block(*shape):
    return pl.BlockSpec((1,) + shape, lambda i: (i,) + (0,) * len(shape))


def call_attention_forward(q, kv, memory, keys_extra, tables, consts):
    clips = q.shape[0]
    return pl.pallas_call(
        attention_forward,
        grid=(clips,),
        in_specs=[
            clip_block(1, ROWS, LW),
            clip_block(2, ROWS, LW),
            pl.BlockSpec((1, 2, MROWS, LW), lambda i: (i + 1, 0, 0, 0)),
            pl.BlockSpec((1, 2, MROWS, LW), lambda i: (i, 0, 0, 0)),
            clip_block(2, KEYS, WIN),
            whole((LH, 2, WIN, 256)),
            whole((2, 2, 256, WIN)),
            whole((2, 8, WIN)),
            whole((ROWS, 256)),
            whole((LH, ROWS, WIN)),
        ],
        out_specs=[
            clip_block(ROWS, LW),
            clip_block(LH, ROWS, WIN),
            clip_block(LW, ROWS),
            clip_block(8, ROWS),
        ],
        out_shape=[
            jax.ShapeDtypeStruct((clips, ROWS, LW), BF16),
            jax.ShapeDtypeStruct((clips, LH, ROWS, WIN), BF16),
            jax.ShapeDtypeStruct((clips, LW, ROWS), F32),
            jax.ShapeDtypeStruct((clips, 8, ROWS), F32),
        ],
        scratch_shapes=[
            pltpu.VMEM((KEYS, LW), BF16),
            pltpu.VMEM((LW, KEYS), BF16),
            pltpu.VMEM((KEYS, ROWS), F32),
            pltpu.VMEM((KEYS, ROWS), BF16),
        ],
        compiler_params=params(),
        cost_estimate=pl.CostEstimate(
            flops=20_000_000_000, bytes_accessed=10_000_000, transcendentals=3_000_000
        ),
    )(q, kv, memory, memory, keys_extra, tables, consts["fold"], consts["one"], consts["own"], consts["lanes"])


EARLY = 16
HEAD_EARLY = 8
LATE = 8
MESH = pl.DeviceIdType.MESH


def remote(src, dst, send, recv, peer):
    made = pltpu.make_async_remote_copy(
        src_ref=src, dst_ref=dst, send_sem=send, recv_sem=recv, device_id=peer, device_id_type=MESH
    )
    made.start()
    return made


def local(src, dst, sem):
    made = pltpu.make_async_copy(src, dst, sem)
    made.start()
    return made


class Place:
    def __init__(self, groups):
        dp = lax.axis_index("dp")
        head = lax.axis_index("head")
        self.groups = groups
        self.dp, self.head = dp, head
        self.core = lax.rem(dp, 2)
        self.xbit = lax.rem(lax.div(dp, 2), 2)
        self.group = lax.div(dp, 4)
        self.to_core = (dp + 1 - 2 * self.core, head)
        self.to_x = (dp + 2 - 4 * self.xbit, head)
        self.to_y = (dp, 1 - head)
        self.peers = [
            (lax.rem(self.group + o, groups) * 4 + lax.rem(dp, 4), head) for o in range(1, groups)
        ]

    def greet(self, more=()):
        barrier = pltpu.get_barrier_semaphore()
        signalled = [self.to_core, self.to_x, self.to_y] + self.peers + list(more)
        for peer in signalled:
            pl.semaphore_signal(barrier, inc=1, device_id=peer, device_id_type=MESH)
        pl.semaphore_wait(barrier, len(signalled))


class Piece:
    def __init__(self, place, rows, source, result, reduce_refs, send, recv):
        self.at = place
        self.half, self.quarter = rows // 2, rows // 4
        self.chunk = rows // 4 // place.groups
        self.source, self.result = source, result
        self.refs = reduce_refs
        self.send, self.recv = send, recv
        self.tile = 16 if reduce_refs is None or reduce_refs[0].dtype == BF16 else 8
        self.flights = {}

    def start(self, key, number, src, dst, peer):
        self.flights[key] = remote(src, dst, self.send.at[number], self.recv.at[number], peer)

    def base(self, g):
        at = self.at
        return pl.multiple_of(at.core * self.half + at.xbit * self.quarter + g * self.chunk, self.tile)

    def a(self):
        theirs = pl.multiple_of((1 - self.at.core) * self.half, self.tile)
        self.start("a", 0, self.source(theirs, self.half), self.refs[0], self.at.to_core)

    def sum_rows(self, which):
        recv_a = self.refs[0]
        first = pl.multiple_of(which * self.quarter, self.tile)
        own = self.source(pl.multiple_of(self.at.core * self.half + which * self.quarter, self.tile), self.quarter)
        return own[...].astype(F32) + recv_a[pl.ds(first, self.quarter)].astype(F32)

    def b(self):
        _, send_b, recv_b, _, _ = self.refs
        self.flights["a"].wait()
        send_b[...] = self.sum_rows(1 - self.at.xbit).astype(send_b.dtype)
        self.start("b", 1, send_b, recv_b, self.at.to_x)

    def c(self):
        _, _, recv_b, send_c, recv_c = self.refs
        self.flights["b"].wait()
        send_c[...] = (self.sum_rows(self.at.xbit) + recv_b[...].astype(F32)).astype(send_c.dtype)
        for o in range(1, self.at.groups):
            first = pl.multiple_of(lax.rem(self.at.group + o, self.at.groups) * self.chunk, self.tile)
            self.start(
                ("c", o), 1 + o, send_c.at[pl.ds(first, self.chunk)], recv_c.at[o - 1], self.at.peers[o - 1]
            )

    def total(self):
        _, _, _, send_c, recv_c = self.refs
        own = send_c[pl.ds(pl.multiple_of(self.at.group * self.chunk, self.tile), self.chunk)].astype(F32)
        for o in range(1, self.at.groups):
            self.flights["c", o].wait()
            own = own + recv_c[o - 1].astype(F32)
        return own

    def d(self, own=None):
        own = self.total() if own is None else own
        mine = self.result(self.base(self.at.group), self.chunk)
        mine[...] = own.astype(mine.dtype)
        for o in range(1, self.at.groups):
            number = self.at.groups + o
            self.start(("d", o), number, mine, mine, self.at.peers[o - 1])

    def e(self):
        for o in range(1, self.at.groups):
            self.flights["d", o].wait()
        mine = self.result(self.base(0), self.quarter)
        self.start("e", 2 * self.at.groups, mine, mine, self.at.to_x)

    def f(self):
        self.flights["e"].wait()
        mine = self.result(pl.multiple_of(self.at.core * self.half, self.tile), self.half)
        self.start("f", 2 * self.at.groups + 1, mine, mine, self.at.to_core)

    def g(self):
        self.flights["f"].wait()


def piece_scratch(rows, groups, width, dtype, count):
    half, quarter = rows // 2, rows // 4
    return [
        pltpu.VMEM((count, half, width), dtype),
        pltpu.VMEM((count, quarter, width), dtype),
        pltpu.VMEM((count, quarter, width), dtype),
        pltpu.VMEM((count, quarter, width), dtype),
        pltpu.VMEM((count, groups - 1, quarter // groups, width), dtype),
    ]


class Small:
    def __init__(self, place, buffer, slots, rows_y, send, recv, base):
        self.at, self.buffer, self.slots, self.rows_y = place, buffer, slots, rows_y
        self.send, self.recv, self.base = send, recv, base
        self.flights = {}

    def start(self, number, src, dst, peer):
        self.flights[number] = remote(
            src, dst, self.send.at[self.base + number], self.recv.at[self.base + number], peer
        )

    def one(self):
        self.start(0, self.buffer.at[0, 0 : self.rows_y], self.slots[0], self.at.to_y)

    def two(self):
        self.flights[0].wait()
        if self.rows_y < self.buffer.shape[1]:
            self.buffer[1, self.rows_y :] = self.buffer[0, self.rows_y :]
        self.buffer[1, 0 : self.rows_y] = self.buffer[0, 0 : self.rows_y] + self.slots[0][...]
        self.start(1, self.buffer.at[1], self.slots[1], self.at.to_core)

    def three(self):
        self.flights[1].wait()
        self.buffer[2] = self.buffer[1] + self.slots[1][...]
        self.start(2, self.buffer.at[2], self.slots[2], self.at.to_x)

    def four(self):
        self.flights[2].wait()
        self.buffer[3] = self.buffer[2] + self.slots[2][...]
        for o in range(1, self.at.groups):
            self.start(2 + o, self.buffer.at[3], self.slots[3].at[o - 1], self.at.peers[o - 1])

    def five(self, target):
        added = self.buffer[3]
        for o in range(1, self.at.groups):
            self.flights[2 + o].wait()
            added = added + self.slots[3][o - 1]
        target[...] = added


def small_scratch(rows, rows_y, groups, width):
    return [
        pltpu.VMEM((4, rows, width), F32),
        pltpu.VMEM((rows_y, width), F32),
        pltpu.VMEM((rows, width), F32),
        pltpu.VMEM((rows, width), F32),
        pltpu.VMEM((groups - 1, rows, width), F32),
    ]


def attention_backward(
    groups,
    q_ref, kv_ref, mem_ref, ke_hbm, qa_hbm, dm_ref, at_hbm, lse_ref, rt_ref, grow_ref, ownt_ref, ekey_ref,
    lanes_ref, g2_ref, g1_ref, early_ref,
    dq_ref, dkv_ref, dr_ref, chunks_ref, early_out,
    ke_ref, qa_ref, at_ref, keys, values, kt, dmt, qms, dms, dqt,
    recv_a, send_b, recv_b, send_c, recv_c, s0, s1, s2, s3, s4,
    loads, sems_send, sems_recv, small_send, small_recv,
):
    place = Place(groups)
    clips = q_ref.shape[0]
    lead = [
        [local(src.at[clip], dst.at[clip], loads.at[3 * clip + n])
         for n, (src, dst) in enumerate(((ke_hbm, ke_ref), (qa_hbm, qa_ref), (at_hbm, at_ref)))]
        for clip in range(clips)
    ]
    place.greet()
    total = g1_ref.shape[0]

    def view(number):
        if number < 4:
            base, col = (number // 2) * total, (number % 2) * LW
            return lambda first, n: g2_ref.at[pl.ds(base + first, n), col : col + LW]
        col = (number - 4) * LW
        return lambda first, n: g1_ref.at[pl.ds(first, n), col : col + LW]

    pieces = [
        Piece(
            place, total, view(number), None,
            [ref.at[number] for ref in (recv_a, send_b, recv_b, send_c, recv_c)],
            sems_send.at[number], sems_recv.at[number],
        )
        for number in range(8)
    ]
    small = Small(place, s0, (s1, s2, s3, s4), HEAD_EARLY, small_send, small_recv, 0)
    s0[0] = early_ref[...]
    small.one()
    for number in range(3):
        pieces[number].a()
    moves = []
    for slot in range(9):
        moves.append([])
        if slot < 8:
            moves[-1].append(pieces[slot].b)
        if slot + 3 < 8:
            moves[-1].append(pieces[slot + 3].a)
        if slot > 0:
            moves[-1].append(pieces[slot - 1].c)
    moves[1].append(small.two)
    moves[2].append(small.three)
    moves[3].append(small.four)
    moves[6].append(partial(small.five, early_out))

    def pump():
        if moves:
            for move in moves.pop(0):
                move()

    dr_ref[...] = jnp.zeros_like(dr_ref)
    for clip in range(clips):
        near, far = mem_ref.at[clip + 1], mem_ref.at[clip]
        keys[0:ROWS] = kv_ref[clip, 0]
        keys[ROWS : ROWS + MROWS] = near[0]
        keys[ROWS + MROWS :] = far[0]
        values[0:ROWS] = kv_ref[clip, 1]
        values[ROWS : ROWS + MROWS] = near[1]
        values[ROWS + MROWS :] = far[1]
        kt[0:LW] = keys[...].T
        kt[LW:] = ekey_ref[...]
        dmt[...] = dm_ref[clip].astype(F32).T
        dqt[...] = jnp.zeros_like(dqt)
        for made in lead[clip]:
            made.wait()
        deltas = []
        for head in range(LH):
            first = window_of(head)
            win = slice(first, first + WIN)
            span = slice(head * HEAD_DIM, (head + 1) * HEAD_DIM)
            qms[head] = q_ref[clip, 0, :, win] * lanes_ref[head]
            dms[head] = dm_ref[clip, :, win] * lanes_ref[head]
            deltas.append(jnp.sum(dmt[span] * at_ref[clip, span], axis=0, keepdims=True))

        def step(number, _):
            rows = pl.ds(pl.multiple_of(number * BLOCK, BLOCK), BLOCK)
            dk_parts, dv_parts = [], []
            for head in range(LH):
                first = window_of(head)
                variant = head // 2
                win = slice(first, first + WIN)
                ka = keys[rows, win] * lanes_ref[head, 0:BLOCK] + ke_ref[clip, variant, rows]
                s = nt(ka, qa_ref[clip, head])
                p = jnp.exp2(s * (SCALE * LOG2E) - lse_ref[clip, head : head + 1])
                dp = nt(values[rows, win], dms[head])
                ds = (p * (dp - deltas[head])).astype(BF16)
                dv_parts.append(nn(p.astype(BF16), dms[head]))
                dk_parts.append(nn(ds, qms[head]) * SCALE)
                kts = jnp.concatenate(
                    [kt[head * HEAD_DIM : (head + 1) * HEAD_DIM, rows], kt[LW:, rows]], axis=0
                )
                dqt[head] += nn(kts, ds)
            for which, parts in ((0, dk_parts), (1, dv_parts)):
                dkv_ref[clip, which, rows] = jnp.concatenate(
                    [
                        parts[0][:, 0:128] + parts[1][:, 0:128],
                        parts[1][:, 128:256] + parts[2][:, 0:128],
                        parts[2][:, 128:256] + parts[3][:, 128:256],
                    ],
                    axis=1,
                )
            return 0

        for begin, end in ((0, 2), (2, 4), (4, 6), (6, 7)):
            pump()
            lax.fori_loop(begin, end, step, 0)
        for head in range(LH):
            first = window_of(head)
            span = slice(head * HEAD_DIM, (head + 1) * HEAD_DIM)
            total_t = dqt[head]
            grown = nn(grow_ref[...], total_t[HEAD_DIM:].astype(BF16)) * ownt_ref[...]
            grown = grown.astype(BF16)
            dmt[span] = dmt[span] + total_t[0:HEAD_DIM] * SCALE + nn(rt_ref[...], grown)
            dr_ref[:, first : first + WIN] += nn(grown, qms[head])
        dq_ref[clip] = dmt[...].T
    while moves:
        pump()
    for number in range(8):
        chunks_ref[number] = pieces[number].total().astype(BF16)


def padded_rows(width, groups):
    return -(-width // (4 * groups) // 16) * 16 * 4 * groups


def call_attention_backward(q, kv, memory, keys_extra, qa, dmix, at, lse, rt, g2, g1, early, consts):
    clips, width = q.shape[0], early.shape[1]
    groups = lax.axis_size("dp") // 4
    total = padded_rows(width, groups)
    if total != width:
        g1 = jnp.pad(g1, ((0, total - width), (0, 0)))
        g2 = jnp.pad(g2.reshape(2, width, width), ((0, 0), (0, total - width), (0, 0))).reshape(-1, width)
    vmem = pl.BlockSpec(memory_space=pltpu.VMEM)
    hbm = pl.BlockSpec(memory_space=pl.ANY)
    return pl.pallas_call(
        partial(attention_backward, groups),
        in_specs=[vmem] * 3 + [hbm] * 2 + [vmem, hbm] + [vmem] * 9,
        out_specs=[vmem] * 5,
        out_shape=[
            jax.ShapeDtypeStruct((clips, ROWS, LW), F32),
            jax.ShapeDtypeStruct((clips, 2, KEYS, LW), F32),
            jax.ShapeDtypeStruct((256, LW), F32),
            jax.ShapeDtypeStruct((8, total // 4 // groups, LW), BF16),
            jax.ShapeDtypeStruct((EARLY, width), F32),
        ],
        scratch_shapes=[
            pltpu.VMEM(keys_extra.shape, BF16),
            pltpu.VMEM(qa.shape, BF16),
            pltpu.VMEM(at.shape, F32),
            pltpu.VMEM((KEYS, LW), BF16),
            pltpu.VMEM((KEYS, LW), BF16),
            pltpu.VMEM((LW + 32, KEYS), BF16),
            pltpu.VMEM((LW, ROWS), F32),
            pltpu.VMEM((LH, ROWS, WIN), BF16),
            pltpu.VMEM((LH, ROWS, WIN), BF16),
            pltpu.VMEM((LH, HEAD_DIM + 32, ROWS), F32),
            *piece_scratch(total, groups, LW, BF16, 8),
            *small_scratch(EARLY, HEAD_EARLY, groups, width),
            pltpu.SemaphoreType.DMA((3 * clips,)),
            pltpu.SemaphoreType.DMA((8, groups + 1)),
            pltpu.SemaphoreType.DMA((8, groups + 1)),
            pltpu.SemaphoreType.DMA((groups + 2,)),
            pltpu.SemaphoreType.DMA((groups + 2,)),
        ],
        compiler_params=params(collective_id=0, has_side_effects=True),
        cost_estimate=pl.CostEstimate(
            flops=40_000_000_000, bytes_accessed=20_000_000, transcendentals=3_000_000
        ),
    )(
        q, kv, memory, keys_extra, qa, dmix, at, lse, rt,
        consts["grow"], consts["ownt"], consts["ekey"], consts["lanes"], g2, g1, early,
    )


SMALL_ROWS = 256
REL_ROWS = 48


def finish_kernel(
    groups, width,
    dq_hbm, dkv_hbm, x0q_hbm, x0kv_hbm, kvf_hbm, taps_hbm, rows_a_hbm, rows_x_hbm, branch_hbm, w_hbm,
    tokens_hbm, middle_hbm, chunks_ref, dr_ref, gain, foldl_ref, pick_ref,
    grad, out2, out1, outp, outq, small_out, late_out,
    dq, dkv, x0q, x0kv, kvf, taps_ref, rows_a, rows_x, branch, w_ref, tokens, middle,
    us, ms, kacc, dx, dmem_send, dmem_recv, res2, res1, resp, grads, stage, stage_t,
    recv_a, send_b, recv_b, send_c, recv_c, sm_raw, sm, sm_y, sm_res, fa, fb, fc, fd, fe,
    send_y, recv_y, l0, l1, l2, l3, l4,
    loads, stores, sems_send, sems_recv, small_send, small_recv, mem_sems,
):
    place = Place(groups)
    clips = dq.shape[0]
    total = rows_a.shape[1]
    names = ("dkv", "dq", "x0q", "taps", "rows_x", "branch", "x0kv", "kvf", "rows_a", "w", "tokens", "middle")
    pairs = (
        (dkv_hbm, dkv), (dq_hbm, dq), (x0q_hbm, x0q), (taps_hbm, taps_ref), (rows_x_hbm, rows_x),
        (branch_hbm, branch), (x0kv_hbm, x0kv), (kvf_hbm, kvf), (rows_a_hbm, rows_a), (w_hbm, w_ref),
        (tokens_hbm, tokens), (middle_hbm, middle),
    )
    lead = {
        name: local(src, dst, loads.at[n]) for n, (name, (src, dst)) in enumerate(zip(names, pairs))
    }
    count = groups * 4
    behind = (lax.rem(place.dp + count - 1, count), place.head)
    ahead = (lax.rem(place.dp + 1, count), place.head)
    place.greet((behind, ahead))

    def view2(number):
        if number < 4:
            base, col = (number // 2) * total, (number % 2) * LW
            return lambda first, n: res2.at[pl.ds(base + first, n), col : col + LW]
        col = (number - 4) * LW
        return lambda first, n: res1.at[pl.ds(first, n), col : col + LW]

    ffn = [
        Piece(place, total, None, view2(number), None, sems_send.at[number], sems_recv.at[number])
        for number in range(8)
    ]

    def rows_of(ref):
        return lambda first, n: ref.at[pl.ds(first, n)]

    late = [
        Piece(
            place, total, rows_of(grads.at[number]), rows_of(resp.at[number]),
            [ref.at[number] for ref in (recv_a, send_b, recv_b, send_c, recv_c)],
            sems_send.at[8 + number], sems_recv.at[8 + number],
        )
        for number in range(4)
    ]
    tiny = Piece(
        place, sm.shape[0], rows_of(sm), rows_of(sm_res),
        [ref.at[0] for ref in (fa, fb, fc, fd, fe)], sems_send.at[12], sems_recv.at[12],
    )
    ends = Small(place, l0, (l1, l2, l3, l4), LATE, small_send, small_recv, 0)

    stored = []

    def flush(source, target):
        slot = len(stored) % 2
        if len(stored) > 1:
            stored[-2].wait()
        stage[slot] = source[...].astype(F32)
        stored.append(local(stage.at[slot], target, stores.at[slot]))

    def store2(number):
        ffn[number].g()
        if number < 4:
            base, col = (number // 2) * total, (number % 2) * LW
            target = out2.at[base : base + total, col : col + LW]
        else:
            col = (number - 4) * LW
            target = out1.at[:, col : col + LW]
        flush(view2(number)(0, total), target)

    def step(k):
        if k < 8:
            ffn[k].d(chunks_ref[k])
        if 1 <= k < 9:
            ffn[k - 1].e()
        if 2 <= k < 10:
            ffn[k - 2].f()
        if 3 <= k < 11:
            store2(k - 3)

    def product(number):
        left, right = (
            (rows_x, branch), (rows_a, dx.at[0]), (rows_a, dx.at[1]), (rows_a, dx.at[2])
        )[number]
        for first in range(0, total, total // 2):
            grads[number, first : first + total // 2] = lax.dot_general(
                left[:, first : first + total // 2], right[...], (((0,), (0,)), ((), ())),
                preferred_element_type=F32,
            ).astype(BF16)
        late[number].a()

    def shifted_store(dst, first, both, lanes):
        both = both.reshape(2 * HGT, PADW, 128)
        for c, shift in ((0, 1), (1, 0), (2, PADW - 1)):
            moved = pltpu.roll(both, shift, axis=1) if shift else both
            dst[c, pl.ds(first, 2), 1 : HGT + 1, :, lanes] = moved.reshape(2, HGT, PADW, 128)

    def pooled(which, clip):
        field = x0q.at[clip, 0] if which == 0 else x0kv.at[clip, which - 1]
        upstream = dq.at[clip] if which == 0 else dkv.at[clip, which - 1]
        if which:
            memory = dmem_recv[clip, which - 1].astype(F32)
            memory = jnp.where(place.dp == count - 1, 0.0, memory)
            for later in range(clip + 1, clips):
                if later == clip + 1:
                    memory = memory + dkv[later, which - 1, ROWS : ROWS + MROWS]
                if later == clip + 2:
                    memory = memory + dkv[later, which - 1, ROWS + MROWS :]
            spread(ms, 0, memory.reshape(TM, HGT, PADW, LW))
        else:
            spread(us, 1, upstream[...].reshape(T_LEN, HGT, PADW, LW))

        def tile_loop(tile, _):
            lanes = pl.ds(pl.multiple_of(tile * 128, 128), 128)
            if which:

                def squeeze_step(pair, _):
                    rows = pl.ds(pl.multiple_of(pair * 112, 112), 112)
                    own = upstream[rows, lanes].reshape(2, HGT, PADW, 128)
                    fields = kvf[clip, which - 1, rows, lanes].astype(F32).reshape(2, HGT, PADW, 128)
                    acc = [own[0], own[1]]
                    for a, d, frame in ((1, 0, 0), (0, 1, 1), (2, 1, 0)):
                        for c in range(3):
                            block = ms[2 - c, pair + frame, :, :, lanes]
                            for b in range(3):
                                at = block[2 - b : 2 - b + HGT]
                                number = a * 9 + b * 3 + c
                                acc[d] = acc[d] + taps_ref[2 + which, number, :, lanes][None] * at
                                kacc[2 + which, number, :, lanes] += jnp.sum(fields[d] * at, axis=0)
                    shifted_store(us, 2 * pair + 1, keep_rows(jnp.stack(acc)), lanes)
                    return 0

                lax.fori_loop(0, TM, squeeze_step, 0)

            def pair_step(pair, _):
                rows = pl.ds(pl.multiple_of(pair * 112, 112), 112)
                fields = field[rows, lanes].astype(F32).reshape(2, HGT, PADW, 128)
                acc = [jnp.zeros((HGT, PADW, 128), F32) for _ in range(2)]
                for a in range(3):
                    for c in range(3):
                        sums = [jnp.zeros((PADW, 128), F32) for _ in range(3)]
                        for d in range(2):
                            block = us[2 - c, 2 * pair + d + 2 - a, :, :, lanes]
                            for b in range(3):
                                at = block[2 - b : 2 - b + HGT]
                                acc[d] = acc[d] + taps_ref[which, a * 9 + b * 3 + c, :, lanes][None] * at
                                sums[b] = sums[b] + jnp.sum(fields[d] * at, axis=0)
                        for b in range(3):
                            kacc[which, a * 9 + b * 3 + c, :, lanes] += sums[b]
                both = keep_rows(jnp.stack(acc))
                out_rows = pl.ds(pl.multiple_of(clip * ROWS + pair * 112, 16), 112)
                dx[which, out_rows, lanes] = both.reshape(112, 128).astype(BF16)
                return 0

            lax.fori_loop(0, T_LEN // 2, pair_step, 0)
            return 0

        lax.fori_loop(0, LW // 128, tile_loop, 0)

    side_rows = ROWS // 2

    def input_gradient(clip, side):
        rows = pl.ds(pl.multiple_of(clip * ROWS + side * side_rows, 16), side_rows)
        return nt(dx[0, rows], w_ref[0]) + nt(dx[1, rows], w_ref[1]) + nt(dx[2, rows], w_ref[2])

    crossing = {}

    def cross(clip):
        send_y[clip] = input_gradient(clip, 1 - place.head).astype(BF16)
        number = groups + 2 + clip
        crossing[clip] = remote(
            send_y.at[clip], recv_y.at[clip], small_send.at[number], small_recv.at[number], place.to_y
        )

    def normed_gradient(clip):
        mine = input_gradient(clip, place.head)
        crossing[clip].wait()
        u = mine + recv_y[clip].astype(F32)
        v = tokens[clip].astype(F32)
        centred = v - jnp.mean(v, axis=-1, keepdims=True)
        scale = lax.rsqrt(jnp.mean(centred * centred, axis=-1, keepdims=True) + EPSILON)
        xhat = centred * scale
        w = u * gain[0:1]
        dv = scale * (
            w - jnp.mean(w, axis=-1, keepdims=True) - xhat * jnp.mean(w * xhat, axis=-1, keepdims=True)
        )
        grad[clip] = middle[clip] + dv
        l0[0, 0:1] += jnp.sum(u * xhat, axis=0, keepdims=True)
        l0[0, 1:2] += jnp.sum(u, axis=0, keepdims=True)

    def exact(a, b):
        return jnp.dot(a, b, precision=HIGHEST, preferred_element_type=F32)

    def small_start():
        folded = exact(dr_ref[...], foldl_ref[...])
        sm_raw[0:REL_ROWS] = exact(pick_ref[...], folded)
        for which in range(5):
            first = REL_ROWS + 32 * which
            sums = jnp.sum(kacc[which], axis=1)
            sums = jnp.concatenate([sums, jnp.zeros((5, LW), F32)], axis=0)
            sm_raw[first : first + 32] = exact(sums, foldl_ref[...])
        number = groups + 2 + clips
        crossing["small"] = remote(
            sm_raw, sm_y, small_send.at[number], small_recv.at[number], place.to_y
        )

    def small_next():
        crossing["small"].wait()
        sm[...] = sm_raw[...] + sm_y[...]
        tiny.a()

    us[...] = jnp.zeros_like(us)
    ms[...] = jnp.zeros_like(ms)
    kacc[...] = jnp.zeros_like(kacc)
    l0[0] = jnp.zeros_like(l0[0])
    sm_raw[...] = jnp.zeros_like(sm_raw)
    step(0)
    lead["dkv"].wait()
    for which in range(2):
        dmem_send[0, which] = dkv[0, which, ROWS + MROWS :].astype(BF16)
        dmem_send[1, which] = (
            dkv[0, which, ROWS : ROWS + MROWS] + dkv[1, which, ROWS + MROWS :]
        ).astype(BF16)
    memory_flight = remote(dmem_send, dmem_recv, mem_sems.at[0], mem_sems.at[1], behind)
    for name in ("dq", "x0q", "taps"):
        lead[name].wait()
    pooled(0, 0)
    step(1)
    lead["rows_x"].wait()
    lead["branch"].wait()
    product(0)
    pooled(0, 1)
    step(2)
    late[0].b()
    lead["rows_a"].wait()
    product(1)
    step(3)
    late[0].c()
    memory_flight.wait()
    lead["x0kv"].wait()
    lead["kvf"].wait()
    pooled(1, 0)
    step(4)
    late[1].b()
    late[0].d()
    pooled(2, 0)
    step(5)
    late[1].c()
    late[0].e()
    lead["w"].wait()
    cross(0)
    pooled(1, 1)
    step(6)
    late[1].d()
    late[0].f()
    product(2)
    step(7)
    late[1].e()
    pooled(2, 1)
    late[2].b()
    product(3)
    step(8)
    late[1].f()
    cross(1)
    late[2].c()
    late[3].b()
    small_start()
    step(9)
    late[0].g()
    stage_t[...] = resp[0].astype(F32).T
    turned = local(stage_t, outp, stores.at[2])
    lead["tokens"].wait()
    lead["middle"].wait()
    normed_gradient(0)
    late[2].d()
    late[3].c()
    step(10)
    small_next()
    late[2].e()
    late[3].d()
    normed_gradient(1)
    ends.one()
    tiny.b()
    late[1].g()
    sent_q = local(resp.at[1], outq.at[0], stores.at[3])
    late[2].f()
    late[3].e()
    ends.two()
    tiny.c()
    late[3].f()
    ends.three()
    tiny.d()
    late[2].g()
    sent_k = local(resp.at[2], outq.at[1], stores.at[4])
    ends.four()
    tiny.e()
    late[3].g()
    sent_v = local(resp.at[3], outq.at[2], stores.at[5])
    tiny.f()
    ends.five(late_out)
    tiny.g()
    small_out[...] = sm_res[...]
    for made in [turned, sent_q, sent_k, sent_v] + stored[-2:]:
        made.wait()


def call_finish(dq, dkv, x0q, x0kv, kvf, all_taps, rows_a, rows_x, branch, weights, tokens, middle, chunks, dr, gain):
    groups = lax.axis_size("dp") // 4
    width = tokens.shape[2]
    total = padded_rows(width, groups)
    clips, side = tokens.shape[:2]
    if total != width:
        extra = ((0, 0), (0, total - width))
        rows_a, rows_x = jnp.pad(rows_a, extra), jnp.pad(rows_x, extra)
    small_rows = -(-SMALL_ROWS // (32 * groups)) * 32 * groups
    foldl = np.zeros((LW, 128), np.float32)
    foldl[np.arange(LW), np.arange(LW) % HEAD_DIM] = 1
    pick = np.zeros((REL_ROWS, 256), np.float32)
    pick[:NREL] = PICK.T
    vmem = pl.BlockSpec(memory_space=pltpu.VMEM)
    hbm = pl.BlockSpec(memory_space=pl.ANY)
    streamed = [dq, dkv, x0q, x0kv, kvf, all_taps, rows_a, rows_x, branch, weights, tokens, middle]
    frame = pltpu.VMEM((3, T_LEN + 2, HGT + 2, PADW, LW), F32)
    return pl.pallas_call(
        partial(finish_kernel, groups, width),
        in_specs=[hbm] * 12 + [vmem] * 5,
        out_specs=[vmem, hbm, hbm, hbm, hbm, vmem, vmem],
        out_shape=[
            jax.ShapeDtypeStruct(tokens.shape, F32),
            jax.ShapeDtypeStruct((2 * total, width), F32),
            jax.ShapeDtypeStruct((total, 4 * LW), F32),
            jax.ShapeDtypeStruct((LW, total), F32),
            jax.ShapeDtypeStruct((3, total, LW), BF16),
            jax.ShapeDtypeStruct((small_rows, 128), F32),
            jax.ShapeDtypeStruct((LATE, width), F32),
        ],
        scratch_shapes=[pltpu.VMEM(array.shape, array.dtype) for array in streamed]
        + [
            frame,
            pltpu.VMEM((3, TM + 1, HGT + 2, PADW, LW), F32),
            pltpu.VMEM((5, 27, 8, LW), F32),
            pltpu.VMEM((3, clips * ROWS, LW), BF16),
            pltpu.VMEM((2, 2, MROWS, LW), BF16),
            pltpu.VMEM((2, 2, MROWS, LW), BF16),
            pltpu.VMEM((2 * total, width), BF16),
            pltpu.VMEM((total, 4 * LW), BF16),
            pltpu.VMEM((4, total, LW), BF16),
            pltpu.VMEM((4, total, LW), BF16),
            pltpu.VMEM((2, total, LW), F32),
            pltpu.VMEM((LW, total), F32),
            *piece_scratch(total, groups, LW, BF16, 4),
            pltpu.VMEM((small_rows, 128), F32),
            pltpu.VMEM((small_rows, 128), F32),
            pltpu.VMEM((small_rows, 128), F32),
            pltpu.VMEM((small_rows, 128), F32),
            *piece_scratch(small_rows, groups, 128, F32, 1),
            pltpu.VMEM((clips, side, width), BF16),
            pltpu.VMEM((clips, side, width), BF16),
            *small_scratch(LATE, LATE, groups, width),
            pltpu.SemaphoreType.DMA((12,)),
            pltpu.SemaphoreType.DMA((6,)),
            pltpu.SemaphoreType.DMA((13, 2 * groups + 2)),
            pltpu.SemaphoreType.DMA((13, 2 * groups + 2)),
            pltpu.SemaphoreType.DMA((groups + 3 + clips,)),
            pltpu.SemaphoreType.DMA((groups + 3 + clips,)),
            pltpu.SemaphoreType.DMA((2,)),
        ],
        compiler_params=params(collective_id=1, has_side_effects=True),
        cost_estimate=pl.CostEstimate(
            flops=60_000_000_000, bytes_accessed=40_000_000, transcendentals=0
        ),
    )(*streamed, chunks, dr, gain, jnp.asarray(foldl), jnp.asarray(pick))


def from_behind(x, axis, by):
    count = lax.axis_size(axis)
    pairs = [(i, i + by) for i in range(count) if 0 <= i + by < count]
    return lax.ppermute(x, axis, pairs)


def layer_norm(values, scaling, offset):
    average = jnp.mean(values, axis=-1, keepdims=True)
    centred = values - average
    variance = jnp.mean(centred * centred, axis=-1, keepdims=True)
    return centred * lax.rsqrt(variance + EPSILON) * scaling + offset


def pad_rows(x):
    lead = x.shape[0]
    frames = x.shape[1] // (HGT * WID)
    grid = x.reshape(lead, frames, HGT, WID, x.shape[-1])
    grid = jnp.pad(grid, ((0, 0), (0, 0), (0, 0), (0, PADW - WID), (0, 0)))
    return grid.reshape(lead, frames * HGT * PADW, x.shape[-1])


def drop_rows(x):
    lead = x.shape[0]
    frames = x.shape[1] // (HGT * PADW)
    grid = x.reshape(lead, frames, HGT, PADW, x.shape[-1])[:, :, :, :WID]
    return grid.reshape(lead, frames * HGT * WID, x.shape[-1])


def swap(x):
    return lax.ppermute(x, "head", [(0, 1), (1, 0)])


def gather_rows(x):
    half = x.shape[1]
    mine = lax.axis_index("head") * half
    both = jnp.concatenate([x, x], axis=1)
    return lax.dynamic_update_slice_in_dim(both, swap(x), half - mine, axis=1)


def scatter_sum(x):
    half = x.shape[1] // 2
    mine = lax.axis_index("head") * half
    theirs = half - mine
    sent = lax.dynamic_slice_in_dim(x, theirs, half, axis=1).astype(BF16)
    kept = lax.dynamic_slice_in_dim(x, mine, half, axis=1)
    return kept + swap(sent).astype(F32)


def taps(kernel):
    return jnp.broadcast_to(jnp.tile(kernel, (1, LH))[:, None, :], (27, 8, LW))


def on_device(
    tokens,
    ln1_gain,
    ln1_bias,
    w_qkv,
    pool_q,
    pool_k,
    pool_v,
    squeeze_k,
    squeeze_v,
    rel_t,
    rel_h,
    rel_w,
    w_proj,
    proj_bias,
    ln2_gain,
    ln2_bias,
    w_fc1,
    fc1_bias,
    w_fc2,
    fc2_bias,
    memory_valid,
    cotangent,
):
    clip_count = tokens.shape[0]
    consts = {
        "fold": jnp.asarray(fold_constants(), BF16),
        "one": jnp.asarray(one_lane(), F32),
        "own": jnp.asarray(OWN_T.T, F32),
        "ownt": jnp.asarray(OWN_T, F32),
        "lanes": jnp.asarray(head_lanes(), BF16),
        "grow": jnp.asarray(FOLD, BF16),
        "ekey": jnp.asarray(EKEY, BF16),
    }
    keys_extra = key_constants(memory_valid)
    rel_all = jnp.concatenate([rel_t, rel_h, rel_w], axis=0)
    pairs = jnp.dot(jnp.asarray(PICK), rel_all, precision=HIGHEST)
    pair_table = (pairs * HEAD_DIM**0.5).T
    table_high = pair_table.astype(BF16)
    table_rest = (pair_table - table_high.astype(F32)).astype(BF16)
    tables = jnp.stack(
        [
            jnp.stack(
                [
                    jnp.pad(
                        part,
                        (
                            (head * HEAD_DIM - window_of(head), WIN - HEAD_DIM - head * HEAD_DIM + window_of(head)),
                            (0, 0),
                        ),
                    )
                    for part in (table_high, table_rest)
                ]
            )
            for head in range(LH)
        ]
    )
    rel_rows = pairs.T.astype(BF16)
    tap_q, tap_kv = taps(pool_q)[None], jnp.stack([taps(pool_k), taps(pool_v)])
    tap_s = jnp.stack([taps(squeeze_k), taps(squeeze_v)])

    inputs_low = pad_rows(tokens)
    inputs = inputs_low.astype(F32)
    upstream_low = pad_rows(cotangent)
    real = (jnp.arange(inputs.shape[1]) % PADW < WID)[None, :, None]
    first_normed = layer_norm(inputs, ln1_gain, ln1_bias)
    first_rows = gather_rows(jnp.where(real, first_normed, 0.0).astype(BF16))
    w_heads = w_qkv.transpose(1, 0, 2)
    upstream_rows = gather_rows(lax.optimization_barrier((upstream_low, first_rows))[0])
    kv0, kv, kvf, mem = call_pool_forward(first_rows, w_heads[1:], tap_kv, tap_s)
    before = from_behind(mem[-2:], "dp", 1)
    q0, q = call_pool_forward(first_rows, w_heads[:1], tap_q)
    memory = jnp.concatenate([before, mem], axis=0)
    branch, qa, at, lse = call_attention_forward(q, kv, memory, keys_extra, tables, consts)
    partial_z = jnp.einsum("ale,ef->alf", branch, w_proj, preferred_element_type=F32)
    middle = inputs + scatter_sum(partial_z) + proj_bias
    second_normed, second_pull = jax.vjp(layer_norm, middle, ln2_gain, ln2_bias)
    second_rows = gather_rows(second_normed.astype(BF16))
    hidden = jnp.einsum("ald,df->alf", second_rows, w_fc1, preferred_element_type=F32) + fc1_bias
    active, gelu_pull = jax.vjp(partial(jax.nn.gelu, approximate=True), hidden)
    active_low = active.astype(BF16)
    partial_m = jnp.einsum("alf,fd->ald", active_low, w_fc2, preferred_element_type=F32)
    output = drop_rows((middle + scatter_sum(partial_m) + fc2_bias).astype(BF16))
    upstream = upstream_low.astype(F32)
    fc2_bias_grad = jnp.sum(upstream, axis=(0, 1))
    w_fc2_grad = jnp.einsum("alf,ald->fd", active_low, upstream_rows, preferred_element_type=F32)
    (hidden_grad,) = gelu_pull(
        jnp.einsum("ald,fd->alf", upstream_rows, w_fc2, preferred_element_type=F32)
    )
    fc1_bias_grad = jnp.sum(hidden_grad, axis=(0, 1))
    hidden_low = hidden_grad.astype(BF16)
    w_fc1_grad = jnp.einsum("ald,alf->df", second_rows, hidden_low, preferred_element_type=F32)
    partial_second = jnp.einsum("alf,df->ald", hidden_low, w_fc1, preferred_element_type=F32)
    middle_part, ln2_gain_grad, ln2_bias_grad = second_pull(scatter_sum(partial_second))
    middle_grad = middle_part + upstream
    proj_bias_grad = jnp.sum(middle_grad, axis=(0, 1))
    middle_rows = gather_rows(middle_grad.astype(BF16))
    dmix = jnp.einsum("alf,ef->ale", middle_rows, w_proj, preferred_element_type=F32).astype(BF16)

    width = tokens.shape[2]
    early = jnp.concatenate(
        [
            jnp.stack([proj_bias_grad, ln2_gain_grad, ln2_bias_grad, fc2_bias_grad]),
            jnp.zeros((HEAD_EARLY - 4, width), F32),
            fc1_bias_grad.reshape(-1, width),
        ]
    )
    early = jnp.pad(early, ((0, EARLY - early.shape[0]), (0, 0)))
    dq, dkv, dr, chunks, early = call_attention_backward(
        q, kv, memory, keys_extra, qa, dmix, at, lse, rel_rows,
        w_fc2_grad.astype(BF16), w_fc1_grad.astype(BF16), early, consts,
    )
    input_grad, w_fc2_grad, w_fc1_grad, w_proj_grad, tail, small, late = call_finish(
        dq, dkv, q0, kv0, kvf, jnp.concatenate([tap_q, tap_kv, tap_s]),
        first_rows.reshape(-1, width),
        middle_rows.reshape(-1, width),
        branch.reshape(-1, LW),
        w_heads,
        inputs_low,
        middle_grad,
        chunks,
        dr,
        ln1_gain.reshape(1, -1),
    )
    input_grad = drop_rows(input_grad)
    total = w_fc1_grad.shape[0]
    if total != width:
        w_fc2_grad = w_fc2_grad.reshape(2, total, width)[:, :width].reshape(2 * width, width)
        w_fc1_grad, w_proj_grad, tail = w_fc1_grad[:width], w_proj_grad[:, :width], tail[:, :width]
    w_qkv_grad = tail.astype(F32).transpose(1, 0, 2)
    fc1_bias_grad = early[HEAD_EARLY : HEAD_EARLY + fc1_bias_grad.size // width].reshape(-1)
    small = small[:, :HEAD_DIM]
    shared = [late[0], late[1]]
    shared += [small[REL_ROWS + 32 * n : REL_ROWS + 32 * n + 27] for n in range(5)]
    shared += [
        small[: 2 * T_LEN - 1],
        small[2 * T_LEN - 1 : 2 * T_LEN + 2 * HGT - 2],
        small[2 * T_LEN + 2 * HGT - 2 : NREL],
    ]
    shared += [early[0], early[1], early[2], early[3]]
    return (
        output,
        input_grad,
        shared[0],
        shared[1],
        w_qkv_grad,
        shared[2],
        shared[3],
        shared[4],
        shared[5],
        shared[6],
        shared[7],
        shared[8],
        shared[9],
        w_proj_grad,
        shared[10],
        shared[11],
        shared[12],
        w_fc1_grad,
        fc1_bias_grad,
        w_fc2_grad,
        shared[13],
    )


def solution(mesh):
    return jax.shard_map(
        on_device,
        mesh=mesh,
        in_specs=(
            P("dp", "head", None),
            P(),
            P(),
            P(None, None, "head"),
            P(),
            P(),
            P(),
            P(),
            P(),
            P(),
            P(),
            P(),
            P("head", None),
            P(),
            P(),
            P(),
            P(None, "head"),
            P("head"),
            P("head", None),
            P(),
            P("dp", None),
            P("dp", "head", None),
        ),
        out_specs=(
            P("dp", "head", None),
            P("dp", "head", None),
            P(),
            P(),
            P(None, None, "head"),
            P(),
            P(),
            P(),
            P(),
            P(),
            P(),
            P(),
            P(),
            P("head", None),
            P(),
            P(),
            P(),
            P(None, "head"),
            P("head"),
            P("head", None),
            P(),
        ),
        check_vma=False,
    )
```

```python
from functools import partial

import jax
import jax.numpy as jnp
import numpy as np
from jax import lax
from jax.experimental import pallas as pl
from jax.experimental.pallas import tpu as pltpu
from jax.sharding import PartitionSpec as P

HEAD_DIM = 96
T_LEN = 8
HGT = 7
WID = 7
PADW = 8
L = 392
ROWS = T_LEN * HGT * PADW
TM = 4
MROWS = TM * HGT * PADW
KEYS = ROWS + 2 * MROWS
LH = 4
LW = LH * HEAD_DIM
WIN = 256
BLOCK = 128
NBLOCK = KEYS // BLOCK

EPSILON = 1e-06
HIGHEST = lax.Precision.HIGHEST
SCALE = HEAD_DIM ** (-0.5)
LOG2E = 1.4426950408889634
F32 = jnp.float32
BF16 = jnp.bfloat16
VMEM_LIMIT = 58 * 1024 * 1024

NB = T_LEN + HGT + WID
NREL = 2 * T_LEN - 1 + 2 * HGT - 1 + 2 * WID - 1
NPAIR = T_LEN * T_LEN + HGT * HGT + WID * WID


def params(**extra):
    return pltpu.CompilerParams(vmem_limit_bytes=VMEM_LIMIT, **extra)


def window_of(head):
    return 0 if head < 2 else BLOCK


def slot_of(head):
    return 192 if head < 2 else 0


def position_constants():
    t, h, w = np.meshgrid(np.arange(T_LEN), np.arange(HGT), np.arange(PADW), indexing="ij")
    t, h, w = t.ravel(), h.ravel(), w.ravel()
    valid = w < WID
    own = np.zeros((256, ROWS), np.float32)
    pick = np.zeros((256, NREL), np.float32)
    fold = np.zeros((256, 32), np.float32)
    ekey = np.zeros((32, KEYS), np.float32)
    row = 0
    base_entry = 0
    base_bias = 0
    for places, length in ((t, T_LEN), (h, HGT), (w, WID)):
        for a in range(length):
            for b in range(length):
                own[row] = (places == a) & valid
                pick[row, base_entry + a - b + length - 1] = 1
                fold[row, base_bias + b] = 1
                row += 1
        for b in range(length):
            ekey[base_bias + b, :ROWS] = (places == b) & valid
        base_entry += 2 * length - 1
        base_bias += length
    return own, pick, fold, ekey, valid


OWN_T, PICK, FOLD, EKEY, ROW_VALID = position_constants()


def fold_constants():
    out = np.zeros((2, 2, 256, WIN), np.float32)
    for variant, slot in enumerate((192, 0)):
        out[variant, 0, :, slot : slot + 32] = FOLD
        out[variant, 1, :, slot + 32 : slot + 64] = FOLD
    return out


def one_lane():
    out = np.zeros((2, 8, WIN), np.float32)
    for variant, slot in enumerate((192, 0)):
        out[variant, :, slot + NB] = 1
    return out


def head_lanes():
    out = np.zeros((LH, ROWS, WIN), np.float32)
    for head in range(LH):
        first = head * HEAD_DIM - window_of(head)
        out[head, :, first : first + HEAD_DIM] = 1
    return out


def key_constants(memory_valid):
    clip_count = memory_valid.shape[0]
    base = np.zeros((2, KEYS, WIN), np.float32)
    lane = np.zeros((2, 1, WIN), np.float32)
    for variant, slot in enumerate((192, 0)):
        base[variant, :, slot : slot + 32] = EKEY.T
        base[variant, :, slot + 32 : slot + 64] = EKEY.T
        lane[variant, :, slot + NB] = 1
    pads = np.concatenate([ROW_VALID, ROW_VALID[:MROWS], ROW_VALID[:MROWS]])
    use = jnp.concatenate(
        [jnp.ones((clip_count, ROWS), bool), jnp.repeat(memory_valid > 0, MROWS, axis=1)], axis=1
    )
    drop = jnp.where(use & jnp.asarray(pads)[None], 0.0, -1e30).astype(F32)
    return (jnp.asarray(base)[None] + drop[:, None, :, None] * jnp.asarray(lane)[None]).astype(BF16)


def nt(a, b):
    return lax.dot_general(a, b, (((1,), (1,)), ((), ())), preferred_element_type=F32)


def nn(a, b):
    return jnp.dot(a, b, preferred_element_type=F32)


def keep_rows(block):
    place = lax.broadcasted_iota(jnp.int32, block.shape, block.ndim - 2)
    return jnp.where(place < WID, block, 0.0)


def spread(dst, first, value):
    n, _, _, c = value.shape
    flat = value.reshape(n * HGT, PADW, c)
    dst[0, pl.ds(first, n), 1 : HGT + 1] = pltpu.roll(flat, 1, axis=1).reshape(n, HGT, PADW, c)
    dst[1, pl.ds(first, n), 1 : HGT + 1] = value
    dst[2, pl.ds(first, n), 1 : HGT + 1] = pltpu.roll(flat, PADW - 1, axis=1).reshape(n, HGT, PADW, c)


def pool_forward(squeeze, *refs):
    if squeeze:
        a_ref, w_ref, k_ref, s_ref, x0_ref, xp_ref, xf_ref, m_ref, xs, ys = refs
    else:
        a_ref, w_ref, k_ref, x0_ref, xp_ref, xs = refs

    @pl.when((pl.program_id(0) == 0) & (pl.program_id(1) == 0))
    def _():
        xs[...] = jnp.zeros_like(xs)
        if squeeze:
            ys[...] = jnp.zeros_like(ys)

    x = nn(a_ref[0], w_ref[0])
    x0_ref[0, 0] = x.astype(BF16)
    spread(xs, 1, x.reshape(T_LEN, HGT, PADW, LW))
    for tile in range(LW // 128):
        lanes = slice(tile * 128, tile * 128 + 128)

        def step(pair, _):
            acc = [jnp.zeros((HGT, PADW, 128), F32) for _ in range(2)]
            for a in range(3):
                for c in range(3):
                    for d in range(2):
                        block = xs[c, 2 * pair + d + a, :, :, lanes]
                        for b in range(3):
                            acc[d] = acc[d] + k_ref[0, a * 9 + b * 3 + c, :, lanes][None] * block[b : b + HGT]
            both = keep_rows(jnp.stack(acc))
            rows = pl.ds(pl.multiple_of(pair * 112, 112), 112)
            flat = both.reshape(112, 128)
            xp_ref[0, 0, rows, lanes] = flat.astype(BF16)
            if squeeze:
                xf_ref[0, 0, rows, lanes] = flat.astype(BF16)
                both = both.reshape(2 * HGT, PADW, 128)
                for c, shift in ((0, 1), (1, 0), (2, PADW - 1)):
                    moved = pltpu.roll(both, shift, axis=1) if shift else both
                    ys[c, pl.ds(2 * pair + 1, 2), 1 : HGT + 1, :, lanes] = moved.reshape(2, HGT, PADW, 128)
            return 0

        lax.fori_loop(0, T_LEN // 2, step, 0)
        if squeeze:

            def squeeze_step(pair, _):
                acc = [jnp.zeros((HGT, PADW, 128), F32) for _ in range(2)]
                for a in range(3):
                    for c in range(3):
                        for d in range(2):
                            block = ys[c, 4 * pair + 2 * d + a, :, :, lanes]
                            for b in range(3):
                                acc[d] = acc[d] + s_ref[0, a * 9 + b * 3 + c, :, lanes][None] * block[b : b + HGT]
                rows = pl.ds(pl.multiple_of(pair * 112, 112), 112)
                m_ref[0, 0, rows, lanes] = keep_rows(jnp.stack(acc)).reshape(112, 128).astype(BF16)
                return 0

            lax.fori_loop(0, TM // 2, squeeze_step, 0)


def call_pool_forward(rows, weights, first, count, kernels, squeezes=None):
    clips = rows.shape[0]
    squeeze = squeezes is not None
    tap = pl.BlockSpec((1, 27, 8, LW), lambda j, i: (j, 0, 0, 0))

    def out(n):
        return pl.BlockSpec((1, 1, n, LW), lambda j, i: (i, j, 0, 0))

    frame = pltpu.VMEM((3, T_LEN + 2, HGT + 2, PADW, LW), F32)
    shapes = [
        jax.ShapeDtypeStruct((clips, count, ROWS, LW), BF16),
        jax.ShapeDtypeStruct((clips, count, ROWS, LW), BF16),
    ]
    specs = [out(ROWS), out(ROWS)]
    if squeeze:
        shapes += [
            jax.ShapeDtypeStruct((clips, count, ROWS, LW), BF16),
            jax.ShapeDtypeStruct((clips, count, MROWS, LW), BF16),
        ]
        specs += [out(ROWS), out(MROWS)]
    return pl.pallas_call(
        partial(pool_forward, squeeze),
        grid=(count, clips),
        in_specs=[
            pl.BlockSpec((1, ROWS, rows.shape[2]), lambda j, i: (i, 0, 0)),
            pl.BlockSpec((1, weights.shape[1], LW), lambda j, i: (j + first, 0, 0)),
            tap,
        ]
        + ([tap] if squeeze else []),
        out_specs=specs,
        out_shape=shapes,
        scratch_shapes=[frame] * (2 if squeeze else 1),
        compiler_params=params(),
        cost_estimate=pl.CostEstimate(
            flops=60_000_000_000 * count // 10, bytes_accessed=4_000_000 * count, transcendentals=0
        ),
    )(rows, weights, kernels, *([squeezes] if squeeze else []))


def attention_forward(
    q_ref, kv_ref, m1_ref, m2_ref, ke_ref, tab_ref, fold_ref, one_ref, own_ref, lanes_ref,
    branch_ref, qa_ref, at_ref, lse_ref, keys, vt, scores, expo,
):
    keys[0:ROWS] = kv_ref[0, 0]
    keys[ROWS : ROWS + MROWS] = m1_ref[0, 0]
    keys[ROWS + MROWS :] = m2_ref[0, 0]
    vt[:, 0:ROWS] = kv_ref[0, 1].T
    memory = jnp.concatenate([m1_ref[0, 1], m2_ref[0, 1]], axis=0).T
    vt[:, ROWS:] = memory
    for head in range(LH):
        first = window_of(head)
        variant = head // 2
        win = slice(first, first + WIN)
        heads = lanes_ref[head]
        qm = q_ref[0, 0, :, win] * heads
        raw = nn(qm, tab_ref[head, 0]) + nn(qm, tab_ref[head, 1])
        raw = raw * own_ref[...]
        high = raw.astype(BF16)
        rest = (raw - high.astype(F32)).astype(BF16)
        placed = nn(high, fold_ref[variant, 0]) + nn(rest, fold_ref[variant, 1]) + one_ref[variant, 0:1]
        qa = qm + placed.astype(BF16)
        qa_ref[0, head] = qa

        def score(number, peak):
            rows = pl.ds(pl.multiple_of(number * BLOCK, BLOCK), BLOCK)
            ka = keys[rows, win] * heads[0:BLOCK] + ke_ref[0, variant, rows]
            s = nt(ka, qa)
            scores[rows] = s
            return jnp.maximum(peak, jnp.max(s, axis=0, keepdims=True))

        peak = lax.fori_loop(0, NBLOCK, score, jnp.full((1, ROWS), -3e38, F32))
        shift = peak * (SCALE * LOG2E)

        def soften(number, total):
            rows = pl.ds(pl.multiple_of(number * BLOCK, BLOCK), BLOCK)
            e = jnp.exp2(scores[rows] * (SCALE * LOG2E) - shift)
            expo[rows] = e.astype(BF16)
            return total + jnp.sum(e, axis=0, keepdims=True)

        total = lax.fori_loop(0, NBLOCK, soften, jnp.zeros((1, ROWS), F32))
        out = nn(vt[head * HEAD_DIM : (head + 1) * HEAD_DIM], expo[...]) * (1.0 / total)
        at_ref[0, head * HEAD_DIM : (head + 1) * HEAD_DIM] = out
        lse_ref[0, head : head + 1] = shift + jnp.log2(total)
    branch_ref[0] = (at_ref[0].T + q_ref[0, 0].astype(F32)).astype(BF16)


def whole(shape):
    return pl.BlockSpec(shape, lambda i: (0,) * len(shape))


def clip_block(*shape):
    return pl.BlockSpec((1,) + shape, lambda i: (i,) + (0,) * len(shape))


def call_attention_forward(clip, q, kv, memory, keys_extra, tables, consts):
    def block(*shape, at=clip):
        return pl.BlockSpec((1,) + shape, lambda i: (at,) + (0,) * len(shape))

    return pl.pallas_call(
        attention_forward,
        grid=(1,),
        in_specs=[
            block(1, ROWS, LW),
            block(2, ROWS, LW),
            block(2, MROWS, LW, at=clip + 1),
            block(2, MROWS, LW, at=clip),
            block(2, KEYS, WIN),
            whole((LH, 2, WIN, 256)),
            whole((2, 2, 256, WIN)),
            whole((2, 8, WIN)),
            whole((ROWS, 256)),
            whole((LH, ROWS, WIN)),
        ],
        out_specs=[
            clip_block(ROWS, LW),
            clip_block(LH, ROWS, WIN),
            clip_block(LW, ROWS),
            clip_block(8, ROWS),
        ],
        out_shape=[
            jax.ShapeDtypeStruct((1, ROWS, LW), BF16),
            jax.ShapeDtypeStruct((1, LH, ROWS, WIN), BF16),
            jax.ShapeDtypeStruct((1, LW, ROWS), F32),
            jax.ShapeDtypeStruct((1, 8, ROWS), F32),
        ],
        scratch_shapes=[
            pltpu.VMEM((KEYS, LW), BF16),
            pltpu.VMEM((LW, KEYS), BF16),
            pltpu.VMEM((KEYS, ROWS), F32),
            pltpu.VMEM((KEYS, ROWS), BF16),
        ],
        compiler_params=params(),
        cost_estimate=pl.CostEstimate(
            flops=13_000_000_000, bytes_accessed=5_000_000, transcendentals=1_500_000
        ),
    )(q, kv, memory, memory, keys_extra, tables, consts["fold"], consts["one"], consts["own"], consts["lanes"])


HALF = ROWS // 2


def simple_call(kernel, out_shape, gflops, *args):
    vmem = pl.BlockSpec(memory_space=pltpu.VMEM)
    many = isinstance(out_shape, list)
    return pl.pallas_call(
        kernel,
        in_specs=[vmem] * len(args),
        out_specs=[vmem] * len(out_shape) if many else vmem,
        out_shape=out_shape,
        compiler_params=params(),
        cost_estimate=pl.CostEstimate(
            flops=int(gflops * 1e9), bytes_accessed=2_000_000, transcendentals=0
        ),
    )(*args)


def half_rows(side):
    return pl.ds(pl.multiple_of(side * HALF, 16), HALF)


def project_kernel(branch, w, kept, sent):
    head = lax.axis_index("head")
    sent[...] = nn(branch[half_rows(1 - head)], w[...]).astype(BF16)
    kept[...] = nn(branch[half_rows(head)], w[...])


def middle_kernel(tokens, kept, recv, vectors, x1_ref, a2_ref):
    x1 = tokens[...].astype(F32) + kept[...] + recv[...].astype(F32) + vectors[0:1]
    x1_ref[...] = x1
    centred = x1 - jnp.mean(x1, axis=-1, keepdims=True)
    scale = lax.rsqrt(jnp.mean(centred * centred, axis=-1, keepdims=True) + EPSILON)
    a2_ref[...] = (centred * scale * vectors[1:2] + vectors[2:3]).astype(BF16)


FFN_BLOCK = 512
GELU_A = 0.7978845608028654
GELU_B = 0.044715


def ffn_kernel(a2, g, w1, b1, w2, act_ref, dpre_ref, da2_ref, out_ref, sums_ref):
    da2 = jnp.zeros(da2_ref.shape, F32)
    out = jnp.zeros(out_ref.shape, F32)
    for first in range(0, w1.shape[1], FFN_BLOCK):
        cols = slice(first, first + FFN_BLOCK)
        pre = nn(a2[...], w1[:, cols]) + b1[0:1, cols]
        square = pre * pre
        bent = jnp.tanh(GELU_A * (pre + GELU_B * (pre * square)))
        gate = 0.5 + 0.5 * bent
        act = (pre * gate).astype(BF16)
        slope = gate + 0.5 * pre * (1.0 - bent * bent) * (GELU_A * (1.0 + 3.0 * GELU_B * square))
        dpre = nt(g[...], w2[cols]) * slope
        low = dpre.astype(BF16)
        sums_ref[0:1, cols] = jnp.sum(dpre, axis=0, keepdims=True)
        act_ref[:, cols] = act
        dpre_ref[:, cols] = low
        da2 = da2 + nt(low, w1[:, cols])
        out = out + nn(act, w2[cols])
    da2_ref[...] = da2.astype(da2_ref.dtype)
    out_ref[...] = out.astype(out_ref.dtype)


def call_ffn(a2, g, w1, b1, w2, dtype):
    hidden = w1.shape[1]
    return simple_call(
        ffn_kernel,
        [
            jax.ShapeDtypeStruct((HALF, hidden), BF16),
            jax.ShapeDtypeStruct((HALF, hidden), BF16),
            jax.ShapeDtypeStruct(a2.shape, dtype),
            jax.ShapeDtypeStruct(a2.shape, dtype),
            jax.ShapeDtypeStruct((1, hidden), F32),
        ],
        5, a2, g, w1, b1, w2,
    )


def tn(a, b):
    return lax.dot_general(a, b, (((0,), (0,)), ((), ())), preferred_element_type=F32)


def weight_kernel(count, *refs):
    acts, dpres, a2s, gs = (refs[n * count : (n + 1) * count] for n in range(4))
    g2, g1 = refs[4 * count :]
    g2[...] = sum(tn(a[...], b[...]) for a, b in zip(acts, gs)).astype(BF16)
    g1[...] = sum(tn(a[...], b[...]) for a, b in zip(a2s, dpres)).astype(BF16)


def call_weights(acts, dpres, a2s, gs):
    hidden, width = acts[0].shape[1], gs[0].shape[1]
    count = len(acts)
    piece = pl.BlockSpec((HALF, LW), lambda i: (0, i))
    full = pl.BlockSpec((HALF, width), lambda i: (0, 0))
    return pl.pallas_call(
        partial(weight_kernel, count),
        grid=(hidden // LW,),
        in_specs=[piece] * (2 * count) + [full] * (2 * count),
        out_specs=[
            pl.BlockSpec((LW, width), lambda i: (i, 0)),
            pl.BlockSpec((width, LW), lambda i: (0, i)),
        ],
        out_shape=[
            jax.ShapeDtypeStruct((hidden, width), BF16),
            jax.ShapeDtypeStruct((width, hidden), BF16),
        ],
        compiler_params=params(),
        cost_estimate=pl.CostEstimate(flops=8_000_000_000, bytes_accessed=15_000_000, transcendentals=0),
    )(*acts, *dpres, *a2s, *gs)


def norm_back_kernel(kept, recv, x1_ref, g, vectors, dx_ref, low_ref, sums):
    u = kept[...] + recv[...].astype(F32)
    x1 = x1_ref[...]
    centred = x1 - jnp.mean(x1, axis=-1, keepdims=True)
    scale = lax.rsqrt(jnp.mean(centred * centred, axis=-1, keepdims=True) + EPSILON)
    xhat = centred * scale
    w = u * vectors[1:2]
    up = g[...].astype(F32)
    dx = up + scale * (
        w - jnp.mean(w, axis=-1, keepdims=True) - xhat * jnp.mean(w * xhat, axis=-1, keepdims=True)
    )
    dx_ref[...] = dx
    low_ref[...] = dx.astype(BF16)
    sums[0:1] = jnp.sum(dx, axis=0, keepdims=True)
    sums[1:2] = jnp.sum(u * xhat, axis=0, keepdims=True)
    sums[2:3] = jnp.sum(u, axis=0, keepdims=True)
    sums[3:4] = jnp.sum(up, axis=0, keepdims=True)
    sums[4:8] = jnp.zeros((4, u.shape[1]), F32)


def mix_kernel(mine, theirs, w, rows_ref, dmix_ref):
    head = lax.axis_index("head")
    for side, part in ((head, mine), (1 - head, theirs)):
        rows_ref[half_rows(side)] = part[...]
        dmix_ref[half_rows(side)] = nt(part[...], w[...]).astype(BF16)


EARLY = 16
HEAD_EARLY = 8
LATE = 8
MESH = pl.DeviceIdType.MESH


def remote(src, dst, send, recv, peer):
    made = pltpu.make_async_remote_copy(
        src_ref=src, dst_ref=dst, send_sem=send, recv_sem=recv, device_id=peer, device_id_type=MESH
    )
    made.start()
    return made


def local(src, dst, sem):
    made = pltpu.make_async_copy(src, dst, sem)
    made.start()
    return made


class Place:
    def __init__(self, groups):
        dp = lax.axis_index("dp")
        head = lax.axis_index("head")
        self.groups = groups
        self.dp, self.head = dp, head
        self.core = lax.rem(dp, 2)
        self.xbit = lax.rem(lax.div(dp, 2), 2)
        self.group = lax.div(dp, 4)
        self.to_core = (dp + 1 - 2 * self.core, head)
        self.to_x = (dp + 2 - 4 * self.xbit, head)
        self.to_y = (dp, 1 - head)
        self.peers = [
            (lax.rem(self.group + o, groups) * 4 + lax.rem(dp, 4), head) for o in range(1, groups)
        ]

    def greet(self, more=()):
        barrier = pltpu.get_barrier_semaphore()
        signalled = [self.to_core, self.to_x, self.to_y] + self.peers + list(more)
        for peer in signalled:
            pl.semaphore_signal(barrier, inc=1, device_id=peer, device_id_type=MESH)
        pl.semaphore_wait(barrier, len(signalled))


class Piece:
    def __init__(self, place, rows, source, result, reduce_refs, send, recv):
        self.at = place
        self.half, self.quarter = rows // 2, rows // 4
        self.chunk = rows // 4 // place.groups
        self.source, self.result = source, result
        self.refs = reduce_refs
        self.send, self.recv = send, recv
        self.tile = 16 if reduce_refs is None or reduce_refs[0].dtype == BF16 else 8
        self.flights = {}

    def start(self, key, number, src, dst, peer):
        self.flights[key] = remote(src, dst, self.send.at[number], self.recv.at[number], peer)

    def base(self, g):
        at = self.at
        return pl.multiple_of(at.core * self.half + at.xbit * self.quarter + g * self.chunk, self.tile)

    def a(self):
        theirs = pl.multiple_of((1 - self.at.core) * self.half, self.tile)
        self.start("a", 0, self.source(theirs, self.half), self.refs[0], self.at.to_core)

    def sum_rows(self, which):
        recv_a = self.refs[0]
        first = pl.multiple_of(which * self.quarter, self.tile)
        own = self.source(pl.multiple_of(self.at.core * self.half + which * self.quarter, self.tile), self.quarter)
        return own[...].astype(F32) + recv_a[pl.ds(first, self.quarter)].astype(F32)

    def b(self):
        _, send_b, recv_b, _, _ = self.refs
        self.flights["a"].wait()
        send_b[...] = self.sum_rows(1 - self.at.xbit).astype(send_b.dtype)
        self.start("b", 1, send_b, recv_b, self.at.to_x)

    def c(self):
        _, _, recv_b, send_c, recv_c = self.refs
        self.flights["b"].wait()
        send_c[...] = (self.sum_rows(self.at.xbit) + recv_b[...].astype(F32)).astype(send_c.dtype)
        for o in range(1, self.at.groups):
            first = pl.multiple_of(lax.rem(self.at.group + o, self.at.groups) * self.chunk, self.tile)
            self.start(
                ("c", o), 1 + o, send_c.at[pl.ds(first, self.chunk)], recv_c.at[o - 1], self.at.peers[o - 1]
            )

    def total(self):
        _, _, _, send_c, recv_c = self.refs
        own = send_c[pl.ds(pl.multiple_of(self.at.group * self.chunk, self.tile), self.chunk)].astype(F32)
        for o in range(1, self.at.groups):
            self.flights["c", o].wait()
            own = own + recv_c[o - 1].astype(F32)
        return own

    def d(self, own=None):
        own = self.total() if own is None else own
        mine = self.result(self.base(self.at.group), self.chunk)
        mine[...] = own.astype(mine.dtype)
        for o in range(1, self.at.groups):
            number = self.at.groups + o
            self.start(("d", o), number, mine, mine, self.at.peers[o - 1])

    def e(self):
        for o in range(1, self.at.groups):
            self.flights["d", o].wait()
        mine = self.result(self.base(0), self.quarter)
        self.start("e", 2 * self.at.groups, mine, mine, self.at.to_x)

    def f(self):
        self.flights["e"].wait()
        mine = self.result(pl.multiple_of(self.at.core * self.half, self.tile), self.half)
        self.start("f", 2 * self.at.groups + 1, mine, mine, self.at.to_core)

    def g(self):
        self.flights["f"].wait()


def piece_scratch(rows, groups, width, dtype, count):
    half, quarter = rows // 2, rows // 4
    return [
        pltpu.VMEM((count, half, width), dtype),
        pltpu.VMEM((count, quarter, width), dtype),
        pltpu.VMEM((count, quarter, width), dtype),
        pltpu.VMEM((count, quarter, width), dtype),
        pltpu.VMEM((count, groups - 1, quarter // groups, width), dtype),
    ]


class Small:
    def __init__(self, place, buffer, slots, rows_y, send, recv, base):
        self.at, self.buffer, self.slots, self.rows_y = place, buffer, slots, rows_y
        self.send, self.recv, self.base = send, recv, base
        self.flights = {}

    def start(self, number, src, dst, peer):
        self.flights[number] = remote(
            src, dst, self.send.at[self.base + number], self.recv.at[self.base + number], peer
        )

    def one(self):
        self.start(0, self.buffer.at[0, 0 : self.rows_y], self.slots[0], self.at.to_y)

    def two(self):
        self.flights[0].wait()
        if self.rows_y < self.buffer.shape[1]:
            self.buffer[1, self.rows_y :] = self.buffer[0, self.rows_y :]
        self.buffer[1, 0 : self.rows_y] = self.buffer[0, 0 : self.rows_y] + self.slots[0][...]
        self.start(1, self.buffer.at[1], self.slots[1], self.at.to_core)

    def three(self):
        self.flights[1].wait()
        self.buffer[2] = self.buffer[1] + self.slots[1][...]
        self.start(2, self.buffer.at[2], self.slots[2], self.at.to_x)

    def four(self):
        self.flights[2].wait()
        self.buffer[3] = self.buffer[2] + self.slots[2][...]
        for o in range(1, self.at.groups):
            self.start(2 + o, self.buffer.at[3], self.slots[3].at[o - 1], self.at.peers[o - 1])

    def five(self, target):
        added = self.buffer[3]
        for o in range(1, self.at.groups):
            self.flights[2 + o].wait()
            added = added + self.slots[3][o - 1]
        target[...] = added


def small_scratch(rows, rows_y, groups, width):
    return [
        pltpu.VMEM((4, rows, width), F32),
        pltpu.VMEM((rows_y, width), F32),
        pltpu.VMEM((rows, width), F32),
        pltpu.VMEM((rows, width), F32),
        pltpu.VMEM((groups - 1, rows, width), F32),
    ]


def attention_backward(
    groups,
    q_ref, kv_ref, mem_ref, ke_hbm, qa_hbm0, qa_hbm1, dm_ref0, dm_ref1, at_hbm0, at_hbm1, lse_ref0, lse_ref1,
    rt_ref, grow_ref, ownt_ref, ekey_ref,
    lanes_ref, g2_ref, g1_ref, sums0, sums1, hidden0, hidden1, hidden2, hidden3,
    dq_ref, dkv_ref, dr_ref, chunks_ref, early_out,
    ke_ref, qa_ref, at_ref, keys, values, kt, dmt, qms, dms, dqt,
    recv_a, send_b, recv_b, send_c, recv_c, s0, s1, s2, s3, s4,
    loads, sems_send, sems_recv, small_send, small_recv,
):
    place = Place(groups)
    clips = q_ref.shape[0]
    dm_refs, lse_refs = (dm_ref0, dm_ref1), (lse_ref0, lse_ref1)
    lead = [
        [
            local(ke_hbm.at[clip], ke_ref.at[clip], loads.at[3 * clip]),
            local((qa_hbm0, qa_hbm1)[clip].at[0], qa_ref.at[clip], loads.at[3 * clip + 1]),
            local((at_hbm0, at_hbm1)[clip].at[0], at_ref.at[clip], loads.at[3 * clip + 2]),
        ]
        for clip in range(clips)
    ]
    place.greet()
    total = g1_ref.shape[0]

    def view(number):
        if number < 4:
            base, col = (number // 2) * total, (number % 2) * LW
            return lambda first, n: g2_ref.at[pl.ds(base + first, n), col : col + LW]
        col = (number - 4) * LW
        return lambda first, n: g1_ref.at[pl.ds(first, n), col : col + LW]

    pieces = [
        Piece(
            place, total, view(number), None,
            [ref.at[number] for ref in (recv_a, send_b, recv_b, send_c, recv_c)],
            sems_send.at[number], sems_recv.at[number],
        )
        for number in range(8)
    ]
    small = Small(place, s0, (s1, s2, s3, s4), HEAD_EARLY, small_send, small_recv, 0)
    s0[0, 0:HEAD_EARLY] = sums0[...] + sums1[...]
    hidden = hidden0[...] + hidden1[...] + hidden2[...] + hidden3[...]
    width = s0.shape[2]
    s0[0, HEAD_EARLY:EARLY] = jnp.zeros((EARLY - HEAD_EARLY, width), F32)
    for n in range(hidden.shape[1] // width):
        s0[0, HEAD_EARLY + n : HEAD_EARLY + n + 1] = hidden[:, n * width : (n + 1) * width]
    small.one()
    for piece in pieces:
        piece.a()
    moves = [
        [pieces[0].b, pieces[1].b],
        [pieces[2].b, small.two],
        [pieces[3].b, pieces[0].c],
        [pieces[4].b, pieces[1].c, small.three],
        [pieces[5].b, pieces[2].c],
        [pieces[6].b, pieces[3].c],
        [pieces[7].b, pieces[4].c],
        [pieces[5].c, small.four],
        [pieces[6].c],
        [pieces[7].c],
        [partial(small.five, early_out)],
    ]

    def pump():
        if moves:
            for move in moves.pop(0):
                move()

    dr_ref[...] = jnp.zeros_like(dr_ref)
    for clip in range(clips):
        near, far = mem_ref.at[clip + 1], mem_ref.at[clip]
        keys[0:ROWS] = kv_ref[clip, 0]
        keys[ROWS : ROWS + MROWS] = near[0]
        keys[ROWS + MROWS :] = far[0]
        values[0:ROWS] = kv_ref[clip, 1]
        values[ROWS : ROWS + MROWS] = near[1]
        values[ROWS + MROWS :] = far[1]
        kt[0:LW] = keys[...].T
        kt[LW:] = ekey_ref[...]
        dmt[...] = dm_refs[clip][...].astype(F32).T
        dqt[...] = jnp.zeros_like(dqt)
        for made in lead[clip]:
            made.wait()
        deltas = []
        for head in range(LH):
            first = window_of(head)
            win = slice(first, first + WIN)
            span = slice(head * HEAD_DIM, (head + 1) * HEAD_DIM)
            qms[head] = q_ref[clip, 0, :, win] * lanes_ref[head]
            dms[head] = dm_refs[clip][:, win] * lanes_ref[head]
            deltas.append(jnp.sum(dmt[span] * at_ref[clip, span], axis=0, keepdims=True))

        def step(number, _):
            rows = pl.ds(pl.multiple_of(number * BLOCK, BLOCK), BLOCK)
            dk_parts, dv_parts = [], []
            for head in range(LH):
                first = window_of(head)
                variant = head // 2
                win = slice(first, first + WIN)
                ka = keys[rows, win] * lanes_ref[head, 0:BLOCK] + ke_ref[clip, variant, rows]
                s = nt(ka, qa_ref[clip, head])
                p = jnp.exp2(s * (SCALE * LOG2E) - lse_refs[clip][0, head : head + 1])
                dp = nt(values[rows, win], dms[head])
                ds = (p * (dp - deltas[head])).astype(BF16)
                dv_parts.append(nn(p.astype(BF16), dms[head]))
                dk_parts.append(nn(ds, qms[head]) * SCALE)
                kts = jnp.concatenate(
                    [kt[head * HEAD_DIM : (head + 1) * HEAD_DIM, rows], kt[LW:, rows]], axis=0
                )
                dqt[head] += nn(kts, ds)
            for which, parts in ((0, dk_parts), (1, dv_parts)):
                dkv_ref[clip, which, rows] = jnp.concatenate(
                    [
                        parts[0][:, 0:128] + parts[1][:, 0:128],
                        parts[1][:, 128:256] + parts[2][:, 0:128],
                        parts[2][:, 128:256] + parts[3][:, 128:256],
                    ],
                    axis=1,
                )
            return 0

        for begin, end in ((0, 2), (2, 4), (4, 6), (6, 7)):
            pump()
            lax.fori_loop(begin, end, step, 0)
        for head in range(LH):
            first = window_of(head)
            span = slice(head * HEAD_DIM, (head + 1) * HEAD_DIM)
            total_t = dqt[head]
            grown = nn(grow_ref[...], total_t[HEAD_DIM:].astype(BF16)) * ownt_ref[...]
            grown = grown.astype(BF16)
            dmt[span] = dmt[span] + total_t[0:HEAD_DIM] * SCALE + nn(rt_ref[...], grown)
            dr_ref[:, first : first + WIN] += nn(grown, qms[head])
        dq_ref[clip] = dmt[...].T
    while moves:
        pump()
    for number in range(8):
        chunks_ref[number] = pieces[number].total().astype(BF16)


def padded_rows(width, groups):
    return -(-width // (4 * groups) // 16) * 16 * 4 * groups


def call_attention_backward(q, kv, memory, keys_extra, qa, dmix, at, lse, rt, g2, g1, sums, hidden, consts):
    clips, width = q.shape[0], sums[0].shape[1]
    groups = lax.axis_size("dp") // 4
    total = padded_rows(width, groups)
    if total != width:
        g1 = jnp.pad(g1, ((0, total - width), (0, 0)))
        g2 = jnp.pad(g2.reshape(2, width, width), ((0, 0), (0, total - width), (0, 0))).reshape(-1, width)
    vmem = pl.BlockSpec(memory_space=pltpu.VMEM)
    hbm = pl.BlockSpec(memory_space=pl.ANY)
    return pl.pallas_call(
        partial(attention_backward, groups),
        in_specs=[vmem] * 3 + [hbm] * 3 + [vmem] * 2 + [hbm] * 2 + [vmem] * 15,
        out_specs=[vmem] * 5,
        out_shape=[
            jax.ShapeDtypeStruct((clips, ROWS, LW), F32),
            jax.ShapeDtypeStruct((clips, 2, KEYS, LW), F32),
            jax.ShapeDtypeStruct((256, LW), F32),
            jax.ShapeDtypeStruct((8, total // 4 // groups, LW), BF16),
            jax.ShapeDtypeStruct((EARLY, width), F32),
        ],
        scratch_shapes=[
            pltpu.VMEM(keys_extra.shape, BF16),
            pltpu.VMEM((clips, LH, ROWS, WIN), BF16),
            pltpu.VMEM((clips, LW, ROWS), F32),
            pltpu.VMEM((KEYS, LW), BF16),
            pltpu.VMEM((KEYS, LW), BF16),
            pltpu.VMEM((LW + 32, KEYS), BF16),
            pltpu.VMEM((LW, ROWS), F32),
            pltpu.VMEM((LH, ROWS, WIN), BF16),
            pltpu.VMEM((LH, ROWS, WIN), BF16),
            pltpu.VMEM((LH, HEAD_DIM + 32, ROWS), F32),
            *piece_scratch(total, groups, LW, BF16, 8),
            *small_scratch(EARLY, HEAD_EARLY, groups, width),
            pltpu.SemaphoreType.DMA((3 * clips,)),
            pltpu.SemaphoreType.DMA((8, groups + 1)),
            pltpu.SemaphoreType.DMA((8, groups + 1)),
            pltpu.SemaphoreType.DMA((groups + 2,)),
            pltpu.SemaphoreType.DMA((groups + 2,)),
        ],
        compiler_params=params(collective_id=0, has_side_effects=True),
        cost_estimate=pl.CostEstimate(
            flops=40_000_000_000, bytes_accessed=20_000_000, transcendentals=3_000_000
        ),
    )(
        q, kv, memory, keys_extra, *qa, *dmix, *at, *lse, rt,
        consts["grow"], consts["ownt"], consts["ekey"], consts["lanes"], g2, g1, *sums, *hidden,
    )


SMALL_ROWS = 256
REL_ROWS = 48


def finish_kernel(
    groups, width,
    dq_hbm, dkv_hbm, x0q_hbm, x0kv_hbm, kvf_hbm, taps_hbm, rows_a_hbm, rows_x0, rows_x1, branch0, branch1,
    w_hbm, tokens_hbm, middle0, middle1, chunks_ref, dr_ref, gain, foldl_ref, pick_ref,
    grad, out2, out1, outp, outq, small_out, late_out,
    dq, dkv, x0q, x0kv, kvf, taps_ref, rows_a, rows_x, branch, w_ref, tokens, middle,
    us, ms, kacc, dx, dmem_send, dmem_recv, res2, res1, resp, grads, stage, stage_t,
    recv_a, send_b, recv_b, send_c, recv_c, sm_raw, sm, sm_y, sm_res, fa, fb, fc, fd, fe,
    send_y, recv_y, l0, l1, l2, l3, l4,
    loads, stores, sems_send, sems_recv, small_send, small_recv, mem_sems,
):
    place = Place(groups)
    clips = dq.shape[0]
    total = rows_a.shape[1]
    names = (
        "dkv", "dq", "x0q", "taps", "rows_x0", "rows_x1", "branch0", "branch1", "x0kv", "kvf", "rows_a", "w",
        "tokens", "middle0", "middle1",
    )
    pairs = (
        (dkv_hbm, dkv), (dq_hbm, dq), (x0q_hbm, x0q), (taps_hbm, taps_ref),
        (rows_x0, rows_x.at[0:ROWS]), (rows_x1, rows_x.at[ROWS:]), (branch0, branch.at[0:ROWS]),
        (branch1, branch.at[ROWS:]), (x0kv_hbm, x0kv), (kvf_hbm, kvf), (rows_a_hbm, rows_a), (w_hbm, w_ref),
        (tokens_hbm, tokens), (middle0, middle.at[0]), (middle1, middle.at[1]),
    )
    lead = {
        name: local(src, dst, loads.at[n]) for n, (name, (src, dst)) in enumerate(zip(names, pairs))
    }
    count = groups * 4
    behind = (lax.rem(place.dp + count - 1, count), place.head)
    ahead = (lax.rem(place.dp + 1, count), place.head)
    place.greet((behind, ahead))

    def view2(number):
        if number < 4:
            base, col = (number // 2) * total, (number % 2) * LW
            return lambda first, n: res2.at[pl.ds(base + first, n), col : col + LW]
        col = (number - 4) * LW
        return lambda first, n: res1.at[pl.ds(first, n), col : col + LW]

    ffn = [
        Piece(place, total, None, view2(number), None, sems_send.at[number], sems_recv.at[number])
        for number in range(8)
    ]

    def rows_of(ref):
        return lambda first, n: ref.at[pl.ds(first, n)]

    late = [
        Piece(
            place, total, rows_of(grads.at[number]), rows_of(resp.at[number]),
            [ref.at[number] for ref in (recv_a, send_b, recv_b, send_c, recv_c)],
            sems_send.at[8 + number], sems_recv.at[8 + number],
        )
        for number in range(4)
    ]
    tiny = Piece(
        place, sm.shape[0], rows_of(sm), rows_of(sm_res),
        [ref.at[0] for ref in (fa, fb, fc, fd, fe)], sems_send.at[12], sems_recv.at[12],
    )
    ends = Small(place, l0, (l1, l2, l3, l4), LATE, small_send, small_recv, 0)

    stored = []

    def flush(source, target):
        slot = len(stored) % 2
        if len(stored) > 1:
            stored[-2].wait()
        stage[slot] = source[...].astype(F32)
        stored.append(local(stage.at[slot], target, stores.at[slot]))

    def store2(number):
        ffn[number].g()
        if number < 4:
            base, col = (number // 2) * total, (number % 2) * LW
            target = out2.at[base : base + total, col : col + LW]
        else:
            col = (number - 4) * LW
            target = out1.at[:, col : col + LW]
        flush(view2(number)(0, total), target)

    def product(number):
        left, right = (
            (rows_x, branch), (rows_a, dx.at[0]), (rows_a, dx.at[1]), (rows_a, dx.at[2])
        )[number]
        for first in range(0, total, total // 2):
            grads[number, first : first + total // 2] = lax.dot_general(
                left[:, first : first + total // 2], right[...], (((0,), (0,)), ((), ())),
                preferred_element_type=F32,
            ).astype(BF16)
        late[number].a()

    def shifted_store(dst, first, both, lanes):
        both = both.reshape(2 * HGT, PADW, 128)
        for c, shift in ((0, 1), (1, 0), (2, PADW - 1)):
            moved = pltpu.roll(both, shift, axis=1) if shift else both
            dst[c, pl.ds(first, 2), 1 : HGT + 1, :, lanes] = moved.reshape(2, HGT, PADW, 128)

    def pooled(which, clip):
        field = x0q.at[clip, 0] if which == 0 else x0kv.at[clip, which - 1]
        upstream = dq.at[clip] if which == 0 else dkv.at[clip, which - 1]
        if which:
            memory = dmem_recv[clip, which - 1].astype(F32)
            memory = jnp.where(place.dp == count - 1, 0.0, memory)
            for later in range(clip + 1, clips):
                if later == clip + 1:
                    memory = memory + dkv[later, which - 1, ROWS : ROWS + MROWS]
                if later == clip + 2:
                    memory = memory + dkv[later, which - 1, ROWS + MROWS :]
            spread(ms, 0, memory.reshape(TM, HGT, PADW, LW))
        else:
            spread(us, 1, upstream[...].reshape(T_LEN, HGT, PADW, LW))

        def tile_loop(tile, _):
            lanes = pl.ds(pl.multiple_of(tile * 128, 128), 128)
            if which:

                def squeeze_step(pair, _):
                    rows = pl.ds(pl.multiple_of(pair * 112, 112), 112)
                    own = upstream[rows, lanes].reshape(2, HGT, PADW, 128)
                    fields = kvf[clip, which - 1, rows, lanes].astype(F32).reshape(2, HGT, PADW, 128)
                    acc = [own[0], own[1]]
                    for a, d, frame in ((1, 0, 0), (0, 1, 1), (2, 1, 0)):
                        for c in range(3):
                            block = ms[2 - c, pair + frame, :, :, lanes]
                            for b in range(3):
                                at = block[2 - b : 2 - b + HGT]
                                number = a * 9 + b * 3 + c
                                acc[d] = acc[d] + taps_ref[2 + which, number, :, lanes][None] * at
                                kacc[2 + which, number, :, lanes] += jnp.sum(fields[d] * at, axis=0)
                    shifted_store(us, 2 * pair + 1, keep_rows(jnp.stack(acc)), lanes)
                    return 0

                lax.fori_loop(0, TM, squeeze_step, 0)

            def pair_step(pair, _):
                rows = pl.ds(pl.multiple_of(pair * 112, 112), 112)
                fields = field[rows, lanes].astype(F32).reshape(2, HGT, PADW, 128)
                acc = [jnp.zeros((HGT, PADW, 128), F32) for _ in range(2)]
                for a in range(3):
                    for c in range(3):
                        sums = [jnp.zeros((PADW, 128), F32) for _ in range(3)]
                        for d in range(2):
                            block = us[2 - c, 2 * pair + d + 2 - a, :, :, lanes]
                            for b in range(3):
                                at = block[2 - b : 2 - b + HGT]
                                acc[d] = acc[d] + taps_ref[which, a * 9 + b * 3 + c, :, lanes][None] * at
                                sums[b] = sums[b] + jnp.sum(fields[d] * at, axis=0)
                        for b in range(3):
                            kacc[which, a * 9 + b * 3 + c, :, lanes] += sums[b]
                both = keep_rows(jnp.stack(acc))
                out_rows = pl.ds(pl.multiple_of(clip * ROWS + pair * 112, 16), 112)
                dx[which, out_rows, lanes] = both.reshape(112, 128).astype(BF16)
                return 0

            lax.fori_loop(0, T_LEN // 2, pair_step, 0)
            return 0

        lax.fori_loop(0, LW // 128, tile_loop, 0)

    side_rows = ROWS // 2

    def input_gradient(clip, side):
        rows = pl.ds(pl.multiple_of(clip * ROWS + side * side_rows, 16), side_rows)
        return nt(dx[0, rows], w_ref[0]) + nt(dx[1, rows], w_ref[1]) + nt(dx[2, rows], w_ref[2])

    crossing = {}

    def cross(clip):
        send_y[clip] = input_gradient(clip, 1 - place.head).astype(BF16)
        number = groups + 2 + clip
        crossing[clip] = remote(
            send_y.at[clip], recv_y.at[clip], small_send.at[number], small_recv.at[number], place.to_y
        )

    def normed_gradient(clip):
        mine = input_gradient(clip, place.head)
        crossing[clip].wait()
        u = mine + recv_y[clip].astype(F32)
        v = tokens[clip].astype(F32)
        centred = v - jnp.mean(v, axis=-1, keepdims=True)
        scale = lax.rsqrt(jnp.mean(centred * centred, axis=-1, keepdims=True) + EPSILON)
        xhat = centred * scale
        w = u * gain[0:1]
        dv = scale * (
            w - jnp.mean(w, axis=-1, keepdims=True) - xhat * jnp.mean(w * xhat, axis=-1, keepdims=True)
        )
        grad[clip] = middle[clip] + dv
        l0[0, 0:1] += jnp.sum(u * xhat, axis=0, keepdims=True)
        l0[0, 1:2] += jnp.sum(u, axis=0, keepdims=True)

    def exact(a, b):
        return jnp.dot(a, b, precision=HIGHEST, preferred_element_type=F32)

    def small_start():
        folded = exact(dr_ref[...], foldl_ref[...])
        sm_raw[0:REL_ROWS] = exact(pick_ref[...], folded)
        for which in range(5):
            first = REL_ROWS + 32 * which
            sums = jnp.sum(kacc[which], axis=1)
            sums = jnp.concatenate([sums, jnp.zeros((5, LW), F32)], axis=0)
            sm_raw[first : first + 32] = exact(sums, foldl_ref[...])
        number = groups + 2 + clips
        crossing["small"] = remote(
            sm_raw, sm_y, small_send.at[number], small_recv.at[number], place.to_y
        )

    def small_next():
        crossing["small"].wait()
        sm[...] = sm_raw[...] + sm_y[...]
        tiny.a()

    ffn[0].d(chunks_ref[0])
    ffn[1].d(chunks_ref[1])
    us[...] = jnp.zeros_like(us)
    ms[...] = jnp.zeros_like(ms)
    kacc[...] = jnp.zeros_like(kacc)
    l0[0] = jnp.zeros_like(l0[0])
    sm_raw[...] = jnp.zeros_like(sm_raw)
    lead["dkv"].wait()
    for which in range(2):
        dmem_send[0, which] = dkv[0, which, ROWS + MROWS :].astype(BF16)
        dmem_send[1, which] = (
            dkv[0, which, ROWS : ROWS + MROWS] + dkv[1, which, ROWS + MROWS :]
        ).astype(BF16)
    memory_flight = remote(dmem_send, dmem_recv, mem_sems.at[0], mem_sems.at[1], behind)
    for name in ("rows_x0", "rows_x1", "branch0", "branch1"):
        lead[name].wait()
    product(0)
    for name in ("dq", "x0q", "taps"):
        lead[name].wait()
    late[0].b()
    ffn[2].d(chunks_ref[2])
    pooled(0, 0)
    ffn[0].e()
    ffn[3].d(chunks_ref[3])
    ffn[1].e()
    pooled(0, 1)
    ffn[4].d(chunks_ref[4])
    ffn[2].e()
    ffn[0].f()
    lead["rows_a"].wait()
    product(1)
    late[0].c()
    memory_flight.wait()
    lead["x0kv"].wait()
    lead["kvf"].wait()
    late[1].b()
    pooled(1, 0)
    ffn[5].d(chunks_ref[5])
    ffn[3].e()
    ffn[1].f()
    late[0].d()
    ffn[4].e()
    pooled(2, 0)
    late[1].c()
    ffn[6].d(chunks_ref[6])
    late[0].e()
    ffn[2].f()
    store2(0)
    lead["w"].wait()
    cross(0)
    ffn[5].e()
    pooled(1, 1)
    late[1].d()
    ffn[7].d(chunks_ref[7])
    product(2)
    late[2].b()
    ffn[6].e()
    ffn[3].f()
    store2(1)
    pooled(2, 1)
    product(3)
    cross(1)
    late[2].c()
    late[3].b()
    small_start()
    ffn[4].f()
    late[0].f()
    store2(2)
    lead["tokens"].wait()
    lead["middle0"].wait()
    lead["middle1"].wait()
    normed_gradient(0)
    small_next()
    late[2].d()
    late[3].c()
    late[1].e()
    ffn[5].f()
    store2(3)
    tiny.b()
    normed_gradient(1)
    ends.one()
    late[3].d()
    tiny.c()
    late[2].e()
    ffn[7].e()
    ends.two()
    ffn[6].f()
    store2(4)
    late[1].f()
    tiny.d()
    ends.three()
    late[0].g()
    stage_t[...] = resp[0].astype(F32).T
    turned = local(stage_t, outp, stores.at[2])
    late[3].e()
    ends.four()
    tiny.e()
    store2(5)
    late[2].f()
    ffn[7].f()
    store2(6)
    late[1].g()
    sent_q = local(resp.at[1], outq.at[0], stores.at[3])
    tiny.f()
    ends.five(late_out)
    store2(7)
    late[2].g()
    sent_k = local(resp.at[2], outq.at[1], stores.at[4])
    late[3].f()
    tiny.g()
    late[3].g()
    sent_v = local(resp.at[3], outq.at[2], stores.at[5])
    small_out[...] = sm_res[...]
    for made in [turned, sent_q, sent_k, sent_v] + stored[-2:]:
        made.wait()


def call_finish(dq, dkv, x0q, x0kv, kvf, all_taps, rows_a, rows_x, branch, weights, tokens, middle, chunks, dr, gain):
    groups = lax.axis_size("dp") // 4
    width = tokens.shape[2]
    total = padded_rows(width, groups)
    clips, side = tokens.shape[:2]
    if total != width:
        extra = ((0, 0), (0, total - width))
        rows_a, rows_x = jnp.pad(rows_a, extra), [jnp.pad(x, extra) for x in rows_x]
    small_rows = -(-SMALL_ROWS // (32 * groups)) * 32 * groups
    foldl = np.zeros((LW, 128), np.float32)
    foldl[np.arange(LW), np.arange(LW) % HEAD_DIM] = 1
    pick = np.zeros((REL_ROWS, 256), np.float32)
    pick[:NREL] = PICK.T
    vmem = pl.BlockSpec(memory_space=pltpu.VMEM)
    hbm = pl.BlockSpec(memory_space=pl.ANY)
    streamed = [dq, dkv, x0q, x0kv, kvf, all_taps, rows_a, *rows_x, *branch, weights, tokens, *middle]
    held = [
        (array.shape, array.dtype)
        for array in (dq, dkv, x0q, x0kv, kvf, all_taps, rows_a)
    ] + [
        ((clips * ROWS, total), BF16), ((clips * ROWS, LW), BF16), (weights.shape, BF16), (tokens.shape, BF16),
        (tokens.shape, F32),
    ]
    frame = pltpu.VMEM((3, T_LEN + 2, HGT + 2, PADW, LW), F32)
    return pl.pallas_call(
        partial(finish_kernel, groups, width),
        in_specs=[hbm] * len(streamed) + [vmem] * 5,
        out_specs=[vmem, hbm, hbm, hbm, hbm, vmem, vmem],
        out_shape=[
            jax.ShapeDtypeStruct(tokens.shape, F32),
            jax.ShapeDtypeStruct((2 * total, width), F32),
            jax.ShapeDtypeStruct((total, 4 * LW), F32),
            jax.ShapeDtypeStruct((LW, total), F32),
            jax.ShapeDtypeStruct((3, total, LW), BF16),
            jax.ShapeDtypeStruct((small_rows, 128), F32),
            jax.ShapeDtypeStruct((LATE, width), F32),
        ],
        scratch_shapes=[pltpu.VMEM(shape, dtype) for shape, dtype in held]
        + [
            frame,
            pltpu.VMEM((3, TM + 1, HGT + 2, PADW, LW), F32),
            pltpu.VMEM((5, 27, 8, LW), F32),
            pltpu.VMEM((3, clips * ROWS, LW), BF16),
            pltpu.VMEM((2, 2, MROWS, LW), BF16),
            pltpu.VMEM((2, 2, MROWS, LW), BF16),
            pltpu.VMEM((2 * total, width), BF16),
            pltpu.VMEM((total, 4 * LW), BF16),
            pltpu.VMEM((4, total, LW), BF16),
            pltpu.VMEM((4, total, LW), BF16),
            pltpu.VMEM((2, total, LW), F32),
            pltpu.VMEM((LW, total), F32),
            *piece_scratch(total, groups, LW, BF16, 4),
            pltpu.VMEM((small_rows, 128), F32),
            pltpu.VMEM((small_rows, 128), F32),
            pltpu.VMEM((small_rows, 128), F32),
            pltpu.VMEM((small_rows, 128), F32),
            *piece_scratch(small_rows, groups, 128, F32, 1),
            pltpu.VMEM((clips, side, width), BF16),
            pltpu.VMEM((clips, side, width), BF16),
            *small_scratch(LATE, LATE, groups, width),
            pltpu.SemaphoreType.DMA((15,)),
            pltpu.SemaphoreType.DMA((6,)),
            pltpu.SemaphoreType.DMA((13, 2 * groups + 2)),
            pltpu.SemaphoreType.DMA((13, 2 * groups + 2)),
            pltpu.SemaphoreType.DMA((groups + 3 + clips,)),
            pltpu.SemaphoreType.DMA((groups + 3 + clips,)),
            pltpu.SemaphoreType.DMA((2,)),
        ],
        compiler_params=params(collective_id=1, has_side_effects=True),
        cost_estimate=pl.CostEstimate(
            flops=60_000_000_000, bytes_accessed=40_000_000, transcendentals=0
        ),
    )(*streamed, chunks, dr, gain, jnp.asarray(foldl), jnp.asarray(pick))


def from_behind(x, axis, by):
    count = lax.axis_size(axis)
    pairs = [(i, i + by) for i in range(count) if 0 <= i + by < count]
    return lax.ppermute(x, axis, pairs)


def layer_norm(values, scaling, offset):
    average = jnp.mean(values, axis=-1, keepdims=True)
    centred = values - average
    variance = jnp.mean(centred * centred, axis=-1, keepdims=True)
    return centred * lax.rsqrt(variance + EPSILON) * scaling + offset


def pad_rows(x):
    lead = x.shape[0]
    frames = x.shape[1] // (HGT * WID)
    grid = x.reshape(lead, frames, HGT, WID, x.shape[-1])
    grid = jnp.pad(grid, ((0, 0), (0, 0), (0, 0), (0, PADW - WID), (0, 0)))
    return grid.reshape(lead, frames * HGT * PADW, x.shape[-1])


def drop_rows(x):
    lead = x.shape[0]
    frames = x.shape[1] // (HGT * PADW)
    grid = x.reshape(lead, frames, HGT, PADW, x.shape[-1])[:, :, :, :WID]
    return grid.reshape(lead, frames * HGT * WID, x.shape[-1])


def swap(x):
    return lax.ppermute(x, "head", [(0, 1), (1, 0)])


def gather_rows(x):
    half = x.shape[1]
    mine = lax.axis_index("head") * half
    both = jnp.concatenate([x, x], axis=1)
    return lax.dynamic_update_slice_in_dim(both, swap(x), half - mine, axis=1)


def taps(kernel):
    return jnp.broadcast_to(jnp.tile(kernel, (1, LH))[:, None, :], (27, 8, LW))


def on_device(
    tokens,
    ln1_gain,
    ln1_bias,
    w_qkv,
    pool_q,
    pool_k,
    pool_v,
    squeeze_k,
    squeeze_v,
    rel_t,
    rel_h,
    rel_w,
    w_proj,
    proj_bias,
    ln2_gain,
    ln2_bias,
    w_fc1,
    fc1_bias,
    w_fc2,
    fc2_bias,
    memory_valid,
    cotangent,
):
    clip_count = tokens.shape[0]
    consts = {
        "fold": jnp.asarray(fold_constants(), BF16),
        "one": jnp.asarray(one_lane(), F32),
        "own": jnp.asarray(OWN_T.T, F32),
        "ownt": jnp.asarray(OWN_T, F32),
        "lanes": jnp.asarray(head_lanes(), BF16),
        "grow": jnp.asarray(FOLD, BF16),
        "ekey": jnp.asarray(EKEY, BF16),
    }
    keys_extra = key_constants(memory_valid)
    rel_all = jnp.concatenate([rel_t, rel_h, rel_w], axis=0)
    pairs = jnp.dot(jnp.asarray(PICK), rel_all, precision=HIGHEST)
    pair_table = (pairs * HEAD_DIM**0.5).T
    table_high = pair_table.astype(BF16)
    table_rest = (pair_table - table_high.astype(F32)).astype(BF16)
    tables = jnp.stack(
        [
            jnp.stack(
                [
                    jnp.pad(
                        part,
                        (
                            (head * HEAD_DIM - window_of(head), WIN - HEAD_DIM - head * HEAD_DIM + window_of(head)),
                            (0, 0),
                        ),
                    )
                    for part in (table_high, table_rest)
                ]
            )
            for head in range(LH)
        ]
    )
    rel_rows = pairs.T.astype(BF16)
    tap_q, tap_kv = taps(pool_q)[None], jnp.stack([taps(pool_k), taps(pool_v)])
    tap_s = jnp.stack([taps(squeeze_k), taps(squeeze_v)])

    width = tokens.shape[2]
    inputs_low = pad_rows(tokens)
    inputs = inputs_low.astype(F32)
    upstream = pad_rows(cotangent)
    real = (jnp.arange(inputs.shape[1]) % PADW < WID)[None, :, None]
    first_normed = layer_norm(inputs, ln1_gain, ln1_bias)
    first_rows = gather_rows(jnp.where(real, first_normed, 0.0).astype(BF16))
    w_heads = w_qkv.transpose(1, 0, 2)
    upstream_other = swap(lax.optimization_barrier((upstream, first_rows))[0])
    kv0, kv, kvf, mem = call_pool_forward(first_rows, w_heads, 1, 2, tap_kv, tap_s)
    before = from_behind(mem[-2:], "dp", 1)
    q0, q = call_pool_forward(first_rows, w_heads, 0, 1, tap_q)
    memory = jnp.concatenate([before, mem], axis=0)
    vectors = jnp.stack([proj_bias, ln2_gain, ln2_bias])
    hidden_bias = fc1_bias.reshape(1, -1)
    rows32 = jax.ShapeDtypeStruct((HALF, width), F32)
    rows16 = jax.ShapeDtypeStruct((HALF, width), BF16)
    clips = range(clip_count)
    branch, qa, at, lse, kept, recv = [], [], [], [], [], []
    for clip in clips:
        made = call_attention_forward(clip, q, kv, memory, keys_extra, tables, consts)
        for store, value in zip((branch, qa, at, lse), made):
            store.append(value)
        own, sent = simple_call(project_kernel, [rows32, rows16], 1, branch[-1][0], w_proj)
        kept.append(own)
        recv.append(swap(sent))
    middle, mine, theirs = [], [], []
    for clip in clips:
        x1, a2 = simple_call(
            middle_kernel, [rows32, rows16], 1, inputs_low[clip], kept[clip], recv[clip], vectors
        )
        middle.append(x1)
        mine.append(a2)
        theirs.append(swap(a2))
    own_parts = [call_ffn(mine[c], upstream[c], w_fc1, hidden_bias, w_fc2, F32) for c in clips]
    other_parts = [call_ffn(theirs[c], upstream_other[c], w_fc1, hidden_bias, w_fc2, BF16) for c in clips]
    second = [swap(other_parts[c][2]) for c in clips]
    dmiddle, low, sums, rows_x, dmix = [], [], [], [], []
    for clip in clips:
        dx, dx_low, total = simple_call(
            norm_back_kernel,
            [rows32, rows16, jax.ShapeDtypeStruct((HEAD_EARLY, width), F32)],
            1,
            own_parts[clip][2], second[clip], middle[clip], upstream[clip], vectors,
        )
        dmiddle.append(dx)
        sums.append(total)
        low.append((dx_low, swap(dx_low)))
    parts = own_parts + other_parts
    w_fc2_grad, w_fc1_grad = call_weights(
        [p[0] for p in parts],
        [p[1] for p in parts],
        mine + theirs,
        [upstream[c] for c in clips] + [upstream_other[c] for c in clips],
    )
    for clip in clips:
        rows, mix = simple_call(
            mix_kernel,
            [jax.ShapeDtypeStruct((ROWS, width), BF16), jax.ShapeDtypeStruct((ROWS, LW), BF16)],
            1,
            *low[clip], w_proj,
        )
        rows_x.append(rows)
        dmix.append(mix)
    last = [lax.optimization_barrier((other_parts[c][3], low[-1][1]))[0] for c in clips]
    last = [swap(x) for x in last]
    dq, dkv, dr, chunks, early = call_attention_backward(
        q, kv, memory, keys_extra, qa, dmix, at, lse, rel_rows,
        w_fc2_grad, w_fc1_grad, sums, [p[4] for p in parts], consts,
    )
    *last, dq = lax.optimization_barrier((*last, dq))
    output = drop_rows(
        jnp.stack(
            [
                (middle[c] + own_parts[c][3] + last[c].astype(F32) + fc2_bias).astype(BF16)
                for c in clips
            ]
        )
    )
    input_grad, w_fc2_grad, w_fc1_grad, w_proj_grad, tail, small, late = call_finish(
        dq, dkv, q0, kv0, kvf, jnp.concatenate([tap_q, tap_kv, tap_s]),
        first_rows.reshape(-1, width),
        rows_x,
        [b[0] for b in branch],
        w_heads,
        inputs_low,
        dmiddle,
        chunks,
        dr,
        ln1_gain.reshape(1, -1),
    )
    input_grad = drop_rows(input_grad)
    total = w_fc1_grad.shape[0]
    if total != width:
        w_fc2_grad = w_fc2_grad.reshape(2, total, width)[:, :width].reshape(2 * width, width)
        w_fc1_grad, w_proj_grad, tail = w_fc1_grad[:width], w_proj_grad[:, :width], tail[:, :width]
    w_qkv_grad = tail.astype(F32).transpose(1, 0, 2)
    fc1_bias_grad = early[HEAD_EARLY : HEAD_EARLY + fc1_bias.size // width].reshape(-1)
    small = small[:, :HEAD_DIM]
    shared = [late[0], late[1]]
    shared += [small[REL_ROWS + 32 * n : REL_ROWS + 32 * n + 27] for n in range(5)]
    shared += [
        small[: 2 * T_LEN - 1],
        small[2 * T_LEN - 1 : 2 * T_LEN + 2 * HGT - 2],
        small[2 * T_LEN + 2 * HGT - 2 : NREL],
    ]
    shared += [early[0], early[1], early[2], early[3]]
    return (
        output,
        input_grad,
        shared[0],
        shared[1],
        w_qkv_grad,
        shared[2],
        shared[3],
        shared[4],
        shared[5],
        shared[6],
        shared[7],
        shared[8],
        shared[9],
        w_proj_grad,
        shared[10],
        shared[11],
        shared[12],
        w_fc1_grad,
        fc1_bias_grad,
        w_fc2_grad,
        shared[13],
    )


def solution(mesh):
    return jax.shard_map(
        on_device,
        mesh=mesh,
        in_specs=(
            P("dp", "head", None),
            P(),
            P(),
            P(None, None, "head"),
            P(),
            P(),
            P(),
            P(),
            P(),
            P(),
            P(),
            P(),
            P("head", None),
            P(),
            P(),
            P(),
            P(None, "head"),
            P("head"),
            P("head", None),
            P(),
            P("dp", None),
            P("dp", "head", None),
        ),
        out_specs=(
            P("dp", "head", None),
            P("dp", "head", None),
            P(),
            P(),
            P(None, None, "head"),
            P(),
            P(),
            P(),
            P(),
            P(),
            P(),
            P(),
            P(),
            P("head", None),
            P(),
            P(),
            P(),
            P(None, "head"),
            P("head"),
            P("head", None),
            P(),
        ),
        check_vma=False,
    )
```

```python
from functools import partial

import jax
import jax.numpy as jnp
import numpy as np
from jax import lax
from jax.experimental import pallas as pl
from jax.experimental.pallas import tpu as pltpu
from jax.sharding import PartitionSpec as P

HEAD_DIM = 96
T_LEN = 8
HGT = 7
WID = 7
PADW = 8
L = 392
ROWS = T_LEN * HGT * PADW
TM = 4
MROWS = TM * HGT * PADW
KEYS = ROWS + 2 * MROWS
LH = 4
LW = LH * HEAD_DIM
WIN = 256
BLOCK = 128
NBLOCK = KEYS // BLOCK

EPSILON = 1e-06
HIGHEST = lax.Precision.HIGHEST
SCALE = HEAD_DIM ** (-0.5)
LOG2E = 1.4426950408889634
F32 = jnp.float32
BF16 = jnp.bfloat16
VMEM_LIMIT = 58 * 1024 * 1024

NB = T_LEN + HGT + WID
NREL = 2 * T_LEN - 1 + 2 * HGT - 1 + 2 * WID - 1
NPAIR = T_LEN * T_LEN + HGT * HGT + WID * WID


def params(**extra):
    return pltpu.CompilerParams(vmem_limit_bytes=VMEM_LIMIT, **extra)


def window_of(head):
    return 0 if head < 2 else BLOCK


def slot_of(head):
    return 192 if head < 2 else 0


def position_constants():
    t, h, w = np.meshgrid(np.arange(T_LEN), np.arange(HGT), np.arange(PADW), indexing="ij")
    t, h, w = t.ravel(), h.ravel(), w.ravel()
    valid = w < WID
    own = np.zeros((256, ROWS), np.float32)
    pick = np.zeros((256, NREL), np.float32)
    fold = np.zeros((256, 32), np.float32)
    ekey = np.zeros((32, KEYS), np.float32)
    row = 0
    base_entry = 0
    base_bias = 0
    for places, length in ((t, T_LEN), (h, HGT), (w, WID)):
        for a in range(length):
            for b in range(length):
                own[row] = (places == a) & valid
                pick[row, base_entry + a - b + length - 1] = 1
                fold[row, base_bias + b] = 1
                row += 1
        for b in range(length):
            ekey[base_bias + b, :ROWS] = (places == b) & valid
        base_entry += 2 * length - 1
        base_bias += length
    return own, pick, fold, ekey, valid


OWN_T, PICK, FOLD, EKEY, ROW_VALID = position_constants()


def fold_constants():
    out = np.zeros((2, 2, 256, WIN), np.float32)
    for variant, slot in enumerate((192, 0)):
        out[variant, 0, :, slot : slot + 32] = FOLD
        out[variant, 1, :, slot + 32 : slot + 64] = FOLD
    return out


def one_lane():
    out = np.zeros((2, 8, WIN), np.float32)
    for variant, slot in enumerate((192, 0)):
        out[variant, :, slot + NB] = 1
    return out


def head_lanes():
    out = np.zeros((LH, ROWS, WIN), np.float32)
    for head in range(LH):
        first = head * HEAD_DIM - window_of(head)
        out[head, :, first : first + HEAD_DIM] = 1
    return out


def key_constants(memory_valid):
    clip_count = memory_valid.shape[0]
    base = np.zeros((2, KEYS, WIN), np.float32)
    lane = np.zeros((2, 1, WIN), np.float32)
    for variant, slot in enumerate((192, 0)):
        base[variant, :, slot : slot + 32] = EKEY.T
        base[variant, :, slot + 32 : slot + 64] = EKEY.T
        lane[variant, :, slot + NB] = 1
    pads = np.concatenate([ROW_VALID, ROW_VALID[:MROWS], ROW_VALID[:MROWS]])
    use = jnp.concatenate(
        [jnp.ones((clip_count, ROWS), bool), jnp.repeat(memory_valid > 0, MROWS, axis=1)], axis=1
    )
    drop = jnp.where(use & jnp.asarray(pads)[None], 0.0, -1e30).astype(F32)
    return (jnp.asarray(base)[None] + drop[:, None, :, None] * jnp.asarray(lane)[None]).astype(BF16)


def nt(a, b):
    return lax.dot_general(a, b, (((1,), (1,)), ((), ())), preferred_element_type=F32)


def nn(a, b):
    return jnp.dot(a, b, preferred_element_type=F32)


def keep_rows(block):
    place = lax.broadcasted_iota(jnp.int32, block.shape, block.ndim - 2)
    return jnp.where(place < WID, block, 0.0)


def spread(dst, first, value):
    n, _, _, c = value.shape
    flat = value.reshape(n * HGT, PADW, c)
    dst[0, pl.ds(first, n), 1 : HGT + 1] = pltpu.roll(flat, 1, axis=1).reshape(n, HGT, PADW, c)
    dst[1, pl.ds(first, n), 1 : HGT + 1] = value
    dst[2, pl.ds(first, n), 1 : HGT + 1] = pltpu.roll(flat, PADW - 1, axis=1).reshape(n, HGT, PADW, c)


def pool_forward(squeeze, *refs):
    if squeeze:
        a_ref, w_ref, k_ref, s_ref, x0_ref, xp_ref, xf_ref, m_ref, xs, ys = refs
    else:
        a_ref, w_ref, k_ref, x0_ref, xp_ref, xs = refs

    @pl.when((pl.program_id(0) == 0) & (pl.program_id(1) == 0))
    def _():
        xs[...] = jnp.zeros_like(xs)
        if squeeze:
            ys[...] = jnp.zeros_like(ys)

    x = nn(a_ref[0], w_ref[0])
    x0_ref[0, 0] = x.astype(BF16)
    spread(xs, 1, x.reshape(T_LEN, HGT, PADW, LW))
    for tile in range(LW // 128):
        lanes = slice(tile * 128, tile * 128 + 128)

        def step(pair, _):
            acc = [jnp.zeros((HGT, PADW, 128), F32) for _ in range(2)]
            for a in range(3):
                for c in range(3):
                    for d in range(2):
                        block = xs[c, 2 * pair + d + a, :, :, lanes]
                        for b in range(3):
                            acc[d] = acc[d] + k_ref[0, a * 9 + b * 3 + c, :, lanes][None] * block[b : b + HGT]
            both = keep_rows(jnp.stack(acc))
            rows = pl.ds(pl.multiple_of(pair * 112, 112), 112)
            flat = both.reshape(112, 128)
            xp_ref[0, 0, rows, lanes] = flat.astype(BF16)
            if squeeze:
                xf_ref[0, 0, rows, lanes] = flat.astype(BF16)
                both = both.reshape(2 * HGT, PADW, 128)
                for c, shift in ((0, 1), (1, 0), (2, PADW - 1)):
                    moved = pltpu.roll(both, shift, axis=1) if shift else both
                    ys[c, pl.ds(2 * pair + 1, 2), 1 : HGT + 1, :, lanes] = moved.reshape(2, HGT, PADW, 128)
            return 0

        lax.fori_loop(0, T_LEN // 2, step, 0)
        if squeeze:

            def squeeze_step(pair, _):
                acc = [jnp.zeros((HGT, PADW, 128), F32) for _ in range(2)]
                for a in range(3):
                    for c in range(3):
                        for d in range(2):
                            block = ys[c, 4 * pair + 2 * d + a, :, :, lanes]
                            for b in range(3):
                                acc[d] = acc[d] + s_ref[0, a * 9 + b * 3 + c, :, lanes][None] * block[b : b + HGT]
                rows = pl.ds(pl.multiple_of(pair * 112, 112), 112)
                m_ref[0, 0, rows, lanes] = keep_rows(jnp.stack(acc)).reshape(112, 128).astype(BF16)
                return 0

            lax.fori_loop(0, TM // 2, squeeze_step, 0)


def call_pool_forward(rows, weights, first, count, kernels, squeezes=None):
    clips = rows.shape[0]
    squeeze = squeezes is not None
    tap = pl.BlockSpec((1, 27, 8, LW), lambda j, i: (j, 0, 0, 0))

    def out(n):
        return pl.BlockSpec((1, 1, n, LW), lambda j, i: (i, j, 0, 0))

    frame = pltpu.VMEM((3, T_LEN + 2, HGT + 2, PADW, LW), F32)
    shapes = [
        jax.ShapeDtypeStruct((clips, count, ROWS, LW), BF16),
        jax.ShapeDtypeStruct((clips, count, ROWS, LW), BF16),
    ]
    specs = [out(ROWS), out(ROWS)]
    if squeeze:
        shapes += [
            jax.ShapeDtypeStruct((clips, count, ROWS, LW), BF16),
            jax.ShapeDtypeStruct((clips, count, MROWS, LW), BF16),
        ]
        specs += [out(ROWS), out(MROWS)]
    return pl.pallas_call(
        partial(pool_forward, squeeze),
        grid=(count, clips),
        in_specs=[
            pl.BlockSpec((1, ROWS, rows.shape[2]), lambda j, i: (i, 0, 0)),
            pl.BlockSpec((1, weights.shape[1], LW), lambda j, i: (j + first, 0, 0)),
            tap,
        ]
        + ([tap] if squeeze else []),
        out_specs=specs,
        out_shape=shapes,
        scratch_shapes=[frame] * (2 if squeeze else 1),
        compiler_params=params(),
        cost_estimate=pl.CostEstimate(
            flops=60_000_000_000 * count // 10, bytes_accessed=4_000_000 * count, transcendentals=0
        ),
    )(rows, weights, kernels, *([squeezes] if squeeze else []))


def attention_forward(
    q_ref, kv_ref, m1_ref, m2_ref, ke_ref, tab_ref, fold_ref, one_ref, own_ref, lanes_ref,
    branch_ref, qa_ref, at_ref, lse_ref, keys, vt, scores, expo,
):
    keys[0:ROWS] = kv_ref[0, 0]
    keys[ROWS : ROWS + MROWS] = m1_ref[0, 0]
    keys[ROWS + MROWS :] = m2_ref[0, 0]
    vt[:, 0:ROWS] = kv_ref[0, 1].T
    memory = jnp.concatenate([m1_ref[0, 1], m2_ref[0, 1]], axis=0).T
    vt[:, ROWS:] = memory
    for head in range(LH):
        first = window_of(head)
        variant = head // 2
        win = slice(first, first + WIN)
        heads = lanes_ref[head]
        qm = q_ref[0, 0, :, win] * heads
        raw = nn(qm, tab_ref[head, 0]) + nn(qm, tab_ref[head, 1])
        raw = raw * own_ref[...]
        high = raw.astype(BF16)
        rest = (raw - high.astype(F32)).astype(BF16)
        placed = nn(high, fold_ref[variant, 0]) + nn(rest, fold_ref[variant, 1]) + one_ref[variant, 0:1]
        qa = qm + placed.astype(BF16)
        qa_ref[0, head] = qa

        def score(number, peak):
            rows = pl.ds(pl.multiple_of(number * BLOCK, BLOCK), BLOCK)
            ka = keys[rows, win] * heads[0:BLOCK] + ke_ref[0, variant, rows]
            s = nt(ka, qa)
            scores[rows] = s
            return jnp.maximum(peak, jnp.max(s, axis=0, keepdims=True))

        peak = lax.fori_loop(0, NBLOCK, score, jnp.full((1, ROWS), -3e38, F32))
        shift = peak * (SCALE * LOG2E)

        def soften(number, total):
            rows = pl.ds(pl.multiple_of(number * BLOCK, BLOCK), BLOCK)
            e = jnp.exp2(scores[rows] * (SCALE * LOG2E) - shift)
            expo[rows] = e.astype(BF16)
            return total + jnp.sum(e, axis=0, keepdims=True)

        total = lax.fori_loop(0, NBLOCK, soften, jnp.zeros((1, ROWS), F32))
        out = nn(vt[head * HEAD_DIM : (head + 1) * HEAD_DIM], expo[...]) * (1.0 / total)
        at_ref[0, head * HEAD_DIM : (head + 1) * HEAD_DIM] = out
        lse_ref[0, head : head + 1] = shift + jnp.log2(total)
    branch_ref[0] = (at_ref[0].T + q_ref[0, 0].astype(F32)).astype(BF16)


def whole(shape):
    return pl.BlockSpec(shape, lambda i: (0,) * len(shape))


def clip_block(*shape):
    return pl.BlockSpec((1,) + shape, lambda i: (i,) + (0,) * len(shape))


def call_attention_forward(clip, q, kv, memory, keys_extra, tables, consts):
    def block(*shape, at=clip):
        return pl.BlockSpec((1,) + shape, lambda i: (at,) + (0,) * len(shape))

    return pl.pallas_call(
        attention_forward,
        grid=(1,),
        in_specs=[
            block(1, ROWS, LW),
            block(2, ROWS, LW),
            block(2, MROWS, LW, at=clip + 1),
            block(2, MROWS, LW, at=clip),
            block(2, KEYS, WIN),
            whole((LH, 2, WIN, 256)),
            whole((2, 2, 256, WIN)),
            whole((2, 8, WIN)),
            whole((ROWS, 256)),
            whole((LH, ROWS, WIN)),
        ],
        out_specs=[
            clip_block(ROWS, LW),
            clip_block(LH, ROWS, WIN),
            clip_block(LW, ROWS),
            clip_block(8, ROWS),
        ],
        out_shape=[
            jax.ShapeDtypeStruct((1, ROWS, LW), BF16),
            jax.ShapeDtypeStruct((1, LH, ROWS, WIN), BF16),
            jax.ShapeDtypeStruct((1, LW, ROWS), F32),
            jax.ShapeDtypeStruct((1, 8, ROWS), F32),
        ],
        scratch_shapes=[
            pltpu.VMEM((KEYS, LW), BF16),
            pltpu.VMEM((LW, KEYS), BF16),
            pltpu.VMEM((KEYS, ROWS), F32),
            pltpu.VMEM((KEYS, ROWS), BF16),
        ],
        compiler_params=params(),
        cost_estimate=pl.CostEstimate(
            flops=13_000_000_000, bytes_accessed=5_000_000, transcendentals=1_500_000
        ),
    )(q, kv, memory, memory, keys_extra, tables, consts["fold"], consts["one"], consts["own"], consts["lanes"])


HALF = ROWS // 2


def simple_call(kernel, out_shape, gflops, *args):
    vmem = pl.BlockSpec(memory_space=pltpu.VMEM)
    many = isinstance(out_shape, list)
    return pl.pallas_call(
        kernel,
        in_specs=[vmem] * len(args),
        out_specs=[vmem] * len(out_shape) if many else vmem,
        out_shape=out_shape,
        compiler_params=params(),
        cost_estimate=pl.CostEstimate(
            flops=int(gflops * 1e9), bytes_accessed=2_000_000, transcendentals=0
        ),
    )(*args)


def half_rows(side):
    return pl.ds(pl.multiple_of(side * HALF, 16), HALF)


def project_kernel(branch, w, kept, sent):
    head = lax.axis_index("head")
    sent[...] = nn(branch[half_rows(1 - head)], w[...]).astype(BF16)
    kept[...] = nn(branch[half_rows(head)], w[...])


def middle_kernel(tokens, kept, recv, vectors, x1_ref, a2_ref):
    x1 = tokens[...].astype(F32) + kept[...] + recv[...].astype(F32) + vectors[0:1]
    x1_ref[...] = x1
    centred = x1 - jnp.mean(x1, axis=-1, keepdims=True)
    scale = lax.rsqrt(jnp.mean(centred * centred, axis=-1, keepdims=True) + EPSILON)
    a2_ref[...] = (centred * scale * vectors[1:2] + vectors[2:3]).astype(BF16)


FFN_BLOCK = 512
GELU_A = 0.7978845608028654
GELU_B = 0.044715


def ffn_kernel(a2, g, w1, b1, w2, act_ref, dpre_ref, da2_ref, out_ref, sums_ref):
    da2 = jnp.zeros(da2_ref.shape, F32)
    out = jnp.zeros(out_ref.shape, F32)
    for first in range(0, w1.shape[1], FFN_BLOCK):
        cols = slice(first, first + FFN_BLOCK)
        pre = nn(a2[...], w1[:, cols]) + b1[0:1, cols]
        square = pre * pre
        bent = jnp.tanh(GELU_A * (pre + GELU_B * (pre * square)))
        gate = 0.5 + 0.5 * bent
        act = (pre * gate).astype(BF16)
        slope = gate + 0.5 * pre * (1.0 - bent * bent) * (GELU_A * (1.0 + 3.0 * GELU_B * square))
        dpre = nt(g[...], w2[cols]) * slope
        low = dpre.astype(BF16)
        sums_ref[0:1, cols] = jnp.sum(dpre, axis=0, keepdims=True)
        act_ref[:, cols] = act
        dpre_ref[:, cols] = low
        da2 = da2 + nt(low, w1[:, cols])
        out = out + nn(act, w2[cols])
    da2_ref[...] = da2.astype(da2_ref.dtype)
    out_ref[...] = out.astype(out_ref.dtype)


def call_ffn(a2, g, w1, b1, w2, dtype):
    hidden = w1.shape[1]
    return simple_call(
        ffn_kernel,
        [
            jax.ShapeDtypeStruct((HALF, hidden), BF16),
            jax.ShapeDtypeStruct((HALF, hidden), BF16),
            jax.ShapeDtypeStruct(a2.shape, dtype),
            jax.ShapeDtypeStruct(a2.shape, dtype),
            jax.ShapeDtypeStruct((1, hidden), F32),
        ],
        5, a2, g, w1, b1, w2,
    )


def tn(a, b):
    return lax.dot_general(a, b, (((0,), (0,)), ((), ())), preferred_element_type=F32)


def weight_kernel(count, *refs):
    acts, dpres, a2s, gs = (refs[n * count : (n + 1) * count] for n in range(4))
    g2, g1 = refs[4 * count :]
    g2[...] = sum(tn(a[...], b[...]) for a, b in zip(acts, gs)).astype(BF16)
    g1[...] = sum(tn(a[...], b[...]) for a, b in zip(a2s, dpres)).astype(BF16)


def call_weights(acts, dpres, a2s, gs):
    hidden, width = acts[0].shape[1], gs[0].shape[1]
    count = len(acts)
    piece = pl.BlockSpec((HALF, LW), lambda i: (0, i))
    full = pl.BlockSpec((HALF, width), lambda i: (0, 0))
    return pl.pallas_call(
        partial(weight_kernel, count),
        grid=(hidden // LW,),
        in_specs=[piece] * (2 * count) + [full] * (2 * count),
        out_specs=[
            pl.BlockSpec((LW, width), lambda i: (i, 0)),
            pl.BlockSpec((width, LW), lambda i: (0, i)),
        ],
        out_shape=[
            jax.ShapeDtypeStruct((hidden, width), BF16),
            jax.ShapeDtypeStruct((width, hidden), BF16),
        ],
        compiler_params=params(),
        cost_estimate=pl.CostEstimate(flops=8_000_000_000, bytes_accessed=15_000_000, transcendentals=0),
    )(*acts, *dpres, *a2s, *gs)


def norm_back_kernel(kept, recv, x1_ref, g, vectors, dx_ref, low_ref, sums):
    u = kept[...] + recv[...].astype(F32)
    x1 = x1_ref[...]
    centred = x1 - jnp.mean(x1, axis=-1, keepdims=True)
    scale = lax.rsqrt(jnp.mean(centred * centred, axis=-1, keepdims=True) + EPSILON)
    xhat = centred * scale
    w = u * vectors[1:2]
    up = g[...].astype(F32)
    dx = up + scale * (
        w - jnp.mean(w, axis=-1, keepdims=True) - xhat * jnp.mean(w * xhat, axis=-1, keepdims=True)
    )
    dx_ref[...] = dx
    low_ref[...] = dx.astype(BF16)
    sums[0:1] = jnp.sum(dx, axis=0, keepdims=True)
    sums[1:2] = jnp.sum(u * xhat, axis=0, keepdims=True)
    sums[2:3] = jnp.sum(u, axis=0, keepdims=True)
    sums[3:4] = jnp.sum(up, axis=0, keepdims=True)
    sums[4:8] = jnp.zeros((4, u.shape[1]), F32)


def mix_kernel(mine, theirs, w, rows_ref, dmix_ref):
    head = lax.axis_index("head")
    for side, part in ((head, mine), (1 - head, theirs)):
        rows_ref[half_rows(side)] = part[...]
        dmix_ref[half_rows(side)] = nt(part[...], w[...]).astype(BF16)


HEAD_EARLY = 8
MESH = pl.DeviceIdType.MESH


def remote(src, dst, send, recv, peer):
    made = pltpu.make_async_remote_copy(
        src_ref=src, dst_ref=dst, send_sem=send, recv_sem=recv, device_id=peer, device_id_type=MESH
    )
    made.start()
    return made


def local(src, dst, sem):
    made = pltpu.make_async_copy(src, dst, sem)
    made.start()
    return made


class Place:
    def __init__(self, groups):
        dp = lax.axis_index("dp")
        head = lax.axis_index("head")
        self.groups = groups
        self.dp, self.head = dp, head
        self.core = lax.rem(dp, 2)
        self.xbit = lax.rem(lax.div(dp, 2), 2)
        self.group = lax.div(dp, 4)
        self.to_core = (dp + 1 - 2 * self.core, head)
        self.to_x = (dp + 2 - 4 * self.xbit, head)
        self.to_y = (dp, 1 - head)
        self.peers = [
            (lax.rem(self.group + o, groups) * 4 + lax.rem(dp, 4), head) for o in range(1, groups)
        ]
        self.number = (head * groups + self.group) * 2 + self.xbit

    def device(self, number):
        side = lax.div(number, 2 * self.groups)
        group = lax.rem(lax.div(number, 2), self.groups)
        return (group * 4 + lax.rem(number, 2) * 2 + self.core, side)

    def greet(self, more=()):
        barrier = pltpu.get_barrier_semaphore()
        signalled = [self.to_core, self.to_x] + self.peers + list(more)
        for peer in signalled:
            pl.semaphore_signal(barrier, inc=1, device_id=peer, device_id_type=MESH)
        pl.semaphore_wait(barrier, len(signalled))


class Piece:
    def __init__(self, place, rows, source, result, reduce_refs, send, recv):
        self.at = place
        self.half, self.quarter = rows // 2, rows // 4
        self.chunk = rows // 4 // place.groups
        self.source, self.result = source, result
        self.refs = reduce_refs
        self.send, self.recv = send, recv
        self.tile = 16 if reduce_refs is None or reduce_refs[0].dtype == BF16 else 8
        self.flights = {}

    def start(self, key, number, src, dst, peer):
        self.flights[key] = remote(src, dst, self.send.at[number], self.recv.at[number], peer)

    def base(self, g):
        at = self.at
        return pl.multiple_of(at.core * self.half + at.xbit * self.quarter + g * self.chunk, self.tile)

    def a(self):
        theirs = pl.multiple_of((1 - self.at.core) * self.half, self.tile)
        self.start("a", 0, self.source(theirs, self.half), self.refs[0], self.at.to_core)

    def sum_rows(self, which):
        recv_a = self.refs[0]
        first = pl.multiple_of(which * self.quarter, self.tile)
        own = self.source(pl.multiple_of(self.at.core * self.half + which * self.quarter, self.tile), self.quarter)
        return own[...].astype(F32) + recv_a[pl.ds(first, self.quarter)].astype(F32)

    def b(self):
        _, send_b, recv_b, _, _ = self.refs
        self.flights["a"].wait()
        send_b[...] = self.sum_rows(1 - self.at.xbit).astype(send_b.dtype)
        self.start("b", 1, send_b, recv_b, self.at.to_x)

    def c(self):
        _, _, recv_b, send_c, recv_c = self.refs
        self.flights["b"].wait()
        send_c[...] = (self.sum_rows(self.at.xbit) + recv_b[...].astype(F32)).astype(send_c.dtype)
        for o in range(1, self.at.groups):
            first = pl.multiple_of(lax.rem(self.at.group + o, self.at.groups) * self.chunk, self.tile)
            self.start(
                ("c", o), 1 + o, send_c.at[pl.ds(first, self.chunk)], recv_c.at[o - 1], self.at.peers[o - 1]
            )

    def total(self):
        _, _, _, send_c, recv_c = self.refs
        own = send_c[pl.ds(pl.multiple_of(self.at.group * self.chunk, self.tile), self.chunk)].astype(F32)
        for o in range(1, self.at.groups):
            self.flights["c", o].wait()
            own = own + recv_c[o - 1].astype(F32)
        return own

    def d(self, own=None):
        own = self.total() if own is None else own
        mine = self.result(self.base(self.at.group), self.chunk)
        mine[...] = own.astype(mine.dtype)
        for o in range(1, self.at.groups):
            number = self.at.groups + o
            self.start(("d", o), number, mine, mine, self.at.peers[o - 1])

    def e(self):
        for o in range(1, self.at.groups):
            self.flights["d", o].wait()
        mine = self.result(self.base(0), self.quarter)
        self.start("e", 2 * self.at.groups, mine, mine, self.at.to_x)

    def f(self):
        self.flights["e"].wait()
        mine = self.result(pl.multiple_of(self.at.core * self.half, self.tile), self.half)
        self.start("f", 2 * self.at.groups + 1, mine, mine, self.at.to_core)

    def g(self):
        self.flights["f"].wait()


def piece_scratch(rows, groups, width, dtype, count):
    half, quarter = rows // 2, rows // 4
    return [
        pltpu.VMEM((count, half, width), dtype),
        pltpu.VMEM((count, quarter, width), dtype),
        pltpu.VMEM((count, quarter, width), dtype),
        pltpu.VMEM((count, quarter, width), dtype),
        pltpu.VMEM((count, groups - 1, quarter // groups, width), dtype),
    ]


class Tiny:
    def __init__(self, place, source, result, refs, send, recv):
        self.at, self.source, self.result = place, source, result
        self.recv_core, self.summed, self.slots = refs
        self.send, self.recv = send, recv
        count = 4 * place.groups
        self.half, self.chunk = source.shape[0] // 2, source.shape[0] // 2 // count
        self.mine = place.number
        self.others = [lax.rem(place.number + o, count) for o in range(1, count)]
        self.flights = {}

    def rows(self, number):
        return pl.ds(pl.multiple_of(number * self.chunk, 8), self.chunk)

    def halves(self, core):
        return pl.ds(pl.multiple_of(core * self.half, 8), self.half)

    def start(self, key, src, dst, peer):
        number = len(self.flights)
        self.flights[key] = remote(src, dst, self.send.at[number], self.recv.at[number], peer)

    def a(self):
        self.start("a", self.source.at[self.halves(1 - self.at.core)], self.recv_core, self.at.to_core)

    def b(self):
        self.flights["a"].wait()
        self.summed[...] = self.source[self.halves(self.at.core)] + self.recv_core[...]
        for o, number in enumerate(self.others):
            self.start(("b", o), self.summed.at[self.rows(number)], self.slots.at[o], self.at.device(number))

    def c(self):
        total = self.summed[self.rows(self.mine)]
        for o, number in enumerate(self.others):
            self.flights["b", o].wait()
            total = total + self.slots[o]
        rows = pl.ds(pl.multiple_of(self.at.core * self.half + self.mine * self.chunk, 8), self.chunk)
        self.result[rows] = total
        for o, number in enumerate(self.others):
            self.start(("c", o), self.result.at[rows], self.result.at[rows], self.at.device(number))

    def d(self):
        for o in range(len(self.others)):
            self.flights["c", o].wait()
        rows = self.halves(self.at.core)
        self.start("d", self.result.at[rows], self.result.at[rows], self.at.to_core)

    def e(self):
        self.flights["d"].wait()


def attention_backward(
    groups,
    q_ref, kv_ref, mem_ref, ke_hbm, qa_hbm0, qa_hbm1, dm_ref0, dm_ref1, at_hbm0, at_hbm1, lse_ref0, lse_ref1,
    rt_ref, grow_ref, ownt_ref, ekey_ref,
    lanes_ref, g2_ref, g1_ref,
    dq_ref, dkv_ref, dr_ref, chunks_ref, out2,
    ke_ref, qa_ref, at_ref, keys, values, kt, dmt, qms, dms, dqt,
    recv_a, send_b, recv_b, send_c, recv_c,
    loads, sems_send, sems_recv,
):
    place = Place(groups)
    clips = q_ref.shape[0]
    dm_refs, lse_refs = (dm_ref0, dm_ref1), (lse_ref0, lse_ref1)
    lead = [
        [
            local(ke_hbm.at[clip], ke_ref.at[clip], loads.at[3 * clip]),
            local((qa_hbm0, qa_hbm1)[clip].at[0], qa_ref.at[clip], loads.at[3 * clip + 1]),
            local((at_hbm0, at_hbm1)[clip].at[0], at_ref.at[clip], loads.at[3 * clip + 2]),
        ]
        for clip in range(clips)
    ]
    place.greet()
    total = g1_ref.shape[0]

    def view(number, ref):
        if number < 4:
            base, col = (number // 2) * total, (number % 2) * LW
            return lambda first, n: ref.at[pl.ds(base + first, n), col : col + LW]
        col = (number - 4) * LW
        return lambda first, n: g1_ref.at[pl.ds(first, n), col : col + LW]

    pieces = [
        Piece(
            place, total, view(number, g2_ref), view(number, out2) if number < 4 else None,
            [ref.at[number] for ref in (recv_a, send_b, recv_b, send_c, recv_c)],
            sems_send.at[number], sems_recv.at[number],
        )
        for number in range(8)
    ]
    moves = [
        [pieces[0].a],
        [pieces[0].b, pieces[1].a],
        [pieces[2].a],
        [pieces[1].b, pieces[3].a],
        [pieces[4].a],
        [pieces[0].c, pieces[2].b, pieces[5].a],
        [pieces[6].a],
        [pieces[1].c, pieces[3].b, pieces[7].a],
        [],
        [pieces[0].d, pieces[4].b],
        [],
        [pieces[1].d, pieces[5].b],
        [],
        [pieces[0].e, pieces[2].c],
        [],
        [pieces[1].e, pieces[3].c],
        [],
        [pieces[0].f, pieces[2].d, pieces[6].b],
        [pieces[1].f, pieces[3].d, pieces[7].b, pieces[2].e, pieces[4].c, pieces[5].c, pieces[3].e, pieces[2].f, pieces[6].c, pieces[3].f, pieces[7].c],
    ]

    def pump():
        if moves:
            for move in moves.pop(0):
                move()

    dr_ref[...] = jnp.zeros_like(dr_ref)
    for clip in range(clips):
        pump()
        near, far = mem_ref.at[clip + 1], mem_ref.at[clip]
        keys[0:ROWS] = kv_ref[clip, 0]
        keys[ROWS : ROWS + MROWS] = near[0]
        keys[ROWS + MROWS :] = far[0]
        values[0:ROWS] = kv_ref[clip, 1]
        values[ROWS : ROWS + MROWS] = near[1]
        values[ROWS + MROWS :] = far[1]
        kt[0:LW] = keys[...].T
        kt[LW:] = ekey_ref[...]
        dmt[...] = dm_refs[clip][...].astype(F32).T
        dqt[...] = jnp.zeros_like(dqt)
        for made in lead[clip]:
            made.wait()
        deltas = []
        for head in range(LH):
            first = window_of(head)
            win = slice(first, first + WIN)
            span = slice(head * HEAD_DIM, (head + 1) * HEAD_DIM)
            qms[head] = q_ref[clip, 0, :, win] * lanes_ref[head]
            dms[head] = dm_refs[clip][:, win] * lanes_ref[head]
            deltas.append(jnp.sum(dmt[span] * at_ref[clip, span], axis=0, keepdims=True))

        def step(number, _):
            rows = slice(number * BLOCK, number * BLOCK + BLOCK)
            dk_parts, dv_parts = [], []
            for head in range(LH):
                first = window_of(head)
                variant = head // 2
                win = slice(first, first + WIN)
                ka = keys[rows, win] * lanes_ref[head, 0:BLOCK] + ke_ref[clip, variant, rows]
                s = nt(ka, qa_ref[clip, head])
                p = jnp.exp2(s * (SCALE * LOG2E) - lse_refs[clip][0, head : head + 1])
                dp = nt(values[rows, win], dms[head])
                ds = (p * (dp - deltas[head])).astype(BF16)
                dv_parts.append(nn(p.astype(BF16), dms[head]))
                dk_parts.append(nn(ds, qms[head]) * SCALE)
                kts = jnp.concatenate(
                    [kt[head * HEAD_DIM : (head + 1) * HEAD_DIM, rows], kt[LW:, rows]], axis=0
                )
                dqt[head] += nn(kts, ds)
            for which, parts in ((0, dk_parts), (1, dv_parts)):
                dkv_ref[clip, which, rows] = jnp.concatenate(
                    [
                        parts[0][:, 0:128] + parts[1][:, 0:128],
                        parts[1][:, 128:256] + parts[2][:, 0:128],
                        parts[2][:, 128:256] + parts[3][:, 128:256],
                    ],
                    axis=1,
                )
            return 0

        for number in range(NBLOCK):
            pump()
            step(number, 0)
        pump()
        for head in range(LH):
            first = window_of(head)
            span = slice(head * HEAD_DIM, (head + 1) * HEAD_DIM)
            total_t = dqt[head]
            grown = nn(grow_ref[...], total_t[HEAD_DIM:].astype(BF16)) * ownt_ref[...]
            grown = grown.astype(BF16)
            dmt[span] = dmt[span] + total_t[0:HEAD_DIM] * SCALE + nn(rt_ref[...], grown)
            dr_ref[:, first : first + WIN] += nn(grown, qms[head])
        dq_ref[clip] = dmt[...].T
    while moves:
        pump()
    for number in range(4):
        pieces[number].g()
        chunks_ref[number] = pieces[4 + number].total().astype(BF16)


def padded_rows(width, groups):
    return -(-width // (4 * groups) // 16) * 16 * 4 * groups


def call_attention_backward(q, kv, memory, keys_extra, qa, dmix, at, lse, rt, g2, g1, consts):
    clips, width = q.shape[0], g2.shape[1]
    groups = lax.axis_size("dp") // 4
    total = padded_rows(width, groups)
    if total != width:
        g1 = jnp.pad(g1, ((0, total - width), (0, 0)))
        g2 = jnp.pad(g2.reshape(2, width, width), ((0, 0), (0, total - width), (0, 0))).reshape(-1, width)
    vmem = pl.BlockSpec(memory_space=pltpu.VMEM)
    hbm = pl.BlockSpec(memory_space=pl.ANY)
    return pl.pallas_call(
        partial(attention_backward, groups),
        in_specs=[vmem] * 3 + [hbm] * 3 + [vmem] * 2 + [hbm] * 2 + [vmem] * 9,
        out_specs=[vmem] * 5,
        out_shape=[
            jax.ShapeDtypeStruct((clips, ROWS, LW), F32),
            jax.ShapeDtypeStruct((clips, 2, KEYS, LW), F32),
            jax.ShapeDtypeStruct((256, LW), F32),
            jax.ShapeDtypeStruct((4, total // 4 // groups, LW), BF16),
            jax.ShapeDtypeStruct(g2.shape, BF16),
        ],
        scratch_shapes=[
            pltpu.VMEM(keys_extra.shape, BF16),
            pltpu.VMEM((clips, LH, ROWS, WIN), BF16),
            pltpu.VMEM((clips, LW, ROWS), F32),
            pltpu.VMEM((KEYS, LW), BF16),
            pltpu.VMEM((KEYS, LW), BF16),
            pltpu.VMEM((LW + 32, KEYS), BF16),
            pltpu.VMEM((LW, ROWS), F32),
            pltpu.VMEM((LH, ROWS, WIN), BF16),
            pltpu.VMEM((LH, ROWS, WIN), BF16),
            pltpu.VMEM((LH, HEAD_DIM + 32, ROWS), F32),
            *piece_scratch(total, groups, LW, BF16, 8),
            pltpu.SemaphoreType.DMA((3 * clips,)),
            pltpu.SemaphoreType.DMA((8, 2 * groups + 2)),
            pltpu.SemaphoreType.DMA((8, 2 * groups + 2)),
        ],
        compiler_params=params(collective_id=0, has_side_effects=True),
        cost_estimate=pl.CostEstimate(
            flops=40_000_000_000, bytes_accessed=20_000_000, transcendentals=3_000_000
        ),
    )(
        q, kv, memory, keys_extra, *qa, *dmix, *at, *lse, rt,
        consts["grow"], consts["ownt"], consts["ekey"], consts["lanes"], g2, g1,
    )


REL_ROWS = 48
TAP_ROW = NREL
NORM_ROW = TAP_ROW + 5 * 27
EARLY_ROW = NORM_ROW + 12
HIDDEN_ROW = EARLY_ROW + 24
SMALL_ROWS = HIDDEN_ROW + 24


def finish_kernel(
    groups, width,
    dq_hbm, dkv_hbm, x0q_hbm, x0kv_hbm, kvf_hbm, taps_hbm, rows_a_hbm, rows_x0, rows_x1, branch0, branch1,
    w_hbm, tokens_hbm, middle0, middle1, chunks_ref, dr_ref, gain, foldl_ref, pick_ref,
    sums0, sums1, hidden0, hidden1, hidden2, hidden3,
    grad, out1, outp, outq, small_out,
    dq, dkv, x0q, x0kv, kvf, taps_ref, rows_a, rows_x, branch, w_ref, tokens, middle,
    us, ms, kacc, dx, dmem_send, dmem_recv, res1, resp, grads, stage, stage_t,
    recv_a, send_b, recv_b, send_c, recv_c,
    strips, strip_res, strip_a, strip_b, strip_bb, strip_c, strip_cc,
    sm, sm_res, sm_core, sm_sum, sm_slots, send_y, recv_y,
    loads, stores, sems_send, sems_recv, tiny_send, tiny_recv, cross_send, cross_recv, mem_sems,
):
    place = Place(groups)
    clips = dq.shape[0]
    total = rows_a.shape[1]
    names = (
        "dkv", "dq", "x0q", "taps", "rows_x0", "rows_x1", "branch0", "branch1", "x0kv", "kvf", "rows_a", "w",
        "tokens", "middle0", "middle1",
    )
    pairs = (
        (dkv_hbm, dkv), (dq_hbm, dq), (x0q_hbm, x0q), (taps_hbm, taps_ref),
        (rows_x0, rows_x.at[0:ROWS]), (rows_x1, rows_x.at[ROWS:]), (branch0, branch.at[0:ROWS]),
        (branch1, branch.at[ROWS:]), (x0kv_hbm, x0kv), (kvf_hbm, kvf), (rows_a_hbm, rows_a), (w_hbm, w_ref),
        (tokens_hbm, tokens), (middle0, middle.at[0]), (middle1, middle.at[1]),
    )
    lead = {
        name: local(src, dst, loads.at[n]) for n, (name, (src, dst)) in enumerate(zip(names, pairs))
    }
    count = groups * 4
    behind = (lax.rem(place.dp + count - 1, count), place.head)
    ahead = (lax.rem(place.dp + 1, count), place.head)
    others = [place.device(lax.rem(place.number + o, count)) for o in range(1, count)]
    barrier = pltpu.get_barrier_semaphore()
    for peer in [place.to_core, behind, ahead] + others:
        pl.semaphore_signal(barrier, inc=1, device_id=peer, device_id_type=MESH)
    pl.semaphore_wait(barrier, 3 + len(others))

    def strip_of(number):
        return lambda first, n: res1.at[pl.ds(first, n), number * LW : number * LW + LW]

    ffn = [
        Piece(place, total, None, strip_of(number), None, sems_send.at[number], sems_recv.at[number])
        for number in range(4)
    ]

    def rows_of(ref):
        return lambda first, n: ref.at[pl.ds(first, n)]

    late = [
        Piece(
            place, total, rows_of(grads.at[number]), rows_of(resp.at[number]),
            [ref.at[number] for ref in (recv_a, send_b, recv_b, send_c, recv_c)],
            sems_send.at[4 + number], sems_recv.at[4 + number],
        )
        for number in range(2)
    ] + [
        Piece(
            place, total, rows_of(strips.at[number]), rows_of(strip_res.at[number]),
            [ref.at[number] for ref in (strip_a, strip_b, strip_bb, strip_c, strip_cc)],
            sems_send.at[6 + number], sems_recv.at[6 + number],
        )
        for number in range(6)
    ]
    tiny = Tiny(place, sm, sm_res, (sm_core, sm_sum, sm_slots), tiny_send, tiny_recv)

    stored = []

    def flush(source, target):
        slot = len(stored) % 2
        if len(stored) > 1:
            stored[-2].wait()
        stage[slot] = source[...].astype(F32)
        stored.append(local(stage.at[slot], target, stores.at[slot]))

    def store1(number):
        ffn[number].g()
        flush(strip_of(number)(0, total), out1.at[:, number * LW : number * LW + LW])

    def product(number):
        if number < 2:
            left, right, target = (rows_x, branch, grads.at[0]) if number == 0 else (rows_a, dx.at[0], grads.at[1])
            lanes = slice(0, LW)
        else:
            left, right, target = rows_a, dx.at[1 + (number - 2) // 3], strips.at[number - 2]
            lanes = slice((number - 2) % 3 * 128, (number - 2) % 3 * 128 + 128)
        for first in range(0, total, total // 2):
            target[first : first + total // 2] = tn(
                left[:, first : first + total // 2], right[:, lanes]
            ).astype(BF16)
        late[number].a()

    def shifted_store(dst, first, both, lanes):
        both = both.reshape(2 * HGT, PADW, 128)
        for c, shift in ((0, 1), (1, 0), (2, PADW - 1)):
            moved = pltpu.roll(both, shift, axis=1) if shift else both
            dst[c, pl.ds(first, 2), 1 : HGT + 1, :, lanes] = moved.reshape(2, HGT, PADW, 128)

    def prepare(which, clip):
        if which:
            memory = dmem_recv[clip, which - 1].astype(F32)
            memory = jnp.where(place.dp == count - 1, 0.0, memory)
            for later in range(clip + 1, clips):
                if later == clip + 1:
                    memory = memory + dkv[later, which - 1, ROWS : ROWS + MROWS]
                if later == clip + 2:
                    memory = memory + dkv[later, which - 1, ROWS + MROWS :]
            spread(ms, 0, memory.reshape(TM, HGT, PADW, LW))
        else:
            spread(us, 1, dq[clip].reshape(T_LEN, HGT, PADW, LW))

    def pooled(which, clip, tile):
        field = x0q.at[clip, 0] if which == 0 else x0kv.at[clip, which - 1]
        upstream = dq.at[clip] if which == 0 else dkv.at[clip, which - 1]
        if tile == 0:
            prepare(which, clip)
        lanes = slice(tile * 128, tile * 128 + 128)
        if which:

            def squeeze_step(pair, _):
                rows = pl.ds(pl.multiple_of(pair * 112, 112), 112)
                own = upstream[rows, lanes].reshape(2, HGT, PADW, 128)
                fields = kvf[clip, which - 1, rows, lanes].astype(F32).reshape(2, HGT, PADW, 128)
                acc = [own[0], own[1]]
                for a, d, frame in ((1, 0, 0), (0, 1, 1), (2, 1, 0)):
                    for c in range(3):
                        block = ms[2 - c, pair + frame, :, :, lanes]
                        for b in range(3):
                            at = block[2 - b : 2 - b + HGT]
                            number = a * 9 + b * 3 + c
                            acc[d] = acc[d] + taps_ref[2 + which, number, :, lanes][None] * at
                            kacc[2 + which, number, :, lanes] += jnp.sum(fields[d] * at, axis=0)
                shifted_store(us, 2 * pair + 1, keep_rows(jnp.stack(acc)), lanes)
                return 0

            lax.fori_loop(0, TM, squeeze_step, 0)

        def pair_step(pair, _):
            rows = pl.ds(pl.multiple_of(pair * 112, 112), 112)
            fields = field[rows, lanes].astype(F32).reshape(2, HGT, PADW, 128)
            acc = [jnp.zeros((HGT, PADW, 128), F32) for _ in range(2)]
            for a in range(3):
                for c in range(3):
                    sums = [jnp.zeros((PADW, 128), F32) for _ in range(3)]
                    for d in range(2):
                        block = us[2 - c, 2 * pair + d + 2 - a, :, :, lanes]
                        for b in range(3):
                            at = block[2 - b : 2 - b + HGT]
                            acc[d] = acc[d] + taps_ref[which, a * 9 + b * 3 + c, :, lanes][None] * at
                            sums[b] = sums[b] + jnp.sum(fields[d] * at, axis=0)
                    for b in range(3):
                        kacc[which, a * 9 + b * 3 + c, :, lanes] += sums[b]
            both = keep_rows(jnp.stack(acc))
            out_rows = pl.ds(pl.multiple_of(clip * ROWS + pair * 112, 16), 112)
            dx[which, out_rows, lanes] = both.reshape(112, 128).astype(BF16)
            return 0

        lax.fori_loop(0, T_LEN // 2, pair_step, 0)

    side_rows = ROWS // 2

    def input_gradient(clip, side):
        rows = pl.ds(pl.multiple_of(clip * ROWS + side * side_rows, 16), side_rows)
        return nt(dx[0, rows], w_ref[0]) + nt(dx[1, rows], w_ref[1]) + nt(dx[2, rows], w_ref[2])

    crossing = {}

    def cross(clip):
        send_y[clip] = input_gradient(clip, 1 - place.head).astype(BF16)
        crossing[clip] = remote(
            send_y.at[clip], recv_y.at[clip], cross_send.at[clip], cross_recv.at[clip], place.to_y
        )

    def normed_gradient(clip):
        mine = input_gradient(clip, place.head)
        crossing[clip].wait()
        u = mine + recv_y[clip].astype(F32)
        v = tokens[clip].astype(F32)
        centred = v - jnp.mean(v, axis=-1, keepdims=True)
        scale = lax.rsqrt(jnp.mean(centred * centred, axis=-1, keepdims=True) + EPSILON)
        xhat = centred * scale
        w = u * gain[0:1]
        dv = scale * (
            w - jnp.mean(w, axis=-1, keepdims=True) - xhat * jnp.mean(w * xhat, axis=-1, keepdims=True)
        )
        grad[clip] = middle[clip] + dv
        for which, value in enumerate((u * xhat, u)):
            value = jnp.sum(value, axis=0, keepdims=True)
            for n in range(width // 128):
                row = NORM_ROW + which * (width // 128) + n
                sm[row : row + 1] += value[:, n * 128 : n * 128 + 128]

    def exact(a, b):
        return jnp.dot(a, b, precision=HIGHEST, preferred_element_type=F32)

    def small_first():
        sm[...] = jnp.zeros_like(sm)
        folded = exact(dr_ref[...], foldl_ref[...])
        sm[0:NREL] = exact(pick_ref[...], folded)[0:NREL]
        early = sums0[...] + sums1[...]
        hidden = hidden0[...] + hidden1[...] + hidden2[...] + hidden3[...]
        strip = width // 128
        for which in range(4):
            for n in range(strip):
                row = EARLY_ROW + which * strip + n
                sm[row : row + 1] = early[which : which + 1, n * 128 : n * 128 + 128]
        count_h = hidden.shape[1] // 128
        for side in range(2):
            for n in range(count_h):
                row = HIDDEN_ROW + side * count_h + n
                part = hidden[:, n * 128 : n * 128 + 128]
                sm[row : row + 1] = jnp.where(place.head == side, part, 0.0)

    def small_taps(which):
        first = TAP_ROW + 27 * which
        sums = jnp.sum(kacc[which], axis=1)
        sums = jnp.concatenate([sums, jnp.zeros((5, LW), F32)], axis=0)
        sm[first : first + 27] = exact(sums, foldl_ref[...])[0:27]

    ffn[0].d(chunks_ref[0])
    us[...] = jnp.zeros_like(us)
    ms[...] = jnp.zeros_like(ms)
    kacc[...] = jnp.zeros_like(kacc)
    small_first()
    lead["dkv"].wait()
    for which in range(2):
        dmem_send[0, which] = dkv[0, which, ROWS + MROWS :].astype(BF16)
        dmem_send[1, which] = (
            dkv[0, which, ROWS : ROWS + MROWS] + dkv[1, which, ROWS + MROWS :]
        ).astype(BF16)
    memory_flight = remote(dmem_send, dmem_recv, mem_sems.at[0], mem_sems.at[1], behind)
    for name in ("rows_x0", "rows_x1", "branch0", "branch1"):
        lead[name].wait()
    product(0)
    for name in ("dq", "x0q", "taps"):
        lead[name].wait()
    pooled(0, 0, 0)
    pooled(0, 0, 1)
    late[0].b()
    pooled(0, 0, 2)
    ffn[1].d(chunks_ref[1])
    pooled(0, 1, 0)
    pooled(0, 1, 1)
    ffn[0].e()
    pooled(0, 1, 2)
    ffn[2].d(chunks_ref[2])
    lead["rows_a"].wait()
    product(1)
    small_taps(0)
    memory_flight.wait()
    lead["x0kv"].wait()
    lead["kvf"].wait()
    pooled(1, 0, 0)
    late[1].b()
    late[0].c()
    pooled(1, 0, 1)
    ffn[0].f()
    pooled(1, 0, 2)
    ffn[1].e()
    ffn[3].d(chunks_ref[3])
    pooled(2, 0, 0)
    store1(0)
    pooled(2, 0, 1)
    late[0].d()
    ffn[2].e()
    pooled(2, 0, 2)
    lead["w"].wait()
    cross(0)
    ffn[1].f()
    pooled(1, 1, 0)
    late[1].c()
    store1(1)
    ffn[3].e()
    product(2)
    pooled(1, 1, 1)
    ffn[2].f()
    product(3)
    pooled(1, 1, 2)
    late[2].b()
    store1(2)
    product(4)
    late[3].b()
    late[1].d()
    small_taps(1)
    small_taps(3)
    late[0].e()
    ffn[3].f()
    pooled(2, 1, 0)
    store1(3)
    product(5)
    late[2].c()
    pooled(2, 1, 1)
    late[3].c()
    late[4].b()
    product(6)
    late[5].b()
    pooled(2, 1, 2)
    late[2].d()
    late[6].b()
    late[0].f()
    product(7)
    late[3].d()
    late[1].e()
    cross(1)
    late[4].c()
    late[0].g()
    stage_t[...] = resp[0].astype(F32).T
    sent = [local(stage_t, outp, stores.at[2])]
    small_taps(2)
    small_taps(4)
    for name in ("tokens", "middle0", "middle1"):
        lead[name].wait()
    normed_gradient(0)
    late[2].e()
    late[5].c()
    late[3].e()
    late[6].c()
    late[4].d()
    late[7].b()
    late[1].f()
    late[5].d()
    late[2].f()
    late[1].g()
    sent.append(local(resp.at[1], outq.at[0], stores.at[3]))
    late[6].d()
    late[2].g()
    sent.append(local(strip_res.at[0], outq.at[1, :, 0 : 128], stores.at[4]))
    late[3].f()
    late[4].e()
    late[7].c()
    late[3].g()
    sent.append(local(strip_res.at[1], outq.at[1, :, 128 : 256], stores.at[5]))
    late[5].e()
    normed_gradient(1)
    tiny.a()
    late[4].f()
    late[6].e()
    late[7].d()
    late[4].g()
    sent.append(local(strip_res.at[2], outq.at[1, :, 256 : 384], stores.at[6]))
    late[5].f()
    tiny.b()
    late[5].g()
    sent.append(local(strip_res.at[3], outq.at[2, :, 0 : 128], stores.at[7]))
    late[6].f()
    late[7].e()
    late[6].g()
    sent.append(local(strip_res.at[4], outq.at[2, :, 128 : 256], stores.at[8]))
    tiny.c()
    late[7].f()
    late[7].g()
    sent.append(local(strip_res.at[5], outq.at[2, :, 256 : 384], stores.at[9]))
    tiny.d()
    tiny.e()
    small_out[...] = sm_res[...]
    for made in sent + stored[-2:]:
        made.wait()

def call_finish(
    dq, dkv, x0q, x0kv, kvf, all_taps, rows_a, rows_x, branch, weights, tokens, middle, chunks, dr, gain, sums, hidden
):
    groups = lax.axis_size("dp") // 4
    width = tokens.shape[2]
    total = padded_rows(width, groups)
    clips, side = tokens.shape[:2]
    if total != width:
        extra = ((0, 0), (0, total - width))
        rows_a, rows_x = jnp.pad(rows_a, extra), [jnp.pad(x, extra) for x in rows_x]
    small_rows = -(-SMALL_ROWS // (64 * groups)) * 64 * groups
    foldl = np.zeros((LW, 128), np.float32)
    foldl[np.arange(LW), np.arange(LW) % HEAD_DIM] = 1
    pick = np.zeros((REL_ROWS, 256), np.float32)
    pick[:NREL] = PICK.T
    vmem = pl.BlockSpec(memory_space=pltpu.VMEM)
    hbm = pl.BlockSpec(memory_space=pl.ANY)
    streamed = [dq, dkv, x0q, x0kv, kvf, all_taps, rows_a, *rows_x, *branch, weights, tokens, *middle]
    held = [
        (array.shape, array.dtype)
        for array in (dq, dkv, x0q, x0kv, kvf, all_taps, rows_a)
    ] + [
        ((clips * ROWS, total), BF16), ((clips * ROWS, LW), BF16), (weights.shape, BF16), (tokens.shape, BF16),
        (tokens.shape, F32),
    ]
    frame = pltpu.VMEM((3, T_LEN + 2, HGT + 2, PADW, LW), F32)
    return pl.pallas_call(
        partial(finish_kernel, groups, width),
        in_specs=[hbm] * len(streamed) + [vmem] * 11,
        out_specs=[vmem, hbm, hbm, hbm, vmem],
        out_shape=[
            jax.ShapeDtypeStruct(tokens.shape, F32),
            jax.ShapeDtypeStruct((total, 4 * LW), F32),
            jax.ShapeDtypeStruct((LW, total), F32),
            jax.ShapeDtypeStruct((3, total, LW), BF16),
            jax.ShapeDtypeStruct((small_rows, 128), F32),
        ],
        scratch_shapes=[pltpu.VMEM(shape, dtype) for shape, dtype in held]
        + [
            frame,
            pltpu.VMEM((3, TM + 1, HGT + 2, PADW, LW), F32),
            pltpu.VMEM((5, 27, 8, LW), F32),
            pltpu.VMEM((3, clips * ROWS, LW), BF16),
            pltpu.VMEM((2, 2, MROWS, LW), BF16),
            pltpu.VMEM((2, 2, MROWS, LW), BF16),
            pltpu.VMEM((total, 4 * LW), BF16),
            pltpu.VMEM((2, total, LW), BF16),
            pltpu.VMEM((2, total, LW), BF16),
            pltpu.VMEM((2, total, LW), F32),
            pltpu.VMEM((LW, total), F32),
            *piece_scratch(total, groups, LW, BF16, 2),
            pltpu.VMEM((6, total, 128), BF16),
            pltpu.VMEM((6, total, 128), BF16),
            *piece_scratch(total, groups, 128, BF16, 6),
            pltpu.VMEM((small_rows, 128), F32),
            pltpu.VMEM((small_rows, 128), F32),
            pltpu.VMEM((small_rows // 2, 128), F32),
            pltpu.VMEM((small_rows // 2, 128), F32),
            pltpu.VMEM((4 * groups - 1, small_rows // 8 // groups, 128), F32),
            pltpu.VMEM((clips, side, width), BF16),
            pltpu.VMEM((clips, side, width), BF16),
            pltpu.SemaphoreType.DMA((15,)),
            pltpu.SemaphoreType.DMA((10,)),
            pltpu.SemaphoreType.DMA((12, 2 * groups + 2)),
            pltpu.SemaphoreType.DMA((12, 2 * groups + 2)),
            pltpu.SemaphoreType.DMA((8 * groups,)),
            pltpu.SemaphoreType.DMA((8 * groups,)),
            pltpu.SemaphoreType.DMA((clips,)),
            pltpu.SemaphoreType.DMA((clips,)),
            pltpu.SemaphoreType.DMA((2,)),
        ],
        compiler_params=params(collective_id=1, has_side_effects=True),
        cost_estimate=pl.CostEstimate(
            flops=60_000_000_000, bytes_accessed=40_000_000, transcendentals=0
        ),
    )(*streamed, chunks, dr, gain, jnp.asarray(foldl), jnp.asarray(pick), *sums, *hidden)


def from_behind(x, axis, by):
    count = lax.axis_size(axis)
    pairs = [(i, i + by) for i in range(count) if 0 <= i + by < count]
    return lax.ppermute(x, axis, pairs)


def layer_norm(values, scaling, offset):
    average = jnp.mean(values, axis=-1, keepdims=True)
    centred = values - average
    variance = jnp.mean(centred * centred, axis=-1, keepdims=True)
    return centred * lax.rsqrt(variance + EPSILON) * scaling + offset


def pad_rows(x):
    lead = x.shape[0]
    frames = x.shape[1] // (HGT * WID)
    grid = x.reshape(lead, frames, HGT, WID, x.shape[-1])
    grid = jnp.pad(grid, ((0, 0), (0, 0), (0, 0), (0, PADW - WID), (0, 0)))
    return grid.reshape(lead, frames * HGT * PADW, x.shape[-1])


def drop_rows(x):
    lead = x.shape[0]
    frames = x.shape[1] // (HGT * PADW)
    grid = x.reshape(lead, frames, HGT, PADW, x.shape[-1])[:, :, :, :WID]
    return grid.reshape(lead, frames * HGT * WID, x.shape[-1])


def swap(x):
    return lax.ppermute(x, "head", [(0, 1), (1, 0)])


def gather_rows(x):
    half = x.shape[1]
    mine = lax.axis_index("head") * half
    both = jnp.concatenate([x, x], axis=1)
    return lax.dynamic_update_slice_in_dim(both, swap(x), half - mine, axis=1)


def taps(kernel):
    return jnp.broadcast_to(jnp.tile(kernel, (1, LH))[:, None, :], (27, 8, LW))


def on_device(
    tokens,
    ln1_gain,
    ln1_bias,
    w_qkv,
    pool_q,
    pool_k,
    pool_v,
    squeeze_k,
    squeeze_v,
    rel_t,
    rel_h,
    rel_w,
    w_proj,
    proj_bias,
    ln2_gain,
    ln2_bias,
    w_fc1,
    fc1_bias,
    w_fc2,
    fc2_bias,
    memory_valid,
    cotangent,
):
    clip_count = tokens.shape[0]
    consts = {
        "fold": jnp.asarray(fold_constants(), BF16),
        "one": jnp.asarray(one_lane(), F32),
        "own": jnp.asarray(OWN_T.T, F32),
        "ownt": jnp.asarray(OWN_T, F32),
        "lanes": jnp.asarray(head_lanes(), BF16),
        "grow": jnp.asarray(FOLD, BF16),
        "ekey": jnp.asarray(EKEY, BF16),
    }
    keys_extra = key_constants(memory_valid)
    rel_all = jnp.concatenate([rel_t, rel_h, rel_w], axis=0)
    pairs = jnp.dot(jnp.asarray(PICK), rel_all, precision=HIGHEST)
    pair_table = (pairs * HEAD_DIM**0.5).T
    table_high = pair_table.astype(BF16)
    table_rest = (pair_table - table_high.astype(F32)).astype(BF16)
    tables = jnp.stack(
        [
            jnp.stack(
                [
                    jnp.pad(
                        part,
                        (
                            (head * HEAD_DIM - window_of(head), WIN - HEAD_DIM - head * HEAD_DIM + window_of(head)),
                            (0, 0),
                        ),
                    )
                    for part in (table_high, table_rest)
                ]
            )
            for head in range(LH)
        ]
    )
    rel_rows = pairs.T.astype(BF16)
    tap_q, tap_kv = taps(pool_q)[None], jnp.stack([taps(pool_k), taps(pool_v)])
    tap_s = jnp.stack([taps(squeeze_k), taps(squeeze_v)])

    width = tokens.shape[2]
    inputs_low = pad_rows(tokens)
    inputs = inputs_low.astype(F32)
    upstream = pad_rows(cotangent)
    real = (jnp.arange(inputs.shape[1]) % PADW < WID)[None, :, None]
    first_normed = layer_norm(inputs, ln1_gain, ln1_bias)
    first_rows = gather_rows(jnp.where(real, first_normed, 0.0).astype(BF16))
    w_heads = w_qkv.transpose(1, 0, 2)
    upstream_other = swap(lax.optimization_barrier((upstream, first_rows))[0])
    kv0, kv, kvf, mem = call_pool_forward(first_rows, w_heads, 1, 2, tap_kv, tap_s)
    before = from_behind(mem[-2:], "dp", 1)
    q0, q = call_pool_forward(first_rows, w_heads, 0, 1, tap_q)
    memory = jnp.concatenate([before, mem], axis=0)
    vectors = jnp.stack([proj_bias, ln2_gain, ln2_bias])
    hidden_bias = fc1_bias.reshape(1, -1)
    rows32 = jax.ShapeDtypeStruct((HALF, width), F32)
    rows16 = jax.ShapeDtypeStruct((HALF, width), BF16)
    clips = range(clip_count)
    branch, qa, at, lse, kept, recv = [], [], [], [], [], []
    for clip in clips:
        made = call_attention_forward(clip, q, kv, memory, keys_extra, tables, consts)
        for store, value in zip((branch, qa, at, lse), made):
            store.append(value)
        own, sent = simple_call(project_kernel, [rows32, rows16], 1, branch[-1][0], w_proj)
        sent, q = lax.optimization_barrier((sent, q)) if clip + 1 < clip_count else (sent, q)
        kept.append(own)
        recv.append(swap(sent))
    middle, mine, theirs = [], [], []
    for clip in clips:
        x1, a2 = simple_call(
            middle_kernel, [rows32, rows16], 1, inputs_low[clip], kept[clip], recv[clip], vectors
        )
        middle.append(x1)
        mine.append(a2)
        theirs.append(swap(a2))
    own_parts = [call_ffn(mine[c], upstream[c], w_fc1, hidden_bias, w_fc2, F32) for c in clips]
    other_parts = [call_ffn(theirs[c], upstream_other[c], w_fc1, hidden_bias, w_fc2, BF16) for c in clips]
    second = [swap(other_parts[c][2]) for c in clips]
    dmiddle, low, sums, rows_x, dmix = [], [], [], [], []
    for clip in clips:
        dx, dx_low, total = simple_call(
            norm_back_kernel,
            [rows32, rows16, jax.ShapeDtypeStruct((HEAD_EARLY, width), F32)],
            1,
            own_parts[clip][2], second[clip], middle[clip], upstream[clip], vectors,
        )
        dmiddle.append(dx)
        sums.append(total)
        low.append((dx_low, swap(dx_low)))
    parts = own_parts + other_parts
    w_fc2_grad, w_fc1_grad = call_weights(
        [p[0] for p in parts],
        [p[1] for p in parts],
        mine + theirs,
        [upstream[c] for c in clips] + [upstream_other[c] for c in clips],
    )
    for clip in clips:
        rows, mix = simple_call(
            mix_kernel,
            [jax.ShapeDtypeStruct((ROWS, width), BF16), jax.ShapeDtypeStruct((ROWS, LW), BF16)],
            1,
            *low[clip], w_proj,
        )
        rows_x.append(rows)
        dmix.append(mix)
    last = [lax.optimization_barrier((other_parts[c][3], low[-1][1]))[0] for c in clips]
    last = [swap(x) for x in last]
    dq, dkv, dr, chunks, w_fc2_grad = call_attention_backward(
        q, kv, memory, keys_extra, qa, dmix, at, lse, rel_rows,
        w_fc2_grad, w_fc1_grad, consts,
    )
    *last, dq = lax.optimization_barrier((*last, dq))
    output = drop_rows(
        jnp.stack(
            [
                (middle[c] + own_parts[c][3] + last[c].astype(F32) + fc2_bias).astype(BF16)
                for c in clips
            ]
        )
    )
    w_fc2_grad = w_fc2_grad.astype(F32)
    input_grad, w_fc1_grad, w_proj_grad, tail, small = call_finish(
        dq, dkv, q0, kv0, kvf, jnp.concatenate([tap_q, tap_kv, tap_s]),
        first_rows.reshape(-1, width),
        rows_x,
        [b[0] for b in branch],
        w_heads,
        inputs_low,
        dmiddle,
        chunks,
        dr,
        ln1_gain.reshape(1, -1),
        sums,
        [p[4] for p in parts],
    )
    input_grad = drop_rows(input_grad)
    total = w_fc1_grad.shape[0]
    if total != width:
        w_fc2_grad = w_fc2_grad.reshape(2, total, width)[:, :width].reshape(2 * width, width)
        w_fc1_grad, w_proj_grad, tail = w_fc1_grad[:width], w_proj_grad[:, :width], tail[:, :width]
    w_qkv_grad = tail.astype(F32).transpose(1, 0, 2)
    norms = small[NORM_ROW:EARLY_ROW].reshape(2, width)
    early = small[EARLY_ROW:HIDDEN_ROW].reshape(4, width)
    fc1_bias_grad = lax.dynamic_index_in_dim(
        small[HIDDEN_ROW:SMALL_ROWS].reshape(2, fc1_bias.size), lax.axis_index("head"), 0, keepdims=False
    )
    small = small[:, :HEAD_DIM]
    shared = [norms[0], norms[1]]
    shared += [small[TAP_ROW + 27 * n : TAP_ROW + 27 * n + 27] for n in range(5)]
    shared += [
        small[: 2 * T_LEN - 1],
        small[2 * T_LEN - 1 : 2 * T_LEN + 2 * HGT - 2],
        small[2 * T_LEN + 2 * HGT - 2 : NREL],
    ]
    shared += [early[0], early[1], early[2], early[3]]
    return (
        output,
        input_grad,
        shared[0],
        shared[1],
        w_qkv_grad,
        shared[2],
        shared[3],
        shared[4],
        shared[5],
        shared[6],
        shared[7],
        shared[8],
        shared[9],
        w_proj_grad,
        shared[10],
        shared[11],
        shared[12],
        w_fc1_grad,
        fc1_bias_grad,
        w_fc2_grad,
        shared[13],
    )


def solution(mesh):
    return jax.shard_map(
        on_device,
        mesh=mesh,
        in_specs=(
            P("dp", "head", None),
            P(),
            P(),
            P(None, None, "head"),
            P(),
            P(),
            P(),
            P(),
            P(),
            P(),
            P(),
            P(),
            P("head", None),
            P(),
            P(),
            P(),
            P(None, "head"),
            P("head"),
            P("head", None),
            P(),
            P("dp", None),
            P("dp", "head", None),
        ),
        out_specs=(
            P("dp", "head", None),
            P("dp", "head", None),
            P(),
            P(),
            P(None, None, "head"),
            P(),
            P(),
            P(),
            P(),
            P(),
            P(),
            P(),
            P(),
            P("head", None),
            P(),
            P(),
            P(),
            P(None, "head"),
            P("head"),
            P("head", None),
            P(),
        ),
        check_vma=False,
    )
```

```python
from functools import partial

import jax
import jax.numpy as jnp
import numpy as np
from jax import lax
from jax.experimental import pallas as pl
from jax.experimental.pallas import tpu as pltpu
from jax.sharding import PartitionSpec as P

HEAD_DIM = 96
T_LEN = 8
HGT = 7
WID = 7
PADW = 8
L = 392
ROWS = T_LEN * HGT * PADW
TM = 4
MROWS = TM * HGT * PADW
KEYS = ROWS + 2 * MROWS
LH = 4
LW = LH * HEAD_DIM
WIN = 256
BLOCK = 128
NBLOCK = KEYS // BLOCK

EPSILON = 1e-06
HIGHEST = lax.Precision.HIGHEST
SCALE = HEAD_DIM ** (-0.5)
LOG2E = 1.4426950408889634
F32 = jnp.float32
BF16 = jnp.bfloat16
VMEM_LIMIT = 58 * 1024 * 1024

NB = T_LEN + HGT + WID
NREL = 2 * T_LEN - 1 + 2 * HGT - 1 + 2 * WID - 1
NPAIR = T_LEN * T_LEN + HGT * HGT + WID * WID


def params(**extra):
    return pltpu.CompilerParams(vmem_limit_bytes=VMEM_LIMIT, **extra)


def window_of(head):
    return 0 if head < 2 else BLOCK


def slot_of(head):
    return 192 if head < 2 else 0


def position_constants():
    t, h, w = np.meshgrid(np.arange(T_LEN), np.arange(HGT), np.arange(PADW), indexing="ij")
    t, h, w = t.ravel(), h.ravel(), w.ravel()
    valid = w < WID
    own = np.zeros((256, ROWS), np.float32)
    pick = np.zeros((256, NREL), np.float32)
    fold = np.zeros((256, 32), np.float32)
    ekey = np.zeros((32, KEYS), np.float32)
    row = 0
    base_entry = 0
    base_bias = 0
    for places, length in ((t, T_LEN), (h, HGT), (w, WID)):
        for a in range(length):
            for b in range(length):
                own[row] = (places == a) & valid
                pick[row, base_entry + a - b + length - 1] = 1
                fold[row, base_bias + b] = 1
                row += 1
        for b in range(length):
            ekey[base_bias + b, :ROWS] = (places == b) & valid
        base_entry += 2 * length - 1
        base_bias += length
    return own, pick, fold, ekey, valid


OWN_T, PICK, FOLD, EKEY, ROW_VALID = position_constants()


def fold_constants():
    out = np.zeros((2, 2, 256, WIN), np.float32)
    for variant, slot in enumerate((192, 0)):
        out[variant, 0, :, slot : slot + 32] = FOLD
        out[variant, 1, :, slot + 32 : slot + 64] = FOLD
    return out


def one_lane():
    out = np.zeros((2, 8, WIN), np.float32)
    for variant, slot in enumerate((192, 0)):
        out[variant, :, slot + NB] = 1
    return out


def head_lanes():
    out = np.zeros((LH, ROWS, WIN), np.float32)
    for head in range(LH):
        first = head * HEAD_DIM - window_of(head)
        out[head, :, first : first + HEAD_DIM] = 1
    return out


def key_constants(memory_valid):
    clip_count = memory_valid.shape[0]
    base = np.zeros((2, KEYS, WIN), np.float32)
    lane = np.zeros((2, 1, WIN), np.float32)
    for variant, slot in enumerate((192, 0)):
        base[variant, :, slot : slot + 32] = EKEY.T
        base[variant, :, slot + 32 : slot + 64] = EKEY.T
        lane[variant, :, slot + NB] = 1
    pads = np.concatenate([ROW_VALID, ROW_VALID[:MROWS], ROW_VALID[:MROWS]])
    use = jnp.concatenate(
        [jnp.ones((clip_count, ROWS), bool), jnp.repeat(memory_valid > 0, MROWS, axis=1)], axis=1
    )
    drop = jnp.where(use & jnp.asarray(pads)[None], 0.0, -1e30).astype(F32)
    return (jnp.asarray(base)[None] + drop[:, None, :, None] * jnp.asarray(lane)[None]).astype(BF16)


def nt(a, b):
    return lax.dot_general(a, b, (((1,), (1,)), ((), ())), preferred_element_type=F32)


def nn(a, b):
    return jnp.dot(a, b, preferred_element_type=F32)


def keep_rows(block):
    place = lax.broadcasted_iota(jnp.int32, block.shape, block.ndim - 2)
    return jnp.where(place < WID, block, 0.0)


def spread(dst, first, value):
    n, _, _, c = value.shape
    flat = value.reshape(n * HGT, PADW, c)
    dst[0, pl.ds(first, n), 1 : HGT + 1] = pltpu.roll(flat, 1, axis=1).reshape(n, HGT, PADW, c)
    dst[1, pl.ds(first, n), 1 : HGT + 1] = value
    dst[2, pl.ds(first, n), 1 : HGT + 1] = pltpu.roll(flat, PADW - 1, axis=1).reshape(n, HGT, PADW, c)


def widened(rows):
    return jnp.broadcast_to(rows[:, None, :], (rows.shape[0], 8, rows.shape[1]))


def pool_forward(squeeze, *refs):
    if squeeze:
        a_ref, w_ref, rows_k, rows_s, x0_ref, xp_ref, xf_ref, m_ref, xs, k_ref, ys, s_ref = refs
    else:
        a_ref, w_ref, rows_k, x0_ref, xp_ref, xs, k_ref = refs

    @pl.when((pl.program_id(0) == 0) & (pl.program_id(1) == 0))
    def _():
        xs[...] = jnp.zeros_like(xs)
        if squeeze:
            ys[...] = jnp.zeros_like(ys)

    @pl.when(pl.program_id(1) == 0)
    def _():
        k_ref[0] = widened(rows_k[0])
        if squeeze:
            s_ref[0] = widened(rows_s[0])

    x = nn(a_ref[0], w_ref[0])
    x0_ref[0, 0] = x.astype(BF16)
    spread(xs, 1, x.reshape(T_LEN, HGT, PADW, LW))
    for tile in range(LW // 128):
        lanes = slice(tile * 128, tile * 128 + 128)

        def step(pair, _):
            acc = [jnp.zeros((HGT, PADW, 128), F32) for _ in range(2)]
            for a in range(3):
                for c in range(3):
                    for d in range(2):
                        block = xs[c, 2 * pair + d + a, :, :, lanes]
                        for b in range(3):
                            acc[d] = acc[d] + k_ref[0, a * 9 + b * 3 + c, :, lanes][None] * block[b : b + HGT]
            both = keep_rows(jnp.stack(acc))
            rows = pl.ds(pl.multiple_of(pair * 112, 112), 112)
            flat = both.reshape(112, 128)
            xp_ref[0, 0, rows, lanes] = flat.astype(BF16)
            if squeeze:
                xf_ref[0, 0, rows, lanes] = flat.astype(BF16)
                both = both.reshape(2 * HGT, PADW, 128)
                for c, shift in ((0, 1), (1, 0), (2, PADW - 1)):
                    moved = pltpu.roll(both, shift, axis=1) if shift else both
                    ys[c, pl.ds(2 * pair + 1, 2), 1 : HGT + 1, :, lanes] = moved.reshape(2, HGT, PADW, 128)
            return 0

        lax.fori_loop(0, T_LEN // 2, step, 0)
        if squeeze:

            def squeeze_step(pair, _):
                acc = [jnp.zeros((HGT, PADW, 128), F32) for _ in range(2)]
                for a in range(3):
                    for c in range(3):
                        for d in range(2):
                            block = ys[c, 4 * pair + 2 * d + a, :, :, lanes]
                            for b in range(3):
                                acc[d] = acc[d] + s_ref[0, a * 9 + b * 3 + c, :, lanes][None] * block[b : b + HGT]
                rows = pl.ds(pl.multiple_of(pair * 112, 112), 112)
                m_ref[0, 0, rows, lanes] = keep_rows(jnp.stack(acc)).reshape(112, 128).astype(BF16)
                return 0

            lax.fori_loop(0, TM // 2, squeeze_step, 0)


def call_pool_forward(rows, weights, first, count, kernels, squeeze):
    clips = rows.shape[0]
    tap = pl.BlockSpec((1, 27, LW), lambda j, i: (j + first, 0, 0))
    tap_squeeze = pl.BlockSpec((1, 27, LW), lambda j, i: (j + first + 2, 0, 0))
    wide = pltpu.VMEM((1, 27, 8, LW), F32)

    def out(n):
        return pl.BlockSpec((1, 1, n, LW), lambda j, i: (i, j, 0, 0))

    frame = pltpu.VMEM((3, T_LEN + 2, HGT + 2, PADW, LW), F32)
    shapes = [
        jax.ShapeDtypeStruct((clips, count, ROWS, LW), BF16),
        jax.ShapeDtypeStruct((clips, count, ROWS, LW), BF16),
    ]
    specs = [out(ROWS), out(ROWS)]
    if squeeze:
        shapes += [
            jax.ShapeDtypeStruct((clips, count, ROWS, LW), BF16),
            jax.ShapeDtypeStruct((clips, count, MROWS, LW), BF16),
        ]
        specs += [out(ROWS), out(MROWS)]
    return pl.pallas_call(
        partial(pool_forward, squeeze),
        grid=(count, clips),
        in_specs=[
            pl.BlockSpec((1, ROWS, rows.shape[2]), lambda j, i: (i, 0, 0)),
            pl.BlockSpec((1, weights.shape[1], LW), lambda j, i: (j + first, 0, 0)),
            tap,
        ]
        + ([tap_squeeze] if squeeze else []),
        out_specs=specs,
        out_shape=shapes,
        scratch_shapes=[frame, wide] * (2 if squeeze else 1),
        compiler_params=params(),
        cost_estimate=pl.CostEstimate(
            flops=60_000_000_000 * count // 10, bytes_accessed=4_000_000 * count, transcendentals=0
        ),
    )(rows, weights, kernels, *([kernels] if squeeze else []))


def attention_forward(
    q_ref, kv_ref, m1_ref, m2_ref, ke_ref, tab_ref, fold_ref, one_ref, own_ref, lanes_ref, w_ref,
    branch_ref, qa_ref, at_ref, lse_ref, kept_ref, sent_ref, keys, vt, scores, expo, table,
):
    keys[0:ROWS] = kv_ref[0, 0]
    keys[ROWS : ROWS + MROWS] = m1_ref[0, 0]
    keys[ROWS + MROWS :] = m2_ref[0, 0]
    vt[:, 0:ROWS] = kv_ref[0, 1].T
    memory = jnp.concatenate([m1_ref[0, 1], m2_ref[0, 1]], axis=0).T
    vt[:, ROWS:] = memory
    for head in range(LH):
        first = window_of(head)
        variant = head // 2
        win = slice(first, first + WIN)
        heads = lanes_ref[head]
        qm = q_ref[0, 0, :, win] * heads
        table[...] = jnp.zeros_like(table)
        for part in range(2):
            table[part, head * HEAD_DIM - first : (head + 1) * HEAD_DIM - first] = tab_ref[part]
        raw = nn(qm, table[0]) + nn(qm, table[1])
        raw = raw * own_ref[...]
        high = raw.astype(BF16)
        rest = (raw - high.astype(F32)).astype(BF16)
        placed = nn(high, fold_ref[variant, 0]) + nn(rest, fold_ref[variant, 1]) + one_ref[variant, 0:1]
        qa = qm + placed.astype(BF16)
        qa_ref[0, head] = qa

        def score(number, peak):
            rows = pl.ds(pl.multiple_of(number * BLOCK, BLOCK), BLOCK)
            ka = keys[rows, win] * heads[0:BLOCK] + ke_ref[0, variant, rows]
            s = nt(ka, qa)
            scores[rows] = s
            return jnp.maximum(peak, jnp.max(s, axis=0, keepdims=True))

        peak = lax.fori_loop(0, NBLOCK, score, jnp.full((1, ROWS), -3e38, F32))
        shift = peak * (SCALE * LOG2E)

        def soften(number, total):
            rows = pl.ds(pl.multiple_of(number * BLOCK, BLOCK), BLOCK)
            e = jnp.exp2(scores[rows] * (SCALE * LOG2E) - shift)
            expo[rows] = e.astype(BF16)
            return total + jnp.sum(e, axis=0, keepdims=True)

        total = lax.fori_loop(0, NBLOCK, soften, jnp.zeros((1, ROWS), F32))
        out = nn(vt[head * HEAD_DIM : (head + 1) * HEAD_DIM], expo[...]) * (1.0 / total)
        at_ref[0, head * HEAD_DIM : (head + 1) * HEAD_DIM] = out
        lse_ref[0, head : head + 1] = shift + jnp.log2(total)
    branch_ref[0] = (at_ref[0].T + q_ref[0, 0].astype(F32)).astype(BF16)
    side = lax.axis_index("head")
    sent_ref[...] = nn(branch_ref[0, half_rows(1 - side)], w_ref[...]).astype(BF16)
    kept_ref[...] = nn(branch_ref[0, half_rows(side)], w_ref[...])


def whole(shape):
    return pl.BlockSpec(shape, lambda i: (0,) * len(shape))


def clip_block(*shape):
    return pl.BlockSpec((1,) + shape, lambda i: (i,) + (0,) * len(shape))


def call_attention_forward(clip, q, kv, memory, keys_extra, tables, w_proj, consts):
    def block(*shape, at=clip):
        return pl.BlockSpec((1,) + shape, lambda i: (at,) + (0,) * len(shape))

    return pl.pallas_call(
        attention_forward,
        grid=(1,),
        in_specs=[
            block(1, ROWS, LW),
            block(2, ROWS, LW),
            block(2, MROWS, LW, at=clip + 1),
            block(2, MROWS, LW, at=clip),
            block(2, KEYS, WIN),
            whole((2, HEAD_DIM, 256)),
            whole((2, 2, 256, WIN)),
            whole((2, 8, WIN)),
            whole((ROWS, 256)),
            whole((LH, ROWS, WIN)),
            whole(w_proj.shape),
        ],
        out_specs=[
            clip_block(ROWS, LW),
            clip_block(LH, ROWS, WIN),
            clip_block(LW, ROWS),
            clip_block(8, ROWS),
            whole((HALF, w_proj.shape[1])),
            whole((HALF, w_proj.shape[1])),
        ],
        out_shape=[
            jax.ShapeDtypeStruct((1, ROWS, LW), BF16),
            jax.ShapeDtypeStruct((1, LH, ROWS, WIN), BF16),
            jax.ShapeDtypeStruct((1, LW, ROWS), F32),
            jax.ShapeDtypeStruct((1, 8, ROWS), F32),
            jax.ShapeDtypeStruct((HALF, w_proj.shape[1]), F32),
            jax.ShapeDtypeStruct((HALF, w_proj.shape[1]), BF16),
        ],
        scratch_shapes=[
            pltpu.VMEM((KEYS, LW), BF16),
            pltpu.VMEM((LW, KEYS), BF16),
            pltpu.VMEM((KEYS, ROWS), F32),
            pltpu.VMEM((KEYS, ROWS), BF16),
            pltpu.VMEM((2, WIN, 256), BF16),
        ],
        compiler_params=params(),
        cost_estimate=pl.CostEstimate(
            flops=1_300_000_000, bytes_accessed=500_000, transcendentals=0
        ),
    )(q, kv, memory, memory, keys_extra, tables, consts["fold"], consts["one"], consts["own"], consts["lanes"], w_proj)


HALF = ROWS // 2


def simple_call(kernel, out_shape, gflops, *args):
    vmem = pl.BlockSpec(memory_space=pltpu.VMEM)
    many = isinstance(out_shape, list)
    return pl.pallas_call(
        kernel,
        in_specs=[vmem] * len(args),
        out_specs=[vmem] * len(out_shape) if many else vmem,
        out_shape=out_shape,
        compiler_params=params(),
        cost_estimate=pl.CostEstimate(
            flops=int(gflops * 1e8), bytes_accessed=200_000, transcendentals=0
        ),
    )(*args)


def half_rows(side):
    return pl.ds(pl.multiple_of(side * HALF, 16), HALF)


def middle_kernel(tokens, kept, recv, vectors, x1_ref, a2_ref):
    x1 = tokens[...].astype(F32) + kept[...] + recv[...].astype(F32) + vectors[0:1]
    x1_ref[...] = x1
    centred = x1 - jnp.mean(x1, axis=-1, keepdims=True)
    scale = lax.rsqrt(jnp.mean(centred * centred, axis=-1, keepdims=True) + EPSILON)
    a2_ref[...] = (centred * scale * vectors[1:2] + vectors[2:3]).astype(BF16)


FFN_BLOCK = 512
GELU_A = 0.7978845608028654
GELU_B = 0.044715


def joined(refs):
    return jnp.concatenate([ref[...] for ref in refs], axis=0) if len(refs) > 1 else refs[0][...]


def ffn_kernel(count, *refs):
    a2 = joined(refs[:count])
    g = joined(refs[count : 2 * count])
    w1, b1, w2 = refs[2 * count : 2 * count + 3]
    outs = refs[2 * count + 3 :]
    act_refs, dpre_refs, da2_refs, out_refs = (outs[n * count : (n + 1) * count] for n in range(4))
    sums_ref = outs[4 * count]
    da2 = jnp.zeros(a2.shape, F32)
    out = jnp.zeros(a2.shape, F32)
    for first in range(0, w1.shape[1], FFN_BLOCK):
        cols = slice(first, first + FFN_BLOCK)
        pre = nn(a2, w1[:, cols]) + b1[0:1, cols]
        square = pre * pre
        bent = jnp.tanh(GELU_A * (pre + GELU_B * (pre * square)))
        gate = 0.5 + 0.5 * bent
        act = (pre * gate).astype(BF16)
        slope = gate + 0.5 * pre * (1.0 - bent * bent) * (GELU_A * (1.0 + 3.0 * GELU_B * square))
        dpre = nt(g, w2[cols]) * slope
        low = dpre.astype(BF16)
        sums_ref[0:1, cols] = jnp.sum(dpre, axis=0, keepdims=True)
        for n in range(count):
            act_refs[n][:, cols] = act[n * HALF : (n + 1) * HALF]
            dpre_refs[n][:, cols] = low[n * HALF : (n + 1) * HALF]
        da2 = da2 + nt(low, w1[:, cols])
        out = out + nn(act, w2[cols])
    for n in range(count):
        da2_refs[n][...] = da2[n * HALF : (n + 1) * HALF].astype(da2_refs[n].dtype)
        out_refs[n][...] = out[n * HALF : (n + 1) * HALF].astype(out_refs[n].dtype)


def call_ffn(parts, w1, b1, w2):
    hidden, width = w2.shape
    count = len(parts)
    made = simple_call(
        partial(ffn_kernel, count),
        [jax.ShapeDtypeStruct((HALF, hidden), BF16)] * (2 * count)
        + [jax.ShapeDtypeStruct((HALF, width), dtype) for _, _, dtype in parts] * 2
        + [jax.ShapeDtypeStruct((1, hidden), F32)],
        5,
        *[part[0] for part in parts],
        *[part[1] for part in parts],
        w1, b1, w2,
    )
    return [tuple(made[n :: count][:4]) for n in range(count)], made[-1]


def tn(a, b):
    return lax.dot_general(a, b, (((0,), (0,)), ((), ())), preferred_element_type=F32)


def weight_kernel(count, *refs):
    acts, dpres, a2s, gs = (refs[n * count : (n + 1) * count] for n in range(4))
    g2, g1 = refs[4 * count :]
    g2[...] = tn(joined(acts), joined(gs)).astype(BF16)
    g1[...] = tn(joined(a2s), joined(dpres)).astype(BF16)


def call_weights(acts, dpres, a2s, gs):
    hidden, width = acts[0].shape[1], gs[0].shape[1]
    count = len(acts)
    piece = pl.BlockSpec((HALF, LW), lambda i: (0, i))
    full = pl.BlockSpec((HALF, width), lambda i: (0, 0))
    return pl.pallas_call(
        partial(weight_kernel, count),
        grid=(hidden // LW,),
        in_specs=[piece] * (2 * count) + [full] * (2 * count),
        out_specs=[
            pl.BlockSpec((LW, width), lambda i: (i, 0)),
            pl.BlockSpec((width, LW), lambda i: (0, i)),
        ],
        out_shape=[
            jax.ShapeDtypeStruct((hidden, width), BF16),
            jax.ShapeDtypeStruct((width, hidden), BF16),
        ],
        compiler_params=params(),
        cost_estimate=pl.CostEstimate(flops=800_000_000, bytes_accessed=1_500_000, transcendentals=0),
    )(*acts, *dpres, *a2s, *gs)


def norm_back_kernel(kept, recv, x1_ref, g, vectors, dx_ref, low_ref, sums):
    u = kept[...] + recv[...].astype(F32)
    x1 = x1_ref[...]
    centred = x1 - jnp.mean(x1, axis=-1, keepdims=True)
    scale = lax.rsqrt(jnp.mean(centred * centred, axis=-1, keepdims=True) + EPSILON)
    xhat = centred * scale
    w = u * vectors[1:2]
    up = g[...].astype(F32)
    dx = up + scale * (
        w - jnp.mean(w, axis=-1, keepdims=True) - xhat * jnp.mean(w * xhat, axis=-1, keepdims=True)
    )
    dx_ref[...] = dx
    low_ref[...] = dx.astype(BF16)
    sums[0:1] = jnp.sum(dx, axis=0, keepdims=True)
    sums[1:2] = jnp.sum(u * xhat, axis=0, keepdims=True)
    sums[2:3] = jnp.sum(u, axis=0, keepdims=True)
    sums[3:4] = jnp.sum(up, axis=0, keepdims=True)
    sums[4:8] = jnp.zeros((4, u.shape[1]), F32)


def mix_kernel(mine, theirs, w, rows_ref, dmix_ref):
    head = lax.axis_index("head")
    for side, part in ((head, mine), (1 - head, theirs)):
        rows_ref[half_rows(side)] = part[...]
        dmix_ref[half_rows(side)] = nt(part[...], w[...]).astype(BF16)


HEAD_EARLY = 8
MESH = pl.DeviceIdType.MESH


def remote(src, dst, send, recv, peer):
    made = pltpu.make_async_remote_copy(
        src_ref=src, dst_ref=dst, send_sem=send, recv_sem=recv, device_id=peer, device_id_type=MESH
    )
    made.start()
    return made


def local(src, dst, sem):
    made = pltpu.make_async_copy(src, dst, sem)
    made.start()
    return made


class Place:
    def __init__(self, groups):
        dp = lax.axis_index("dp")
        head = lax.axis_index("head")
        self.groups = groups
        self.dp, self.head = dp, head
        self.core = lax.rem(dp, 2)
        self.xbit = lax.rem(lax.div(dp, 2), 2)
        self.group = lax.div(dp, 4)
        self.to_core = (dp + 1 - 2 * self.core, head)
        self.to_x = (dp + 2 - 4 * self.xbit, head)
        self.to_y = (dp, 1 - head)
        self.peers = [
            (lax.rem(self.group + o, groups) * 4 + lax.rem(dp, 4), head) for o in range(1, groups)
        ]
        self.number = (head * groups + self.group) * 2 + self.xbit

    def device(self, number):
        side = lax.div(number, 2 * self.groups)
        group = lax.rem(lax.div(number, 2), self.groups)
        return (group * 4 + lax.rem(number, 2) * 2 + self.core, side)

    def greet(self, more=()):
        barrier = pltpu.get_barrier_semaphore()
        signalled = [self.to_core, self.to_x] + self.peers + list(more)
        for peer in signalled:
            pl.semaphore_signal(barrier, inc=1, device_id=peer, device_id_type=MESH)
        pl.semaphore_wait(barrier, len(signalled))


class Piece:
    def __init__(self, place, rows, source, result, reduce_refs, send, recv):
        self.at = place
        self.half, self.quarter = rows // 2, rows // 4
        self.chunk = rows // 4 // place.groups
        self.source, self.result = source, result
        self.refs = reduce_refs
        self.send, self.recv = send, recv
        self.tile = 16 if reduce_refs is None or reduce_refs[0].dtype == BF16 else 8
        self.flights = {}

    def start(self, key, number, src, dst, peer):
        self.flights[key] = remote(src, dst, self.send.at[number], self.recv.at[number], peer)

    def base(self, g):
        at = self.at
        return pl.multiple_of(at.core * self.half + at.xbit * self.quarter + g * self.chunk, self.tile)

    def a(self):
        theirs = pl.multiple_of((1 - self.at.core) * self.half, self.tile)
        self.start("a", 0, self.source(theirs, self.half), self.refs[0], self.at.to_core)

    def sum_rows(self, which):
        recv_a = self.refs[0]
        first = pl.multiple_of(which * self.quarter, self.tile)
        own = self.source(pl.multiple_of(self.at.core * self.half + which * self.quarter, self.tile), self.quarter)
        return own[...].astype(F32) + recv_a[pl.ds(first, self.quarter)].astype(F32)

    def b(self):
        _, send_b, recv_b, _, _ = self.refs
        self.flights["a"].wait()
        send_b[...] = self.sum_rows(1 - self.at.xbit).astype(send_b.dtype)
        self.start("b", 1, send_b, recv_b, self.at.to_x)

    def c(self):
        _, _, recv_b, send_c, recv_c = self.refs
        self.flights["b"].wait()
        send_c[...] = (self.sum_rows(self.at.xbit) + recv_b[...].astype(F32)).astype(send_c.dtype)
        for o in range(1, self.at.groups):
            first = pl.multiple_of(lax.rem(self.at.group + o, self.at.groups) * self.chunk, self.tile)
            self.start(
                ("c", o), 1 + o, send_c.at[pl.ds(first, self.chunk)], recv_c.at[o - 1], self.at.peers[o - 1]
            )

    def total(self):
        _, _, _, send_c, recv_c = self.refs
        own = send_c[pl.ds(pl.multiple_of(self.at.group * self.chunk, self.tile), self.chunk)].astype(F32)
        for o in range(1, self.at.groups):
            self.flights["c", o].wait()
            own = own + recv_c[o - 1].astype(F32)
        return own

    def d(self, own=None):
        own = self.total() if own is None else own
        mine = self.result(self.base(self.at.group), self.chunk)
        mine[...] = own.astype(mine.dtype)
        for o in range(1, self.at.groups):
            number = self.at.groups + o
            self.start(("d", o), number, mine, mine, self.at.peers[o - 1])

    def e(self):
        for o in range(1, self.at.groups):
            self.flights["d", o].wait()
        mine = self.result(self.base(0), self.quarter)
        self.start("e", 2 * self.at.groups, mine, mine, self.at.to_x)

    def f(self):
        self.flights["e"].wait()
        mine = self.result(pl.multiple_of(self.at.core * self.half, self.tile), self.half)
        self.start("f", 2 * self.at.groups + 1, mine, mine, self.at.to_core)

    def g(self):
        self.flights["f"].wait()


def piece_scratch(rows, groups, width, dtype, count):
    half, quarter = rows // 2, rows // 4
    return [
        pltpu.VMEM((count, half, width), dtype),
        pltpu.VMEM((count, quarter, width), dtype),
        pltpu.VMEM((count, quarter, width), dtype),
        pltpu.VMEM((count, quarter, width), dtype),
        pltpu.VMEM((count, groups - 1, quarter // groups, width), dtype),
    ]


class Tiny:
    def __init__(self, place, source, result, refs, send, recv):
        self.at, self.source, self.result = place, source, result
        self.recv_core, self.summed, self.slots = refs
        self.send, self.recv = send, recv
        count = 4 * place.groups
        self.half, self.chunk = source.shape[0] // 2, source.shape[0] // 2 // count
        self.mine = place.number
        self.others = [lax.rem(place.number + o, count) for o in range(1, count)]
        self.flights = {}

    def rows(self, number):
        return pl.ds(pl.multiple_of(number * self.chunk, 8), self.chunk)

    def halves(self, core):
        return pl.ds(pl.multiple_of(core * self.half, 8), self.half)

    def start(self, key, src, dst, peer):
        number = len(self.flights)
        self.flights[key] = remote(src, dst, self.send.at[number], self.recv.at[number], peer)

    def a(self):
        self.start("a", self.source.at[self.halves(1 - self.at.core)], self.recv_core, self.at.to_core)

    def b(self):
        self.flights["a"].wait()
        self.summed[...] = self.source[self.halves(self.at.core)] + self.recv_core[...]
        for o, number in enumerate(self.others):
            self.start(("b", o), self.summed.at[self.rows(number)], self.slots.at[o], self.at.device(number))

    def c(self):
        total = self.summed[self.rows(self.mine)]
        for o, number in enumerate(self.others):
            self.flights["b", o].wait()
            total = total + self.slots[o]
        rows = pl.ds(pl.multiple_of(self.at.core * self.half + self.mine * self.chunk, 8), self.chunk)
        self.result[rows] = total
        for o, number in enumerate(self.others):
            self.start(("c", o), self.result.at[rows], self.result.at[rows], self.at.device(number))

    def d(self):
        for o in range(len(self.others)):
            self.flights["c", o].wait()
        rows = self.halves(self.at.core)
        self.start("d", self.result.at[rows], self.result.at[rows], self.at.to_core)

    def e(self):
        self.flights["d"].wait()


def attention_backward(
    groups,
    q_ref, kv_ref, mem_ref, ke_hbm, qa_hbm0, qa_hbm1, dm_ref0, dm_ref1, at_hbm0, at_hbm1, lse_ref0, lse_ref1,
    rt_ref, grow_ref, ownt_ref, ekey_ref,
    lanes_ref, g2_ref, g1_ref,
    dq_ref, dkv_ref, dr_ref, chunks_ref, out2,
    ke_ref, qa_ref, at_ref, keys, values, kt, dmt, qms, dms, dqt,
    recv_a, send_b, recv_b, send_c, recv_c,
    loads, sems_send, sems_recv,
):
    place = Place(groups)
    clips = q_ref.shape[0]
    dm_refs, lse_refs = (dm_ref0, dm_ref1), (lse_ref0, lse_ref1)
    lead = [
        [
            local(ke_hbm.at[clip], ke_ref.at[clip], loads.at[3 * clip]),
            local((qa_hbm0, qa_hbm1)[clip].at[0], qa_ref.at[clip], loads.at[3 * clip + 1]),
            local((at_hbm0, at_hbm1)[clip].at[0], at_ref.at[clip], loads.at[3 * clip + 2]),
        ]
        for clip in range(clips)
    ]
    place.greet()
    total = g1_ref.shape[0]

    def view(number, ref):
        if number < 4:
            base, col = (number // 2) * total, (number % 2) * LW
            return lambda first, n: ref.at[pl.ds(base + first, n), col : col + LW]
        col = (number - 4) * LW
        return lambda first, n: g1_ref.at[pl.ds(first, n), col : col + LW]

    pieces = [
        Piece(
            place, total, view(number, g2_ref), view(number, out2) if number < 4 else None,
            [ref.at[number] for ref in (recv_a, send_b, recv_b, send_c, recv_c)],
            sems_send.at[number], sems_recv.at[number],
        )
        for number in range(8)
    ]
    moves = [
        [pieces[0].a],
        [pieces[0].b, pieces[1].a],
        [pieces[2].a],
        [pieces[1].b, pieces[3].a],
        [pieces[4].a],
        [pieces[0].c, pieces[2].b, pieces[5].a],
        [pieces[6].a],
        [pieces[1].c, pieces[3].b, pieces[7].a],
        [],
        [pieces[0].d, pieces[4].b],
        [],
        [pieces[1].d, pieces[5].b],
        [],
        [pieces[0].e, pieces[2].c],
        [],
        [pieces[1].e, pieces[3].c],
        [],
        [pieces[0].f, pieces[2].d, pieces[6].b],
        [pieces[1].f, pieces[3].d, pieces[7].b, pieces[2].e, pieces[4].c, pieces[5].c, pieces[3].e, pieces[2].f, pieces[6].c, pieces[3].f, pieces[7].c],
    ]

    def pump():
        if moves:
            for move in moves.pop(0):
                move()

    dr_ref[...] = jnp.zeros_like(dr_ref)
    for clip in range(clips):
        pump()
        near, far = mem_ref.at[clip + 1], mem_ref.at[clip]
        keys[0:ROWS] = kv_ref[clip, 0]
        keys[ROWS : ROWS + MROWS] = near[0]
        keys[ROWS + MROWS :] = far[0]
        values[0:ROWS] = kv_ref[clip, 1]
        values[ROWS : ROWS + MROWS] = near[1]
        values[ROWS + MROWS :] = far[1]
        kt[0:LW] = keys[...].T
        kt[LW:] = ekey_ref[...]
        dmt[...] = dm_refs[clip][...].astype(F32).T
        dqt[...] = jnp.zeros_like(dqt)
        for made in lead[clip]:
            made.wait()
        deltas = []
        for head in range(LH):
            first = window_of(head)
            win = slice(first, first + WIN)
            span = slice(head * HEAD_DIM, (head + 1) * HEAD_DIM)
            qms[head] = q_ref[clip, 0, :, win] * lanes_ref[head]
            dms[head] = dm_refs[clip][:, win] * lanes_ref[head]
            deltas.append(jnp.sum(dmt[span] * at_ref[clip, span], axis=0, keepdims=True))

        def step(number, _):
            rows = slice(number * BLOCK, number * BLOCK + BLOCK)
            dk_parts, dv_parts = [], []
            for head in range(LH):
                first = window_of(head)
                variant = head // 2
                win = slice(first, first + WIN)
                ka = keys[rows, win] * lanes_ref[head, 0:BLOCK] + ke_ref[clip, variant, rows]
                s = nt(ka, qa_ref[clip, head])
                p = jnp.exp2(s * (SCALE * LOG2E) - lse_refs[clip][0, head : head + 1])
                dp = nt(values[rows, win], dms[head])
                ds = (p * (dp - deltas[head])).astype(BF16)
                dv_parts.append(nn(p.astype(BF16), dms[head]))
                dk_parts.append(nn(ds, qms[head]) * SCALE)
                kts = jnp.concatenate(
                    [kt[head * HEAD_DIM : (head + 1) * HEAD_DIM, rows], kt[LW:, rows]], axis=0
                )
                dqt[head] += nn(kts, ds)
            for which, parts in ((0, dk_parts), (1, dv_parts)):
                dkv_ref[clip, which, rows] = jnp.concatenate(
                    [
                        parts[0][:, 0:128] + parts[1][:, 0:128],
                        parts[1][:, 128:256] + parts[2][:, 0:128],
                        parts[2][:, 128:256] + parts[3][:, 128:256],
                    ],
                    axis=1,
                )
            return 0

        for number in range(NBLOCK):
            pump()
            step(number, 0)
        pump()
        for head in range(LH):
            first = window_of(head)
            span = slice(head * HEAD_DIM, (head + 1) * HEAD_DIM)
            total_t = dqt[head]
            grown = nn(grow_ref[...], total_t[HEAD_DIM:].astype(BF16)) * ownt_ref[...]
            grown = grown.astype(BF16)
            dmt[span] = dmt[span] + total_t[0:HEAD_DIM] * SCALE + nn(rt_ref[...], grown)
            dr_ref[:, first : first + WIN] += nn(grown, qms[head])
        dq_ref[clip] = dmt[...].T
    while moves:
        pump()
    for number in range(4):
        pieces[number].g()
        chunks_ref[number] = pieces[4 + number].total().astype(BF16)


def padded_rows(width, groups):
    return -(-width // (4 * groups) // 16) * 16 * 4 * groups


def call_attention_backward(q, kv, memory, keys_extra, qa, dmix, at, lse, rt, g2, g1, consts):
    clips, width = q.shape[0], g2.shape[1]
    groups = lax.axis_size("dp") // 4
    total = padded_rows(width, groups)
    if total != width:
        g1 = jnp.pad(g1, ((0, total - width), (0, 0)))
        g2 = jnp.pad(g2.reshape(2, width, width), ((0, 0), (0, total - width), (0, 0))).reshape(-1, width)
    vmem = pl.BlockSpec(memory_space=pltpu.VMEM)
    hbm = pl.BlockSpec(memory_space=pl.ANY)
    return pl.pallas_call(
        partial(attention_backward, groups),
        in_specs=[vmem] * 3 + [hbm] * 3 + [vmem] * 2 + [hbm] * 2 + [vmem] * 9,
        out_specs=[vmem] * 5,
        out_shape=[
            jax.ShapeDtypeStruct((clips, ROWS, LW), F32),
            jax.ShapeDtypeStruct((clips, 2, KEYS, LW), F32),
            jax.ShapeDtypeStruct((256, LW), F32),
            jax.ShapeDtypeStruct((4, total // 4 // groups, LW), BF16),
            jax.ShapeDtypeStruct(g2.shape, BF16),
        ],
        scratch_shapes=[
            pltpu.VMEM(keys_extra.shape, BF16),
            pltpu.VMEM((clips, LH, ROWS, WIN), BF16),
            pltpu.VMEM((clips, LW, ROWS), F32),
            pltpu.VMEM((KEYS, LW), BF16),
            pltpu.VMEM((KEYS, LW), BF16),
            pltpu.VMEM((LW + 32, KEYS), BF16),
            pltpu.VMEM((LW, ROWS), F32),
            pltpu.VMEM((LH, ROWS, WIN), BF16),
            pltpu.VMEM((LH, ROWS, WIN), BF16),
            pltpu.VMEM((LH, HEAD_DIM + 32, ROWS), F32),
            *piece_scratch(total, groups, LW, BF16, 8),
            pltpu.SemaphoreType.DMA((3 * clips,)),
            pltpu.SemaphoreType.DMA((8, 2 * groups + 2)),
            pltpu.SemaphoreType.DMA((8, 2 * groups + 2)),
        ],
        compiler_params=params(collective_id=0, has_side_effects=True),
        cost_estimate=pl.CostEstimate(
            flops=40_000_000_000, bytes_accessed=20_000_000, transcendentals=3_000_000
        ),
    )(
        q, kv, memory, keys_extra, *qa, *dmix, *at, *lse, rt,
        consts["grow"], consts["ownt"], consts["ekey"], consts["lanes"], g2, g1,
    )


REL_ROWS = 48
TAP_ROW = NREL
NORM_ROW = TAP_ROW + 5 * 27
EARLY_ROW = NORM_ROW + 12
HIDDEN_ROW = EARLY_ROW + 24
SMALL_ROWS = HIDDEN_ROW + 24


def finish_kernel(
    groups, width,
    dq_hbm, dkv_hbm, x0q_hbm, x0kv_hbm, kvf_hbm, rows_taps, rows_a_hbm, rows_x0, rows_x1, branch0, branch1,
    w_hbm, tokens_hbm, middle0, middle1, chunks_ref, dr_ref, gain, foldl_ref, pick_ref,
    sums0, sums1, hidden0, hidden1, hidden2,
    grad, out1, outp, outq, small_out,
    dq, dkv, x0q, x0kv, kvf, taps_ref, rows_a, rows_x, branch, w_ref, tokens, middle,
    us, ms, kacc, dx, dmem_send, dmem_recv, resp, grads, stage_t,
    recv_a, send_b, recv_b, send_c, recv_c,
    strips, strip_res, strip_a, strip_b, strip_bb, strip_c, strip_cc,
    sm, sm_res, sm_core, sm_sum, sm_slots, send_y, recv_y,
    loads, stores, sems_send, sems_recv, tiny_send, tiny_recv, cross_send, cross_recv, mem_sems,
):
    place = Place(groups)
    clips = dq.shape[0]
    total = rows_a.shape[1]
    names = (
        "dkv", "dq", "x0q", "rows_x0", "rows_x1", "branch0", "branch1", "x0kv", "kvf", "rows_a", "w",
        "tokens", "middle0", "middle1",
    )
    pairs = (
        (dkv_hbm, dkv), (dq_hbm, dq), (x0q_hbm, x0q),
        (rows_x0, rows_x.at[0:ROWS]), (rows_x1, rows_x.at[ROWS:]), (branch0, branch.at[0:ROWS]),
        (branch1, branch.at[ROWS:]), (x0kv_hbm, x0kv), (kvf_hbm, kvf), (rows_a_hbm, rows_a), (w_hbm, w_ref),
        (tokens_hbm, tokens), (middle0, middle.at[0]), (middle1, middle.at[1]),
    )
    lead = {
        name: local(src, dst, loads.at[n]) for n, (name, (src, dst)) in enumerate(zip(names, pairs))
    }
    count = groups * 4
    behind = (lax.rem(place.dp + count - 1, count), place.head)
    ahead = (lax.rem(place.dp + 1, count), place.head)
    others = [place.device(lax.rem(place.number + o, count)) for o in range(1, count)]
    barrier = pltpu.get_barrier_semaphore()
    for peer in [place.to_core, behind, ahead] + others:
        pl.semaphore_signal(barrier, inc=1, device_id=peer, device_id_type=MESH)
    pl.semaphore_wait(barrier, 3 + len(others))

    def strip_of(number):
        return lambda first, n: out1.at[pl.ds(first, n), number * LW : number * LW + LW]

    ffn = [
        Piece(place, total, None, strip_of(number), None, sems_send.at[number], sems_recv.at[number])
        for number in range(4)
    ]

    def rows_of(ref):
        return lambda first, n: ref.at[pl.ds(first, n)]

    late = [
        Piece(
            place, total, rows_of(grads.at[number]), rows_of(resp.at[number]),
            [ref.at[number] for ref in (recv_a, send_b, recv_b, send_c, recv_c)],
            sems_send.at[4 + number], sems_recv.at[4 + number],
        )
        for number in range(2)
    ] + [
        Piece(
            place, total, rows_of(strips.at[number]), rows_of(strip_res.at[number]),
            [ref.at[number] for ref in (strip_a, strip_b, strip_bb, strip_c, strip_cc)],
            sems_send.at[6 + number], sems_recv.at[6 + number],
        )
        for number in range(6)
    ]
    tiny = Tiny(place, sm, sm_res, (sm_core, sm_sum, sm_slots), tiny_send, tiny_recv)

    def product(number):
        if number < 2:
            left, right, target = (rows_x, branch, grads.at[0]) if number == 0 else (rows_a, dx.at[0], grads.at[1])
            lanes = slice(0, LW)
        else:
            left, right, target = rows_a, dx.at[1 + (number - 2) // 3], strips.at[number - 2]
            lanes = slice((number - 2) % 3 * 128, (number - 2) % 3 * 128 + 128)
        for first in range(0, total, total // 2):
            target[first : first + total // 2] = tn(
                left[:, first : first + total // 2], right[:, lanes]
            ).astype(BF16)
        late[number].a()

    def shifted_store(dst, first, both, lanes):
        both = both.reshape(2 * HGT, PADW, 128)
        for c, shift in ((0, 1), (1, 0), (2, PADW - 1)):
            moved = pltpu.roll(both, shift, axis=1) if shift else both
            dst[c, pl.ds(first, 2), 1 : HGT + 1, :, lanes] = moved.reshape(2, HGT, PADW, 128)

    def prepare(which, clip):
        if which:
            memory = dmem_recv[clip, which - 1].astype(F32)
            memory = jnp.where(place.dp == count - 1, 0.0, memory)
            for later in range(clip + 1, clips):
                if later == clip + 1:
                    memory = memory + dkv[later, which - 1, ROWS : ROWS + MROWS]
                if later == clip + 2:
                    memory = memory + dkv[later, which - 1, ROWS + MROWS :]
            spread(ms, 0, memory.reshape(TM, HGT, PADW, LW))
        else:
            spread(us, 1, dq[clip].reshape(T_LEN, HGT, PADW, LW))

    def pooled(which, clip, tile):
        field = x0q.at[clip, 0] if which == 0 else x0kv.at[clip, which - 1]
        upstream = dq.at[clip] if which == 0 else dkv.at[clip, which - 1]
        if tile == 0:
            prepare(which, clip)
        lanes = slice(tile * 128, tile * 128 + 128)
        if which:

            def squeeze_step(pair, _):
                rows = pl.ds(pl.multiple_of(pair * 112, 112), 112)
                own = upstream[rows, lanes].reshape(2, HGT, PADW, 128)
                fields = kvf[clip, which - 1, rows, lanes].astype(F32).reshape(2, HGT, PADW, 128)
                acc = [own[0], own[1]]
                for a, d, frame in ((1, 0, 0), (0, 1, 1), (2, 1, 0)):
                    for c in range(3):
                        block = ms[2 - c, pair + frame, :, :, lanes]
                        for b in range(3):
                            at = block[2 - b : 2 - b + HGT]
                            number = a * 9 + b * 3 + c
                            acc[d] = acc[d] + taps_ref[2 + which, number, :, lanes][None] * at
                            kacc[2 + which, number, :, lanes] += jnp.sum(fields[d] * at, axis=0)
                shifted_store(us, 2 * pair + 1, keep_rows(jnp.stack(acc)), lanes)
                return 0

            lax.fori_loop(0, TM, squeeze_step, 0)

        def pair_step(pair, _):
            rows = pl.ds(pl.multiple_of(pair * 112, 112), 112)
            fields = field[rows, lanes].astype(F32).reshape(2, HGT, PADW, 128)
            acc = [jnp.zeros((HGT, PADW, 128), F32) for _ in range(2)]
            for a in range(3):
                for c in range(3):
                    sums = [jnp.zeros((PADW, 128), F32) for _ in range(3)]
                    for d in range(2):
                        block = us[2 - c, 2 * pair + d + 2 - a, :, :, lanes]
                        for b in range(3):
                            at = block[2 - b : 2 - b + HGT]
                            acc[d] = acc[d] + taps_ref[which, a * 9 + b * 3 + c, :, lanes][None] * at
                            sums[b] = sums[b] + jnp.sum(fields[d] * at, axis=0)
                    for b in range(3):
                        kacc[which, a * 9 + b * 3 + c, :, lanes] += sums[b]
            both = keep_rows(jnp.stack(acc))
            out_rows = pl.ds(pl.multiple_of(clip * ROWS + pair * 112, 16), 112)
            dx[which, out_rows, lanes] = both.reshape(112, 128).astype(BF16)
            return 0

        lax.fori_loop(0, T_LEN // 2, pair_step, 0)

    side_rows = ROWS // 2

    def input_gradient(clip, side):
        rows = pl.ds(pl.multiple_of(clip * ROWS + side * side_rows, 16), side_rows)
        return nt(dx[0, rows], w_ref[0]) + nt(dx[1, rows], w_ref[1]) + nt(dx[2, rows], w_ref[2])

    crossing = {}

    def cross(clip):
        send_y[clip] = input_gradient(clip, 1 - place.head).astype(BF16)
        crossing[clip] = remote(
            send_y.at[clip], recv_y.at[clip], cross_send.at[clip], cross_recv.at[clip], place.to_y
        )

    def normed_gradient(clip):
        mine = input_gradient(clip, place.head)
        crossing[clip].wait()
        u = mine + recv_y[clip].astype(F32)
        v = tokens[clip].astype(F32)
        centred = v - jnp.mean(v, axis=-1, keepdims=True)
        scale = lax.rsqrt(jnp.mean(centred * centred, axis=-1, keepdims=True) + EPSILON)
        xhat = centred * scale
        w = u * gain[0:1]
        dv = scale * (
            w - jnp.mean(w, axis=-1, keepdims=True) - xhat * jnp.mean(w * xhat, axis=-1, keepdims=True)
        )
        grad[clip] = middle[clip] + dv
        for which, value in enumerate((u * xhat, u)):
            value = jnp.sum(value, axis=0, keepdims=True)
            for n in range(width // 128):
                row = NORM_ROW + which * (width // 128) + n
                sm[row : row + 1] += value[:, n * 128 : n * 128 + 128]

    def exact(a, b):
        return jnp.dot(a, b, precision=HIGHEST, preferred_element_type=F32)

    def small_first():
        sm[...] = jnp.zeros_like(sm)
        folded = exact(dr_ref[...], foldl_ref[...])
        sm[0:NREL] = exact(pick_ref[...], folded)[0:NREL]
        early = sums0[...] + sums1[...]
        hidden = hidden0[...] + hidden1[...] + hidden2[...]
        strip = width // 128
        for which in range(4):
            for n in range(strip):
                row = EARLY_ROW + which * strip + n
                sm[row : row + 1] = early[which : which + 1, n * 128 : n * 128 + 128]
        count_h = hidden.shape[1] // 128
        for side in range(2):
            for n in range(count_h):
                row = HIDDEN_ROW + side * count_h + n
                part = hidden[:, n * 128 : n * 128 + 128]
                sm[row : row + 1] = jnp.where(place.head == side, part, 0.0)

    def small_taps(which):
        first = TAP_ROW + 27 * which
        sums = jnp.sum(kacc[which], axis=1)
        sums = jnp.concatenate([sums, jnp.zeros((5, LW), F32)], axis=0)
        sm[first : first + 27] = exact(sums, foldl_ref[...])[0:27]

    ffn[0].d(chunks_ref[0])
    us[...] = jnp.zeros_like(us)
    ms[...] = jnp.zeros_like(ms)
    kacc[...] = jnp.zeros_like(kacc)
    for which in range(5):
        taps_ref[which] = widened(rows_taps[which])
    small_first()
    lead["dkv"].wait()
    for which in range(2):
        dmem_send[0, which] = dkv[0, which, ROWS + MROWS :].astype(BF16)
        dmem_send[1, which] = (
            dkv[0, which, ROWS : ROWS + MROWS] + dkv[1, which, ROWS + MROWS :]
        ).astype(BF16)
    memory_flight = remote(dmem_send, dmem_recv, mem_sems.at[0], mem_sems.at[1], behind)
    for name in ("rows_x0", "rows_x1", "branch0", "branch1"):
        lead[name].wait()
    product(0)
    for name in ("dq", "x0q"):
        lead[name].wait()
    pooled(0, 0, 0)
    pooled(0, 0, 1)
    late[0].b()
    pooled(0, 0, 2)
    ffn[1].d(chunks_ref[1])
    pooled(0, 1, 0)
    pooled(0, 1, 1)
    ffn[0].e()
    pooled(0, 1, 2)
    ffn[2].d(chunks_ref[2])
    lead["rows_a"].wait()
    product(1)
    small_taps(0)
    memory_flight.wait()
    lead["x0kv"].wait()
    lead["kvf"].wait()
    pooled(1, 0, 0)
    late[1].b()
    late[0].c()
    pooled(1, 0, 1)
    ffn[0].f()
    pooled(1, 0, 2)
    ffn[1].e()
    ffn[3].d(chunks_ref[3])
    pooled(2, 0, 0)
    ffn[0].g()
    pooled(2, 0, 1)
    late[0].d()
    ffn[2].e()
    pooled(2, 0, 2)
    lead["w"].wait()
    cross(0)
    ffn[1].f()
    pooled(1, 1, 0)
    late[1].c()
    ffn[1].g()
    ffn[3].e()
    product(2)
    pooled(1, 1, 1)
    ffn[2].f()
    product(3)
    pooled(1, 1, 2)
    late[2].b()
    ffn[2].g()
    product(4)
    late[3].b()
    late[1].d()
    small_taps(1)
    small_taps(3)
    late[0].e()
    ffn[3].f()
    pooled(2, 1, 0)
    ffn[3].g()
    product(5)
    late[2].c()
    pooled(2, 1, 1)
    late[3].c()
    late[4].b()
    product(6)
    late[5].b()
    pooled(2, 1, 2)
    late[2].d()
    late[6].b()
    late[0].f()
    product(7)
    late[3].d()
    late[1].e()
    cross(1)
    late[4].c()
    late[0].g()
    stage_t[...] = resp[0].astype(F32).T
    sent = [local(stage_t, outp, stores.at[2])]
    small_taps(2)
    small_taps(4)
    for name in ("tokens", "middle0", "middle1"):
        lead[name].wait()
    normed_gradient(0)
    late[2].e()
    late[5].c()
    late[3].e()
    late[6].c()
    late[4].d()
    late[7].b()
    late[1].f()
    late[5].d()
    late[2].f()
    late[1].g()
    sent.append(local(resp.at[1], outq.at[0], stores.at[3]))
    late[6].d()
    late[2].g()
    sent.append(local(strip_res.at[0], outq.at[1, :, 0 : 128], stores.at[4]))
    late[3].f()
    late[4].e()
    late[7].c()
    late[3].g()
    sent.append(local(strip_res.at[1], outq.at[1, :, 128 : 256], stores.at[5]))
    late[5].e()
    normed_gradient(1)
    tiny.a()
    late[4].f()
    late[6].e()
    late[7].d()
    late[4].g()
    sent.append(local(strip_res.at[2], outq.at[1, :, 256 : 384], stores.at[6]))
    late[5].f()
    tiny.b()
    late[5].g()
    sent.append(local(strip_res.at[3], outq.at[2, :, 0 : 128], stores.at[7]))
    late[6].f()
    late[7].e()
    late[6].g()
    sent.append(local(strip_res.at[4], outq.at[2, :, 128 : 256], stores.at[8]))
    tiny.c()
    late[7].f()
    late[7].g()
    sent.append(local(strip_res.at[5], outq.at[2, :, 256 : 384], stores.at[9]))
    tiny.d()
    tiny.e()
    small_out[...] = sm_res[...]
    for made in sent:
        made.wait()

def call_finish(
    dq, dkv, x0q, x0kv, kvf, all_taps, rows_a, rows_x, branch, weights, tokens, middle, chunks, dr, gain, sums, hidden
):
    groups = lax.axis_size("dp") // 4
    width = tokens.shape[2]
    total = padded_rows(width, groups)
    clips, side = tokens.shape[:2]
    if total != width:
        extra = ((0, 0), (0, total - width))
        rows_a, rows_x = jnp.pad(rows_a, extra), [jnp.pad(x, extra) for x in rows_x]
    small_rows = -(-SMALL_ROWS // (64 * groups)) * 64 * groups
    foldl = np.zeros((LW, 128), np.float32)
    foldl[np.arange(LW), np.arange(LW) % HEAD_DIM] = 1
    pick = np.zeros((REL_ROWS, 256), np.float32)
    pick[:NREL] = PICK.T
    vmem = pl.BlockSpec(memory_space=pltpu.VMEM)
    hbm = pl.BlockSpec(memory_space=pl.ANY)
    streamed = [dq, dkv, x0q, x0kv, kvf, all_taps, rows_a, *rows_x, *branch, weights, tokens, *middle]
    held = [
        (array.shape, array.dtype)
        for array in (dq, dkv, x0q, x0kv, kvf)
    ] + [
        ((5, 27, 8, LW), F32), (rows_a.shape, BF16),
        ((clips * ROWS, total), BF16), ((clips * ROWS, LW), BF16), (weights.shape, BF16), (tokens.shape, BF16),
        (tokens.shape, F32),
    ]
    frame = pltpu.VMEM((3, T_LEN + 2, HGT + 2, PADW, LW), F32)
    return pl.pallas_call(
        partial(finish_kernel, groups, width),
        in_specs=[hbm] * 5 + [vmem] + [hbm] * (len(streamed) - 6) + [vmem] * 10,
        out_specs=[vmem, vmem, hbm, hbm, vmem],
        out_shape=[
            jax.ShapeDtypeStruct(tokens.shape, F32),
            jax.ShapeDtypeStruct((total, 4 * LW), BF16),
            jax.ShapeDtypeStruct((LW, total), F32),
            jax.ShapeDtypeStruct((3, total, LW), BF16),
            jax.ShapeDtypeStruct((small_rows, 128), F32),
        ],
        scratch_shapes=[pltpu.VMEM(shape, dtype) for shape, dtype in held]
        + [
            frame,
            pltpu.VMEM((3, TM + 1, HGT + 2, PADW, LW), F32),
            pltpu.VMEM((5, 27, 8, LW), F32),
            pltpu.VMEM((3, clips * ROWS, LW), BF16),
            pltpu.VMEM((2, 2, MROWS, LW), BF16),
            pltpu.VMEM((2, 2, MROWS, LW), BF16),
            pltpu.VMEM((2, total, LW), BF16),
            pltpu.VMEM((2, total, LW), BF16),
            pltpu.VMEM((LW, total), F32),
            *piece_scratch(total, groups, LW, BF16, 2),
            pltpu.VMEM((6, total, 128), BF16),
            pltpu.VMEM((6, total, 128), BF16),
            *piece_scratch(total, groups, 128, BF16, 6),
            pltpu.VMEM((small_rows, 128), F32),
            pltpu.VMEM((small_rows, 128), F32),
            pltpu.VMEM((small_rows // 2, 128), F32),
            pltpu.VMEM((small_rows // 2, 128), F32),
            pltpu.VMEM((4 * groups - 1, small_rows // 8 // groups, 128), F32),
            pltpu.VMEM((clips, side, width), BF16),
            pltpu.VMEM((clips, side, width), BF16),
            pltpu.SemaphoreType.DMA((15,)),
            pltpu.SemaphoreType.DMA((10,)),
            pltpu.SemaphoreType.DMA((12, 2 * groups + 2)),
            pltpu.SemaphoreType.DMA((12, 2 * groups + 2)),
            pltpu.SemaphoreType.DMA((8 * groups,)),
            pltpu.SemaphoreType.DMA((8 * groups,)),
            pltpu.SemaphoreType.DMA((clips,)),
            pltpu.SemaphoreType.DMA((clips,)),
            pltpu.SemaphoreType.DMA((2,)),
        ],
        compiler_params=params(collective_id=1, has_side_effects=True),
        cost_estimate=pl.CostEstimate(
            flops=60_000_000_000, bytes_accessed=40_000_000, transcendentals=0
        ),
    )(*streamed, chunks, dr, gain, jnp.asarray(foldl), jnp.asarray(pick), *sums, *hidden)


def from_behind(x, axis, by):
    count = lax.axis_size(axis)
    pairs = [(i, i + by) for i in range(count) if 0 <= i + by < count]
    return lax.ppermute(x, axis, pairs)


def layer_norm(values, scaling, offset):
    average = jnp.mean(values, axis=-1, keepdims=True)
    centred = values - average
    variance = jnp.mean(centred * centred, axis=-1, keepdims=True)
    return centred * lax.rsqrt(variance + EPSILON) * scaling + offset


def pad_rows(x):
    lead = x.shape[0]
    frames = x.shape[1] // (HGT * WID)
    grid = x.reshape(lead, frames, HGT, WID, x.shape[-1])
    grid = jnp.pad(grid, ((0, 0), (0, 0), (0, 0), (0, PADW - WID), (0, 0)))
    return grid.reshape(lead, frames * HGT * PADW, x.shape[-1])


def drop_rows(x):
    lead = x.shape[0]
    frames = x.shape[1] // (HGT * PADW)
    grid = x.reshape(lead, frames, HGT, PADW, x.shape[-1])[:, :, :, :WID]
    return grid.reshape(lead, frames * HGT * WID, x.shape[-1])


def swap(x):
    return lax.ppermute(x, "head", [(0, 1), (1, 0)])


def gather_rows(x):
    half = x.shape[1]
    mine = lax.axis_index("head") * half
    both = jnp.concatenate([x, x], axis=1)
    return lax.dynamic_update_slice_in_dim(both, swap(x), half - mine, axis=1)


def taps(*kernels):
    return jnp.tile(jnp.stack(kernels), (1, 1, LH))


def on_device(
    tokens,
    ln1_gain,
    ln1_bias,
    w_qkv,
    pool_q,
    pool_k,
    pool_v,
    squeeze_k,
    squeeze_v,
    rel_t,
    rel_h,
    rel_w,
    w_proj,
    proj_bias,
    ln2_gain,
    ln2_bias,
    w_fc1,
    fc1_bias,
    w_fc2,
    fc2_bias,
    memory_valid,
    cotangent,
):
    clip_count = tokens.shape[0]
    consts = {
        "fold": jnp.asarray(fold_constants(), BF16),
        "one": jnp.asarray(one_lane(), F32),
        "own": jnp.asarray(OWN_T.T, F32),
        "ownt": jnp.asarray(OWN_T, F32),
        "lanes": jnp.asarray(head_lanes(), BF16),
        "grow": jnp.asarray(FOLD, BF16),
        "ekey": jnp.asarray(EKEY, BF16),
    }
    keys_extra = key_constants(memory_valid)
    rel_all = jnp.concatenate([rel_t, rel_h, rel_w], axis=0)
    pairs = jnp.dot(jnp.asarray(PICK), rel_all, precision=HIGHEST)
    pair_table = (pairs * HEAD_DIM**0.5).T
    table_high = pair_table.astype(BF16)
    table_rest = (pair_table - table_high.astype(F32)).astype(BF16)
    tables = jnp.stack([table_high, table_rest])
    rel_rows = pairs.T.astype(BF16)
    all_taps = taps(pool_q, pool_k, pool_v, squeeze_k, squeeze_v)

    width = tokens.shape[2]
    inputs_low = pad_rows(tokens)
    inputs = inputs_low.astype(F32)
    upstream = pad_rows(cotangent)
    real = (jnp.arange(inputs.shape[1]) % PADW < WID)[None, :, None]
    first_normed = layer_norm(inputs, ln1_gain, ln1_bias)
    first_rows = gather_rows(jnp.where(real, first_normed, 0.0).astype(BF16))
    w_heads = w_qkv.transpose(1, 0, 2)
    upstream_other = swap(lax.optimization_barrier((upstream, first_rows))[0])
    kv0, kv, kvf, mem = call_pool_forward(first_rows, w_heads, 1, 2, all_taps, True)
    before = from_behind(mem[-2:], "dp", 1)
    q0, q = call_pool_forward(first_rows, w_heads, 0, 1, all_taps, False)
    memory = jnp.concatenate([before, mem], axis=0)
    vectors = jnp.stack([proj_bias, ln2_gain, ln2_bias])
    hidden_bias = fc1_bias.reshape(1, -1)
    rows32 = jax.ShapeDtypeStruct((HALF, width), F32)
    rows16 = jax.ShapeDtypeStruct((HALF, width), BF16)
    clips = range(clip_count)
    branch, qa, at, lse, kept, recv = [], [], [], [], [], []
    for clip in clips:
        *made, own, sent = call_attention_forward(clip, q, kv, memory, keys_extra, tables, w_proj, consts)
        for store, value in zip((branch, qa, at, lse), made):
            store.append(value)
        sent, q = lax.optimization_barrier((sent, q)) if clip + 1 < clip_count else (sent, q)
        kept.append(own)
        recv.append(swap(sent))

    def after(value, *earlier):
        return lax.optimization_barrier((value, *earlier))[0]

    middle, mine, theirs = [], [], []
    own_parts, other_parts, second = [None] * clip_count, [None] * clip_count, [None] * clip_count

    hidden_sums = []

    def through(*rows):
        made, total = call_ffn(
            [
                (mine[clip], upstream[clip], F32) if own else (theirs[clip], upstream_other[clip], BF16)
                for clip, own in rows
            ],
            w_fc1, hidden_bias, w_fc2,
        )
        hidden_sums.append(total)
        for (clip, own), part in zip(rows, made):
            if own:
                own_parts[clip] = part
            else:
                other_parts[clip] = part
                second[clip] = swap(part[2])

    for clip in clips:
        landed = after(recv[clip], own_parts[clip - 1][2]) if clip else recv[clip]
        x1, a2 = simple_call(middle_kernel, [rows32, rows16], 1, inputs_low[clip], kept[clip], landed, vectors)
        middle.append(x1)
        mine.append(a2)
        theirs.append(swap(a2))
        if clip == 0:
            through((0, True))
        else:
            through((clip, True), (clip - 1, False))
    theirs[-1] = after(theirs[-1], own_parts[-1][2])
    through((clip_count - 1, False))
    dmiddle, low, sums, rows_x, dmix = [], [], [], [], []
    parts = own_parts + other_parts
    for clip in clips:
        if clip + 1 == clip_count:
            w_fc2_grad, w_fc1_grad = call_weights(
                [p[0] for p in parts],
                [p[1] for p in parts],
                mine + theirs,
                [after(upstream[0], low[0][0])]
                + [upstream[c] for c in clips[1:]]
                + [upstream_other[c] for c in clips],
            )
        landed = after(second[clip], w_fc2_grad if clip + 1 == clip_count else other_parts[-1][2])
        dx, dx_low, total = simple_call(
            norm_back_kernel,
            [rows32, rows16, jax.ShapeDtypeStruct((HEAD_EARLY, width), F32)],
            1,
            own_parts[clip][2], landed, middle[clip], upstream[clip], vectors,
        )
        dmiddle.append(dx)
        sums.append(total)
        low.append((dx_low, swap(dx_low)))
    for clip in clips:
        received = after(low[clip][1], low[-1][0])
        rows, mix = simple_call(
            mix_kernel,
            [jax.ShapeDtypeStruct((ROWS, width), BF16), jax.ShapeDtypeStruct((ROWS, LW), BF16)],
            1,
            low[clip][0], received, w_proj,
        )
        rows_x.append(rows)
        dmix.append(mix)
    last = [lax.optimization_barrier((other_parts[c][3], dmix[-1]))[0] for c in clips]
    last = [swap(x) for x in last]
    dq, dkv, dr, chunks, w_fc2_grad = call_attention_backward(
        q, kv, memory, keys_extra, qa, dmix, at, lse, rel_rows,
        w_fc2_grad, w_fc1_grad, consts,
    )
    *last, dq = lax.optimization_barrier((*last, dq))
    output = drop_rows(
        jnp.stack(
            [
                (middle[c] + own_parts[c][3] + last[c].astype(F32) + fc2_bias).astype(BF16)
                for c in clips
            ]
        )
    )
    w_fc2_grad = w_fc2_grad.astype(F32)
    input_grad, w_fc1_grad, w_proj_grad, tail, small = call_finish(
        dq, dkv, q0, kv0, kvf, all_taps,
        first_rows.reshape(-1, width),
        rows_x,
        [b[0] for b in branch],
        w_heads,
        inputs_low,
        dmiddle,
        chunks,
        dr,
        ln1_gain.reshape(1, -1),
        sums,
        hidden_sums,
    )
    input_grad = drop_rows(input_grad)
    w_fc1_grad = w_fc1_grad.astype(F32)
    total = w_fc1_grad.shape[0]
    if total != width:
        w_fc2_grad = w_fc2_grad.reshape(2, total, width)[:, :width].reshape(2 * width, width)
        w_fc1_grad, w_proj_grad, tail = w_fc1_grad[:width], w_proj_grad[:, :width], tail[:, :width]
    w_qkv_grad = tail.astype(F32).transpose(1, 0, 2)
    norms = small[NORM_ROW:EARLY_ROW].reshape(2, width)
    early = small[EARLY_ROW:HIDDEN_ROW].reshape(4, width)
    fc1_bias_grad = lax.dynamic_index_in_dim(
        small[HIDDEN_ROW:SMALL_ROWS].reshape(2, fc1_bias.size), lax.axis_index("head"), 0, keepdims=False
    )
    small = small[:, :HEAD_DIM]
    shared = [norms[0], norms[1]]
    shared += [small[TAP_ROW + 27 * n : TAP_ROW + 27 * n + 27] for n in range(5)]
    shared += [
        small[: 2 * T_LEN - 1],
        small[2 * T_LEN - 1 : 2 * T_LEN + 2 * HGT - 2],
        small[2 * T_LEN + 2 * HGT - 2 : NREL],
    ]
    shared += [early[0], early[1], early[2], early[3]]
    return (
        output,
        input_grad,
        shared[0],
        shared[1],
        w_qkv_grad,
        shared[2],
        shared[3],
        shared[4],
        shared[5],
        shared[6],
        shared[7],
        shared[8],
        shared[9],
        w_proj_grad,
        shared[10],
        shared[11],
        shared[12],
        w_fc1_grad,
        fc1_bias_grad,
        w_fc2_grad,
        shared[13],
    )


def solution(mesh):
    return jax.shard_map(
        on_device,
        mesh=mesh,
        in_specs=(
            P("dp", "head", None),
            P(),
            P(),
            P(None, None, "head"),
            P(),
            P(),
            P(),
            P(),
            P(),
            P(),
            P(),
            P(),
            P("head", None),
            P(),
            P(),
            P(),
            P(None, "head"),
            P("head"),
            P("head", None),
            P(),
            P("dp", None),
            P("dp", "head", None),
        ),
        out_specs=(
            P("dp", "head", None),
            P("dp", "head", None),
            P(),
            P(),
            P(None, None, "head"),
            P(),
            P(),
            P(),
            P(),
            P(),
            P(),
            P(),
            P(),
            P("head", None),
            P(),
            P(),
            P(),
            P(None, "head"),
            P("head"),
            P("head", None),
            P(),
        ),
        check_vma=False,
    )
```

```python
from functools import partial

import jax
import jax.numpy as jnp
import numpy as np
from jax import lax
from jax.experimental import pallas as pl
from jax.experimental.pallas import tpu as pltpu
from jax.sharding import PartitionSpec as P

HEAD_DIM = 96
T_LEN = 8
HGT = 7
WID = 7
PADW = 8
L = 392
ROWS = T_LEN * HGT * PADW
TM = 4
MROWS = TM * HGT * PADW
KEYS = ROWS + 2 * MROWS
LH = 4
LW = LH * HEAD_DIM
WIN = 256
BLOCK = 128
NBLOCK = KEYS // BLOCK

EPSILON = 1e-06
HIGHEST = lax.Precision.HIGHEST
SCALE = HEAD_DIM ** (-0.5)
LOG2E = 1.4426950408889634
F32 = jnp.float32
BF16 = jnp.bfloat16
VMEM_LIMIT = 58 * 1024 * 1024

NB = T_LEN + HGT + WID
NREL = 2 * T_LEN - 1 + 2 * HGT - 1 + 2 * WID - 1
NPAIR = T_LEN * T_LEN + HGT * HGT + WID * WID


def params(**extra):
    return pltpu.CompilerParams(vmem_limit_bytes=VMEM_LIMIT, **extra)


def window_of(head):
    return 0 if head < 2 else BLOCK


def slot_of(head):
    return 192 if head < 2 else 0


def position_constants():
    t, h, w = np.meshgrid(np.arange(T_LEN), np.arange(HGT), np.arange(PADW), indexing="ij")
    t, h, w = t.ravel(), h.ravel(), w.ravel()
    valid = w < WID
    own = np.zeros((256, ROWS), np.float32)
    pick = np.zeros((256, NREL), np.float32)
    fold = np.zeros((256, 32), np.float32)
    ekey = np.zeros((32, KEYS), np.float32)
    row = 0
    base_entry = 0
    base_bias = 0
    for places, length in ((t, T_LEN), (h, HGT), (w, WID)):
        for a in range(length):
            for b in range(length):
                own[row] = (places == a) & valid
                pick[row, base_entry + a - b + length - 1] = 1
                fold[row, base_bias + b] = 1
                row += 1
        for b in range(length):
            ekey[base_bias + b, :ROWS] = (places == b) & valid
        base_entry += 2 * length - 1
        base_bias += length
    return own, pick, fold, ekey, valid


OWN_T, PICK, FOLD, EKEY, ROW_VALID = position_constants()


def fold_constants():
    out = np.zeros((2, 2, 256, WIN), np.float32)
    for variant, slot in enumerate((192, 0)):
        out[variant, 0, :, slot : slot + 32] = FOLD
        out[variant, 1, :, slot + 32 : slot + 64] = FOLD
    return out


def one_lane():
    out = np.zeros((2, 8, WIN), np.float32)
    for variant, slot in enumerate((192, 0)):
        out[variant, :, slot + NB] = 1
    return out


def head_lanes():
    out = np.zeros((LH, ROWS, WIN), np.float32)
    for head in range(LH):
        first = head * HEAD_DIM - window_of(head)
        out[head, :, first : first + HEAD_DIM] = 1
    return out


def key_constants(memory_valid):
    clip_count = memory_valid.shape[0]
    base = np.zeros((2, KEYS, WIN), np.float32)
    lane = np.zeros((2, 1, WIN), np.float32)
    for variant, slot in enumerate((192, 0)):
        base[variant, :, slot : slot + 32] = EKEY.T
        base[variant, :, slot + 32 : slot + 64] = EKEY.T
        lane[variant, :, slot + NB] = 1
    pads = np.concatenate([ROW_VALID, ROW_VALID[:MROWS], ROW_VALID[:MROWS]])
    use = jnp.concatenate(
        [jnp.ones((clip_count, ROWS), bool), jnp.repeat(memory_valid > 0, MROWS, axis=1)], axis=1
    )
    drop = jnp.where(use & jnp.asarray(pads)[None], 0.0, -1e30).astype(F32)
    return (jnp.asarray(base)[None] + drop[:, None, :, None] * jnp.asarray(lane)[None]).astype(BF16)


def nt(a, b):
    return lax.dot_general(a, b, (((1,), (1,)), ((), ())), preferred_element_type=F32)


def nn(a, b):
    return jnp.dot(a, b, preferred_element_type=F32)


def keep_rows(block):
    place = lax.broadcasted_iota(jnp.int32, block.shape, block.ndim - 2)
    return jnp.where(place < WID, block, 0.0)


def spread(dst, first, value):
    n, _, _, c = value.shape
    flat = value.reshape(n * HGT, PADW, c)
    dst[0, pl.ds(first, n), 1 : HGT + 1] = pltpu.roll(flat, 1, axis=1).reshape(n, HGT, PADW, c)
    dst[1, pl.ds(first, n), 1 : HGT + 1] = value
    dst[2, pl.ds(first, n), 1 : HGT + 1] = pltpu.roll(flat, PADW - 1, axis=1).reshape(n, HGT, PADW, c)


def widened(rows):
    return jnp.broadcast_to(rows[:, None, :], (rows.shape[0], 8, rows.shape[1]))


def pool_forward(squeeze, carried, *refs):
    given = 4 if squeeze else 3
    refs = refs[:given] + refs[given + carried :]
    if squeeze:
        a_ref, w_ref, rows_k, rows_s, x0_ref, xp_ref, xf_ref, m_ref, xs, k_ref, ys, s_ref = refs
    else:
        a_ref, w_ref, rows_k, x0_ref, xp_ref, xs, k_ref = refs

    @pl.when((pl.program_id(0) == 0) & (pl.program_id(1) == 0))
    def _():
        xs[...] = jnp.zeros_like(xs)
        if squeeze:
            ys[...] = jnp.zeros_like(ys)

    @pl.when(pl.program_id(1) == 0)
    def _():
        k_ref[0] = widened(rows_k[0])
        if squeeze:
            s_ref[0] = widened(rows_s[0])

    x = nn(a_ref[0], w_ref[0])
    x0_ref[0, 0] = x.astype(BF16)
    spread(xs, 1, x.reshape(T_LEN, HGT, PADW, LW))
    for tile in range(LW // 128):
        lanes = slice(tile * 128, tile * 128 + 128)

        def step(pair, _):
            acc = [jnp.zeros((HGT, PADW, 128), F32) for _ in range(2)]
            for a in range(3):
                for c in range(3):
                    for d in range(2):
                        block = xs[c, 2 * pair + d + a, :, :, lanes]
                        for b in range(3):
                            acc[d] = acc[d] + k_ref[0, a * 9 + b * 3 + c, :, lanes][None] * block[b : b + HGT]
            both = keep_rows(jnp.stack(acc))
            rows = pl.ds(pl.multiple_of(pair * 112, 112), 112)
            flat = both.reshape(112, 128)
            xp_ref[0, 0, rows, lanes] = flat.astype(BF16)
            if squeeze:
                xf_ref[0, 0, rows, lanes] = flat.astype(BF16)
                both = both.reshape(2 * HGT, PADW, 128)
                for c, shift in ((0, 1), (1, 0), (2, PADW - 1)):
                    moved = pltpu.roll(both, shift, axis=1) if shift else both
                    ys[c, pl.ds(2 * pair + 1, 2), 1 : HGT + 1, :, lanes] = moved.reshape(2, HGT, PADW, 128)
            return 0

        lax.fori_loop(0, T_LEN // 2, step, 0, unroll=2)
        if squeeze:

            def squeeze_step(pair, _):
                acc = [jnp.zeros((HGT, PADW, 128), F32) for _ in range(2)]
                for a in range(3):
                    for c in range(3):
                        for d in range(2):
                            block = ys[c, 4 * pair + 2 * d + a, :, :, lanes]
                            for b in range(3):
                                acc[d] = acc[d] + s_ref[0, a * 9 + b * 3 + c, :, lanes][None] * block[b : b + HGT]
                rows = pl.ds(pl.multiple_of(pair * 112, 112), 112)
                m_ref[0, 0, rows, lanes] = keep_rows(jnp.stack(acc)).reshape(112, 128).astype(BF16)
                return 0

            lax.fori_loop(0, TM // 2, squeeze_step, 0)


def call_pool_forward(clip, clips, rows, weights, first, count, kernels, squeeze, earlier=()):
    tap = pl.BlockSpec((1, 27, LW), lambda j, i: (j + first, 0, 0))
    tap_squeeze = pl.BlockSpec((1, 27, LW), lambda j, i: (j + first + 2, 0, 0))
    wide = pltpu.VMEM((1, 27, 8, LW), F32)

    def out(n):
        return pl.BlockSpec((1, 1, n, LW), lambda j, i: (clip, j, 0, 0))

    frame = pltpu.VMEM((3, T_LEN + 2, HGT + 2, PADW, LW), F32)
    sizes = [ROWS, ROWS, ROWS, MROWS] if squeeze else [ROWS, ROWS]
    given = 4 if squeeze else 3
    return pl.pallas_call(
        partial(pool_forward, squeeze, len(earlier)),
        grid=(count, 1),
        in_specs=[
            pl.BlockSpec((1, ROWS, rows.shape[2]), lambda j, i: (0, 0, 0)),
            pl.BlockSpec((1, weights.shape[1], LW), lambda j, i: (j + first, 0, 0)),
            tap,
        ]
        + ([tap_squeeze] if squeeze else [])
        + [pl.BlockSpec(memory_space=pl.ANY)] * len(earlier),
        out_specs=[out(n) for n in sizes],
        out_shape=[jax.ShapeDtypeStruct((clips, count, n, LW), BF16) for n in sizes],
        scratch_shapes=[frame, wide] * (2 if squeeze else 1),
        input_output_aliases={given + n: n for n in range(len(earlier))},
        compiler_params=params(),
        cost_estimate=pl.CostEstimate(
            flops=300_000_000 * count, bytes_accessed=200_000 * count, transcendentals=0
        ),
    )(rows, weights, kernels, *([kernels] if squeeze else []), *earlier)


def attention_forward(
    q_ref, kv_ref, m1_ref, m2_ref, ke_ref, tab_ref, fold_ref, one_ref, own_ref, lanes_ref, w_ref,
    branch_ref, qa_ref, at_ref, lse_ref, kept_ref, sent_ref, keys, vt, scores, expo, table,
):
    keys[0:ROWS] = kv_ref[0, 0]
    keys[ROWS : ROWS + MROWS] = m1_ref[0, 0]
    keys[ROWS + MROWS :] = m2_ref[0, 0]
    vt[:, 0:ROWS] = kv_ref[0, 1].T
    memory = jnp.concatenate([m1_ref[0, 1], m2_ref[0, 1]], axis=0).T
    vt[:, ROWS:] = memory
    for head in range(LH):
        first = window_of(head)
        variant = head // 2
        win = slice(first, first + WIN)
        heads = lanes_ref[head]
        qm = q_ref[0, 0, :, win] * heads
        table[...] = jnp.zeros_like(table)
        for part in range(2):
            table[part, head * HEAD_DIM - first : (head + 1) * HEAD_DIM - first] = tab_ref[part]
        raw = nn(qm, table[0]) + nn(qm, table[1])
        raw = raw * own_ref[...]
        high = raw.astype(BF16)
        rest = (raw - high.astype(F32)).astype(BF16)
        placed = nn(high, fold_ref[variant, 0]) + nn(rest, fold_ref[variant, 1]) + one_ref[variant, 0:1]
        qa = qm + placed.astype(BF16)
        qa_ref[0, head] = qa.T

        def score(number, peak):
            rows = pl.ds(pl.multiple_of(number * BLOCK, BLOCK), BLOCK)
            ka = keys[rows, win] * heads[0:BLOCK] + ke_ref[0, variant, rows]
            s = nn(ka, qa_ref[0, head])
            scores[rows] = s
            return jnp.maximum(peak, jnp.max(s, axis=0, keepdims=True))

        peak = lax.fori_loop(0, NBLOCK, score, jnp.full((1, ROWS), -3e38, F32), unroll=True)
        shift = peak * (SCALE * LOG2E)

        def soften(number, total):
            rows = pl.ds(pl.multiple_of(number * BLOCK, BLOCK), BLOCK)
            e = jnp.exp2(scores[rows] * (SCALE * LOG2E) - shift)
            expo[rows] = e.astype(BF16)
            return total + jnp.sum(e, axis=0, keepdims=True)

        total = lax.fori_loop(0, NBLOCK, soften, jnp.zeros((1, ROWS), F32), unroll=True)
        out = nn(vt[head * HEAD_DIM : (head + 1) * HEAD_DIM], expo[...]) * (1.0 / total)
        at_ref[0, head * HEAD_DIM : (head + 1) * HEAD_DIM] = out
        lse_ref[0, head : head + 1] = shift + jnp.log2(total)
    branch_ref[0] = (at_ref[0].T + q_ref[0, 0].astype(F32)).astype(BF16)
    side = lax.axis_index("head")
    sent_ref[...] = nn(branch_ref[0, half_rows(1 - side)], w_ref[...]).astype(BF16)
    kept_ref[...] = nn(branch_ref[0, half_rows(side)], w_ref[...])


def whole(shape):
    return pl.BlockSpec(shape, lambda i: (0,) * len(shape))


def clip_block(*shape):
    return pl.BlockSpec((1,) + shape, lambda i: (i,) + (0,) * len(shape))


def call_attention_forward(clip, q, kv, memory, keys_extra, tables, w_proj, consts):
    def block(*shape, at=clip):
        return pl.BlockSpec((1,) + shape, lambda i: (at,) + (0,) * len(shape))

    return pl.pallas_call(
        attention_forward,
        grid=(1,),
        in_specs=[
            block(1, ROWS, LW),
            block(2, ROWS, LW),
            block(2, MROWS, LW, at=clip + 1),
            block(2, MROWS, LW, at=clip),
            block(2, KEYS, WIN),
            whole((2, HEAD_DIM, 256)),
            whole((2, 2, 256, WIN)),
            whole((2, 8, WIN)),
            whole((ROWS, 256)),
            whole((LH, ROWS, WIN)),
            whole(w_proj.shape),
        ],
        out_specs=[
            clip_block(ROWS, LW),
            clip_block(LH, WIN, ROWS),
            clip_block(LW, ROWS),
            clip_block(8, ROWS),
            whole((HALF, w_proj.shape[1])),
            whole((HALF, w_proj.shape[1])),
        ],
        out_shape=[
            jax.ShapeDtypeStruct((1, ROWS, LW), BF16),
            jax.ShapeDtypeStruct((1, LH, WIN, ROWS), BF16),
            jax.ShapeDtypeStruct((1, LW, ROWS), F32),
            jax.ShapeDtypeStruct((1, 8, ROWS), F32),
            jax.ShapeDtypeStruct((HALF, w_proj.shape[1]), F32),
            jax.ShapeDtypeStruct((HALF, w_proj.shape[1]), BF16),
        ],
        scratch_shapes=[
            pltpu.VMEM((KEYS, LW), BF16),
            pltpu.VMEM((LW, KEYS), BF16),
            pltpu.VMEM((KEYS, ROWS), F32),
            pltpu.VMEM((KEYS, ROWS), BF16),
            pltpu.VMEM((2, WIN, 256), BF16),
        ],
        compiler_params=params(),
        cost_estimate=pl.CostEstimate(
            flops=1_300_000_000, bytes_accessed=500_000, transcendentals=0
        ),
    )(q, kv, memory, memory, keys_extra, tables, consts["fold"], consts["one"], consts["own"], consts["lanes"], w_proj)


HALF = ROWS // 2


def simple_call(kernel, out_shape, gflops, *args):
    vmem = pl.BlockSpec(memory_space=pltpu.VMEM)
    many = isinstance(out_shape, list)
    return pl.pallas_call(
        kernel,
        in_specs=[vmem] * len(args),
        out_specs=[vmem] * len(out_shape) if many else vmem,
        out_shape=out_shape,
        compiler_params=params(),
        cost_estimate=pl.CostEstimate(
            flops=int(gflops * 1e8), bytes_accessed=200_000, transcendentals=0
        ),
    )(*args)


def half_rows(side):
    return pl.ds(pl.multiple_of(side * HALF, 16), HALF)


def middle_kernel(tokens, kept, recv, vectors, x1_ref, a2_ref):
    x1 = tokens[...].astype(F32) + kept[...] + recv[...].astype(F32) + vectors[0:1]
    x1_ref[...] = x1
    centred = x1 - jnp.mean(x1, axis=-1, keepdims=True)
    scale = lax.rsqrt(jnp.mean(centred * centred, axis=-1, keepdims=True) + EPSILON)
    a2_ref[...] = (centred * scale * vectors[1:2] + vectors[2:3]).astype(BF16)


FFN_BLOCK = 512
GELU_A = 0.7978845608028654
GELU_B = 0.044715


def joined(refs):
    return jnp.concatenate([ref[...] for ref in refs], axis=0) if len(refs) > 1 else refs[0][...]


def ffn_kernel(count, *refs):
    a2 = joined(refs[:count])
    g = joined(refs[count : 2 * count])
    w1, b1, w2 = refs[2 * count : 2 * count + 3]
    outs = refs[2 * count + 3 :]
    act_refs, dpre_refs, da2_refs, out_refs = (outs[n * count : (n + 1) * count] for n in range(4))
    sums_ref = outs[4 * count]
    da2 = jnp.zeros(a2.shape, F32)
    out = jnp.zeros(a2.shape, F32)
    for first in range(0, w1.shape[1], FFN_BLOCK):
        cols = slice(first, first + FFN_BLOCK)
        pre = nn(a2, w1[:, cols]) + b1[0:1, cols]
        square = pre * pre
        bent = jnp.tanh(GELU_A * (pre + GELU_B * (pre * square)))
        gate = 0.5 + 0.5 * bent
        act = (pre * gate).astype(BF16)
        slope = gate + 0.5 * pre * (1.0 - bent * bent) * (GELU_A * (1.0 + 3.0 * GELU_B * square))
        dpre = nt(g, w2[cols]) * slope
        low = dpre.astype(BF16)
        sums_ref[0:1, cols] = jnp.sum(dpre, axis=0, keepdims=True)
        for n in range(count):
            act_refs[n][:, cols] = act[n * HALF : (n + 1) * HALF]
            dpre_refs[n][:, cols] = low[n * HALF : (n + 1) * HALF]
        da2 = da2 + nt(low, w1[:, cols])
        out = out + nn(act, w2[cols])
    for n in range(count):
        da2_refs[n][...] = da2[n * HALF : (n + 1) * HALF].astype(da2_refs[n].dtype)
        out_refs[n][...] = out[n * HALF : (n + 1) * HALF].astype(out_refs[n].dtype)


def call_ffn(parts, w1, b1, w2):
    hidden, width = w2.shape
    count = len(parts)
    made = simple_call(
        partial(ffn_kernel, count),
        [jax.ShapeDtypeStruct((HALF, hidden), BF16)] * (2 * count)
        + [jax.ShapeDtypeStruct((HALF, width), dtype) for _, _, dtype in parts] * 2
        + [jax.ShapeDtypeStruct((1, hidden), F32)],
        5,
        *[part[0] for part in parts],
        *[part[1] for part in parts],
        w1, b1, w2,
    )
    return [tuple(made[n :: count][:4]) for n in range(count)], made[-1]


def tn(a, b):
    return lax.dot_general(a, b, (((0,), (0,)), ((), ())), preferred_element_type=F32)


def weight_kernel(count, *refs):
    acts, dpres, a2s, gs = (refs[n * count : (n + 1) * count] for n in range(4))
    g2, g1 = refs[4 * count :]
    g2[...] = tn(joined(acts), joined(gs)).astype(BF16)
    g1[...] = tn(joined(a2s), joined(dpres)).astype(BF16)


def call_weights(acts, dpres, a2s, gs):
    hidden, width = acts[0].shape[1], gs[0].shape[1]
    count = len(acts)
    piece = pl.BlockSpec((HALF, LW), lambda i: (0, i))
    full = pl.BlockSpec((HALF, width), lambda i: (0, 0))
    return pl.pallas_call(
        partial(weight_kernel, count),
        grid=(hidden // LW,),
        in_specs=[piece] * (2 * count) + [full] * (2 * count),
        out_specs=[
            pl.BlockSpec((LW, width), lambda i: (i, 0)),
            pl.BlockSpec((width, LW), lambda i: (0, i)),
        ],
        out_shape=[
            jax.ShapeDtypeStruct((hidden, width), BF16),
            jax.ShapeDtypeStruct((width, hidden), BF16),
        ],
        compiler_params=params(),
        cost_estimate=pl.CostEstimate(flops=800_000_000, bytes_accessed=1_500_000, transcendentals=0),
    )(*acts, *dpres, *a2s, *gs)


def widen_kernel(a, b, x, y):
    x[...] = a[...].astype(F32)
    y[...] = b[...].astype(F32)


def call_widen(a, b):
    steps = 8
    specs = [pl.BlockSpec((v.shape[0] // steps, v.shape[1]), lambda i: (i, 0)) for v in (a, b)]
    return pl.pallas_call(
        widen_kernel,
        grid=(steps,),
        in_specs=specs,
        out_specs=specs,
        out_shape=[jax.ShapeDtypeStruct(v.shape, F32) for v in (a, b)],
        compiler_params=params(),
    )(a, b)


def norm_back_kernel(kept, recv, x1_ref, g, vectors, dx_ref, low_ref, sums):
    u = kept[...] + recv[...].astype(F32)
    x1 = x1_ref[...]
    centred = x1 - jnp.mean(x1, axis=-1, keepdims=True)
    scale = lax.rsqrt(jnp.mean(centred * centred, axis=-1, keepdims=True) + EPSILON)
    xhat = centred * scale
    w = u * vectors[1:2]
    up = g[...].astype(F32)
    dx = up + scale * (
        w - jnp.mean(w, axis=-1, keepdims=True) - xhat * jnp.mean(w * xhat, axis=-1, keepdims=True)
    )
    dx_ref[...] = dx
    low_ref[...] = dx.astype(BF16)
    sums[0:1] = jnp.sum(dx, axis=0, keepdims=True)
    sums[1:2] = jnp.sum(u * xhat, axis=0, keepdims=True)
    sums[2:3] = jnp.sum(u, axis=0, keepdims=True)
    sums[3:4] = jnp.sum(up, axis=0, keepdims=True)
    sums[4:8] = jnp.zeros((4, u.shape[1]), F32)


def mix_kernel(mine, theirs, w, rows_ref, dmix_ref):
    head = lax.axis_index("head")
    for side, part in ((head, mine), (1 - head, theirs)):
        rows_ref[half_rows(side)] = part[...]
        dmix_ref[half_rows(side)] = nt(part[...], w[...]).astype(BF16)


HEAD_EARLY = 8
MESH = pl.DeviceIdType.MESH


def remote(src, dst, send, recv, peer):
    made = pltpu.make_async_remote_copy(
        src_ref=src, dst_ref=dst, send_sem=send, recv_sem=recv, device_id=peer, device_id_type=MESH
    )
    made.start()
    return made


def local(src, dst, sem):
    made = pltpu.make_async_copy(src, dst, sem)
    made.start()
    return made


class Place:
    def __init__(self, groups):
        dp = lax.axis_index("dp")
        head = lax.axis_index("head")
        self.groups = groups
        self.dp, self.head = dp, head
        self.core = lax.rem(dp, 2)
        self.xbit = lax.rem(lax.div(dp, 2), 2)
        self.group = lax.div(dp, 4)
        self.to_core = (dp + 1 - 2 * self.core, head)
        self.to_x = (dp + 2 - 4 * self.xbit, head)
        self.to_y = (dp, 1 - head)
        self.peers = [
            (lax.rem(self.group + o, groups) * 4 + lax.rem(dp, 4), head) for o in range(1, groups)
        ]
        self.number = (head * groups + self.group) * 2 + self.xbit

    def device(self, number):
        side = lax.div(number, 2 * self.groups)
        group = lax.rem(lax.div(number, 2), self.groups)
        return (group * 4 + lax.rem(number, 2) * 2 + self.core, side)

    def greet(self, more=()):
        barrier = pltpu.get_barrier_semaphore()
        signalled = [self.to_core, self.to_x] + self.peers + list(more)
        for peer in signalled:
            pl.semaphore_signal(barrier, inc=1, device_id=peer, device_id_type=MESH)
        pl.semaphore_wait(barrier, len(signalled))


class Piece:
    def __init__(self, place, rows, source, result, reduce_refs, send, recv):
        self.at = place
        self.half, self.quarter = rows // 2, rows // 4
        self.chunk = rows // 4 // place.groups
        self.source, self.result = source, result
        self.refs = reduce_refs
        self.send, self.recv = send, recv
        self.tile = 16 if reduce_refs is None or reduce_refs[0].dtype == BF16 else 8
        self.flights = {}

    def start(self, key, number, src, dst, peer):
        self.flights[key] = remote(src, dst, self.send.at[number], self.recv.at[number], peer)

    def base(self, g):
        at = self.at
        return pl.multiple_of(at.core * self.half + at.xbit * self.quarter + g * self.chunk, self.tile)

    def a(self):
        theirs = pl.multiple_of((1 - self.at.core) * self.half, self.tile)
        self.start("a", 0, self.source(theirs, self.half), self.refs[0], self.at.to_core)

    def sum_rows(self, which):
        recv_a = self.refs[0]
        first = pl.multiple_of(which * self.quarter, self.tile)
        own = self.source(pl.multiple_of(self.at.core * self.half + which * self.quarter, self.tile), self.quarter)
        return own[...].astype(F32) + recv_a[pl.ds(first, self.quarter)].astype(F32)

    def b(self):
        _, send_b, recv_b, _, _ = self.refs
        self.flights["a"].wait()
        send_b[...] = self.sum_rows(1 - self.at.xbit).astype(send_b.dtype)
        self.start("b", 1, send_b, recv_b, self.at.to_x)

    def c(self):
        _, _, recv_b, send_c, recv_c = self.refs
        self.flights["b"].wait()
        send_c[...] = (self.sum_rows(self.at.xbit) + recv_b[...].astype(F32)).astype(send_c.dtype)
        for o in range(1, self.at.groups):
            first = pl.multiple_of(lax.rem(self.at.group + o, self.at.groups) * self.chunk, self.tile)
            self.start(
                ("c", o), 1 + o, send_c.at[pl.ds(first, self.chunk)], recv_c.at[o - 1], self.at.peers[o - 1]
            )

    def total(self):
        _, _, _, send_c, recv_c = self.refs
        own = send_c[pl.ds(pl.multiple_of(self.at.group * self.chunk, self.tile), self.chunk)].astype(F32)
        for o in range(1, self.at.groups):
            self.flights["c", o].wait()
            own = own + recv_c[o - 1].astype(F32)
        return own

    def d(self, own=None):
        own = self.total() if own is None else own
        mine = self.result(self.base(self.at.group), self.chunk)
        mine[...] = own.astype(mine.dtype)
        for o in range(1, self.at.groups):
            number = self.at.groups + o
            self.start(("d", o), number, mine, mine, self.at.peers[o - 1])

    def e(self):
        for o in range(1, self.at.groups):
            self.flights["d", o].wait()
        mine = self.result(self.base(0), self.quarter)
        self.start("e", 2 * self.at.groups, mine, mine, self.at.to_x)

    def f(self):
        self.flights["e"].wait()
        mine = self.result(pl.multiple_of(self.at.core * self.half, self.tile), self.half)
        self.start("f", 2 * self.at.groups + 1, mine, mine, self.at.to_core)

    def g(self):
        self.flights["f"].wait()


def piece_scratch(rows, groups, width, dtype, count):
    half, quarter = rows // 2, rows // 4
    return [
        pltpu.VMEM((count, half, width), dtype),
        pltpu.VMEM((count, quarter, width), dtype),
        pltpu.VMEM((count, quarter, width), dtype),
        pltpu.VMEM((count, quarter, width), dtype),
        pltpu.VMEM((count, groups - 1, quarter // groups, width), dtype),
    ]


class Tiny:
    def __init__(self, place, source, result, refs, send, recv):
        self.at, self.source, self.result = place, source, result
        self.recv_core, self.summed, self.slots = refs
        self.send, self.recv = send, recv
        count = 4 * place.groups
        self.half, self.chunk = source.shape[0] // 2, source.shape[0] // 2 // count
        self.mine = place.number
        self.others = [lax.rem(place.number + o, count) for o in range(1, count)]
        self.flights = {}

    def rows(self, number):
        return pl.ds(pl.multiple_of(number * self.chunk, 8), self.chunk)

    def halves(self, core):
        return pl.ds(pl.multiple_of(core * self.half, 8), self.half)

    def start(self, key, src, dst, peer):
        number = len(self.flights)
        self.flights[key] = remote(src, dst, self.send.at[number], self.recv.at[number], peer)

    def a(self):
        self.start("a", self.source.at[self.halves(1 - self.at.core)], self.recv_core, self.at.to_core)

    def b(self):
        self.flights["a"].wait()
        self.summed[...] = self.source[self.halves(self.at.core)] + self.recv_core[...]
        for o, number in enumerate(self.others):
            self.start(("b", o), self.summed.at[self.rows(number)], self.slots.at[o], self.at.device(number))

    def c(self):
        total = self.summed[self.rows(self.mine)]
        for o, number in enumerate(self.others):
            self.flights["b", o].wait()
            total = total + self.slots[o]
        rows = pl.ds(pl.multiple_of(self.at.core * self.half + self.mine * self.chunk, 8), self.chunk)
        self.result[rows] = total
        for o, number in enumerate(self.others):
            self.start(("c", o), self.result.at[rows], self.result.at[rows], self.at.device(number))

    def d(self):
        for o in range(len(self.others)):
            self.flights["c", o].wait()
        rows = self.halves(self.at.core)
        self.start("d", self.result.at[rows], self.result.at[rows], self.at.to_core)

    def e(self):
        self.flights["d"].wait()


class Burst:
    def __init__(self, place, source, refs, send, recv):
        self.at, self.source = place, source
        self.recv_core, self.summed, self.slots = refs
        self.send, self.recv = send, recv
        count = 4 * place.groups
        self.others = [lax.rem(place.number + o, count) for o in range(1, count)]
        self.flights = []

    def start(self, src, dst, peer):
        number = len(self.flights)
        self.flights.append(remote(src, dst, self.send.at[number], self.recv.at[number], peer))

    def a(self):
        self.start(self.source, self.recv_core, self.at.to_core)

    def b(self):
        self.flights[0].wait()
        self.summed[...] = self.source[...] + self.recv_core[...]
        for o, number in enumerate(self.others):
            self.start(self.summed, self.slots.at[o], self.at.device(number))

    def c(self, target):
        total = self.summed[...]
        for o, made in enumerate(self.flights[1:]):
            made.wait()
            total = total + self.slots[o]
        target[...] = total


def attention_backward(
    groups,
    q_ref, kv_ref, mem_ref, ke_hbm, qa_hbm0, qa_hbm1, dm_ref0, dm_ref1, at_hbm0, at_hbm1, lse_ref0, lse_ref1,
    rt_ref, grow_ref, ownt_ref, ekey_ref,
    lanes_ref, g2_ref, g1_ref,
    dq_ref, dkv_ref, dr_ref, chunks_ref, out2,
    ke_ref, qa_ref, at_ref, keys, values, kt, dmt, qms, dms, dmst, dqt,
    recv_a, send_b, recv_b, send_c, recv_c,
    loads, sems_send, sems_recv,
):
    place = Place(groups)
    clips = q_ref.shape[0]
    dm_refs, lse_refs = (dm_ref0, dm_ref1), (lse_ref0, lse_ref1)
    lead = [
        [
            local(ke_hbm.at[clip], ke_ref.at[clip], loads.at[3 * clip]),
            local((qa_hbm0, qa_hbm1)[clip].at[0], qa_ref.at[clip], loads.at[3 * clip + 1]),
            local((at_hbm0, at_hbm1)[clip].at[0], at_ref.at[clip], loads.at[3 * clip + 2]),
        ]
        for clip in range(clips)
    ]
    place.greet()
    total = g1_ref.shape[0]

    def view(number, ref):
        if number < 4:
            base, col = (number // 2) * total, (number % 2) * LW
            return lambda first, n: ref.at[pl.ds(base + first, n), col : col + LW]
        col = (number - 4) * LW
        return lambda first, n: g1_ref.at[pl.ds(first, n), col : col + LW]

    pieces = [
        Piece(
            place, total, view(number, g2_ref), view(number, out2) if number < 4 else None,
            [ref.at[number] for ref in (recv_a, send_b, recv_b, send_c, recv_c)],
            sems_send.at[number], sems_recv.at[number],
        )
        for number in range(8)
    ]
    moves = [
        [pieces[0].a],
        [pieces[0].b, pieces[1].a],
        [pieces[2].a],
        [pieces[1].b, pieces[3].a],
        [pieces[4].a],
        [pieces[0].c, pieces[2].b, pieces[5].a],
        [pieces[6].a],
        [pieces[1].c, pieces[3].b, pieces[7].a],
        [],
        [pieces[0].d, pieces[4].b],
        [],
        [pieces[1].d, pieces[5].b],
        [],
        [pieces[0].e, pieces[2].c],
        [],
        [pieces[1].e, pieces[3].c],
        [],
        [pieces[0].f, pieces[2].d, pieces[6].b],
        [pieces[1].f, pieces[3].d, pieces[7].b, pieces[2].e, pieces[4].c, pieces[5].c, pieces[3].e, pieces[2].f, pieces[6].c, pieces[3].f, pieces[7].c],
    ]

    def pump():
        if moves:
            for move in moves.pop(0):
                move()

    dr_ref[...] = jnp.zeros_like(dr_ref)
    for clip in range(clips):
        pump()
        near, far = mem_ref.at[clip + 1], mem_ref.at[clip]
        keys[0:ROWS] = kv_ref[clip, 0]
        keys[ROWS : ROWS + MROWS] = near[0]
        keys[ROWS + MROWS :] = far[0]
        values[0:ROWS] = kv_ref[clip, 1]
        values[ROWS : ROWS + MROWS] = near[1]
        values[ROWS + MROWS :] = far[1]
        kt[0:LW] = keys[...].T
        kt[LW:] = ekey_ref[...]
        dmt[...] = dm_refs[clip][...].astype(F32).T
        dqt[...] = jnp.zeros_like(dqt)
        for made in lead[clip]:
            made.wait()
        deltas = []
        for head in range(LH):
            first = window_of(head)
            win = slice(first, first + WIN)
            span = slice(head * HEAD_DIM, (head + 1) * HEAD_DIM)
            qms[head] = q_ref[clip, 0, :, win] * lanes_ref[head]
            dms[head] = dm_refs[clip][:, win] * lanes_ref[head]
            dmst[head] = jnp.zeros(dmst.shape[1:], BF16)
            dmst[head, head * HEAD_DIM - first : (head + 1) * HEAD_DIM - first] = dmt[span].astype(BF16)
            deltas.append(jnp.sum(dmt[span] * at_ref[clip, span], axis=0, keepdims=True))

        def step(number, _):
            rows = slice(number * BLOCK, number * BLOCK + BLOCK)
            dk_parts, dv_parts = [], []
            for head in range(LH):
                first = window_of(head)
                variant = head // 2
                win = slice(first, first + WIN)
                ka = keys[rows, win] * lanes_ref[head, 0:BLOCK] + ke_ref[clip, variant, rows]
                s = nn(ka, qa_ref[clip, head])
                p = jnp.exp2(s * (SCALE * LOG2E) - lse_refs[clip][0, head : head + 1])
                dp = nn(values[rows, win], dmst[head])
                ds = (p * (dp - deltas[head])).astype(BF16)
                dv_parts.append(nn(p.astype(BF16), dms[head]))
                dk_parts.append(nn(ds, qms[head]) * SCALE)
                kts = jnp.concatenate(
                    [kt[head * HEAD_DIM : (head + 1) * HEAD_DIM, rows], kt[LW:, rows]], axis=0
                )
                dqt[head] += nn(kts, ds)
            for which, parts in ((0, dk_parts), (1, dv_parts)):
                dkv_ref[clip, which, rows] = jnp.concatenate(
                    [
                        parts[0][:, 0:128] + parts[1][:, 0:128],
                        parts[1][:, 128:256] + parts[2][:, 0:128],
                        parts[2][:, 128:256] + parts[3][:, 128:256],
                    ],
                    axis=1,
                )
            return 0

        for number in range(NBLOCK):
            pump()
            step(number, 0)
        pump()
        for head in range(LH):
            first = window_of(head)
            span = slice(head * HEAD_DIM, (head + 1) * HEAD_DIM)
            total_t = dqt[head]
            grown = nn(grow_ref[...], total_t[HEAD_DIM:].astype(BF16)) * ownt_ref[...]
            grown = grown.astype(BF16)
            dmt[span] = dmt[span] + total_t[0:HEAD_DIM] * SCALE + nn(rt_ref[...], grown)
            dr_ref[:, first : first + WIN] += nn(grown, qms[head])
        dq_ref[clip] = dmt[...].T
    while moves:
        pump()
    for number in range(4):
        pieces[number].g()
        chunks_ref[number] = pieces[4 + number].total().astype(BF16)


def padded_rows(width, groups):
    return -(-width // (4 * groups) // 16) * 16 * 4 * groups


def call_attention_backward(q, kv, memory, keys_extra, qa, dmix, at, lse, rt, g2, g1, consts):
    clips, width = q.shape[0], g2.shape[1]
    groups = lax.axis_size("dp") // 4
    total = padded_rows(width, groups)
    if total != width:
        g1 = jnp.pad(g1, ((0, total - width), (0, 0)))
        g2 = jnp.pad(g2.reshape(2, width, width), ((0, 0), (0, total - width), (0, 0))).reshape(-1, width)
    vmem = pl.BlockSpec(memory_space=pltpu.VMEM)
    hbm = pl.BlockSpec(memory_space=pl.ANY)
    return pl.pallas_call(
        partial(attention_backward, groups),
        in_specs=[vmem] * 3 + [hbm] * 3 + [vmem] * 2 + [hbm] * 2 + [vmem] * 9,
        out_specs=[vmem] * 5,
        out_shape=[
            jax.ShapeDtypeStruct((clips, ROWS, LW), F32),
            jax.ShapeDtypeStruct((clips, 2, KEYS, LW), F32),
            jax.ShapeDtypeStruct((256, LW), F32),
            jax.ShapeDtypeStruct((4, total // 4 // groups, LW), BF16),
            jax.ShapeDtypeStruct(g2.shape, BF16),
        ],
        scratch_shapes=[
            pltpu.VMEM(keys_extra.shape, BF16),
            pltpu.VMEM((clips, LH, WIN, ROWS), BF16),
            pltpu.VMEM((clips, LW, ROWS), F32),
            pltpu.VMEM((KEYS, LW), BF16),
            pltpu.VMEM((KEYS, LW), BF16),
            pltpu.VMEM((LW + 32, KEYS), BF16),
            pltpu.VMEM((LW, ROWS), F32),
            pltpu.VMEM((LH, ROWS, WIN), BF16),
            pltpu.VMEM((LH, ROWS, WIN), BF16),
            pltpu.VMEM((LH, WIN, ROWS), BF16),
            pltpu.VMEM((LH, HEAD_DIM + 32, ROWS), F32),
            *piece_scratch(total, groups, LW, BF16, 8),
            pltpu.SemaphoreType.DMA((3 * clips,)),
            pltpu.SemaphoreType.DMA((8, 2 * groups + 2)),
            pltpu.SemaphoreType.DMA((8, 2 * groups + 2)),
        ],
        compiler_params=params(collective_id=0, has_side_effects=True),
        cost_estimate=pl.CostEstimate(
            flops=40_000_000_000, bytes_accessed=20_000_000, transcendentals=3_000_000
        ),
    )(
        q, kv, memory, keys_extra, *qa, *dmix, *at, *lse, rt,
        consts["grow"], consts["ownt"], consts["ekey"], consts["lanes"], g2, g1,
    )


REL_ROWS = 48
TAP_ROW = NREL
EARLY_ROW = TAP_ROW + 5 * 27
NORM_ROWS = 16
HIDDEN_ROW = EARLY_ROW + 24
SMALL_ROWS = HIDDEN_ROW + 24


def finish_kernel(
    groups, width,
    dq_hbm, dkv_hbm, x0q_hbm, x0kv_hbm, kvf_hbm, rows_taps, rows_a0, rows_a1, rows_x0, rows_x1, branch0, branch1,
    w_hbm, tokens_hbm, middle0, middle1, chunks_ref, dr_ref, gain, foldl_ref, pick_ref,
    sums0, sums1, hidden0, hidden1, hidden2,
    grad, out1, outp, outq, small_out, norm_out,
    dq, dkv, x0q, x0kv, kvf, taps_ref, rows_a, rows_x, branch, w_ref, tokens, middle,
    us, ms, kacc, dx, dmem_send, dmem_recv, resp, grads, stage_t,
    recv_a, send_b, recv_b, send_c, recv_c,
    strips, strip_res, strip_a, strip_b, strip_bb, strip_c, strip_cc,
    sm, sm_res, sm_core, sm_sum, sm_slots, nm, nm_core, nm_sum, nm_slots, send_y, recv_y,
    loads, stores, sems_send, sems_recv, tiny_send, tiny_recv, burst_send, burst_recv, cross_send, cross_recv, mem_sems,
):
    place = Place(groups)
    clips = dq.shape[0]
    total = rows_a.shape[1]
    names = (
        "dkv", "dq", "x0q", "rows_x0", "rows_x1", "branch0", "branch1", "x0kv", "kvf", "rows_a0", "rows_a1", "w",
        "tokens", "middle0", "middle1",
    )
    pairs = (
        (dkv_hbm, dkv), (dq_hbm, dq), (x0q_hbm, x0q),
        (rows_x0, rows_x.at[0:ROWS]), (rows_x1, rows_x.at[ROWS:]), (branch0, branch.at[0:ROWS]),
        (branch1, branch.at[ROWS:]), (x0kv_hbm, x0kv), (kvf_hbm, kvf), (rows_a0, rows_a.at[0:ROWS]),
        (rows_a1, rows_a.at[ROWS:]), (w_hbm, w_ref),
        (tokens_hbm, tokens), (middle0, middle.at[0]), (middle1, middle.at[1]),
    )
    lead = {
        name: local(src, dst, loads.at[n]) for n, (name, (src, dst)) in enumerate(zip(names, pairs))
    }
    count = groups * 4
    behind = (lax.rem(place.dp + count - 1, count), place.head)
    ahead = (lax.rem(place.dp + 1, count), place.head)
    others = [place.device(lax.rem(place.number + o, count)) for o in range(1, count)]
    barrier = pltpu.get_barrier_semaphore()
    for peer in [place.to_core, behind, ahead] + others:
        pl.semaphore_signal(barrier, inc=1, device_id=peer, device_id_type=MESH)
    pl.semaphore_wait(barrier, 3 + len(others))

    def strip_of(number):
        return lambda first, n: out1.at[pl.ds(first, n), number * LW : number * LW + LW]

    ffn = [
        Piece(place, total, None, strip_of(number), None, sems_send.at[number], sems_recv.at[number])
        for number in range(4)
    ]

    def rows_of(ref):
        return lambda first, n: ref.at[pl.ds(first, n)]

    late = [
        Piece(
            place, total, rows_of(grads.at[number]), rows_of(resp.at[number]),
            [ref.at[number] for ref in (recv_a, send_b, recv_b, send_c, recv_c)],
            sems_send.at[4 + number], sems_recv.at[4 + number],
        )
        for number in range(2)
    ] + [
        Piece(
            place, total, rows_of(strips.at[number]), rows_of(strip_res.at[number]),
            [ref.at[number] for ref in (strip_a, strip_b, strip_bb, strip_c, strip_cc)],
            sems_send.at[6 + number], sems_recv.at[6 + number],
        )
        for number in range(6)
    ]
    burst = Burst(place, nm, (nm_core, nm_sum, nm_slots), burst_send, burst_recv)
    tiny = Tiny(place, sm, sm_res, (sm_core, sm_sum, sm_slots), tiny_send, tiny_recv)

    def product(number):
        if number < 2:
            left, right, target = (rows_x, branch, grads.at[0]) if number == 0 else (rows_a, dx.at[0], grads.at[1])
            lanes = slice(0, LW)
        else:
            left, right, target = rows_a, dx.at[1 + (number - 2) // 3], strips.at[number - 2]
            lanes = slice((number - 2) % 3 * 128, (number - 2) % 3 * 128 + 128)
        for first in range(0, total, total // 2):
            target[first : first + total // 2] = tn(
                left[:, first : first + total // 2], right[:, lanes]
            ).astype(BF16)
        late[number].a()

    def shifted_store(dst, first, both, lanes):
        both = both.reshape(2 * HGT, PADW, 128)
        for c, shift in ((0, 1), (1, 0), (2, PADW - 1)):
            moved = pltpu.roll(both, shift, axis=1) if shift else both
            dst[c, pl.ds(first, 2), 1 : HGT + 1, :, lanes] = moved.reshape(2, HGT, PADW, 128)

    def prepare(which, clip):
        if which:
            memory = dmem_recv[clip, which - 1].astype(F32)
            memory = jnp.where(place.dp == count - 1, 0.0, memory)
            for later in range(clip + 1, clips):
                if later == clip + 1:
                    memory = memory + dkv[later, which - 1, ROWS : ROWS + MROWS]
                if later == clip + 2:
                    memory = memory + dkv[later, which - 1, ROWS + MROWS :]
            spread(ms, 0, memory.reshape(TM, HGT, PADW, LW))
        else:
            spread(us, 1, dq[clip].reshape(T_LEN, HGT, PADW, LW))

    def pooled(which, clip, tile):
        field = x0q.at[clip, 0] if which == 0 else x0kv.at[clip, which - 1]
        upstream = dq.at[clip] if which == 0 else dkv.at[clip, which - 1]
        if tile == 0:
            prepare(which, clip)
        lanes = slice(tile * 128, tile * 128 + 128)
        if which:

            def squeeze_step(pair, _):
                rows = pl.ds(pl.multiple_of(pair * 112, 112), 112)
                own = upstream[rows, lanes].reshape(2, HGT, PADW, 128)
                fields = kvf[clip, which - 1, rows, lanes].astype(F32).reshape(2, HGT, PADW, 128)
                acc = [own[0], own[1]]
                for a, d, frame in ((1, 0, 0), (0, 1, 1), (2, 1, 0)):
                    for c in range(3):
                        block = ms[2 - c, pair + frame, :, :, lanes]
                        for b in range(3):
                            at = block[2 - b : 2 - b + HGT]
                            number = a * 9 + b * 3 + c
                            acc[d] = acc[d] + taps_ref[2 + which, number, :, lanes][None] * at
                            kacc[2 + which, number, :, lanes] += jnp.sum(fields[d] * at, axis=0)
                shifted_store(us, 2 * pair + 1, keep_rows(jnp.stack(acc)), lanes)
                return 0

            lax.fori_loop(0, TM, squeeze_step, 0)

        def pair_step(pair, _):
            rows = pl.ds(pl.multiple_of(pair * 112, 112), 112)
            fields = field[rows, lanes].astype(F32).reshape(2, HGT, PADW, 128)
            acc = [jnp.zeros((HGT, PADW, 128), F32) for _ in range(2)]
            for a in range(3):
                for c in range(3):
                    sums = [jnp.zeros((PADW, 128), F32) for _ in range(3)]
                    for d in range(2):
                        block = us[2 - c, 2 * pair + d + 2 - a, :, :, lanes]
                        for b in range(3):
                            at = block[2 - b : 2 - b + HGT]
                            acc[d] = acc[d] + taps_ref[which, a * 9 + b * 3 + c, :, lanes][None] * at
                            sums[b] = sums[b] + jnp.sum(fields[d] * at, axis=0)
                    for b in range(3):
                        kacc[which, a * 9 + b * 3 + c, :, lanes] += sums[b]
            both = keep_rows(jnp.stack(acc))
            out_rows = pl.ds(pl.multiple_of(clip * ROWS + pair * 112, 16), 112)
            dx[which, out_rows, lanes] = both.reshape(112, 128).astype(BF16)
            return 0

        lax.fori_loop(0, T_LEN // 2, pair_step, 0)

    side_rows = ROWS // 2

    def input_gradient(clip, side):
        rows = pl.ds(pl.multiple_of(clip * ROWS + side * side_rows, 16), side_rows)
        return nt(dx[0, rows], w_ref[0]) + nt(dx[1, rows], w_ref[1]) + nt(dx[2, rows], w_ref[2])

    crossing = {}

    def cross(clip):
        send_y[clip] = input_gradient(clip, 1 - place.head).astype(BF16)
        crossing[clip] = remote(
            send_y.at[clip], recv_y.at[clip], cross_send.at[clip], cross_recv.at[clip], place.to_y
        )

    def normed_gradient(clip):
        mine = input_gradient(clip, place.head)
        crossing[clip].wait()
        u = mine + recv_y[clip].astype(F32)
        v = tokens[clip].astype(F32)
        centred = v - jnp.mean(v, axis=-1, keepdims=True)
        scale = lax.rsqrt(jnp.mean(centred * centred, axis=-1, keepdims=True) + EPSILON)
        xhat = centred * scale
        w = u * gain[0:1]
        dv = scale * (
            w - jnp.mean(w, axis=-1, keepdims=True) - xhat * jnp.mean(w * xhat, axis=-1, keepdims=True)
        )
        grad[clip] = middle[clip] + dv
        for which, value in enumerate((u * xhat, u)):
            value = jnp.sum(value, axis=0, keepdims=True)
            for n in range(width // 128):
                row = which * (width // 128) + n
                nm[row : row + 1] += value[:, n * 128 : n * 128 + 128]

    def exact(a, b):
        return jnp.dot(a, b, precision=HIGHEST, preferred_element_type=F32)

    def small_first():
        sm[...] = jnp.zeros_like(sm)
        nm[...] = jnp.zeros_like(nm)
        folded = exact(dr_ref[...], foldl_ref[...])
        sm[0:NREL] = exact(pick_ref[...], folded)[0:NREL]
        early = sums0[...] + sums1[...]
        hidden = hidden0[...] + hidden1[...] + hidden2[...]
        strip = width // 128
        for which in range(4):
            for n in range(strip):
                row = EARLY_ROW + which * strip + n
                sm[row : row + 1] = early[which : which + 1, n * 128 : n * 128 + 128]
        count_h = hidden.shape[1] // 128
        for side in range(2):
            for n in range(count_h):
                row = HIDDEN_ROW + side * count_h + n
                part = hidden[:, n * 128 : n * 128 + 128]
                sm[row : row + 1] = jnp.where(place.head == side, part, 0.0)

    def small_taps(which):
        first = TAP_ROW + 27 * which
        sums = jnp.sum(kacc[which], axis=1)
        sums = jnp.concatenate([sums, jnp.zeros((5, LW), F32)], axis=0)
        sm[first : first + 27] = exact(sums, foldl_ref[...])[0:27]

    ffn[0].d(chunks_ref[0])
    us[...] = jnp.zeros_like(us)
    ms[...] = jnp.zeros_like(ms)
    kacc[...] = jnp.zeros_like(kacc)
    for which in range(5):
        taps_ref[which] = widened(rows_taps[which])
    small_first()
    lead["dkv"].wait()
    for which in range(2):
        dmem_send[0, which] = dkv[0, which, ROWS + MROWS :].astype(BF16)
        dmem_send[1, which] = (
            dkv[0, which, ROWS : ROWS + MROWS] + dkv[1, which, ROWS + MROWS :]
        ).astype(BF16)
    memory_flight = remote(dmem_send, dmem_recv, mem_sems.at[0], mem_sems.at[1], behind)
    for name in ("rows_x0", "rows_x1", "branch0", "branch1"):
        lead[name].wait()
    product(0)
    for name in ("dq", "x0q"):
        lead[name].wait()
    pooled(0, 0, 0)
    pooled(0, 0, 1)
    late[0].b()
    pooled(0, 0, 2)
    ffn[1].d(chunks_ref[1])
    pooled(0, 1, 0)
    pooled(0, 1, 1)
    ffn[0].e()
    pooled(0, 1, 2)
    ffn[2].d(chunks_ref[2])
    lead["rows_a0"].wait()
    lead["rows_a1"].wait()
    product(1)
    small_taps(0)
    memory_flight.wait()
    lead["x0kv"].wait()
    lead["kvf"].wait()
    pooled(1, 0, 0)
    late[1].b()
    late[0].c()
    pooled(1, 0, 1)
    ffn[0].f()
    pooled(1, 0, 2)
    ffn[1].e()
    ffn[3].d(chunks_ref[3])
    pooled(2, 0, 0)
    ffn[0].g()
    pooled(2, 0, 1)
    late[0].d()
    ffn[2].e()
    pooled(2, 0, 2)
    lead["w"].wait()
    cross(0)
    ffn[1].f()
    pooled(1, 1, 0)
    late[1].c()
    ffn[1].g()
    ffn[3].e()
    product(2)
    pooled(1, 1, 1)
    ffn[2].f()
    product(3)
    pooled(1, 1, 2)
    late[2].b()
    ffn[2].g()
    product(4)
    late[3].b()
    late[1].d()
    small_taps(1)
    small_taps(3)
    late[0].e()
    ffn[3].f()
    pooled(2, 1, 0)
    ffn[3].g()
    product(5)
    late[2].c()
    pooled(2, 1, 1)
    late[3].c()
    late[4].b()
    product(6)
    late[5].b()
    pooled(2, 1, 2)
    late[2].d()
    late[6].b()
    late[0].f()
    cross(1)
    late[3].d()
    late[1].e()
    product(7)
    late[0].g()
    stage_t[...] = resp[0].astype(F32).T
    sent = [local(stage_t, outp, stores.at[2])]
    late[4].c()
    small_taps(2)
    small_taps(4)
    tiny.a()
    for name in ("tokens", "middle0", "middle1"):
        lead[name].wait()
    normed_gradient(0)
    late[5].c()
    late[2].e()
    tiny.b()
    late[6].c()
    late[3].e()
    late[4].d()
    late[7].b()
    late[1].f()
    late[5].d()
    late[2].f()
    late[1].g()
    sent.append(local(resp.at[1], outq.at[0], stores.at[3]))
    late[6].d()
    late[2].g()
    sent.append(local(strip_res.at[0], outq.at[1, :, 0 : 128], stores.at[4]))
    late[3].f()
    tiny.c()
    late[4].e()
    late[7].c()
    late[3].g()
    sent.append(local(strip_res.at[1], outq.at[1, :, 128 : 256], stores.at[5]))
    normed_gradient(1)
    burst.a()
    late[5].e()
    late[6].e()
    late[4].f()
    late[7].d()
    burst.b()
    tiny.d()
    late[4].g()
    sent.append(local(strip_res.at[2], outq.at[1, :, 256 : 384], stores.at[6]))
    tiny.e()
    small_out[...] = sm_res[...]
    late[5].f()
    late[6].f()
    late[5].g()
    sent.append(local(strip_res.at[3], outq.at[2, :, 0 : 128], stores.at[7]))
    late[7].e()
    late[6].g()
    sent.append(local(strip_res.at[4], outq.at[2, :, 128 : 256], stores.at[8]))
    burst.c(norm_out)
    late[7].f()
    late[7].g()
    sent.append(local(strip_res.at[5], outq.at[2, :, 256 : 384], stores.at[9]))
    for made in sent:
        made.wait()


def call_finish(
    dq, dkv, x0q, x0kv, kvf, all_taps, rows_a, rows_x, branch, weights, tokens, middle, chunks, dr, gain, sums, hidden
):
    groups = lax.axis_size("dp") // 4
    width = tokens.shape[2]
    total = padded_rows(width, groups)
    clips, side = tokens.shape[:2]
    if total != width:
        extra = ((0, 0), (0, total - width))
        rows_a, rows_x = [jnp.pad(x, extra) for x in rows_a], [jnp.pad(x, extra) for x in rows_x]
    small_rows = -(-SMALL_ROWS // (64 * groups)) * 64 * groups
    foldl = np.zeros((LW, 128), np.float32)
    foldl[np.arange(LW), np.arange(LW) % HEAD_DIM] = 1
    pick = np.zeros((REL_ROWS, 256), np.float32)
    pick[:NREL] = PICK.T
    vmem = pl.BlockSpec(memory_space=pltpu.VMEM)
    hbm = pl.BlockSpec(memory_space=pl.ANY)
    streamed = [dq, dkv, x0q, x0kv, kvf, all_taps, *rows_a, *rows_x, *branch, weights, tokens, *middle]
    held = [
        (array.shape, array.dtype)
        for array in (dq, dkv, x0q, x0kv, kvf)
    ] + [
        ((5, 27, 8, LW), F32), ((clips * ROWS, total), BF16),
        ((clips * ROWS, total), BF16), ((clips * ROWS, LW), BF16), (weights.shape, BF16), (tokens.shape, BF16),
        (tokens.shape, F32),
    ]
    frame = pltpu.VMEM((3, T_LEN + 2, HGT + 2, PADW, LW), F32)
    return pl.pallas_call(
        partial(finish_kernel, groups, width),
        in_specs=[hbm] * 5 + [vmem] + [hbm] * (len(streamed) - 6) + [vmem] * 10,
        out_specs=[vmem, vmem, hbm, hbm, vmem, vmem],
        out_shape=[
            jax.ShapeDtypeStruct(tokens.shape, F32),
            jax.ShapeDtypeStruct((total, 4 * LW), BF16),
            jax.ShapeDtypeStruct((LW, total), F32),
            jax.ShapeDtypeStruct((3, total, LW), BF16),
            jax.ShapeDtypeStruct((small_rows, 128), F32),
            jax.ShapeDtypeStruct((NORM_ROWS, 128), F32),
        ],
        scratch_shapes=[pltpu.VMEM(shape, dtype) for shape, dtype in held]
        + [
            frame,
            pltpu.VMEM((3, TM + 1, HGT + 2, PADW, LW), F32),
            pltpu.VMEM((5, 27, 8, LW), F32),
            pltpu.VMEM((3, clips * ROWS, LW), BF16),
            pltpu.VMEM((2, 2, MROWS, LW), BF16),
            pltpu.VMEM((2, 2, MROWS, LW), BF16),
            pltpu.VMEM((2, total, LW), BF16),
            pltpu.VMEM((2, total, LW), BF16),
            pltpu.VMEM((LW, total), F32),
            *piece_scratch(total, groups, LW, BF16, 2),
            pltpu.VMEM((6, total, 128), BF16),
            pltpu.VMEM((6, total, 128), BF16),
            *piece_scratch(total, groups, 128, BF16, 6),
            pltpu.VMEM((small_rows, 128), F32),
            pltpu.VMEM((small_rows, 128), F32),
            pltpu.VMEM((small_rows // 2, 128), F32),
            pltpu.VMEM((small_rows // 2, 128), F32),
            pltpu.VMEM((4 * groups - 1, small_rows // 8 // groups, 128), F32),
            pltpu.VMEM((NORM_ROWS, 128), F32),
            pltpu.VMEM((NORM_ROWS, 128), F32),
            pltpu.VMEM((NORM_ROWS, 128), F32),
            pltpu.VMEM((4 * groups - 1, NORM_ROWS, 128), F32),
            pltpu.VMEM((clips, side, width), BF16),
            pltpu.VMEM((clips, side, width), BF16),
            pltpu.SemaphoreType.DMA((16,)),
            pltpu.SemaphoreType.DMA((10,)),
            pltpu.SemaphoreType.DMA((12, 2 * groups + 2)),
            pltpu.SemaphoreType.DMA((12, 2 * groups + 2)),
            pltpu.SemaphoreType.DMA((8 * groups,)),
            pltpu.SemaphoreType.DMA((8 * groups,)),
            pltpu.SemaphoreType.DMA((4 * groups,)),
            pltpu.SemaphoreType.DMA((4 * groups,)),
            pltpu.SemaphoreType.DMA((clips,)),
            pltpu.SemaphoreType.DMA((clips,)),
            pltpu.SemaphoreType.DMA((2,)),
        ],
        compiler_params=params(collective_id=1, has_side_effects=True),
        cost_estimate=pl.CostEstimate(
            flops=60_000_000_000, bytes_accessed=40_000_000, transcendentals=0
        ),
    )(*streamed, chunks, dr, gain, jnp.asarray(foldl), jnp.asarray(pick), *sums, *hidden)


def from_behind(x, axis, by):
    count = lax.axis_size(axis)
    pairs = [(i, i + by) for i in range(count) if 0 <= i + by < count]
    return lax.ppermute(x, axis, pairs)


def layer_norm(values, scaling, offset):
    average = jnp.mean(values, axis=-1, keepdims=True)
    centred = values - average
    variance = jnp.mean(centred * centred, axis=-1, keepdims=True)
    return centred * lax.rsqrt(variance + EPSILON) * scaling + offset


def pad_rows(x):
    lead = x.shape[0]
    frames = x.shape[1] // (HGT * WID)
    grid = x.reshape(lead, frames, HGT, WID, x.shape[-1])
    grid = jnp.pad(grid, ((0, 0), (0, 0), (0, 0), (0, PADW - WID), (0, 0)))
    return grid.reshape(lead, frames * HGT * PADW, x.shape[-1])


def drop_rows(x):
    lead = x.shape[0]
    frames = x.shape[1] // (HGT * PADW)
    grid = x.reshape(lead, frames, HGT, PADW, x.shape[-1])[:, :, :, :WID]
    return grid.reshape(lead, frames * HGT * WID, x.shape[-1])


def swap(x):
    return lax.ppermute(x, "head", [(0, 1), (1, 0)])


def gather_rows(x):
    half = x.shape[1]
    mine = lax.axis_index("head") * half
    both = jnp.concatenate([x, x], axis=1)
    return lax.dynamic_update_slice_in_dim(both, swap(x), half - mine, axis=1)


def taps(*kernels):
    return jnp.tile(jnp.stack(kernels), (1, 1, LH))


def on_device(
    tokens,
    ln1_gain,
    ln1_bias,
    w_qkv,
    pool_q,
    pool_k,
    pool_v,
    squeeze_k,
    squeeze_v,
    rel_t,
    rel_h,
    rel_w,
    w_proj,
    proj_bias,
    ln2_gain,
    ln2_bias,
    w_fc1,
    fc1_bias,
    w_fc2,
    fc2_bias,
    memory_valid,
    cotangent,
):
    clip_count = tokens.shape[0]
    consts = {
        "fold": jnp.asarray(fold_constants(), BF16),
        "one": jnp.asarray(one_lane(), F32),
        "own": jnp.asarray(OWN_T.T, F32),
        "ownt": jnp.asarray(OWN_T, F32),
        "lanes": jnp.asarray(head_lanes(), BF16),
        "grow": jnp.asarray(FOLD, BF16),
        "ekey": jnp.asarray(EKEY, BF16),
    }
    keys_extra = key_constants(memory_valid)
    rel_all = jnp.concatenate([rel_t, rel_h, rel_w], axis=0)
    pairs = jnp.dot(jnp.asarray(PICK), rel_all, precision=HIGHEST)
    pair_table = (pairs * HEAD_DIM**0.5).T
    table_high = pair_table.astype(BF16)
    table_rest = (pair_table - table_high.astype(F32)).astype(BF16)
    tables = jnp.stack([table_high, table_rest])
    rel_rows = pairs.T.astype(BF16)
    all_taps = taps(pool_q, pool_k, pool_v, squeeze_k, squeeze_v)

    width = tokens.shape[2]
    inputs_low = pad_rows(tokens)
    inputs = inputs_low.astype(F32)
    upstream = pad_rows(cotangent)
    real = (jnp.arange(inputs.shape[1]) % PADW < WID)[None, :, None]
    first_normed = layer_norm(inputs, ln1_gain, ln1_bias)
    first_low = jnp.where(real, first_normed, 0.0).astype(BF16)
    first_rows = []
    for clip in range(clip_count):
        one = first_low[clip : clip + 1]
        if clip:
            one = lax.optimization_barrier((one, first_rows[-1]))[0]
        first_rows.append(gather_rows(one))
    w_heads = w_qkv.transpose(1, 0, 2)
    upstream_other = swap(lax.optimization_barrier((upstream, first_rows[-1]))[0])
    pooled = ()
    for clip in range(clip_count):
        pooled = call_pool_forward(clip, clip_count, first_rows[clip], w_heads, 1, 2, all_taps, True, pooled)
    kv0, kv, kvf, mem = pooled
    before = from_behind(mem[-2:], "dp", 1)
    pooled = ()
    for clip in range(clip_count):
        pooled = call_pool_forward(clip, clip_count, first_rows[clip], w_heads, 0, 1, all_taps, False, pooled)
    q0, q = pooled
    memory = jnp.concatenate([before, mem], axis=0)
    vectors = jnp.stack([proj_bias, ln2_gain, ln2_bias])
    hidden_bias = fc1_bias.reshape(1, -1)
    rows32 = jax.ShapeDtypeStruct((HALF, width), F32)
    rows16 = jax.ShapeDtypeStruct((HALF, width), BF16)
    clips = range(clip_count)
    branch, qa, at, lse, kept, recv = [], [], [], [], [], []
    for clip in clips:
        *made, own, sent = call_attention_forward(clip, q, kv, memory, keys_extra, tables, w_proj, consts)
        for store, value in zip((branch, qa, at, lse), made):
            store.append(value)
        sent, q = lax.optimization_barrier((sent, q)) if clip + 1 < clip_count else (sent, q)
        kept.append(own)
        recv.append(swap(sent))

    def after(value, *earlier):
        return lax.optimization_barrier((value, *earlier))[0]

    middle, mine, theirs = [], [], []
    own_parts, other_parts, second = [None] * clip_count, [None] * clip_count, [None] * clip_count

    hidden_sums = []

    def through(*rows):
        made, total = call_ffn(
            [
                (mine[clip], upstream[clip], F32) if own else (theirs[clip], upstream_other[clip], BF16)
                for clip, own in rows
            ],
            w_fc1, hidden_bias, w_fc2,
        )
        hidden_sums.append(total)
        for (clip, own), part in zip(rows, made):
            if own:
                own_parts[clip] = part
            else:
                other_parts[clip] = part
                second[clip] = swap(part[2])

    for clip in clips:
        landed = after(recv[clip], own_parts[clip - 1][2]) if clip else recv[clip]
        x1, a2 = simple_call(middle_kernel, [rows32, rows16], 1, inputs_low[clip], kept[clip], landed, vectors)
        middle.append(x1)
        mine.append(a2)
        theirs.append(swap(a2))
        if clip == 0:
            through((0, True))
        else:
            through((clip, True), (clip - 1, False))
    theirs[-1] = after(theirs[-1], own_parts[-1][2])
    through((clip_count - 1, False))
    dmiddle, low, sums, rows_x, dmix = [], [], [], [], []
    parts = own_parts + other_parts
    for clip in clips:
        if clip + 1 == clip_count:
            w_fc2_grad, w_fc1_grad = call_weights(
                [p[0] for p in parts],
                [p[1] for p in parts],
                mine + theirs,
                [after(upstream[0], low[0][0])]
                + [upstream[c] for c in clips[1:]]
                + [upstream_other[c] for c in clips],
            )
        landed = after(second[clip], w_fc2_grad if clip + 1 == clip_count else other_parts[-1][2])
        dx, dx_low, total = simple_call(
            norm_back_kernel,
            [rows32, rows16, jax.ShapeDtypeStruct((HEAD_EARLY, width), F32)],
            1,
            own_parts[clip][2], landed, middle[clip], upstream[clip], vectors,
        )
        dmiddle.append(dx)
        sums.append(total)
        low.append((dx_low, swap(dx_low)))
    for clip in clips:
        received = after(low[clip][1], low[-1][0])
        rows, mix = simple_call(
            mix_kernel,
            [jax.ShapeDtypeStruct((ROWS, width), BF16), jax.ShapeDtypeStruct((ROWS, LW), BF16)],
            1,
            low[clip][0], received, w_proj,
        )
        rows_x.append(rows)
        dmix.append(mix)
    last = [lax.optimization_barrier((other_parts[c][3], dmix[-1]))[0] for c in clips]
    last = [swap(x) for x in last]
    dq, dkv, dr, chunks, w_fc2_grad = call_attention_backward(
        q, kv, memory, keys_extra, qa, dmix, at, lse, rel_rows,
        w_fc2_grad, w_fc1_grad, consts,
    )
    *last, dq = lax.optimization_barrier((*last, dq))
    output = drop_rows(
        jnp.stack(
            [
                (middle[c] + own_parts[c][3] + last[c].astype(F32) + fc2_bias).astype(BF16)
                for c in clips
            ]
        )
    )
    input_grad, w_fc1_grad, w_proj_grad, tail, small, norms = call_finish(
        dq, dkv, q0, kv0, kvf, all_taps,
        [x[0] for x in first_rows],
        rows_x,
        [b[0] for b in branch],
        w_heads,
        inputs_low,
        dmiddle,
        chunks,
        dr,
        ln1_gain.reshape(1, -1),
        sums,
        hidden_sums,
    )
    input_grad = drop_rows(input_grad)
    w_fc2_grad, w_fc1_grad = call_widen(w_fc2_grad, w_fc1_grad)
    total = w_fc1_grad.shape[0]
    if total != width:
        w_fc2_grad = w_fc2_grad.reshape(2, total, width)[:, :width].reshape(2 * width, width)
        w_fc1_grad, w_proj_grad, tail = w_fc1_grad[:width], w_proj_grad[:, :width], tail[:, :width]
    w_qkv_grad = tail.astype(F32).transpose(1, 0, 2)
    norms = norms[: 2 * width // 128].reshape(2, width)
    early = small[EARLY_ROW:HIDDEN_ROW].reshape(4, width)
    fc1_bias_grad = lax.dynamic_index_in_dim(
        small[HIDDEN_ROW:SMALL_ROWS].reshape(2, fc1_bias.size), lax.axis_index("head"), 0, keepdims=False
    )
    small = small[:, :HEAD_DIM]
    shared = [norms[0], norms[1]]
    shared += [small[TAP_ROW + 27 * n : TAP_ROW + 27 * n + 27] for n in range(5)]
    shared += [
        small[: 2 * T_LEN - 1],
        small[2 * T_LEN - 1 : 2 * T_LEN + 2 * HGT - 2],
        small[2 * T_LEN + 2 * HGT - 2 : NREL],
    ]
    shared += [early[0], early[1], early[2], early[3]]
    return (
        output,
        input_grad,
        shared[0],
        shared[1],
        w_qkv_grad,
        shared[2],
        shared[3],
        shared[4],
        shared[5],
        shared[6],
        shared[7],
        shared[8],
        shared[9],
        w_proj_grad,
        shared[10],
        shared[11],
        shared[12],
        w_fc1_grad,
        fc1_bias_grad,
        w_fc2_grad,
        shared[13],
    )


def solution(mesh):
    return jax.shard_map(
        on_device,
        mesh=mesh,
        in_specs=(
            P("dp", "head", None),
            P(),
            P(),
            P(None, None, "head"),
            P(),
            P(),
            P(),
            P(),
            P(),
            P(),
            P(),
            P(),
            P("head", None),
            P(),
            P(),
            P(),
            P(None, "head"),
            P("head"),
            P("head", None),
            P(),
            P("dp", None),
            P("dp", "head", None),
        ),
        out_specs=(
            P("dp", "head", None),
            P("dp", "head", None),
            P(),
            P(),
            P(None, None, "head"),
            P(),
            P(),
            P(),
            P(),
            P(),
            P(),
            P(),
            P(),
            P("head", None),
            P(),
            P(),
            P(),
            P(None, "head"),
            P("head"),
            P("head", None),
            P(),
        ),
        check_vma=False,
    )
```

```python
from functools import partial

import jax
import jax.numpy as jnp
import numpy as np
from jax import lax
from jax.experimental import pallas as pl
from jax.experimental.pallas import tpu as pltpu
from jax.sharding import PartitionSpec as P

HEAD_DIM = 96
T_LEN = 8
HGT = 7
WID = 7
PADW = 8
L = 392
ROWS = T_LEN * HGT * PADW
TM = 4
MROWS = TM * HGT * PADW
KEYS = ROWS + 2 * MROWS
LH = 4
LW = LH * HEAD_DIM
WIN = 256
BLOCK = 128
NBLOCK = KEYS // BLOCK

EPSILON = 1e-06
HIGHEST = lax.Precision.HIGHEST
SCALE = HEAD_DIM ** (-0.5)
LOG2E = 1.4426950408889634
F32 = jnp.float32
BF16 = jnp.bfloat16
VMEM_LIMIT = 58 * 1024 * 1024

NB = T_LEN + HGT + WID
NREL = 2 * T_LEN - 1 + 2 * HGT - 1 + 2 * WID - 1
NPAIR = T_LEN * T_LEN + HGT * HGT + WID * WID


def params(**extra):
    return pltpu.CompilerParams(vmem_limit_bytes=VMEM_LIMIT, **extra)


def window_of(head):
    return 0 if head < 2 else BLOCK


def slot_of(head):
    return 192 if head < 2 else 0


def position_constants():
    t, h, w = np.meshgrid(np.arange(T_LEN), np.arange(HGT), np.arange(PADW), indexing="ij")
    t, h, w = t.ravel(), h.ravel(), w.ravel()
    valid = w < WID
    own = np.zeros((256, ROWS), np.float32)
    pick = np.zeros((256, NREL), np.float32)
    fold = np.zeros((256, 32), np.float32)
    ekey = np.zeros((32, KEYS), np.float32)
    row = 0
    base_entry = 0
    base_bias = 0
    for places, length in ((t, T_LEN), (h, HGT), (w, WID)):
        for a in range(length):
            for b in range(length):
                own[row] = (places == a) & valid
                pick[row, base_entry + a - b + length - 1] = 1
                fold[row, base_bias + b] = 1
                row += 1
        for b in range(length):
            ekey[base_bias + b, :ROWS] = (places == b) & valid
        base_entry += 2 * length - 1
        base_bias += length
    return own, pick, fold, ekey, valid


OWN_T, PICK, FOLD, EKEY, ROW_VALID = position_constants()


def fold_constants():
    out = np.zeros((2, 2, 256, WIN), np.float32)
    for variant, slot in enumerate((192, 0)):
        out[variant, 0, :, slot : slot + 32] = FOLD
        out[variant, 1, :, slot + 32 : slot + 64] = FOLD
    return out


def one_lane():
    out = np.zeros((2, 8, WIN), np.float32)
    for variant, slot in enumerate((192, 0)):
        out[variant, :, slot + NB] = 1
    return out


def head_lanes():
    out = np.zeros((LH, ROWS, WIN), np.float32)
    for head in range(LH):
        first = head * HEAD_DIM - window_of(head)
        out[head, :, first : first + HEAD_DIM] = 1
    return out


def key_constants(memory_valid):
    clip_count = memory_valid.shape[0]
    base = np.zeros((2, KEYS, WIN), np.float32)
    lane = np.zeros((2, 1, WIN), np.float32)
    for variant, slot in enumerate((192, 0)):
        base[variant, :, slot : slot + 32] = EKEY.T
        base[variant, :, slot + 32 : slot + 64] = EKEY.T
        lane[variant, :, slot + NB] = 1
    pads = np.concatenate([ROW_VALID, ROW_VALID[:MROWS], ROW_VALID[:MROWS]])
    use = jnp.concatenate(
        [jnp.ones((clip_count, ROWS), bool), jnp.repeat(memory_valid > 0, MROWS, axis=1)], axis=1
    )
    drop = jnp.where(use & jnp.asarray(pads)[None], 0.0, -1e30).astype(F32)
    return (jnp.asarray(base)[None] + drop[:, None, :, None] * jnp.asarray(lane)[None]).astype(BF16)


def nt(a, b):
    return lax.dot_general(a, b, (((1,), (1,)), ((), ())), preferred_element_type=F32)


def nn(a, b):
    return jnp.dot(a, b, preferred_element_type=F32)


def keep_rows(block):
    place = lax.broadcasted_iota(jnp.int32, block.shape, block.ndim - 2)
    return jnp.where(place < WID, block, 0.0)


def spread(dst, first, value):
    n, _, _, c = value.shape
    flat = value.reshape(n * HGT, PADW, c)
    dst[0, pl.ds(first, n), 1 : HGT + 1] = pltpu.roll(flat, 1, axis=1).reshape(n, HGT, PADW, c)
    dst[1, pl.ds(first, n), 1 : HGT + 1] = value
    dst[2, pl.ds(first, n), 1 : HGT + 1] = pltpu.roll(flat, PADW - 1, axis=1).reshape(n, HGT, PADW, c)


def widened(rows):
    return jnp.broadcast_to(rows[:, None, :], (rows.shape[0], 8, rows.shape[1]))


def pool_forward(squeeze, carried, *refs):
    given = 4 if squeeze else 3
    refs = refs[:given] + refs[given + carried :]
    if squeeze:
        a_ref, w_ref, rows_k, rows_s, x0_ref, xp_ref, xf_ref, m_ref, xs, k_ref, ys, s_ref = refs
    else:
        a_ref, w_ref, rows_k, x0_ref, xp_ref, xs, k_ref = refs

    @pl.when((pl.program_id(0) == 0) & (pl.program_id(1) == 0))
    def _():
        xs[...] = jnp.zeros_like(xs)
        if squeeze:
            ys[...] = jnp.zeros_like(ys)

    @pl.when(pl.program_id(1) == 0)
    def _():
        k_ref[0] = widened(rows_k[0])
        if squeeze:
            s_ref[0] = widened(rows_s[0])

    x = nn(a_ref[0], w_ref[0])
    x0_ref[0, 0] = x.astype(BF16)
    spread(xs, 1, x.reshape(T_LEN, HGT, PADW, LW))
    for tile in range(LW // 128):
        lanes = slice(tile * 128, tile * 128 + 128)

        def step(pair, _):
            acc = [jnp.zeros((HGT, PADW, 128), F32) for _ in range(2)]
            for a in range(3):
                for c in range(3):
                    for d in range(2):
                        block = xs[c, 2 * pair + d + a, :, :, lanes]
                        for b in range(3):
                            acc[d] = acc[d] + k_ref[0, a * 9 + b * 3 + c, :, lanes][None] * block[b : b + HGT]
            both = keep_rows(jnp.stack(acc))
            rows = pl.ds(pl.multiple_of(pair * 112, 112), 112)
            flat = both.reshape(112, 128)
            xp_ref[0, 0, rows, lanes] = flat.astype(BF16)
            if squeeze:
                xf_ref[0, 0, rows, lanes] = flat.astype(BF16)
                both = both.reshape(2 * HGT, PADW, 128)
                for c, shift in ((0, 1), (1, 0), (2, PADW - 1)):
                    moved = pltpu.roll(both, shift, axis=1) if shift else both
                    ys[c, pl.ds(2 * pair + 1, 2), 1 : HGT + 1, :, lanes] = moved.reshape(2, HGT, PADW, 128)
            return 0

        lax.fori_loop(0, T_LEN // 2, step, 0, unroll=2)
        if squeeze:

            def squeeze_step(pair, _):
                acc = [jnp.zeros((HGT, PADW, 128), F32) for _ in range(2)]
                for a in range(3):
                    for c in range(3):
                        for d in range(2):
                            block = ys[c, 4 * pair + 2 * d + a, :, :, lanes]
                            for b in range(3):
                                acc[d] = acc[d] + s_ref[0, a * 9 + b * 3 + c, :, lanes][None] * block[b : b + HGT]
                rows = pl.ds(pl.multiple_of(pair * 112, 112), 112)
                m_ref[0, 0, rows, lanes] = keep_rows(jnp.stack(acc)).reshape(112, 128).astype(BF16)
                return 0

            lax.fori_loop(0, TM // 2, squeeze_step, 0)


def call_pool_forward(clip, clips, rows, weights, first, count, kernels, squeeze, earlier=()):
    tap = pl.BlockSpec((1, 27, LW), lambda j, i: (j + first, 0, 0))
    tap_squeeze = pl.BlockSpec((1, 27, LW), lambda j, i: (j + first + 2, 0, 0))
    wide = pltpu.VMEM((1, 27, 8, LW), F32)

    def out(n):
        return pl.BlockSpec((1, 1, n, LW), lambda j, i: (clip, j, 0, 0))

    frame = pltpu.VMEM((3, T_LEN + 2, HGT + 2, PADW, LW), F32)
    sizes = [ROWS, ROWS, ROWS, MROWS] if squeeze else [ROWS, ROWS]
    given = 4 if squeeze else 3
    return pl.pallas_call(
        partial(pool_forward, squeeze, len(earlier)),
        grid=(count, 1),
        in_specs=[
            pl.BlockSpec((1, ROWS, rows.shape[2]), lambda j, i: (0, 0, 0)),
            pl.BlockSpec((1, weights.shape[1], LW), lambda j, i: (j + first, 0, 0)),
            tap,
        ]
        + ([tap_squeeze] if squeeze else [])
        + [pl.BlockSpec(memory_space=pl.ANY)] * len(earlier),
        out_specs=[out(n) for n in sizes],
        out_shape=[jax.ShapeDtypeStruct((clips, count, n, LW), BF16) for n in sizes],
        scratch_shapes=[frame, wide] * (2 if squeeze else 1),
        input_output_aliases={given + n: n for n in range(len(earlier))},
        compiler_params=params(),
        cost_estimate=pl.CostEstimate(
            flops=300_000_000 * count, bytes_accessed=200_000 * count, transcendentals=0
        ),
    )(rows, weights, kernels, *([kernels] if squeeze else []), *earlier)


def attention_forward(
    q_ref, kv_ref, m1_ref, m2_ref, ke_ref, tab_ref, fold_ref, one_ref, own_ref, lanes_ref, w_ref,
    branch_ref, qa_ref, at_ref, lse_ref, kept_ref, sent_ref, keys, vt, scores, expo, table,
):
    keys[0:ROWS] = kv_ref[0, 0]
    keys[ROWS : ROWS + MROWS] = m1_ref[0, 0]
    keys[ROWS + MROWS :] = m2_ref[0, 0]
    vt[:, 0:ROWS] = kv_ref[0, 1].T
    memory = jnp.concatenate([m1_ref[0, 1], m2_ref[0, 1]], axis=0).T
    vt[:, ROWS:] = memory
    for head in range(LH):
        first = window_of(head)
        variant = head // 2
        win = slice(first, first + WIN)
        heads = lanes_ref[head]
        qm = q_ref[0, 0, :, win] * heads
        table[...] = jnp.zeros_like(table)
        for part in range(2):
            table[part, head * HEAD_DIM - first : (head + 1) * HEAD_DIM - first] = tab_ref[part]
        raw = nn(qm, table[0]) + nn(qm, table[1])
        raw = raw * own_ref[...]
        high = raw.astype(BF16)
        rest = (raw - high.astype(F32)).astype(BF16)
        placed = nn(high, fold_ref[variant, 0]) + nn(rest, fold_ref[variant, 1]) + one_ref[variant, 0:1]
        qa = qm + placed.astype(BF16)
        qa_ref[0, head] = qa.T

        def score(number, peak):
            rows = pl.ds(pl.multiple_of(number * BLOCK, BLOCK), BLOCK)
            ka = keys[rows, win] * heads[0:BLOCK] + ke_ref[0, variant, rows]
            s = nn(ka, qa_ref[0, head])
            scores[rows] = s
            return jnp.maximum(peak, jnp.max(s, axis=0, keepdims=True))

        peak = lax.fori_loop(0, NBLOCK, score, jnp.full((1, ROWS), -3e38, F32), unroll=True)
        shift = peak * (SCALE * LOG2E)

        def soften(number, total):
            rows = pl.ds(pl.multiple_of(number * BLOCK, BLOCK), BLOCK)
            e = jnp.exp2(scores[rows] * (SCALE * LOG2E) - shift)
            expo[rows] = e.astype(BF16)
            return total + jnp.sum(e, axis=0, keepdims=True)

        total = lax.fori_loop(0, NBLOCK, soften, jnp.zeros((1, ROWS), F32), unroll=True)
        out = nn(vt[head * HEAD_DIM : (head + 1) * HEAD_DIM], expo[...]) * (1.0 / total)
        at_ref[0, head * HEAD_DIM : (head + 1) * HEAD_DIM] = out
        lse_ref[0, head : head + 1] = shift + jnp.log2(total)
    branch_ref[0] = (at_ref[0].T + q_ref[0, 0].astype(F32)).astype(BF16)
    side = lax.axis_index("head")
    sent_ref[...] = nn(branch_ref[0, half_rows(1 - side)], w_ref[...]).astype(BF16)
    kept_ref[...] = nn(branch_ref[0, half_rows(side)], w_ref[...])


def whole(shape):
    return pl.BlockSpec(shape, lambda i: (0,) * len(shape))


def clip_block(*shape):
    return pl.BlockSpec((1,) + shape, lambda i: (i,) + (0,) * len(shape))


def call_attention_forward(clip, q, kv, memory, keys_extra, tables, w_proj, consts):
    def block(*shape, at=clip):
        return pl.BlockSpec((1,) + shape, lambda i: (at,) + (0,) * len(shape))

    return pl.pallas_call(
        attention_forward,
        grid=(1,),
        in_specs=[
            block(1, ROWS, LW),
            block(2, ROWS, LW),
            block(2, MROWS, LW, at=clip + 1),
            block(2, MROWS, LW, at=clip),
            block(2, KEYS, WIN),
            whole((2, HEAD_DIM, 256)),
            whole((2, 2, 256, WIN)),
            whole((2, 8, WIN)),
            whole((ROWS, 256)),
            whole((LH, ROWS, WIN)),
            whole(w_proj.shape),
        ],
        out_specs=[
            clip_block(ROWS, LW),
            clip_block(LH, WIN, ROWS),
            clip_block(LW, ROWS),
            clip_block(8, ROWS),
            whole((HALF, w_proj.shape[1])),
            whole((HALF, w_proj.shape[1])),
        ],
        out_shape=[
            jax.ShapeDtypeStruct((1, ROWS, LW), BF16),
            jax.ShapeDtypeStruct((1, LH, WIN, ROWS), BF16),
            jax.ShapeDtypeStruct((1, LW, ROWS), F32),
            jax.ShapeDtypeStruct((1, 8, ROWS), F32),
            jax.ShapeDtypeStruct((HALF, w_proj.shape[1]), F32),
            jax.ShapeDtypeStruct((HALF, w_proj.shape[1]), BF16),
        ],
        scratch_shapes=[
            pltpu.VMEM((KEYS, LW), BF16),
            pltpu.VMEM((LW, KEYS), BF16),
            pltpu.VMEM((KEYS, ROWS), F32),
            pltpu.VMEM((KEYS, ROWS), BF16),
            pltpu.VMEM((2, WIN, 256), BF16),
        ],
        compiler_params=params(),
        cost_estimate=pl.CostEstimate(
            flops=1_300_000_000, bytes_accessed=500_000, transcendentals=0
        ),
    )(q, kv, memory, memory, keys_extra, tables, consts["fold"], consts["one"], consts["own"], consts["lanes"], w_proj)


HALF = ROWS // 2


def simple_call(kernel, out_shape, gflops, *args):
    vmem = pl.BlockSpec(memory_space=pltpu.VMEM)
    many = isinstance(out_shape, list)
    return pl.pallas_call(
        kernel,
        in_specs=[vmem] * len(args),
        out_specs=[vmem] * len(out_shape) if many else vmem,
        out_shape=out_shape,
        compiler_params=params(),
        cost_estimate=pl.CostEstimate(
            flops=int(gflops * 1e8), bytes_accessed=200_000, transcendentals=0
        ),
    )(*args)


def half_rows(side):
    return pl.ds(pl.multiple_of(side * HALF, 16), HALF)


def middle_kernel(tokens, kept, recv, vectors, x1_ref, a2_ref):
    x1 = tokens[...].astype(F32) + kept[...] + recv[...].astype(F32) + vectors[0:1]
    x1_ref[...] = x1
    centred = x1 - jnp.mean(x1, axis=-1, keepdims=True)
    scale = lax.rsqrt(jnp.mean(centred * centred, axis=-1, keepdims=True) + EPSILON)
    a2_ref[...] = (centred * scale * vectors[1:2] + vectors[2:3]).astype(BF16)


FFN_BLOCK = 512
GELU_A = 0.7978845608028654
GELU_B = 0.044715


def joined(refs):
    return jnp.concatenate([ref[...] for ref in refs], axis=0) if len(refs) > 1 else refs[0][...]


def ffn_kernel(count, *refs):
    a2 = joined(refs[:count])
    g = joined(refs[count : 2 * count])
    w1, b1, w2 = refs[2 * count : 2 * count + 3]
    outs = refs[2 * count + 3 :]
    act_refs, dpre_refs, da2_refs, out_refs = (outs[n * count : (n + 1) * count] for n in range(4))
    sums_ref = outs[4 * count]
    da2 = jnp.zeros(a2.shape, F32)
    out = jnp.zeros(a2.shape, F32)
    for first in range(0, w1.shape[1], FFN_BLOCK):
        cols = slice(first, first + FFN_BLOCK)
        pre = nn(a2, w1[:, cols]) + b1[0:1, cols]
        square = pre * pre
        bent = jnp.tanh(GELU_A * (pre + GELU_B * (pre * square)))
        gate = 0.5 + 0.5 * bent
        act = (pre * gate).astype(BF16)
        slope = gate + 0.5 * pre * (1.0 - bent * bent) * (GELU_A * (1.0 + 3.0 * GELU_B * square))
        dpre = nt(g, w2[cols]) * slope
        low = dpre.astype(BF16)
        sums_ref[0:1, cols] = jnp.sum(dpre, axis=0, keepdims=True)
        for n in range(count):
            act_refs[n][:, cols] = act[n * HALF : (n + 1) * HALF]
            dpre_refs[n][:, cols] = low[n * HALF : (n + 1) * HALF]
        da2 = da2 + nt(low, w1[:, cols])
        out = out + nn(act, w2[cols])
    for n in range(count):
        da2_refs[n][...] = da2[n * HALF : (n + 1) * HALF].astype(da2_refs[n].dtype)
        out_refs[n][...] = out[n * HALF : (n + 1) * HALF].astype(out_refs[n].dtype)


def call_ffn(parts, w1, b1, w2):
    hidden, width = w2.shape
    count = len(parts)
    made = simple_call(
        partial(ffn_kernel, count),
        [jax.ShapeDtypeStruct((HALF, hidden), BF16)] * (2 * count)
        + [jax.ShapeDtypeStruct((HALF, width), dtype) for _, _, dtype in parts] * 2
        + [jax.ShapeDtypeStruct((1, hidden), F32)],
        5,
        *[part[0] for part in parts],
        *[part[1] for part in parts],
        w1, b1, w2,
    )
    return [tuple(made[n :: count][:4]) for n in range(count)], made[-1]


def tn(a, b):
    return lax.dot_general(a, b, (((0,), (0,)), ((), ())), preferred_element_type=F32)


def weight_kernel(count, *refs):
    acts, dpres, a2s, gs = (refs[n * count : (n + 1) * count] for n in range(4))
    g2, g1 = refs[4 * count :]
    g2[...] = tn(joined(acts), joined(gs)).astype(BF16)
    g1[...] = tn(joined(a2s), joined(dpres)).astype(BF16)


def call_weights(acts, dpres, a2s, gs):
    hidden, width = acts[0].shape[1], gs[0].shape[1]
    count = len(acts)
    piece = pl.BlockSpec((HALF, LW), lambda i: (0, i))
    full = pl.BlockSpec((HALF, width), lambda i: (0, 0))
    return pl.pallas_call(
        partial(weight_kernel, count),
        grid=(hidden // LW,),
        in_specs=[piece] * (2 * count) + [full] * (2 * count),
        out_specs=[
            pl.BlockSpec((LW, width), lambda i: (i, 0)),
            pl.BlockSpec((width, LW), lambda i: (0, i)),
        ],
        out_shape=[
            jax.ShapeDtypeStruct((hidden, width), BF16),
            jax.ShapeDtypeStruct((width, hidden), BF16),
        ],
        compiler_params=params(),
        cost_estimate=pl.CostEstimate(flops=800_000_000, bytes_accessed=1_500_000, transcendentals=0),
    )(*acts, *dpres, *a2s, *gs)


TABLE_ROWS = (2 * T_LEN - 1, 2 * HGT - 1, 2 * WID - 1, 27, 27, 27, 27, 27)


def widen_kernel(a, b, small, x, y, *tables):
    x[...] = a[...].astype(F32)
    y[...] = b[...].astype(F32)

    @pl.when(pl.program_id(0) == 0)
    def _():
        first = 0
        for rows, table in zip(TABLE_ROWS, tables):
            table[...] = small[first : first + rows, 0:HEAD_DIM]
            first += rows


def call_widen(a, b, small):
    steps = 8
    specs = [pl.BlockSpec((v.shape[0] // steps, v.shape[1]), lambda i: (i, 0)) for v in (a, b)]
    tables = [whole((rows, HEAD_DIM)) for rows in TABLE_ROWS]
    return pl.pallas_call(
        widen_kernel,
        grid=(steps,),
        in_specs=specs + [whole(small.shape)],
        out_specs=specs + tables,
        out_shape=[jax.ShapeDtypeStruct(v.shape, F32) for v in (a, b)]
        + [jax.ShapeDtypeStruct((rows, HEAD_DIM), F32) for rows in TABLE_ROWS],
        compiler_params=params(),
    )(a, b, small)


def norm_back_kernel(kept, recv, x1_ref, g, vectors, dx_ref, low_ref, sums):
    u = kept[...] + recv[...].astype(F32)
    x1 = x1_ref[...]
    centred = x1 - jnp.mean(x1, axis=-1, keepdims=True)
    scale = lax.rsqrt(jnp.mean(centred * centred, axis=-1, keepdims=True) + EPSILON)
    xhat = centred * scale
    w = u * vectors[1:2]
    up = g[...].astype(F32)
    dx = up + scale * (
        w - jnp.mean(w, axis=-1, keepdims=True) - xhat * jnp.mean(w * xhat, axis=-1, keepdims=True)
    )
    dx_ref[...] = dx
    low_ref[...] = dx.astype(BF16)
    sums[0:1] = jnp.sum(dx, axis=0, keepdims=True)
    sums[1:2] = jnp.sum(u * xhat, axis=0, keepdims=True)
    sums[2:3] = jnp.sum(u, axis=0, keepdims=True)
    sums[3:4] = jnp.sum(up, axis=0, keepdims=True)
    sums[4:8] = jnp.zeros((4, u.shape[1]), F32)


def mix_kernel(mine, theirs, w, rows_ref, dmix_ref):
    head = lax.axis_index("head")
    for side, part in ((head, mine), (1 - head, theirs)):
        rows_ref[half_rows(side)] = part[...]
        dmix_ref[half_rows(side)] = nt(part[...], w[...]).astype(BF16)


HEAD_EARLY = 8
MESH = pl.DeviceIdType.MESH


def remote(src, dst, send, recv, peer):
    made = pltpu.make_async_remote_copy(
        src_ref=src, dst_ref=dst, send_sem=send, recv_sem=recv, device_id=peer, device_id_type=MESH
    )
    made.start()
    return made


def local(src, dst, sem):
    made = pltpu.make_async_copy(src, dst, sem)
    made.start()
    return made


class Place:
    def __init__(self, groups):
        dp = lax.axis_index("dp")
        head = lax.axis_index("head")
        self.groups = groups
        self.dp, self.head = dp, head
        self.core = lax.rem(dp, 2)
        self.xbit = lax.rem(lax.div(dp, 2), 2)
        self.group = lax.div(dp, 4)
        self.to_core = (dp + 1 - 2 * self.core, head)
        self.to_x = (dp + 2 - 4 * self.xbit, head)
        self.to_y = (dp, 1 - head)
        self.peers = [
            (lax.rem(self.group + o, groups) * 4 + lax.rem(dp, 4), head) for o in range(1, groups)
        ]
        self.number = (head * groups + self.group) * 2 + self.xbit

    def device(self, number):
        side = lax.div(number, 2 * self.groups)
        group = lax.rem(lax.div(number, 2), self.groups)
        return (group * 4 + lax.rem(number, 2) * 2 + self.core, side)

    def greet(self, more=()):
        barrier = pltpu.get_barrier_semaphore()
        signalled = [self.to_core, self.to_x] + self.peers + list(more)
        for peer in signalled:
            pl.semaphore_signal(barrier, inc=1, device_id=peer, device_id_type=MESH)
        pl.semaphore_wait(barrier, len(signalled))


class Piece:
    def __init__(self, place, rows, source, result, reduce_refs, send, recv):
        self.at = place
        self.half, self.quarter = rows // 2, rows // 4
        self.chunk = rows // 4 // place.groups
        self.source, self.result = source, result
        self.refs = reduce_refs
        self.send, self.recv = send, recv
        self.tile = 16 if reduce_refs is None or reduce_refs[0].dtype == BF16 else 8
        self.flights = {}

    def start(self, key, number, src, dst, peer):
        self.flights[key] = remote(src, dst, self.send.at[number], self.recv.at[number], peer)

    def base(self, g):
        at = self.at
        return pl.multiple_of(at.core * self.half + at.xbit * self.quarter + g * self.chunk, self.tile)

    def a(self):
        theirs = pl.multiple_of((1 - self.at.core) * self.half, self.tile)
        self.start("a", 0, self.source(theirs, self.half), self.refs[0], self.at.to_core)

    def sum_rows(self, which):
        recv_a = self.refs[0]
        first = pl.multiple_of(which * self.quarter, self.tile)
        own = self.source(pl.multiple_of(self.at.core * self.half + which * self.quarter, self.tile), self.quarter)
        return own[...].astype(F32) + recv_a[pl.ds(first, self.quarter)].astype(F32)

    def b(self):
        _, send_b, recv_b, _, _ = self.refs
        self.flights["a"].wait()
        send_b[...] = self.sum_rows(1 - self.at.xbit).astype(send_b.dtype)
        self.start("b", 1, send_b, recv_b, self.at.to_x)

    def c(self):
        _, _, recv_b, send_c, recv_c = self.refs
        self.flights["b"].wait()
        send_c[...] = (self.sum_rows(self.at.xbit) + recv_b[...].astype(F32)).astype(send_c.dtype)
        for o in range(1, self.at.groups):
            first = pl.multiple_of(lax.rem(self.at.group + o, self.at.groups) * self.chunk, self.tile)
            self.start(
                ("c", o), 1 + o, send_c.at[pl.ds(first, self.chunk)], recv_c.at[o - 1], self.at.peers[o - 1]
            )

    def total(self):
        _, _, _, send_c, recv_c = self.refs
        own = send_c[pl.ds(pl.multiple_of(self.at.group * self.chunk, self.tile), self.chunk)].astype(F32)
        for o in range(1, self.at.groups):
            self.flights["c", o].wait()
            own = own + recv_c[o - 1].astype(F32)
        return own

    def d(self, own=None):
        own = self.total() if own is None else own
        mine = self.result(self.base(self.at.group), self.chunk)
        mine[...] = own.astype(mine.dtype)
        for o in range(1, self.at.groups):
            number = self.at.groups + o
            self.start(("d", o), number, mine, mine, self.at.peers[o - 1])

    def e(self):
        for o in range(1, self.at.groups):
            self.flights["d", o].wait()
        mine = self.result(self.base(0), self.quarter)
        self.start("e", 2 * self.at.groups, mine, mine, self.at.to_x)

    def f(self):
        self.flights["e"].wait()
        mine = self.result(pl.multiple_of(self.at.core * self.half, self.tile), self.half)
        self.start("f", 2 * self.at.groups + 1, mine, mine, self.at.to_core)

    def g(self):
        self.flights["f"].wait()


def piece_scratch(rows, groups, width, dtype, count):
    half, quarter = rows // 2, rows // 4
    return [
        pltpu.VMEM((count, half, width), dtype),
        pltpu.VMEM((count, quarter, width), dtype),
        pltpu.VMEM((count, quarter, width), dtype),
        pltpu.VMEM((count, quarter, width), dtype),
        pltpu.VMEM((count, groups - 1, quarter // groups, width), dtype),
    ]


class Tiny:
    def __init__(self, place, source, result, refs, send, recv):
        self.at, self.source, self.result = place, source, result
        self.recv_core, self.summed, self.slots = refs
        self.send, self.recv = send, recv
        count = 4 * place.groups
        self.half, self.chunk = source.shape[0] // 2, source.shape[0] // 2 // count
        self.mine = place.number
        self.others = [lax.rem(place.number + o, count) for o in range(1, count)]
        self.flights = {}

    def rows(self, number):
        return pl.ds(pl.multiple_of(number * self.chunk, 8), self.chunk)

    def halves(self, core):
        return pl.ds(pl.multiple_of(core * self.half, 8), self.half)

    def start(self, key, src, dst, peer):
        number = len(self.flights)
        self.flights[key] = remote(src, dst, self.send.at[number], self.recv.at[number], peer)

    def a(self):
        self.start("a", self.source.at[self.halves(1 - self.at.core)], self.recv_core, self.at.to_core)

    def b(self):
        self.flights["a"].wait()
        self.summed[...] = self.source[self.halves(self.at.core)] + self.recv_core[...]
        for o, number in enumerate(self.others):
            self.start(("b", o), self.summed.at[self.rows(number)], self.slots.at[o], self.at.device(number))

    def c(self):
        total = self.summed[self.rows(self.mine)]
        for o, number in enumerate(self.others):
            self.flights["b", o].wait()
            total = total + self.slots[o]
        rows = pl.ds(pl.multiple_of(self.at.core * self.half + self.mine * self.chunk, 8), self.chunk)
        self.result[rows] = total
        for o, number in enumerate(self.others):
            self.start(("c", o), self.result.at[rows], self.result.at[rows], self.at.device(number))

    def d(self):
        for o in range(len(self.others)):
            self.flights["c", o].wait()
        rows = self.halves(self.at.core)
        self.start("d", self.result.at[rows], self.result.at[rows], self.at.to_core)

    def e(self):
        self.flights["d"].wait()


class Burst:
    def __init__(self, place, source, refs, send, recv):
        self.at, self.source = place, source
        self.recv_core, self.summed, self.slots = refs
        self.send, self.recv = send, recv
        count = 4 * place.groups
        self.others = [lax.rem(place.number + o, count) for o in range(1, count)]
        self.flights = []

    def start(self, src, dst, peer):
        number = len(self.flights)
        self.flights.append(remote(src, dst, self.send.at[number], self.recv.at[number], peer))

    def a(self):
        self.start(self.source, self.recv_core, self.at.to_core)

    def b(self):
        self.flights[0].wait()
        self.summed[...] = self.source[...] + self.recv_core[...]
        for o, number in enumerate(self.others):
            self.start(self.summed, self.slots.at[o], self.at.device(number))

    def c(self, target):
        total = self.summed[...]
        for o, made in enumerate(self.flights[1:]):
            made.wait()
            total = total + self.slots[o]
        target[...] = total


def attention_backward(
    groups,
    q_ref, kv_ref, mem_ref, ke_hbm, qa_hbm0, qa_hbm1, dm_ref0, dm_ref1, at_hbm0, at_hbm1, lse_ref0, lse_ref1,
    rt_ref, grow_ref, ownt_ref, ekey_ref,
    lanes_ref, g2_ref, g1_ref,
    dq_ref, dkv_ref, dr_ref, chunks_ref, out2,
    ke_ref, qa_ref, at_ref, keys, values, kt, dmt, qms, dms, dmst, dqt,
    recv_a, send_b, recv_b, send_c, recv_c,
    loads, sems_send, sems_recv,
):
    place = Place(groups)
    clips = q_ref.shape[0]
    dm_refs, lse_refs = (dm_ref0, dm_ref1), (lse_ref0, lse_ref1)
    lead = [
        [
            local(ke_hbm.at[clip], ke_ref.at[clip], loads.at[3 * clip]),
            local((qa_hbm0, qa_hbm1)[clip].at[0], qa_ref.at[clip], loads.at[3 * clip + 1]),
            local((at_hbm0, at_hbm1)[clip].at[0], at_ref.at[clip], loads.at[3 * clip + 2]),
        ]
        for clip in range(clips)
    ]
    place.greet()
    total = g1_ref.shape[0]

    def view(number, ref):
        if number < 4:
            base, col = (number // 2) * total, (number % 2) * LW
            return lambda first, n: ref.at[pl.ds(base + first, n), col : col + LW]
        col = (number - 4) * LW
        return lambda first, n: g1_ref.at[pl.ds(first, n), col : col + LW]

    pieces = [
        Piece(
            place, total, view(number, g2_ref), view(number, out2) if number < 4 else None,
            [ref.at[number] for ref in (recv_a, send_b, recv_b, send_c, recv_c)],
            sems_send.at[number], sems_recv.at[number],
        )
        for number in range(8)
    ]
    moves = [
        [pieces[0].a],
        [pieces[0].b, pieces[1].a],
        [pieces[2].a],
        [pieces[1].b, pieces[3].a],
        [pieces[4].a],
        [pieces[0].c, pieces[2].b, pieces[5].a],
        [pieces[6].a],
        [pieces[1].c, pieces[3].b, pieces[7].a],
        [],
        [pieces[0].d, pieces[4].b],
        [],
        [pieces[1].d, pieces[5].b],
        [],
        [pieces[0].e, pieces[2].c],
        [],
        [pieces[1].e, pieces[3].c],
        [],
        [pieces[0].f, pieces[2].d, pieces[6].b],
        [pieces[1].f, pieces[3].d, pieces[7].b, pieces[2].e, pieces[4].c, pieces[5].c, pieces[3].e, pieces[2].f, pieces[6].c, pieces[3].f, pieces[7].c],
    ]

    def pump():
        if moves:
            for move in moves.pop(0):
                move()

    dr_ref[...] = jnp.zeros_like(dr_ref)
    for clip in range(clips):
        pump()
        near, far = mem_ref.at[clip + 1], mem_ref.at[clip]
        keys[0:ROWS] = kv_ref[clip, 0]
        keys[ROWS : ROWS + MROWS] = near[0]
        keys[ROWS + MROWS :] = far[0]
        values[0:ROWS] = kv_ref[clip, 1]
        values[ROWS : ROWS + MROWS] = near[1]
        values[ROWS + MROWS :] = far[1]
        kt[0:LW] = keys[...].T
        kt[LW:] = ekey_ref[...]
        dmt[...] = dm_refs[clip][...].astype(F32).T
        dqt[...] = jnp.zeros_like(dqt)
        for made in lead[clip]:
            made.wait()
        deltas = []
        for head in range(LH):
            first = window_of(head)
            win = slice(first, first + WIN)
            span = slice(head * HEAD_DIM, (head + 1) * HEAD_DIM)
            qms[head] = q_ref[clip, 0, :, win] * lanes_ref[head]
            dms[head] = dm_refs[clip][:, win] * lanes_ref[head]
            dmst[head] = jnp.zeros(dmst.shape[1:], BF16)
            dmst[head, head * HEAD_DIM - first : (head + 1) * HEAD_DIM - first] = dmt[span].astype(BF16)
            deltas.append(jnp.sum(dmt[span] * at_ref[clip, span], axis=0, keepdims=True))

        def step(number, _):
            rows = slice(number * BLOCK, number * BLOCK + BLOCK)
            dk_parts, dv_parts = [], []
            for head in range(LH):
                first = window_of(head)
                variant = head // 2
                win = slice(first, first + WIN)
                ka = keys[rows, win] * lanes_ref[head, 0:BLOCK] + ke_ref[clip, variant, rows]
                s = nn(ka, qa_ref[clip, head])
                p = jnp.exp2(s * (SCALE * LOG2E) - lse_refs[clip][0, head : head + 1])
                dp = nn(values[rows, win], dmst[head])
                ds = (p * (dp - deltas[head])).astype(BF16)
                dv_parts.append(nn(p.astype(BF16), dms[head]))
                dk_parts.append(nn(ds, qms[head]) * SCALE)
                kts = jnp.concatenate(
                    [kt[head * HEAD_DIM : (head + 1) * HEAD_DIM, rows], kt[LW:, rows]], axis=0
                )
                dqt[head] += nn(kts, ds)
            for which, parts in ((0, dk_parts), (1, dv_parts)):
                dkv_ref[clip, which, rows] = jnp.concatenate(
                    [
                        parts[0][:, 0:128] + parts[1][:, 0:128],
                        parts[1][:, 128:256] + parts[2][:, 0:128],
                        parts[2][:, 128:256] + parts[3][:, 128:256],
                    ],
                    axis=1,
                )
            return 0

        for number in range(NBLOCK):
            pump()
            step(number, 0)
        pump()
        for head in range(LH):
            first = window_of(head)
            span = slice(head * HEAD_DIM, (head + 1) * HEAD_DIM)
            total_t = dqt[head]
            grown = nn(grow_ref[...], total_t[HEAD_DIM:].astype(BF16)) * ownt_ref[...]
            grown = grown.astype(BF16)
            dmt[span] = dmt[span] + total_t[0:HEAD_DIM] * SCALE + nn(rt_ref[...], grown)
            dr_ref[:, first : first + WIN] += nn(grown, qms[head])
        dq_ref[clip] = dmt[...].T
    while moves:
        pump()
    for number in range(4):
        pieces[number].g()
        chunks_ref[number] = pieces[4 + number].total().astype(BF16)


def padded_rows(width, groups):
    return -(-width // (4 * groups) // 16) * 16 * 4 * groups


def call_attention_backward(q, kv, memory, keys_extra, qa, dmix, at, lse, rt, g2, g1, consts):
    clips, width = q.shape[0], g2.shape[1]
    groups = lax.axis_size("dp") // 4
    total = padded_rows(width, groups)
    if total != width:
        g1 = jnp.pad(g1, ((0, total - width), (0, 0)))
        g2 = jnp.pad(g2.reshape(2, width, width), ((0, 0), (0, total - width), (0, 0))).reshape(-1, width)
    vmem = pl.BlockSpec(memory_space=pltpu.VMEM)
    hbm = pl.BlockSpec(memory_space=pl.ANY)
    return pl.pallas_call(
        partial(attention_backward, groups),
        in_specs=[vmem] * 3 + [hbm] * 3 + [vmem] * 2 + [hbm] * 2 + [vmem] * 9,
        out_specs=[vmem] * 5,
        out_shape=[
            jax.ShapeDtypeStruct((clips, ROWS, LW), F32),
            jax.ShapeDtypeStruct((clips, 2, KEYS, LW), F32),
            jax.ShapeDtypeStruct((256, LW), F32),
            jax.ShapeDtypeStruct((4, total // 4 // groups, LW), BF16),
            jax.ShapeDtypeStruct(g2.shape, BF16),
        ],
        scratch_shapes=[
            pltpu.VMEM(keys_extra.shape, BF16),
            pltpu.VMEM((clips, LH, WIN, ROWS), BF16),
            pltpu.VMEM((clips, LW, ROWS), F32),
            pltpu.VMEM((KEYS, LW), BF16),
            pltpu.VMEM((KEYS, LW), BF16),
            pltpu.VMEM((LW + 32, KEYS), BF16),
            pltpu.VMEM((LW, ROWS), F32),
            pltpu.VMEM((LH, ROWS, WIN), BF16),
            pltpu.VMEM((LH, ROWS, WIN), BF16),
            pltpu.VMEM((LH, WIN, ROWS), BF16),
            pltpu.VMEM((LH, HEAD_DIM + 32, ROWS), F32),
            *piece_scratch(total, groups, LW, BF16, 8),
            pltpu.SemaphoreType.DMA((3 * clips,)),
            pltpu.SemaphoreType.DMA((8, 2 * groups + 2)),
            pltpu.SemaphoreType.DMA((8, 2 * groups + 2)),
        ],
        compiler_params=params(collective_id=0, has_side_effects=True),
        cost_estimate=pl.CostEstimate(
            flops=40_000_000_000, bytes_accessed=20_000_000, transcendentals=3_000_000
        ),
    )(
        q, kv, memory, keys_extra, *qa, *dmix, *at, *lse, rt,
        consts["grow"], consts["ownt"], consts["ekey"], consts["lanes"], g2, g1,
    )


REL_ROWS = 48
TAP_ROW = NREL
EARLY_ROW = TAP_ROW + 5 * 27
NORM_ROWS = 16
HIDDEN_ROW = EARLY_ROW + 24
SMALL_ROWS = HIDDEN_ROW + 24


def finish_kernel(
    groups, width,
    dq_hbm, dkv_hbm, x0q_hbm, x0kv_hbm, kvf_hbm, rows_taps, rows_a0, rows_a1, rows_x0, rows_x1, branch0, branch1,
    w_hbm, tokens_hbm, middle0, middle1, chunks_ref, dr_ref, gain, foldl_ref, pick_ref,
    sums0, sums1, hidden0, hidden1, hidden2,
    grad, out1, outp, outq, small_out, norm_out,
    dq, dkv, x0q, x0kv, kvf, taps_ref, rows_a, rows_x, branch, w_ref, tokens, middle,
    us, ms, kacc, dx, dmem_send, dmem_recv, resp, grads, stage_t,
    recv_a, send_b, recv_b, send_c, recv_c,
    strips, strip_res, strip_a, strip_b, strip_bb, strip_c, strip_cc,
    sm, sm_res, sm_core, sm_sum, sm_slots, nm, nm_core, nm_sum, nm_slots, send_y, recv_y,
    loads, stores, sems_send, sems_recv, tiny_send, tiny_recv, burst_send, burst_recv, cross_send, cross_recv, mem_sems,
):
    place = Place(groups)
    clips = dq.shape[0]
    total = rows_a.shape[1]
    names = (
        "dkv", "dq", "x0q", "rows_x0", "rows_x1", "branch0", "branch1", "x0kv", "kvf", "rows_a0", "rows_a1", "w",
        "tokens", "middle0", "middle1",
    )
    pairs = (
        (dkv_hbm, dkv), (dq_hbm, dq), (x0q_hbm, x0q),
        (rows_x0, rows_x.at[0:ROWS]), (rows_x1, rows_x.at[ROWS:]), (branch0, branch.at[0:ROWS]),
        (branch1, branch.at[ROWS:]), (x0kv_hbm, x0kv), (kvf_hbm, kvf), (rows_a0, rows_a.at[0:ROWS]),
        (rows_a1, rows_a.at[ROWS:]), (w_hbm, w_ref),
        (tokens_hbm, tokens), (middle0, middle.at[0]), (middle1, middle.at[1]),
    )
    lead = {
        name: local(src, dst, loads.at[n]) for n, (name, (src, dst)) in enumerate(zip(names, pairs))
    }
    count = groups * 4
    behind = (lax.rem(place.dp + count - 1, count), place.head)
    ahead = (lax.rem(place.dp + 1, count), place.head)
    others = [place.device(lax.rem(place.number + o, count)) for o in range(1, count)]
    barrier = pltpu.get_barrier_semaphore()
    for peer in [place.to_core, behind, ahead] + others:
        pl.semaphore_signal(barrier, inc=1, device_id=peer, device_id_type=MESH)
    pl.semaphore_wait(barrier, 3 + len(others))

    def strip_of(number):
        return lambda first, n: out1.at[pl.ds(first, n), number * LW : number * LW + LW]

    ffn = [
        Piece(place, total, None, strip_of(number), None, sems_send.at[number], sems_recv.at[number])
        for number in range(4)
    ]

    def rows_of(ref):
        return lambda first, n: ref.at[pl.ds(first, n)]

    late = [
        Piece(
            place, total, rows_of(grads.at[number]), rows_of(resp.at[number]),
            [ref.at[number] for ref in (recv_a, send_b, recv_b, send_c, recv_c)],
            sems_send.at[4 + number], sems_recv.at[4 + number],
        )
        for number in range(2)
    ] + [
        Piece(
            place, total, rows_of(strips.at[number]), rows_of(strip_res.at[number]),
            [ref.at[number] for ref in (strip_a, strip_b, strip_bb, strip_c, strip_cc)],
            sems_send.at[6 + number], sems_recv.at[6 + number],
        )
        for number in range(6)
    ]
    burst = Burst(place, nm, (nm_core, nm_sum, nm_slots), burst_send, burst_recv)
    tiny = Tiny(place, sm, sm_res, (sm_core, sm_sum, sm_slots), tiny_send, tiny_recv)

    def product(number):
        if number < 2:
            left, right, target = (rows_x, branch, grads.at[0]) if number == 0 else (rows_a, dx.at[0], grads.at[1])
            lanes = slice(0, LW)
        else:
            left, right, target = rows_a, dx.at[1 + (number - 2) // 3], strips.at[number - 2]
            lanes = slice((number - 2) % 3 * 128, (number - 2) % 3 * 128 + 128)
        for first in range(0, total, total // 2):
            target[first : first + total // 2] = tn(
                left[:, first : first + total // 2], right[:, lanes]
            ).astype(BF16)
        late[number].a()

    def shifted_store(dst, first, both, lanes):
        both = both.reshape(2 * HGT, PADW, 128)
        for c, shift in ((0, 1), (1, 0), (2, PADW - 1)):
            moved = pltpu.roll(both, shift, axis=1) if shift else both
            dst[c, pl.ds(first, 2), 1 : HGT + 1, :, lanes] = moved.reshape(2, HGT, PADW, 128)

    def prepare(which, clip):
        if which:
            memory = dmem_recv[clip, which - 1].astype(F32)
            memory = jnp.where(place.dp == count - 1, 0.0, memory)
            for later in range(clip + 1, clips):
                if later == clip + 1:
                    memory = memory + dkv[later, which - 1, ROWS : ROWS + MROWS]
                if later == clip + 2:
                    memory = memory + dkv[later, which - 1, ROWS + MROWS :]
            spread(ms, 0, memory.reshape(TM, HGT, PADW, LW))
        else:
            spread(us, 1, dq[clip].reshape(T_LEN, HGT, PADW, LW))

    def pooled(which, clip, tile):
        field = x0q.at[clip, 0] if which == 0 else x0kv.at[clip, which - 1]
        upstream = dq.at[clip] if which == 0 else dkv.at[clip, which - 1]
        if tile == 0:
            prepare(which, clip)
        lanes = slice(tile * 128, tile * 128 + 128)
        if which:

            def squeeze_step(pair, _):
                rows = pl.ds(pl.multiple_of(pair * 112, 112), 112)
                own = upstream[rows, lanes].reshape(2, HGT, PADW, 128)
                fields = kvf[clip, which - 1, rows, lanes].astype(F32).reshape(2, HGT, PADW, 128)
                acc = [own[0], own[1]]
                for a, d, frame in ((1, 0, 0), (0, 1, 1), (2, 1, 0)):
                    for c in range(3):
                        block = ms[2 - c, pair + frame, :, :, lanes]
                        for b in range(3):
                            at = block[2 - b : 2 - b + HGT]
                            number = a * 9 + b * 3 + c
                            acc[d] = acc[d] + taps_ref[2 + which, number, :, lanes][None] * at
                            kacc[2 + which, number, :, lanes] += jnp.sum(fields[d] * at, axis=0)
                shifted_store(us, 2 * pair + 1, keep_rows(jnp.stack(acc)), lanes)
                return 0

            lax.fori_loop(0, TM, squeeze_step, 0)

        def pair_step(pair, _):
            rows = pl.ds(pl.multiple_of(pair * 112, 112), 112)
            fields = field[rows, lanes].astype(F32).reshape(2, HGT, PADW, 128)
            acc = [jnp.zeros((HGT, PADW, 128), F32) for _ in range(2)]
            for a in range(3):
                for c in range(3):
                    sums = [jnp.zeros((PADW, 128), F32) for _ in range(3)]
                    for d in range(2):
                        block = us[2 - c, 2 * pair + d + 2 - a, :, :, lanes]
                        for b in range(3):
                            at = block[2 - b : 2 - b + HGT]
                            acc[d] = acc[d] + taps_ref[which, a * 9 + b * 3 + c, :, lanes][None] * at
                            sums[b] = sums[b] + jnp.sum(fields[d] * at, axis=0)
                    for b in range(3):
                        kacc[which, a * 9 + b * 3 + c, :, lanes] += sums[b]
            both = keep_rows(jnp.stack(acc))
            out_rows = pl.ds(pl.multiple_of(clip * ROWS + pair * 112, 16), 112)
            dx[which, out_rows, lanes] = both.reshape(112, 128).astype(BF16)
            return 0

        lax.fori_loop(0, T_LEN // 2, pair_step, 0)

    side_rows = ROWS // 2

    def input_gradient(clip, side):
        rows = pl.ds(pl.multiple_of(clip * ROWS + side * side_rows, 16), side_rows)
        return nt(dx[0, rows], w_ref[0]) + nt(dx[1, rows], w_ref[1]) + nt(dx[2, rows], w_ref[2])

    crossing = {}

    def cross(clip):
        send_y[clip] = input_gradient(clip, 1 - place.head).astype(BF16)
        crossing[clip] = remote(
            send_y.at[clip], recv_y.at[clip], cross_send.at[clip], cross_recv.at[clip], place.to_y
        )

    def normed_gradient(clip):
        mine = input_gradient(clip, place.head)
        crossing[clip].wait()
        u = mine + recv_y[clip].astype(F32)
        v = tokens[clip].astype(F32)
        centred = v - jnp.mean(v, axis=-1, keepdims=True)
        scale = lax.rsqrt(jnp.mean(centred * centred, axis=-1, keepdims=True) + EPSILON)
        xhat = centred * scale
        w = u * gain[0:1]
        dv = scale * (
            w - jnp.mean(w, axis=-1, keepdims=True) - xhat * jnp.mean(w * xhat, axis=-1, keepdims=True)
        )
        grad[clip] = middle[clip] + dv
        for which, value in enumerate((u * xhat, u)):
            value = jnp.sum(value, axis=0, keepdims=True)
            for n in range(width // 128):
                row = which * (width // 128) + n
                nm[row : row + 1] += value[:, n * 128 : n * 128 + 128]

    def exact(a, b):
        return jnp.dot(a, b, precision=HIGHEST, preferred_element_type=F32)

    def small_first():
        sm[...] = jnp.zeros_like(sm)
        nm[...] = jnp.zeros_like(nm)
        folded = exact(dr_ref[...], foldl_ref[...])
        sm[0:NREL] = exact(pick_ref[...], folded)[0:NREL]
        early = sums0[...] + sums1[...]
        hidden = hidden0[...] + hidden1[...] + hidden2[...]
        strip = width // 128
        for which in range(4):
            for n in range(strip):
                row = EARLY_ROW + which * strip + n
                sm[row : row + 1] = early[which : which + 1, n * 128 : n * 128 + 128]
        count_h = hidden.shape[1] // 128
        for side in range(2):
            for n in range(count_h):
                row = HIDDEN_ROW + side * count_h + n
                part = hidden[:, n * 128 : n * 128 + 128]
                sm[row : row + 1] = jnp.where(place.head == side, part, 0.0)

    def small_taps(which):
        first = TAP_ROW + 27 * which
        sums = jnp.sum(kacc[which], axis=1)
        sums = jnp.concatenate([sums, jnp.zeros((5, LW), F32)], axis=0)
        sm[first : first + 27] = exact(sums, foldl_ref[...])[0:27]

    ffn[0].d(chunks_ref[0])
    us[...] = jnp.zeros_like(us)
    ms[...] = jnp.zeros_like(ms)
    kacc[...] = jnp.zeros_like(kacc)
    for which in range(5):
        taps_ref[which] = widened(rows_taps[which])
    small_first()
    lead["dkv"].wait()
    for which in range(2):
        dmem_send[0, which] = dkv[0, which, ROWS + MROWS :].astype(BF16)
        dmem_send[1, which] = (
            dkv[0, which, ROWS : ROWS + MROWS] + dkv[1, which, ROWS + MROWS :]
        ).astype(BF16)
    memory_flight = remote(dmem_send, dmem_recv, mem_sems.at[0], mem_sems.at[1], behind)
    for name in ("rows_x0", "rows_x1", "branch0", "branch1"):
        lead[name].wait()
    product(0)
    for name in ("dq", "x0q"):
        lead[name].wait()
    pooled(0, 0, 0)
    pooled(0, 0, 1)
    late[0].b()
    pooled(0, 0, 2)
    ffn[1].d(chunks_ref[1])
    pooled(0, 1, 0)
    pooled(0, 1, 1)
    ffn[0].e()
    pooled(0, 1, 2)
    ffn[2].d(chunks_ref[2])
    lead["rows_a0"].wait()
    lead["rows_a1"].wait()
    product(1)
    small_taps(0)
    memory_flight.wait()
    lead["x0kv"].wait()
    lead["kvf"].wait()
    pooled(1, 0, 0)
    late[1].b()
    late[0].c()
    pooled(1, 0, 1)
    ffn[0].f()
    pooled(1, 0, 2)
    ffn[1].e()
    ffn[3].d(chunks_ref[3])
    pooled(2, 0, 0)
    ffn[0].g()
    pooled(2, 0, 1)
    late[0].d()
    ffn[2].e()
    pooled(2, 0, 2)
    lead["w"].wait()
    cross(0)
    ffn[1].f()
    pooled(1, 1, 0)
    late[1].c()
    ffn[1].g()
    ffn[3].e()
    product(2)
    pooled(1, 1, 1)
    ffn[2].f()
    product(3)
    pooled(1, 1, 2)
    late[2].b()
    ffn[2].g()
    product(4)
    late[3].b()
    late[1].d()
    small_taps(1)
    small_taps(3)
    late[0].e()
    ffn[3].f()
    pooled(2, 1, 0)
    ffn[3].g()
    product(5)
    late[2].c()
    pooled(2, 1, 1)
    late[3].c()
    late[4].b()
    product(6)
    late[5].b()
    pooled(2, 1, 2)
    late[2].d()
    late[6].b()
    late[0].f()
    cross(1)
    late[3].d()
    late[1].e()
    product(7)
    late[0].g()
    stage_t[...] = resp[0].astype(F32).T
    sent = [local(stage_t, outp, stores.at[2])]
    late[4].c()
    small_taps(2)
    small_taps(4)
    tiny.a()
    for name in ("tokens", "middle0", "middle1"):
        lead[name].wait()
    normed_gradient(0)
    late[5].c()
    late[2].e()
    tiny.b()
    late[6].c()
    late[3].e()
    late[4].d()
    late[7].b()
    late[1].f()
    late[5].d()
    late[2].f()
    late[1].g()
    sent.append(local(resp.at[1], outq.at[0], stores.at[3]))
    late[6].d()
    late[2].g()
    sent.append(local(strip_res.at[0], outq.at[1, :, 0 : 128], stores.at[4]))
    late[3].f()
    tiny.c()
    late[4].e()
    late[7].c()
    late[3].g()
    sent.append(local(strip_res.at[1], outq.at[1, :, 128 : 256], stores.at[5]))
    normed_gradient(1)
    burst.a()
    late[5].e()
    late[6].e()
    late[4].f()
    late[7].d()
    burst.b()
    tiny.d()
    late[4].g()
    sent.append(local(strip_res.at[2], outq.at[1, :, 256 : 384], stores.at[6]))
    tiny.e()
    small_out[...] = sm_res[...]
    late[5].f()
    late[6].f()
    late[5].g()
    sent.append(local(strip_res.at[3], outq.at[2, :, 0 : 128], stores.at[7]))
    late[7].e()
    late[6].g()
    sent.append(local(strip_res.at[4], outq.at[2, :, 128 : 256], stores.at[8]))
    burst.c(norm_out)
    late[7].f()
    late[7].g()
    sent.append(local(strip_res.at[5], outq.at[2, :, 256 : 384], stores.at[9]))
    for made in sent:
        made.wait()


def call_finish(
    dq, dkv, x0q, x0kv, kvf, all_taps, rows_a, rows_x, branch, weights, tokens, middle, chunks, dr, gain, sums, hidden
):
    groups = lax.axis_size("dp") // 4
    width = tokens.shape[2]
    total = padded_rows(width, groups)
    clips, side = tokens.shape[:2]
    if total != width:
        extra = ((0, 0), (0, total - width))
        rows_a, rows_x = [jnp.pad(x, extra) for x in rows_a], [jnp.pad(x, extra) for x in rows_x]
    small_rows = -(-SMALL_ROWS // (64 * groups)) * 64 * groups
    foldl = np.zeros((LW, 128), np.float32)
    foldl[np.arange(LW), np.arange(LW) % HEAD_DIM] = 1
    pick = np.zeros((REL_ROWS, 256), np.float32)
    pick[:NREL] = PICK.T
    vmem = pl.BlockSpec(memory_space=pltpu.VMEM)
    hbm = pl.BlockSpec(memory_space=pl.ANY)
    streamed = [dq, dkv, x0q, x0kv, kvf, all_taps, *rows_a, *rows_x, *branch, weights, tokens, *middle]
    held = [
        (array.shape, array.dtype)
        for array in (dq, dkv, x0q, x0kv, kvf)
    ] + [
        ((5, 27, 8, LW), F32), ((clips * ROWS, total), BF16),
        ((clips * ROWS, total), BF16), ((clips * ROWS, LW), BF16), (weights.shape, BF16), (tokens.shape, BF16),
        (tokens.shape, F32),
    ]
    frame = pltpu.VMEM((3, T_LEN + 2, HGT + 2, PADW, LW), F32)
    return pl.pallas_call(
        partial(finish_kernel, groups, width),
        in_specs=[hbm] * 5 + [vmem] + [hbm] * (len(streamed) - 6) + [vmem] * 10,
        out_specs=[vmem, vmem, hbm, hbm, vmem, vmem],
        out_shape=[
            jax.ShapeDtypeStruct(tokens.shape, F32),
            jax.ShapeDtypeStruct((total, 4 * LW), BF16),
            jax.ShapeDtypeStruct((LW, total), F32),
            jax.ShapeDtypeStruct((3, total, LW), BF16),
            jax.ShapeDtypeStruct((small_rows, 128), F32),
            jax.ShapeDtypeStruct((NORM_ROWS, 128), F32),
        ],
        scratch_shapes=[pltpu.VMEM(shape, dtype) for shape, dtype in held]
        + [
            frame,
            pltpu.VMEM((3, TM + 1, HGT + 2, PADW, LW), F32),
            pltpu.VMEM((5, 27, 8, LW), F32),
            pltpu.VMEM((3, clips * ROWS, LW), BF16),
            pltpu.VMEM((2, 2, MROWS, LW), BF16),
            pltpu.VMEM((2, 2, MROWS, LW), BF16),
            pltpu.VMEM((2, total, LW), BF16),
            pltpu.VMEM((2, total, LW), BF16),
            pltpu.VMEM((LW, total), F32),
            *piece_scratch(total, groups, LW, BF16, 2),
            pltpu.VMEM((6, total, 128), BF16),
            pltpu.VMEM((6, total, 128), BF16),
            *piece_scratch(total, groups, 128, BF16, 6),
            pltpu.VMEM((small_rows, 128), F32),
            pltpu.VMEM((small_rows, 128), F32),
            pltpu.VMEM((small_rows // 2, 128), F32),
            pltpu.VMEM((small_rows // 2, 128), F32),
            pltpu.VMEM((4 * groups - 1, small_rows // 8 // groups, 128), F32),
            pltpu.VMEM((NORM_ROWS, 128), F32),
            pltpu.VMEM((NORM_ROWS, 128), F32),
            pltpu.VMEM((NORM_ROWS, 128), F32),
            pltpu.VMEM((4 * groups - 1, NORM_ROWS, 128), F32),
            pltpu.VMEM((clips, side, width), BF16),
            pltpu.VMEM((clips, side, width), BF16),
            pltpu.SemaphoreType.DMA((16,)),
            pltpu.SemaphoreType.DMA((10,)),
            pltpu.SemaphoreType.DMA((12, 2 * groups + 2)),
            pltpu.SemaphoreType.DMA((12, 2 * groups + 2)),
            pltpu.SemaphoreType.DMA((8 * groups,)),
            pltpu.SemaphoreType.DMA((8 * groups,)),
            pltpu.SemaphoreType.DMA((4 * groups,)),
            pltpu.SemaphoreType.DMA((4 * groups,)),
            pltpu.SemaphoreType.DMA((clips,)),
            pltpu.SemaphoreType.DMA((clips,)),
            pltpu.SemaphoreType.DMA((2,)),
        ],
        compiler_params=params(collective_id=1, has_side_effects=True),
        cost_estimate=pl.CostEstimate(
            flops=60_000_000_000, bytes_accessed=40_000_000, transcendentals=0
        ),
    )(*streamed, chunks, dr, gain, jnp.asarray(foldl), jnp.asarray(pick), *sums, *hidden)


def from_behind(x, axis, by):
    count = lax.axis_size(axis)
    pairs = [(i, i + by) for i in range(count) if 0 <= i + by < count]
    return lax.ppermute(x, axis, pairs)


def layer_norm(values, scaling, offset):
    average = jnp.mean(values, axis=-1, keepdims=True)
    centred = values - average
    variance = jnp.mean(centred * centred, axis=-1, keepdims=True)
    return centred * lax.rsqrt(variance + EPSILON) * scaling + offset


def pad_rows(x):
    lead = x.shape[0]
    frames = x.shape[1] // (HGT * WID)
    grid = x.reshape(lead, frames, HGT, WID, x.shape[-1])
    grid = jnp.pad(grid, ((0, 0), (0, 0), (0, 0), (0, PADW - WID), (0, 0)))
    return grid.reshape(lead, frames * HGT * PADW, x.shape[-1])


def drop_rows(x):
    lead = x.shape[0]
    frames = x.shape[1] // (HGT * PADW)
    grid = x.reshape(lead, frames, HGT, PADW, x.shape[-1])[:, :, :, :WID]
    return grid.reshape(lead, frames * HGT * WID, x.shape[-1])


def swap(x):
    return lax.ppermute(x, "head", [(0, 1), (1, 0)])


def gather_rows(x):
    half = x.shape[1]
    mine = lax.axis_index("head") * half
    both = jnp.concatenate([x, x], axis=1)
    return lax.dynamic_update_slice_in_dim(both, swap(x), half - mine, axis=1)


def taps(*kernels):
    return jnp.tile(jnp.stack(kernels), (1, 1, LH))


def on_device(
    tokens,
    ln1_gain,
    ln1_bias,
    w_qkv,
    pool_q,
    pool_k,
    pool_v,
    squeeze_k,
    squeeze_v,
    rel_t,
    rel_h,
    rel_w,
    w_proj,
    proj_bias,
    ln2_gain,
    ln2_bias,
    w_fc1,
    fc1_bias,
    w_fc2,
    fc2_bias,
    memory_valid,
    cotangent,
):
    clip_count = tokens.shape[0]
    consts = {
        "fold": jnp.asarray(fold_constants(), BF16),
        "one": jnp.asarray(one_lane(), F32),
        "own": jnp.asarray(OWN_T.T, F32),
        "ownt": jnp.asarray(OWN_T, F32),
        "lanes": jnp.asarray(head_lanes(), BF16),
        "grow": jnp.asarray(FOLD, BF16),
        "ekey": jnp.asarray(EKEY, BF16),
    }
    keys_extra = key_constants(memory_valid)
    rel_all = jnp.concatenate([rel_t, rel_h, rel_w], axis=0)
    pairs = jnp.dot(jnp.asarray(PICK), rel_all, precision=HIGHEST)
    pair_table = (pairs * HEAD_DIM**0.5).T
    table_high = pair_table.astype(BF16)
    table_rest = (pair_table - table_high.astype(F32)).astype(BF16)
    tables = jnp.stack([table_high, table_rest])
    rel_rows = pairs.T.astype(BF16)
    all_taps = taps(pool_q, pool_k, pool_v, squeeze_k, squeeze_v)

    width = tokens.shape[2]
    inputs_low = pad_rows(tokens)
    inputs = inputs_low.astype(F32)
    upstream = pad_rows(cotangent)
    real = (jnp.arange(inputs.shape[1]) % PADW < WID)[None, :, None]
    first_normed = layer_norm(inputs, ln1_gain, ln1_bias)
    first_low = jnp.where(real, first_normed, 0.0).astype(BF16)
    first_rows = []
    for clip in range(clip_count):
        one = first_low[clip : clip + 1]
        if clip:
            one = lax.optimization_barrier((one, first_rows[-1]))[0]
        first_rows.append(gather_rows(one))
    w_heads = w_qkv.transpose(1, 0, 2)
    upstream_other = swap(lax.optimization_barrier((upstream, first_rows[-1]))[0])
    pooled = ()
    for clip in range(clip_count):
        pooled = call_pool_forward(clip, clip_count, first_rows[clip], w_heads, 1, 2, all_taps, True, pooled)
    kv0, kv, kvf, mem = pooled
    before = from_behind(mem[-2:], "dp", 1)
    pooled = ()
    for clip in range(clip_count):
        pooled = call_pool_forward(clip, clip_count, first_rows[clip], w_heads, 0, 1, all_taps, False, pooled)
    q0, q = pooled
    memory = jnp.concatenate([before, mem], axis=0)
    vectors = jnp.stack([proj_bias, ln2_gain, ln2_bias])
    hidden_bias = fc1_bias.reshape(1, -1)
    rows32 = jax.ShapeDtypeStruct((HALF, width), F32)
    rows16 = jax.ShapeDtypeStruct((HALF, width), BF16)
    clips = range(clip_count)
    branch, qa, at, lse, kept, recv = [], [], [], [], [], []
    for clip in clips:
        *made, own, sent = call_attention_forward(clip, q, kv, memory, keys_extra, tables, w_proj, consts)
        for store, value in zip((branch, qa, at, lse), made):
            store.append(value)
        sent, q = lax.optimization_barrier((sent, q)) if clip + 1 < clip_count else (sent, q)
        kept.append(own)
        recv.append(swap(sent))

    def after(value, *earlier):
        return lax.optimization_barrier((value, *earlier))[0]

    middle, mine, theirs = [], [], []
    own_parts, other_parts, second = [None] * clip_count, [None] * clip_count, [None] * clip_count

    hidden_sums = []

    def through(*rows):
        made, total = call_ffn(
            [
                (mine[clip], upstream[clip], F32) if own else (theirs[clip], upstream_other[clip], BF16)
                for clip, own in rows
            ],
            w_fc1, hidden_bias, w_fc2,
        )
        hidden_sums.append(total)
        for (clip, own), part in zip(rows, made):
            if own:
                own_parts[clip] = part
            else:
                other_parts[clip] = part
                second[clip] = swap(part[2])

    for clip in clips:
        landed = after(recv[clip], own_parts[clip - 1][2]) if clip else recv[clip]
        x1, a2 = simple_call(middle_kernel, [rows32, rows16], 1, inputs_low[clip], kept[clip], landed, vectors)
        middle.append(x1)
        mine.append(a2)
        theirs.append(swap(a2))
        if clip == 0:
            through((0, True))
        else:
            through((clip, True), (clip - 1, False))
    theirs[-1] = after(theirs[-1], own_parts[-1][2])
    through((clip_count - 1, False))
    dmiddle, low, sums, rows_x, dmix = [], [], [], [], []
    parts = own_parts + other_parts
    for clip in clips:
        if clip + 1 == clip_count:
            w_fc2_grad, w_fc1_grad = call_weights(
                [p[0] for p in parts],
                [p[1] for p in parts],
                mine + theirs,
                [after(upstream[0], low[0][0])]
                + [upstream[c] for c in clips[1:]]
                + [upstream_other[c] for c in clips],
            )
        landed = after(second[clip], w_fc2_grad if clip + 1 == clip_count else other_parts[-1][2])
        dx, dx_low, total = simple_call(
            norm_back_kernel,
            [rows32, rows16, jax.ShapeDtypeStruct((HEAD_EARLY, width), F32)],
            1,
            own_parts[clip][2], landed, middle[clip], upstream[clip], vectors,
        )
        dmiddle.append(dx)
        sums.append(total)
        low.append((dx_low, swap(dx_low)))
    for clip in clips:
        received = after(low[clip][1], low[-1][0])
        rows, mix = simple_call(
            mix_kernel,
            [jax.ShapeDtypeStruct((ROWS, width), BF16), jax.ShapeDtypeStruct((ROWS, LW), BF16)],
            1,
            low[clip][0], received, w_proj,
        )
        rows_x.append(rows)
        dmix.append(mix)
    last = [lax.optimization_barrier((other_parts[c][3], dmix[-1]))[0] for c in clips]
    last = [swap(x) for x in last]
    dq, dkv, dr, chunks, w_fc2_grad = call_attention_backward(
        q, kv, memory, keys_extra, qa, dmix, at, lse, rel_rows,
        w_fc2_grad, w_fc1_grad, consts,
    )
    *last, dq = lax.optimization_barrier((*last, dq))
    output = drop_rows(
        jnp.stack(
            [
                (middle[c] + own_parts[c][3] + last[c].astype(F32) + fc2_bias).astype(BF16)
                for c in clips
            ]
        )
    )
    input_grad, w_fc1_grad, w_proj_grad, tail, small, norms = call_finish(
        dq, dkv, q0, kv0, kvf, all_taps,
        [x[0] for x in first_rows],
        rows_x,
        [b[0] for b in branch],
        w_heads,
        inputs_low,
        dmiddle,
        chunks,
        dr,
        ln1_gain.reshape(1, -1),
        sums,
        hidden_sums,
    )
    input_grad = drop_rows(input_grad)
    w_fc2_grad, w_fc1_grad, *tables = call_widen(w_fc2_grad, w_fc1_grad, small)
    total = w_fc1_grad.shape[0]
    if total != width:
        w_fc2_grad = w_fc2_grad.reshape(2, total, width)[:, :width].reshape(2 * width, width)
        w_fc1_grad, w_proj_grad, tail = w_fc1_grad[:width], w_proj_grad[:, :width], tail[:, :width]
    w_qkv_grad = tail.astype(F32).transpose(1, 0, 2)
    norms = norms[: 2 * width // 128].reshape(2, width)
    early = small[EARLY_ROW:HIDDEN_ROW].reshape(4, width)
    fc1_bias_grad = lax.dynamic_index_in_dim(
        small[HIDDEN_ROW:SMALL_ROWS].reshape(2, fc1_bias.size), lax.axis_index("head"), 0, keepdims=False
    )
    shared = [norms[0], norms[1], *tables[3:], *tables[:3]]
    shared += [early[0], early[1], early[2], early[3]]
    return (
        output,
        input_grad,
        shared[0],
        shared[1],
        w_qkv_grad,
        shared[2],
        shared[3],
        shared[4],
        shared[5],
        shared[6],
        shared[7],
        shared[8],
        shared[9],
        w_proj_grad,
        shared[10],
        shared[11],
        shared[12],
        w_fc1_grad,
        fc1_bias_grad,
        w_fc2_grad,
        shared[13],
    )


def solution(mesh):
    return jax.shard_map(
        on_device,
        mesh=mesh,
        in_specs=(
            P("dp", "head", None),
            P(),
            P(),
            P(None, None, "head"),
            P(),
            P(),
            P(),
            P(),
            P(),
            P(),
            P(),
            P(),
            P("head", None),
            P(),
            P(),
            P(),
            P(None, "head"),
            P("head"),
            P("head", None),
            P(),
            P("dp", None),
            P("dp", "head", None),
        ),
        out_specs=(
            P("dp", "head", None),
            P("dp", "head", None),
            P(),
            P(),
            P(None, None, "head"),
            P(),
            P(),
            P(),
            P(),
            P(),
            P(),
            P(),
            P(),
            P("head", None),
            P(),
            P(),
            P(),
            P(None, "head"),
            P("head"),
            P("head", None),
            P(),
        ),
        check_vma=False,
    )
```
